32 devices in a mesh: dp: 4 (over z), seq: 2 (over y), opt: 4 (over x, core).
Axes of the slice: x: 2, y: 2, z: 4, core: 2. Of those that a mesh axis runs over, the one named last changes fastest.
Arguments:
- token_ids: int32 [4, 2048], P('dp', ('seq', 'opt')), may hold values from 0 to 50303
- doc_ids: int32 [4, 2048], P('dp', ('seq', 'opt')), may hold values from 0 to 2, as said below
- embed: bfloat16 [50304, 512], P(None, ('seq', 'opt')), may hold values from -6 to 6
- norm_gains: float32 [2, 512], replicated, may hold values from 0.5 to 1.5
- norm_shifts: float32 [2, 512], replicated, may hold values from -1 to 1
- qkv_weight: bfloat16 [512, 1536], replicated, may hold values from -0.25 to 0.25
- out_weight: bfloat16 [512, 512], replicated, may hold values from -0.5 to 0.5
- up_weight: bfloat16 [512, 2048], replicated, may hold values from -0.25 to 0.25
- down_weight: bfloat16 [2048, 512], replicated, may hold values from -0.125 to 0.125
- proj_biases: float32 [4608], replicated, may hold values from -0.6 to 0.6
- enc_weight: float32 [32768, 512], P(('dp', 'seq', 'opt')), may hold values from -0.0625 to 0.0625
- dec_weight: float32 [32768, 512], P(('dp', 'seq', 'opt')), may hold values from -0.53033009 to 0.53033009
- enc_bias: float32 [32768], P(('dp', 'seq', 'opt')), may hold values from -1 to 1
- dec_bias: float32 [512], replicated, may hold values from -1.5 to 1.5
- enc_first: float32 [32768, 512], P(('dp', 'seq', 'opt')), may hold values from -3.45267e-05 to 3.45267e-05, as said below
- enc_second: float32 [32768, 512], P(('dp', 'seq', 'opt')), may hold values from 1.4901162e-11 to 2.384186e-10
- dec_first: float32 [32768, 512], P(('dp', 'seq', 'opt')), may hold values from -3.45267e-05 to 3.45267e-05, as said below
- dec_second: float32 [32768, 512], P(('dp', 'seq', 'opt')), may hold values from 1.4901162e-11 to 2.384186e-10
- enc_bias_first: float32 [32768], P(('dp', 'seq', 'opt')), may hold values from -0.0001381068 to 0.0001381068, as said below
- enc_bias_second: float32 [32768], P(('dp', 'seq', 'opt')), may hold values from 2.384186e-10 to 3.8146974e-09
- dec_bias_first: float32 [512], replicated, may hold values from -0.0001381068 to 0.0001381068, as said below
- dec_bias_second: float32 [512], replicated, may hold values from 2.384186e-10 to 3.8146974e-09
Outputs:
- enc_weight_new: float32 [32768, 512], P(('dp', 'seq', 'opt'))
- enc_first_new: float32 [32768, 512], P(('dp', 'seq', 'opt'))
- enc_second_new: float32 [32768, 512], P(('dp', 'seq', 'opt'))
- dec_weight_new: float32 [32768, 512], P(('dp', 'seq', 'opt'))
- dec_first_new: float32 [32768, 512], P(('dp', 'seq', 'opt'))
- dec_second_new: float32 [32768, 512], P(('dp', 'seq', 'opt'))
- enc_bias_new: float32 [32768], P(('dp', 'seq', 'opt'))
- enc_bias_first_new: float32 [32768], P(('dp', 'seq', 'opt'))
- enc_bias_second_new: float32 [32768], P(('dp', 'seq', 'opt'))
- dec_bias_new: float32 [512], replicated
- dec_bias_first_new: float32 [512], replicated
- dec_bias_second_new: float32 [512], replicated
- grad_norm: float32 [], replicated
- loss_sum: float32 [], replicated
The draws below stay inside these ranges and needn't reach their ends.
Inputs may be any that keep to these rules, and one draw needn't show every extreme that they name: `doc_ids`: document numbers never fall along a context; each context holds three documents, and its middle one begins at a position from 1 to 128 and has its last position between 1919 and 2046. `enc_first`: no entry is zero. `dec_first`: no entry is zero. `enc_bias_first`: no entry is zero. `dec_bias_first`: no entry is zero.
All inputs are finite; a program needn't handle non-finite values.
Results may differ from the reference program's by a relative error of at most 0.004.
Values may be sent and summed in bfloat16 or wider, within the bound.
A program may use at most 576 MiB of HBM per device.

```python
import math
import jax
import jax.numpy as jnp
import numpy as np
from jax import lax

D = 512
HEADS = 8
HEAD = 64
ROT = 16
FF = 2048
VOCAB = 50304
DICT = 32768
CTX_LEN = 2048
STEP = 4
RAMP = 80
CONTEXTS = 4


def signed_draw(key, shape, magnitude_scale):
    key_size, key_sign = jax.random.split(key)
    magnitude = jnp.exp(jax.random.uniform(key_size, shape, jnp.float32, jnp.log(0.05), jnp.log(0.2)))
    signs = 2.0 * jax.random.randint(key_sign, shape, 0, 2).astype(jnp.float32) - 1.0
    return magnitude * signs * magnitude_scale


def draw_enc_first(key, part):
    key = jax.random.fold_in(key, 3)
    return signed_draw(key, (DICT, D), (2.0 * DICT * D) ** (-0.5))


def draw_dec_first(key, part):
    key = jax.random.fold_in(key, 4)
    return signed_draw(key, (DICT, D), (2.0 * DICT * D) ** (-0.5))


def draw_enc_bias_first(key, part):
    key = jax.random.fold_in(key, 6)
    return signed_draw(key, (DICT,), 4.0 * (2.0 * DICT * D) ** (-0.5))


def draw_dec_bias_first(key, part):
    key = jax.random.fold_in(key, 7)
    return signed_draw(key, (D,), 4.0 * (2.0 * DICT * D) ** (-0.5))


def draw_dec_weight(key, part):
    key = jax.random.fold_in(key, 5)
    placement = jnp.arange(DICT, dtype=jnp.float32) / DICT
    base = jax.random.truncated_normal(key, -4.0, 4.0, (DICT, D), jnp.float32)
    rising = 1.0 + 2.0 * placement
    return base * rising[:, None] / jnp.sqrt(float(D))


def draw_doc_ids(key, part):
    key = jax.random.fold_in(key, 11)
    key_start, key_end = jax.random.split(key)
    opening = jax.random.randint(key_start, (CONTEXTS, 1), 1, CTX_LEN // 16 + 1)
    closing = jax.random.randint(key_end, (CONTEXTS, 1), CTX_LEN - CTX_LEN // 16, CTX_LEN)
    places = jnp.arange(CTX_LEN, dtype=jnp.int32)[None, :]
    return (places >= opening).astype(jnp.int32) + (places >= closing).astype(jnp.int32)


def plant(values, own_key, least, high):
    extent = values.shape
    index_at = [jax.random.randint(jax.random.fold_in(own_key, axis), (), 0, extent[axis]) for axis in range(len(extent))]
    values = values.at[tuple(index_at)].set(least)
    longest = extent.index(max(extent))
    index_at[longest] = (index_at[longest] + 1) % extent[longest]
    return values.at[tuple(index_at)].set(high)


def levels(stream_key, dims, cuts, smallest, high):
    loudness = 1.0
    for position, shards_of in cuts:
        steps = jax.random.uniform(jax.random.fold_in(jax.random.fold_in(stream_key, 6), position), (shards_of,), jnp.float32, smallest / len(cuts), high / len(cuts))
        loudness = loudness * jnp.repeat(jnp.exp(steps), dims[position] // shards_of).reshape((-1,) + (1,) * (len(dims) - 1 - position))
    return loudness


def rank_bounds(count, skew):
    portions = [(1 << 20) // math.isqrt(standing ** skew) + 1 for standing in range(1, count + 1)]
    deviation = 1 + sum(portions) // (1 << 30)
    return np.cumsum(np.array([max(1, weight // deviation) for weight in portions]))


def ranked_ids(stream_key, shape, number_of, lean):
    table = rank_bounds(number_of, lean)
    pick = jax.random.randint(jax.random.fold_in(stream_key, 1), shape, 0, int(table[number_of - 1]))
    rank = jnp.searchsorted(jnp.asarray(table, jnp.int32), pick, side="right")
    return jax.random.permutation(jax.random.fold_in(stream_key, 2), number_of)[rank].astype(jnp.int32)


def normal_values(key, dims, width, bound, cuts=(), held_as=jnp.bfloat16):
    array = width * jax.random.normal(key, dims, jnp.float32)
    if cuts:
        array = array * levels(key, dims, cuts, -0.22, 0.18)
    return jnp.clip(array, -bound, bound).astype(held_as)


def setup_inputs(seed: int = 0) -> dict:
    streams_of = jax.random.split(jax.random.key(seed), 23)
    return {
        "token_ids": plant(ranked_ids(streams_of[0], (CONTEXTS, CTX_LEN), VOCAB, 2), jax.random.fold_in(streams_of[0], 3), 0, VOCAB - 1).astype(jnp.int32),
        "doc_ids": draw_doc_ids(jax.random.fold_in(streams_of[22], 71), 0),
        "embed": normal_values(streams_of[2], (VOCAB, D), 1.0, 6.0, ((1, 8),)),
        "norm_gains": jnp.clip(1.0 + 0.1 * jax.random.normal(streams_of[3], (2, D), jnp.float32), 0.5, 1.5),
        "norm_shifts": normal_values(streams_of[4], (2, D), 0.2, 1.0, (), jnp.float32),
        "qkv_weight": normal_values(streams_of[5], (D, 3 * D), D ** -0.5, 0.25),
        "out_weight": normal_values(streams_of[6], (D, D), (D // 4) ** -0.5, 0.5),
        "up_weight": normal_values(streams_of[7], (D, FF), D ** -0.5, 0.25),
        "down_weight": normal_values(streams_of[8], (FF, D), FF ** -0.5, 0.125),
        "proj_biases": normal_values(streams_of[9], (5 * D + FF,), 0.1, 0.6, (), jnp.float32),
        "enc_weight": normal_values(streams_of[10], (DICT, D), (20 * D) ** -0.5, 0.0625, ((0, 32),), jnp.float32),
        "dec_weight": draw_dec_weight(jax.random.fold_in(streams_of[22], 71), 0),
        "enc_bias": normal_values(streams_of[12], (DICT,), 0.2, 1.0, ((0, 32),), jnp.float32),
        "dec_bias": normal_values(streams_of[13], (D,), 0.3, 1.5, (), jnp.float32),
        "enc_first": draw_enc_first(jax.random.fold_in(streams_of[22], 71), 0),
        "enc_second": jnp.clip(jnp.exp(math.log(2.3841859042583735e-10) - 2.7725887 * jax.random.uniform(streams_of[15], (DICT, D), jnp.float32) ** levels(streams_of[15], (DICT, D), ((0, 32),), -0.2, 0.2)), 1.4901161901614834e-11, 2.3841859042583735e-10),
        "dec_first": draw_dec_first(jax.random.fold_in(streams_of[22], 71), 0),
        "dec_second": jnp.clip(jnp.exp(math.log(2.3841859042583735e-10) - 2.7725887 * jax.random.uniform(streams_of[17], (DICT, D), jnp.float32) ** levels(streams_of[17], (DICT, D), ((0, 32),), -0.2, 0.2)), 1.4901161901614834e-11, 2.3841859042583735e-10),
        "enc_bias_first": draw_enc_bias_first(jax.random.fold_in(streams_of[22], 71), 0),
        "enc_bias_second": jnp.clip(jnp.exp(math.log(3.814697446813398e-09) - 2.7725887 * jax.random.uniform(streams_of[19], (DICT,), jnp.float32) ** levels(streams_of[19], (DICT,), ((0, 32),), -0.2, 0.2)), 2.3841859042583735e-10, 3.814697446813398e-09),
        "dec_bias_first": draw_dec_bias_first(jax.random.fold_in(streams_of[22], 71), 0),
        "dec_bias_second": jnp.clip(jnp.exp(jax.random.uniform(streams_of[21], (D,), jnp.float32, math.log(2.3841859042583735e-10), math.log(3.814697446813398e-09))), 2.3841859042583735e-10, 3.814697446813398e-09),
    }


LAYER_EPSILON = 1e-05
NORM_EPSILON = 1e-08
BETA_FIRST = 0.9
BETA_SECOND = 0.999
ADAM_EPSILON = 1e-08
RATE_MATRIX = 0.02
RATE_BIAS = 0.1
WEIGHT_DECAY = 0.01
CLIP_NORM = 1.0
SPARSITY_TOP = 5.0

@jax.custom_vjp
def low(v):
    return lax.optimization_barrier(v.astype(jnp.bfloat16)).astype(jnp.float32)

@jax.custom_vjp
def low_back(v):
    return v

def low_keep(v):
    return (low(v), None)

def low_pass(kept, grad):
    return (grad,)

def back_keep(v):
    return (v, None)

def back_low(kept, grad):
    return (low(grad),)
low.defvjp(low_keep, low_pass)
low_back.defvjp(back_keep, back_low)

def exact_dot(left, right):
    return jnp.dot(left, right, precision=lax.Precision.HIGHEST, preferred_element_type=jnp.float32)

def layer_norm(values, gains, shifts):
    center = values - lax.optimization_barrier(jnp.mean(values, axis=-1, keepdims=True))
    variance = lax.optimization_barrier(jnp.mean(center * center, axis=-1, keepdims=True))
    return center * lax.rsqrt(variance + LAYER_EPSILON) * gains + shifts

def rotate(values, positions):
    half_rot = ROT // 2
    frequency = 10000.0 ** (-2.0 * jnp.arange(half_rot, dtype=jnp.float32) / ROT)
    angles = positions.astype(jnp.float32)[:, None] * frequency[None, :]
    cosine_vals = jnp.cos(angles)[:, None, :]
    sine_vals = jnp.sin(angles)[:, None, :]
    first_half = values[..., :half_rot]
    second_half = values[..., half_rot:ROT]
    return jnp.concatenate([first_half * cosine_vals - second_half * sine_vals, second_half * cosine_vals + first_half * sine_vals, values[..., ROT:]], axis=-1)

def adam_step(parameter, moment_one, moment_two, gradient, clip_scale, step_rate, decay_rate):
    gradient = gradient * clip_scale
    moment_one = BETA_FIRST * moment_one + (1.0 - BETA_FIRST) * gradient
    moment_two = BETA_SECOND * moment_two + (1.0 - BETA_SECOND) * gradient * gradient
    adjust = moment_one / (1.0 - BETA_FIRST ** STEP) / (jnp.sqrt(moment_two / (1.0 - BETA_SECOND ** STEP)) + ADAM_EPSILON)
    return (parameter - step_rate * (adjust + decay_rate * parameter), moment_one, moment_two)

def reference(token_ids, doc_ids, embed, norm_gains, norm_shifts, qkv_weight, out_weight, up_weight, down_weight, proj_biases, enc_weight, dec_weight, enc_bias, dec_bias, enc_first, enc_second, dec_first, dec_second, enc_bias_first, enc_bias_second, dec_bias_first, dec_bias_second):
    table = embed.astype(jnp.float32)
    qkv_full = qkv_weight.astype(jnp.float32)
    out_full = out_weight.astype(jnp.float32)
    up_full = up_weight.astype(jnp.float32)
    down_full = down_weight.astype(jnp.float32)
    positions = jnp.arange(CTX_LEN)

    def context(pair):
        token_row, doc_row = pair
        residual = jnp.take(table, token_row, axis=0)
        first_norm = low(layer_norm(residual, norm_gains[0], norm_shifts[0]))
        qkv_proj = exact_dot(first_norm, qkv_full) + proj_biases[:3 * D]
        queries = low(rotate(qkv_proj[:, :D].reshape(CTX_LEN, HEADS, HEAD), positions))
        keys = low(rotate(qkv_proj[:, D:2 * D].reshape(CTX_LEN, HEADS, HEAD), positions))
        values = low(qkv_proj[:, 2 * D:].reshape(CTX_LEN, HEADS, HEAD))
        scores = jnp.einsum('qhe,khe->hqk', queries, keys, precision=lax.Precision.HIGHEST) * HEAD ** (-0.5)
        allowed = (positions[None, :] <= positions[:, None]) & (doc_row[:, None] == doc_row[None, :])
        scores = jnp.where(allowed[None], scores, -1e+30)
        attn_probs = low(jax.nn.softmax(scores, axis=-1))
        mixed_heads = low(jnp.einsum('hqk,khe->qhe', attn_probs, values, precision=lax.Precision.HIGHEST).reshape(CTX_LEN, D))
        attn_out = exact_dot(mixed_heads, out_full) + proj_biases[3 * D:4 * D]
        second_norm = low(layer_norm(residual, norm_gains[1], norm_shifts[1]))
        hidden = low(jax.nn.gelu(exact_dot(second_norm, up_full) + proj_biases[4 * D:4 * D + FF], approximate=False))
        return residual + attn_out + exact_dot(hidden, down_full) + proj_biases[4 * D + FF:]
    stream = lax.map(context, (token_ids, doc_ids))
    stream_low = low(stream)
    coefficient = SPARSITY_TOP * min(1.0, STEP / RAMP)

    def loss_of(params):
        enc_full, dec_full, enc_shift, dec_shift = params
        enc_low = low(enc_full)
        dec_low = low(dec_full)
        norms = jnp.sqrt(lax.optimization_barrier(jnp.sum(dec_low * dec_low, axis=1)) + NORM_EPSILON)

        def block(running, block_rows):
            inputs_low, target = block_rows
            pre_act = low_back(exact_dot(inputs_low, enc_low.T) + enc_shift)
            activ = jnp.square(jax.nn.relu(pre_act))
            recon = low_back(exact_dot(low(activ), dec_low) + dec_shift)
            error = recon - target
            return (running + jnp.sum(error * error) + coefficient * jnp.sum(activ * norms[None, :]), None)
        total, _ = lax.scan(jax.checkpoint(block), jnp.zeros((), jnp.float32), (stream_low, stream))
        return total
    loss_sum, pullback = jax.vjp(loss_of, (enc_weight, dec_weight, enc_bias, dec_bias))
    (enc_grad, dec_grad, enc_bias_grad, dec_bias_grad), = pullback(jnp.ones((), jnp.float32))
    squares = jnp.sum(enc_grad * enc_grad) + jnp.sum(dec_grad * dec_grad)
    squares = squares + jnp.sum(enc_bias_grad * enc_bias_grad) + jnp.sum(dec_bias_grad * dec_bias_grad)
    grad_norm = jnp.sqrt(squares)
    clip_scale = jnp.minimum(1.0, CLIP_NORM / (grad_norm + 1e-06))
    enc_new, enc_one, enc_two = adam_step(enc_weight, enc_first, enc_second, enc_grad, clip_scale, RATE_MATRIX, WEIGHT_DECAY)
    dec_new, dec_one, dec_two = adam_step(dec_weight, dec_first, dec_second, dec_grad, clip_scale, RATE_MATRIX, WEIGHT_DECAY)
    dec_new = dec_new * lax.rsqrt(lax.optimization_barrier(jnp.sum(dec_new * dec_new, axis=1, keepdims=True)) + NORM_EPSILON)
    eb_new, eb_one, eb_two = adam_step(enc_bias, enc_bias_first, enc_bias_second, enc_bias_grad, clip_scale, RATE_BIAS, 0.0)
    db_new, db_one, db_two = adam_step(dec_bias, dec_bias_first, dec_bias_second, dec_bias_grad, clip_scale, RATE_BIAS, 0.0)
    return (enc_new, enc_one, enc_two, dec_new, dec_one, dec_two, eb_new, eb_one, eb_two, db_new, db_one, db_two, grad_norm, loss_sum)
```

```python
import functools

import jax
import jax.numpy as jnp
from jax import lax
from jax.experimental import pallas as pl
from jax.experimental.pallas import tpu as pltpu
from jax.sharding import PartitionSpec as P

HEADS = 8
HEAD = 64
ROT = 16
STEP = 4
RAMP = 80


LAYER_EPSILON = 1e-05
NORM_EPSILON = 1e-08
BETA_FIRST = 0.9
BETA_SECOND = 0.999
ADAM_EPSILON = 1e-08
RATE_MATRIX = 0.02
RATE_BIAS = 0.1
WEIGHT_DECAY = 0.01
CLIP_NORM = 1.0
SPARSITY_TOP = 5.0
COEFFICIENT = SPARSITY_TOP * min(1.0, STEP / RAMP)
LAST_LAST = (((1,), (1,)), ((), ()))
MESH = pl.DeviceIdType.MESH
ANY = pl.BlockSpec(memory_space=pl.ANY)
VMEM = pl.BlockSpec(memory_space=pltpu.VMEM)
LANES = 128


def layer_norm(values, gains, shifts):
    center = values - jnp.mean(values, axis=-1, keepdims=True)
    variance = jnp.mean(center * center, axis=-1, keepdims=True)
    return center * lax.rsqrt(variance + LAYER_EPSILON) * gains + shifts


def rotate(values, positions):
    half_rot = ROT // 2
    frequency = 10000.0 ** (-2.0 * jnp.arange(half_rot, dtype=jnp.float32) / ROT)
    angles = positions.astype(jnp.float32)[:, None] * frequency[None, :]
    cosine_vals = jnp.cos(angles)[:, None, :]
    sine_vals = jnp.sin(angles)[:, None, :]
    first_half = values[..., :half_rot]
    second_half = values[..., half_rot:ROT]
    return jnp.concatenate(
        [
            first_half * cosine_vals - second_half * sine_vals,
            second_half * cosine_vals + first_half * sine_vals,
            values[..., ROT:],
        ],
        axis=-1,
    )


def row_norms(matrix_low):
    return jnp.sqrt(jnp.sum(jnp.square(matrix_low.astype(jnp.float32)), axis=1) + NORM_EPSILON)


def adam_step(parameter, moment_one, moment_two, gradient, clip_scale, step_rate, decay_rate):
    gradient = gradient * clip_scale
    moment_one = BETA_FIRST * moment_one + (1.0 - BETA_FIRST) * gradient
    moment_two = BETA_SECOND * moment_two + (1.0 - BETA_SECOND) * gradient * gradient
    adjust = (
        moment_one
        / (1.0 - BETA_FIRST**STEP)
        / (jnp.sqrt(moment_two / (1.0 - BETA_SECOND**STEP)) + ADAM_EPSILON)
    )
    return (parameter - step_rate * (adjust + decay_rate * parameter), moment_one, moment_two)


def exclusive_or(left, right, size):
    total, bit = 0, 1
    while bit < size:
        total = total + ((left // bit + right // bit) % 2) * bit
        bit *= 2
    return total


def peers(depth):
    layer, row, column = lax.axis_index("dp"), lax.axis_index("seq"), lax.axis_index("opt")
    along = [(exclusive_or(layer, step, depth), row, column) for step in range(depth)]
    across = (layer, row, (column + 2) % 4)
    beside = (layer, 1 - row, column)
    partner = (layer, row, column + 1 - 2 * (column % 2))
    return along, across, beside, partner


def remote(source, target, send, receive, device):
    return pltpu.make_async_remote_copy(
        src_ref=source,
        dst_ref=target,
        send_sem=send,
        recv_sem=receive,
        device_id=device,
        device_id_type=MESH,
    )


def greet(devices):
    barrier = pltpu.get_barrier_semaphore()
    for device in devices:
        pl.semaphore_signal(barrier, inc=1, device_id=device, device_id_type=MESH)
    pl.semaphore_wait(barrier, len(devices))


class Gather:
    def __init__(self, depth, rows, held, send, receive, where):
        self.depth, self.rows, self.held = depth, rows, held
        self.send, self.receive = send, receive
        self.along, self.across, self.beside, _ = where

    def block(self, step, column, part=None):
        first, rows = column * self.rows, self.rows
        if part is not None:
            rows = self.rows // 2
            first = first + part * rows
        return self.held.at[step, pl.ds(first, rows)]

    def copy_along(self, step):
        return remote(
            self.block(0, 0), self.block(step, 0), self.send.at[0, step], self.receive.at[0, step], self.along[step]
        )

    def copy_across(self, step):
        return remote(
            self.block(step, 0), self.block(step, 1), self.send.at[1, step], self.receive.at[1, step], self.across
        )

    def copy_beside(self, step):
        return remote(
            self.block(step, 0), self.block(step, 2), self.send.at[2, step], self.receive.at[2, step], self.beside
        )

    def pass_across(self, step):
        return remote(
            self.block(step, 2, 0), self.block(step, 3, 0), self.send.at[3, step], self.receive.at[3, step], self.across
        )

    def pass_beside(self, step):
        return remote(
            self.block(step, 1, 1), self.block(step, 3, 1), self.send.at[4, step], self.receive.at[4, step], self.beside
        )

    def wait_along(self, step):
        remote(
            self.block(0, 0), self.block(step, 0), self.send.at[0, step], self.receive.at[0, step], self.along[0]
        ).wait_recv()

    def open(self):
        self.copy_across(0).start()
        self.copy_beside(0).start()
        for step in range(1, self.depth):
            self.copy_along(step).start()

    def spread(self, step):
        self.wait_along(step)
        self.copy_across(step).start()
        self.copy_beside(step).start()

    def hand_on(self, step):
        self.copy_across(step).wait_recv()
        self.pass_beside(step).start()
        self.copy_beside(step).wait_recv()
        self.pass_across(step).start()

    def wait_diagonal(self, step):
        self.pass_across(step).wait_recv()
        self.pass_beside(step).wait_recv()

    def close(self):
        for step in range(1, self.depth):
            self.copy_along(step).wait_send()

        def done(step, carry):
            self.copy_across(step).wait_send()
            self.copy_beside(step).wait_send()
            self.pass_across(step).wait_send()
            self.pass_beside(step).wait_send()
            return carry

        lax.fori_loop(0, self.depth, done, 0)


def forward_kernel(
    depth,
    own_ref,
    enc_ref,
    dec_ref,
    bias_ref,
    gathered_ref,
    relu_ref,
    recon_ref,
    total_ref,
    held,
    enc,
    dec,
    bias,
    staged,
    parts,
    send_one,
    send_two,
    send_three,
    got_one,
    got_two,
    got_three,
    load_sem,
    relu_sem,
    held_sem,
    send,
    receive,
    sum_send,
    sum_receive,
):
    rows = own_ref.shape[0]
    entries = enc.shape[0]
    width = held.shape[2]
    half = width // 2
    piece = min(entries, 1024)
    where = peers(depth)
    along, across, beside, _ = where
    loads = [
        pltpu.make_async_copy(own_ref, held.at[0, pl.ds(0, rows)], load_sem.at[0]),
        pltpu.make_async_copy(enc_ref, enc, load_sem.at[1]),
        pltpu.make_async_copy(bias_ref, bias, load_sem.at[2]),
        pltpu.make_async_copy(dec_ref, dec, load_sem.at[3]),
    ]
    for load in loads:
        load.start()
    greet(along[1:] + [across, beside])
    loads[0].wait()
    gather = Gather(depth, rows, held, send, receive, where)
    gather.open()
    total_ref[...] = jnp.zeros_like(total_ref)
    for load in loads[1:]:
        load.wait()

    def copy_one(step, part):
        source = send_one.at[step % 2, pl.ds(part * half, half)]
        device = beside if part else across
        return remote(source, got_one.at[part, step], sum_send.at[part, step], sum_receive.at[part, step], device)

    def copy_two(step, part):
        device = beside if part else across
        return remote(
            send_two.at[part, step % 2],
            got_two.at[part, step],
            sum_send.at[2 + part, step],
            sum_receive.at[2 + part, step],
            device,
        )

    def copy_three(step, device):
        return remote(
            send_three.at[step], got_three.at[step], sum_send.at[4, step], sum_receive.at[4, step], device
        )

    def copy_relu(order):
        step, column = order // 4, order % 4
        return pltpu.make_async_copy(
            staged.at[order % 2],
            relu_ref.at[step, :, pl.ds(pl.multiple_of(column * rows, rows), rows)],
            relu_sem.at[order % 2],
        )

    def copy_held(step):
        return pltpu.make_async_copy(held.at[step], gathered_ref.at[step], held_sem.at[step])

    def sum_two(step):
        copy_one(step, 0).wait_recv()
        copy_one(step, 1).wait_recv()

        @pl.when(step >= 2)
        def _():
            copy_two(step - 2, 0).wait_send()
            copy_two(step - 2, 1).wait_send()

        slot = step % 3
        upper, lower = pl.ds(0, half), pl.ds(half, half)
        send_two[1, step % 2, upper] = (parts[2, slot, upper] + got_one[0, step].astype(jnp.float32)).astype(
            jnp.bfloat16
        )
        send_two[1, step % 2, lower] = parts[2, slot, lower].astype(jnp.bfloat16)
        copy_two(step, 1).start()
        send_two[0, step % 2, upper] = parts[1, slot, upper].astype(jnp.bfloat16)
        send_two[0, step % 2, lower] = (parts[1, slot, lower] + got_one[1, step].astype(jnp.float32)).astype(
            jnp.bfloat16
        )
        copy_two(step, 0).start()

    def column_sum(step):
        copy_two(step, 0).wait_recv()
        copy_two(step, 1).wait_recv()
        return parts[0, step % 3] + got_two[0, step].astype(jnp.float32) + got_two[1, step].astype(jnp.float32)

    def sum_three(step):
        value = column_sum(step)

        @pl.when(step == 0)
        def _():
            recon_ref[...] = value

        @pl.when(step > 0)
        def _():
            send_three[step] = value.astype(jnp.bfloat16)
            layer = lax.axis_index("dp")
            target = (exclusive_or(layer, step, depth), along[0][1], along[0][2])
            copy_three(step, target).start()

    def one_block(order, carry):
        step, column = order // 4, order % 4

        @pl.when(column == 1)
        def _():
            gather.hand_on(step)

        @pl.when(column == 3)
        def _():
            gather.wait_diagonal(step)
            copy_held(step).start()

        @pl.when(order >= 2)
        def _():
            copy_relu(order - 2).wait()

        block = held[step, pl.ds(pl.multiple_of(column * rows, rows), rows)]
        recon = None
        for first in range(0, entries, piece):
            span = pl.ds(first, piece)
            shift = bias[span]
            pre = lax.dot_general(enc[span], block, LAST_LAST, preferred_element_type=jnp.float32)
            positive = jnp.maximum(pre + jnp.concatenate([shift] * (rows // LANES), axis=1), 0.0)
            staged[order % 2, span] = positive
            active = positive * positive
            folded = active[:, :LANES]
            for lane in range(LANES, rows, LANES):
                folded = folded + active[:, lane : lane + LANES]
            total_ref[span] += folded
            term = jnp.dot(dec[:, first : first + piece], active.astype(jnp.bfloat16), preferred_element_type=jnp.float32)
            recon = term if recon is None else recon + term
        copy_relu(order).start()

        @pl.when(column < 3)
        def _():
            parts[column, step % 3] = recon

        @pl.when(column == 3)
        def _():
            @pl.when(step >= 2)
            def _():
                copy_one(step - 2, 0).wait_send()
                copy_one(step - 2, 1).wait_send()

            send_one[step % 2] = recon.astype(jnp.bfloat16)
            copy_one(step, 0).start()
            copy_one(step, 1).start()

            @pl.when(step >= 1)
            def _():
                sum_two(step - 1)

        @pl.when((column == 0) & (step + 1 < depth))
        def _():
            gather.spread(step + 1)

        @pl.when((column == 2) & (step >= 2))
        def _():
            sum_three(step - 2)

        return carry

    lax.fori_loop(0, 4 * depth, one_block, 0)
    sum_two(depth - 1)
    if depth >= 2:
        sum_three(depth - 2)
    sum_three(depth - 1)
    for step in range(1, depth):
        copy_three(step, along[step]).wait_recv()
        recon_ref[...] += got_three[step].astype(jnp.float32)
    gather.close()
    for step in range(max(depth - 2, 0), depth):
        for part in range(2):
            copy_one(step, part).wait_send()
            copy_two(step, part).wait_send()
    for step in range(1, depth):
        copy_three(step, along[step]).wait_send()
    copy_relu(4 * depth - 2).wait()
    copy_relu(4 * depth - 1).wait()
    for step in range(depth):
        copy_held(step).wait()


def forward(depth, own, enc, dec_turned, bias):
    rows, width = own.shape
    entries = enc.shape[0]
    bf16, f32 = jnp.bfloat16, jnp.float32
    dma = pltpu.SemaphoreType.DMA
    return pl.pallas_call(
        functools.partial(forward_kernel, depth),
        out_shape=(
            jax.ShapeDtypeStruct((depth, 4 * rows, width), bf16),
            jax.ShapeDtypeStruct((depth, entries, 4 * rows), f32),
            jax.ShapeDtypeStruct((width, rows), f32),
            jax.ShapeDtypeStruct((entries, LANES), f32),
        ),
        in_specs=[ANY] * 4,
        out_specs=(ANY, ANY, VMEM, VMEM),
        scratch_shapes=[
            pltpu.VMEM((depth, 4 * rows, width), bf16),
            pltpu.VMEM((entries, width), bf16),
            pltpu.VMEM((width, entries), bf16),
            pltpu.VMEM((entries, LANES), f32),
            pltpu.VMEM((2, entries, rows), f32),
            pltpu.VMEM((3, 3, width, rows), f32),
            pltpu.VMEM((2, width, rows), bf16),
            pltpu.VMEM((2, 2, width, rows), bf16),
            pltpu.VMEM((depth, width, rows), bf16),
            pltpu.VMEM((2, depth, width // 2, rows), bf16),
            pltpu.VMEM((2, depth, width, rows), bf16),
            pltpu.VMEM((depth, width, rows), bf16),
            dma((4,)),
            dma((2,)),
            dma((depth,)),
            dma((5, depth)),
            dma((5, depth)),
            dma((5, depth)),
            dma((5, depth)),
        ],
        compiler_params=pltpu.CompilerParams(
            collective_id=0, has_side_effects=True, vmem_limit_bytes=60 * 2**20
        ),
        cost_estimate=pl.CostEstimate(
            flops=16 * depth * rows * entries * width, bytes_accessed=16 * depth * rows * entries, transcendentals=0
        ),
        name="forward_blocks",
    )(own, enc, dec_turned, bias)


def backward_kernel(
    depth,
    everyone,
    own_ref,
    gathered_ref,
    relu_ref,
    dec_ref,
    scale_ref,
    share_ref,
    active_ref,
    small_ref,
    enc_out,
    dec_out,
    bias_out,
    small_out,
    squares_out,
    held,
    inputs,
    dec,
    scale,
    tile,
    enc_sum,
    dec_sum,
    bias_sum,
    enc_got,
    dec_got,
    bias_got,
    active,
    active_got,
    share,
    small,
    small_got,
    squares,
    squares_got,
    load_sem,
    tile_sem,
    store_sem,
    send,
    receive,
    pair_send,
    pair_receive,
    all_send,
    all_receive,
):
    rows = own_ref.shape[0]
    entries = dec.shape[0]
    mine = entries // 2
    piece = tile.shape[1]
    tiles = entries // piece
    where = peers(depth)
    along, across, beside, partner = where
    layer, row, column = along[0]
    core = column % 2
    loads = [
        pltpu.make_async_copy(own_ref, held.at[0, pl.ds(0, rows)], load_sem.at[0]),
        pltpu.make_async_copy(dec_ref, dec, load_sem.at[1]),
        pltpu.make_async_copy(scale_ref, scale, load_sem.at[2]),
        pltpu.make_async_copy(gathered_ref, inputs, load_sem.at[3]),
        pltpu.make_async_copy(active_ref, active, load_sem.at[4]),
        pltpu.make_async_copy(small_ref, small, load_sem.at[5]),
        pltpu.make_async_copy(share_ref, share, load_sem.at[6]),
    ]
    for load in loads:
        load.start()

    def place(turn):
        return (turn + (1 - core) * (tiles // 2)) % tiles

    def copy_tile(order):
        first = pl.multiple_of(place(order % tiles) * piece, piece)
        return pltpu.make_async_copy(
            relu_ref.at[order // tiles, pl.ds(first, piece)], tile.at[order % 2], tile_sem.at[order % 2]
        )

    copy_tile(0).start()

    others = [
        ((layer + dz) % depth, (row + dy) % 2, (column + dx) % 4)
        for dz in range(depth)
        for dy in range(2)
        for dx in range(4)
    ][1:]
    greet(others)
    loads[0].wait()
    gather = Gather(depth, rows, held, send, receive, where)
    gather.open()
    for load in loads[1:]:
        load.wait()

    def small_copy(index):
        return remote(
            small, small_got.at[index], all_send.at[0, index], all_receive.at[0, index], others[index - 1]
        )

    def squares_copy(index):
        return remote(
            squares, squares_got.at[index], all_send.at[1, index], all_receive.at[1, index], others[index - 1]
        )

    for index in range(1, everyone):
        small_copy(index).start()

    theirs = (1 - core) * mine
    active_copy = remote(
        active.at[pl.ds(pl.multiple_of(theirs, mine), mine)], active_got, pair_send.at[3, 0], pair_receive.at[3, 0], partner
    )
    active_copy.start()
    enc_sum[...] = jnp.zeros_like(enc_sum)
    dec_sum[...] = jnp.zeros_like(dec_sum)
    bias_sum[...] = jnp.zeros_like(bias_sum)

    def pair_copy(kind, turn):
        source, target = ((enc_sum, enc_got), (dec_sum, dec_got), (bias_sum, bias_got))[kind]
        first = pl.multiple_of(theirs + turn * piece, piece)
        return remote(
            source.at[pl.ds(first, piece)],
            target.at[pl.ds(pl.multiple_of(turn * piece, piece), piece)],
            pair_send.at[kind, turn],
            pair_receive.at[kind, turn],
            partner,
        )

    def prepare(step):
        gather.hand_on(step)

    if depth > 1:
        gather.spread(1)
    prepare(0)

    def one_tile(order, carry):
        step, turn = order // tiles, order % tiles

        @pl.when(order + 1 < depth * tiles)
        def _():
            copy_tile(order + 1).start()

        @pl.when(turn == 0)
        def _():
            gather.wait_diagonal(step)

        copy_tile(order).wait()
        span = pl.ds(pl.multiple_of(place(turn) * piece, piece), piece)
        upstream = held[step]
        back = lax.dot_general(dec[span], upstream, LAST_LAST, preferred_element_type=jnp.float32)
        positive = tile[order % 2]
        shift = jnp.concatenate([scale[span]] * (4 * rows // LANES), axis=1)
        slope = ((back + shift) * (2.0 * positive)).astype(jnp.bfloat16)
        act_low = (positive * positive).astype(jnp.bfloat16)
        wide = slope.astype(jnp.float32)
        folded = wide[:, :LANES]
        for lane in range(LANES, 4 * rows, LANES):
            folded = folded + wide[:, lane : lane + LANES]
        bias_sum[span] += folded
        enc_sum[span] += jnp.dot(slope, inputs[step], preferred_element_type=jnp.float32)
        dec_sum[span] += jnp.dot(act_low, upstream, preferred_element_type=jnp.float32)

        @pl.when((turn == 0) & (step + 2 < depth))
        def _():
            gather.spread(step + 2)

        @pl.when((turn == tiles // 2) & (step + 1 < depth))
        def _():
            prepare(step + 1)

        @pl.when((step == depth - 1) & (turn < tiles // 2))
        def _():
            for kind in range(3):
                pair_copy(kind, turn).start()

        return carry

    lax.fori_loop(0, depth * tiles, one_tile, 0)

    ours = core * mine
    active_copy.wait_recv()
    span = pl.ds(pl.multiple_of(ours, mine), mine)
    act_total = jnp.sum(active[span] + active_got[...], axis=1, keepdims=True)
    partial = jnp.zeros((8, LANES), jnp.float32)

    def fold(values):
        total = values[:8]
        for first in range(8, values.shape[0], 8):
            total = total + values[first : first + 8]
        narrow = total[:, :LANES]
        for lane in range(LANES, values.shape[1], LANES):
            narrow = narrow + total[:, lane : lane + LANES]
        return narrow

    stores = []
    for turn in range(tiles // 2):
        for kind in range(3):
            pair_copy(kind, turn).wait_recv()
        near = pl.ds(pl.multiple_of(ours + turn * piece, piece), piece)
        there = pl.ds(turn * piece, piece)
        enc_grad = enc_sum[near] + enc_got[there]
        enc_got[there] = enc_grad
        partial = partial + fold(enc_grad * enc_grad)
        dec_grad = dec_sum[near] + dec_got[there]
        dec_grad = dec_grad + (
            COEFFICIENT * act_total[turn * piece : (turn + 1) * piece] / share[there, :1]
        ) * dec[near].astype(jnp.float32)
        dec_got[there] = dec_grad
        partial = partial + fold(dec_grad * dec_grad)
        bias_grad = jnp.sum(bias_sum[near] + bias_got[there], axis=1, keepdims=True)
        bias_out[there] = jnp.broadcast_to(bias_grad, (piece, LANES))
        partial = partial + fold(jnp.broadcast_to(bias_grad * bias_grad, (piece, LANES)) * (1.0 / LANES))
    squares[...] = partial
    for index in range(1, everyone):
        squares_copy(index).start()
    stores = [
        pltpu.make_async_copy(enc_got, enc_out, store_sem.at[0]),
        pltpu.make_async_copy(dec_got, dec_out, store_sem.at[1]),
    ]
    for store in stores:
        store.start()
    total_small = small[...]
    for index in range(1, everyone):
        small_copy(index).wait_recv()
        total_small = total_small + small_got[index]
    small_out[...] = total_small
    total_squares = squares[...]
    for index in range(1, everyone):
        squares_copy(index).wait_recv()
        total_squares = total_squares + squares_got[index]
    squares_out[...] = total_squares
    gather.close()
    for index in range(1, everyone):
        small_copy(index).wait_send()
        squares_copy(index).wait_send()
    active_copy.wait_send()
    for turn in range(tiles // 2):
        for kind in range(3):
            pair_copy(kind, turn).wait_send()
    for store in stores:
        store.wait()


def backward(depth, own, gathered, relu, dec, scale, share, active, small):
    rows, width = own.shape
    entries = dec.shape[0]
    mine = entries // 2
    piece = min(512, mine)
    everyone = depth * 8
    bf16, f32 = jnp.bfloat16, jnp.float32
    dma = pltpu.SemaphoreType.DMA
    return pl.pallas_call(
        functools.partial(backward_kernel, depth, everyone),
        out_shape=(
            jax.ShapeDtypeStruct((mine, width), f32),
            jax.ShapeDtypeStruct((mine, width), f32),
            jax.ShapeDtypeStruct((mine, LANES), f32),
            jax.ShapeDtypeStruct(small.shape, f32),
            jax.ShapeDtypeStruct((8, LANES), f32),
        ),
        in_specs=[ANY] * 8,
        out_specs=(ANY, ANY, VMEM, VMEM, VMEM),
        scratch_shapes=[
            pltpu.VMEM((depth, 4 * rows, width), bf16),
            pltpu.VMEM((depth, 4 * rows, width), bf16),
            pltpu.VMEM((entries, width), bf16),
            pltpu.VMEM((entries, LANES), f32),
            pltpu.VMEM((2, piece, 4 * rows), f32),
            pltpu.VMEM((entries, width), f32),
            pltpu.VMEM((entries, width), f32),
            pltpu.VMEM((entries, LANES), f32),
            pltpu.VMEM((mine, width), f32),
            pltpu.VMEM((mine, width), f32),
            pltpu.VMEM((mine, LANES), f32),
            pltpu.VMEM((entries, LANES), f32),
            pltpu.VMEM((mine, LANES), f32),
            pltpu.VMEM((mine, LANES), f32),
            pltpu.VMEM(small.shape, f32),
            pltpu.VMEM((everyone,) + small.shape, f32),
            pltpu.VMEM((8, LANES), f32),
            pltpu.VMEM((everyone, 8, LANES), f32),
            dma((7,)),
            dma((2,)),
            dma((2,)),
            dma((5, depth)),
            dma((5, depth)),
            dma((4, entries // piece)),
            dma((4, entries // piece)),
            dma((2, everyone)),
            dma((2, everyone)),
        ],
        compiler_params=pltpu.CompilerParams(
            collective_id=1, has_side_effects=True, vmem_limit_bytes=60 * 2**20
        ),
        cost_estimate=pl.CostEstimate(
            flops=24 * depth * rows * entries * width, bytes_accessed=16 * depth * rows * entries, transcendentals=0
        ),
        name="backward_blocks",
    )(own, gathered, relu, dec, scale, share, active, small)


def body(
    depth,
    token_ids,
    doc_ids,
    embed,
    norm_gains,
    norm_shifts,
    qkv_weight,
    out_weight,
    up_weight,
    down_weight,
    proj_biases,
    enc_weight,
    dec_weight,
    enc_bias,
    dec_bias,
    enc_first,
    enc_second,
    dec_first,
    dec_second,
    enc_bias_first,
    enc_bias_second,
    dec_bias_first,
    dec_bias_second,
):
    groups = token_ids.shape[0]
    all_ids, all_docs = (
        lax.all_gather(token_ids, ("seq", "opt"), axis=1, tiled=True),
        lax.all_gather(doc_ids, ("seq", "opt"), axis=1, tiled=True),
    )
    context_len = all_ids.shape[1]
    columns = jnp.take(embed, all_ids, axis=0)
    residual = lax.all_to_all(
        columns, ("seq", "opt"), split_axis=1, concat_axis=2, tiled=True
    ).astype(jnp.float32)
    row_count = residual.shape[1]
    model_width = residual.shape[2]
    first_pos = lax.axis_index(("seq", "opt")) * row_count
    local_pos = first_pos + jnp.arange(row_count, dtype=jnp.int32)
    all_pos = jnp.arange(context_len, dtype=jnp.int32)
    local_docs = lax.dynamic_slice_in_dim(all_docs, first_pos, row_count, 1)
    first_norm = layer_norm(residual, norm_gains[0], norm_shifts[0]).astype(jnp.bfloat16)
    qkv_proj = (
        jnp.dot(first_norm, qkv_weight, preferred_element_type=jnp.float32)
        + proj_biases[: 3 * model_width]
    )
    queries = rotate(
        qkv_proj[..., :model_width].reshape(groups, row_count, HEADS, HEAD), local_pos
    ).astype(jnp.bfloat16)
    key_low = rotate(
        qkv_proj[..., model_width : 2 * model_width].reshape(groups, row_count, HEADS, HEAD),
        local_pos,
    ).astype(jnp.bfloat16)
    value_low = qkv_proj[..., 2 * model_width :].astype(jnp.bfloat16)
    all_keys, all_values = (
        lax.all_gather(
            key_low.reshape(groups, row_count, model_width), ("seq", "opt"), axis=1, tiled=True
        ),
        lax.all_gather(value_low, ("seq", "opt"), axis=1, tiled=True),
    )
    all_keys = all_keys.reshape(groups, context_len, HEADS, HEAD)
    all_values = all_values.reshape(groups, context_len, HEADS, HEAD)
    scores = jnp.einsum(
        "gqhe,gkhe->ghqk", queries, all_keys, preferred_element_type=jnp.float32
    ) * HEAD ** (-0.5)
    allowed = (all_pos[None, None, :] <= local_pos[None, :, None]) & (
        local_docs[:, :, None] == all_docs[:, None, :]
    )
    scores = jnp.where(allowed[:, None], scores, -1e30)
    attn_probs = jax.nn.softmax(scores, axis=-1).astype(jnp.bfloat16)
    mixed_heads = jnp.einsum(
        "ghqk,gkhe->gqhe", attn_probs, all_values, preferred_element_type=jnp.float32
    )
    mixed_heads = mixed_heads.astype(jnp.bfloat16).reshape(groups, row_count, model_width)
    attn_out = (
        jnp.dot(mixed_heads, out_weight, preferred_element_type=jnp.float32)
        + proj_biases[3 * model_width : 4 * model_width]
    )
    second_norm = layer_norm(residual, norm_gains[1], norm_shifts[1]).astype(jnp.bfloat16)
    ff_width = up_weight.shape[1]
    hidden = jax.nn.gelu(
        jnp.dot(second_norm, up_weight, preferred_element_type=jnp.float32)
        + proj_biases[4 * model_width : 4 * model_width + ff_width],
        approximate=False,
    ).astype(jnp.bfloat16)
    stream = (
        residual
        + attn_out
        + jnp.dot(hidden, down_weight, preferred_element_type=jnp.float32)
        + proj_biases[4 * model_width + ff_width :]
    )
    target = stream.reshape(-1, model_width)
    inputs_low = target.astype(jnp.bfloat16)

    enc_own = enc_weight.astype(jnp.bfloat16)
    dec_own = dec_weight.astype(jnp.bfloat16)
    norms_own = row_norms(dec_own)
    pairs = [[0, 1], [2, 3]]

    def both(values):
        return lax.all_gather(values, "opt", axis=0, tiled=True, axis_index_groups=pairs)

    enc_both, dec_both = both(enc_own), both(dec_own)
    bias_both = both(enc_bias)
    norms_both = row_norms(dec_both)
    gathered, relu, recon_turned, active = forward(
        depth,
        inputs_low,
        enc_both,
        dec_both.T,
        jnp.broadcast_to(bias_both[:, None], bias_both.shape + (LANES,)),
    )
    error = recon_turned.T + dec_bias - target
    grad_out = (2.0 * error).astype(jnp.bfloat16)
    entry_count = enc_own.shape[0]
    loss_part = jnp.sum(error * error) + COEFFICIENT * jnp.sum(active * norms_both[:, None])
    dec_bias_part = jnp.sum(grad_out.astype(jnp.float32), axis=0)
    small = jnp.concatenate(
        [
            dec_bias_part[None],
            jnp.full((1, model_width), loss_part, jnp.float32),
            jnp.zeros((6, model_width), jnp.float32),
        ]
    )
    enc_acc, dec_grad, enc_bias_wide, small_sum, squares = backward(
        depth,
        grad_out,
        gathered,
        relu,
        dec_both,
        jnp.broadcast_to((COEFFICIENT * norms_both)[:, None], (2 * entry_count, LANES)),
        jnp.broadcast_to(norms_own[:, None], (entry_count, LANES)),
        active,
        small,
    )
    enc_bias_grad = enc_bias_wide[:, 0]
    dec_bias_grad = small_sum[0]
    loss_sum = small_sum[1, 0]
    grad_norm = jnp.sqrt(jnp.sum(squares) + jnp.sum(dec_bias_grad * dec_bias_grad))
    clip_scale = jnp.minimum(1.0, CLIP_NORM / (grad_norm + 1e-06))
    enc_new, enc_one, enc_two = adam_step(
        enc_weight, enc_first, enc_second, enc_acc, clip_scale, RATE_MATRIX, WEIGHT_DECAY
    )
    dec_new, dec_one, dec_two = adam_step(
        dec_weight, dec_first, dec_second, dec_grad, clip_scale, RATE_MATRIX, WEIGHT_DECAY
    )
    dec_new = dec_new * lax.rsqrt(jnp.sum(dec_new * dec_new, axis=1, keepdims=True) + NORM_EPSILON)
    bias_new, bias_one, bias_two = adam_step(
        enc_bias, enc_bias_first, enc_bias_second, enc_bias_grad, clip_scale, RATE_BIAS, 0.0
    )
    shift_new, shift_one, shift_two = adam_step(
        dec_bias, dec_bias_first, dec_bias_second, dec_bias_grad, clip_scale, RATE_BIAS, 0.0
    )
    return (
        enc_new,
        enc_one,
        enc_two,
        dec_new,
        dec_one,
        dec_two,
        bias_new,
        bias_one,
        bias_two,
        shift_new,
        shift_one,
        shift_two,
        grad_norm,
        loss_sum,
    )


def solution(mesh):
    split = P(("dp", "seq", "opt"), None)
    split_vector = P(("dp", "seq", "opt"))
    in_specs = (
        P("dp", ("seq", "opt")),
        P("dp", ("seq", "opt")),
        P(None, ("seq", "opt")),
        P(),
        P(),
        P(),
        P(),
        P(),
        P(),
        P(),
        split,
        split,
        split_vector,
        P(),
        split,
        split,
        split,
        split,
        split_vector,
        split_vector,
        P(),
        P(),
    )
    out_specs = (split,) * 6 + (split_vector,) * 3 + (P(),) * 5
    return jax.shard_map(
        functools.partial(body, mesh.shape["dp"]),
        mesh=mesh,
        in_specs=in_specs,
        out_specs=out_specs,
        check_vma=False,
    )
```

```python
import functools

import jax
import jax.numpy as jnp
import numpy as np
from jax import lax
from jax.experimental import pallas as pl
from jax.experimental.pallas import tpu as pltpu
from jax.sharding import PartitionSpec as P

HEAD = 64
ROT = 16
STEP = 4
RAMP = 80


LAYER_EPSILON = 1e-05
NORM_EPSILON = 1e-08
BETA_FIRST = 0.9
BETA_SECOND = 0.999
ADAM_EPSILON = 1e-08
RATE_MATRIX = 0.02
RATE_BIAS = 0.1
WEIGHT_DECAY = 0.01
CLIP_NORM = 1.0
SPARSITY_TOP = 5.0
COEFFICIENT = SPARSITY_TOP * min(1.0, STEP / RAMP)
LAST_LAST = (((1,), (1,)), ((), ()))
MESH = pl.DeviceIdType.MESH
ANY = pl.BlockSpec(memory_space=pl.ANY)
VMEM = pl.BlockSpec(memory_space=pltpu.VMEM)
LANES = 128


def row_norms(matrix_low):
    return jnp.sqrt(jnp.sum(jnp.square(matrix_low.astype(jnp.float32)), axis=1) + NORM_EPSILON)


def adam_step(parameter, moment_one, moment_two, gradient, clip_scale, step_rate, decay_rate):
    gradient = gradient * clip_scale
    moment_one = BETA_FIRST * moment_one + (1.0 - BETA_FIRST) * gradient
    moment_two = BETA_SECOND * moment_two + (1.0 - BETA_SECOND) * gradient * gradient
    adjust = (
        moment_one
        / (1.0 - BETA_FIRST**STEP)
        / (jnp.sqrt(moment_two / (1.0 - BETA_SECOND**STEP)) + ADAM_EPSILON)
    )
    return (parameter - step_rate * (adjust + decay_rate * parameter), moment_one, moment_two)


def exclusive_or(left, right, size):
    total, bit = 0, 1
    while bit < size:
        total = total + ((left // bit + right // bit) % 2) * bit
        bit *= 2
    return total


def peers(depth):
    layer, row, column = lax.axis_index("dp"), lax.axis_index("seq"), lax.axis_index("opt")
    along = [(exclusive_or(layer, step, depth), row, column) for step in range(depth)]
    across = (layer, row, (column + 2) % 4)
    beside = (layer, 1 - row, column)
    partner = (layer, row, column + 1 - 2 * (column % 2))
    return along, across, beside, partner


def remote(source, target, send, receive, device):
    return pltpu.make_async_remote_copy(
        src_ref=source,
        dst_ref=target,
        send_sem=send,
        recv_sem=receive,
        device_id=device,
        device_id_type=MESH,
    )


def greet(devices):
    barrier = pltpu.get_barrier_semaphore()
    for device in devices:
        pl.semaphore_signal(barrier, inc=1, device_id=device, device_id_type=MESH)
    pl.semaphore_wait(barrier, len(devices))


class Gather:
    def __init__(self, depth, rows, held, send, receive, where):
        self.depth, self.rows, self.held = depth, rows, held
        self.send, self.receive = send, receive
        self.along, self.across, self.beside, _ = where

    def block(self, step, column, part=None):
        first, rows = column * self.rows, self.rows
        if part is not None:
            rows = self.rows // 2
            first = first + part * rows
        return self.held.at[step, pl.ds(first, rows)]

    def copy_along(self, step):
        return remote(
            self.block(0, 0), self.block(step, 0), self.send.at[0, step], self.receive.at[0, step], self.along[step]
        )

    def copy_across(self, step):
        return remote(
            self.block(step, 0), self.block(step, 1), self.send.at[1, step], self.receive.at[1, step], self.across
        )

    def copy_beside(self, step):
        return remote(
            self.block(step, 0), self.block(step, 2), self.send.at[2, step], self.receive.at[2, step], self.beside
        )

    def pass_across(self, step):
        return remote(
            self.block(step, 2, 0), self.block(step, 3, 0), self.send.at[3, step], self.receive.at[3, step], self.across
        )

    def pass_beside(self, step):
        return remote(
            self.block(step, 1, 1), self.block(step, 3, 1), self.send.at[4, step], self.receive.at[4, step], self.beside
        )

    def wait_along(self, step):
        remote(
            self.block(0, 0), self.block(step, 0), self.send.at[0, step], self.receive.at[0, step], self.along[0]
        ).wait_recv()

    def open(self):
        self.copy_across(0).start()
        self.copy_beside(0).start()
        for step in range(1, self.depth):
            self.copy_along(step).start()

    def spread(self, step):
        self.wait_along(step)
        self.copy_across(step).start()
        self.copy_beside(step).start()

    def hand_on(self, step):
        self.copy_across(step).wait_recv()
        self.pass_beside(step).start()
        self.copy_beside(step).wait_recv()
        self.pass_across(step).start()

    def wait_diagonal(self, step):
        self.pass_across(step).wait_recv()
        self.pass_beside(step).wait_recv()

    def close(self):
        for step in range(1, self.depth):
            self.copy_along(step).wait_send()

        def done(step, carry):
            self.copy_across(step).wait_send()
            self.copy_beside(step).wait_send()
            self.pass_across(step).wait_send()
            self.pass_beside(step).wait_send()
            return carry

        lax.fori_loop(0, self.depth, done, 0)


def ids_kernel(ids_ref, docs_ref, ids_out, docs_out, ids_all, docs_all, load_sem, send, receive):
    group = ids_all.shape[0]
    layer, row, column = lax.axis_index("dp"), lax.axis_index("seq"), lax.axis_index("opt")
    here = row * 4 + column
    others = [(here + step) % group for step in range(group)]
    devices = [(layer, index // 4, index % 4) for index in others]
    loads = [
        pltpu.make_async_copy(ids_ref, ids_all.at[here], load_sem.at[0]),
        pltpu.make_async_copy(docs_ref, docs_all.at[here], load_sem.at[1]),
    ]
    for load in loads:
        load.start()
    greet(devices[1:])
    for load in loads:
        load.wait()
    copies = []
    for step in range(1, group):
        for kind, held in enumerate((ids_all, docs_all)):
            copies.append(
                remote(held.at[here], held.at[here], send.at[kind, step], receive.at[kind, step], devices[step])
            )
    for copy in copies:
        copy.start()
    for copy in copies:
        copy.wait()
    ids_out[...] = ids_all[...]
    docs_out[...] = docs_all[...]


def gather_ids(ids, docs, group):
    rows = ids.shape[1]
    dma = pltpu.SemaphoreType.DMA
    whole = jax.ShapeDtypeStruct((group, 1, rows), jnp.int32)
    return pl.pallas_call(
        ids_kernel,
        out_shape=(whole, whole),
        in_specs=[ANY] * 2,
        out_specs=(VMEM, VMEM),
        scratch_shapes=[
            pltpu.VMEM((group, 1, rows), jnp.int32),
            pltpu.VMEM((group, 1, rows), jnp.int32),
            dma((2,)),
            dma((2, group)),
            dma((2, group)),
        ],
        compiler_params=pltpu.CompilerParams(collective_id=3, has_side_effects=True, vmem_limit_bytes=2**20),
        name="gather_ids",
    )(ids, docs)


def pick_kernel(ids_ref, table, picked):
    group, _, rows = ids_ref.shape
    share = table.shape[0]
    lanes = lax.broadcasted_iota(jnp.int32, (share, LANES), 1)

    def some(part, carry):
        source, first = part // (rows // LANES), part % (rows // LANES) * LANES

        def one(turn, found):
            for extra in range(16):
                place = turn * 16 + extra
                token = ids_ref[source, 0, first + place]
                start = lax.bitwise_and(token, -LANES)
                tile = table[:, pl.ds(pl.multiple_of(start, LANES), LANES)].astype(jnp.float32)
                moved = pltpu.roll(tile, lax.bitwise_and(place - token, LANES - 1), 1)
                found = jnp.where(lanes == place, moved, found)
            return found

        found = lax.fori_loop(0, LANES // 16, one, jnp.zeros((share, LANES), jnp.float32))
        picked[source, :, pl.ds(pl.multiple_of(first, LANES), LANES)] = found.astype(jnp.bfloat16)
        return carry

    lax.fori_loop(0, group * rows // LANES, some, 0)


def pick(ids, table):
    group, _, rows = ids.shape
    share = table.shape[0]
    return pl.pallas_call(
        pick_kernel,
        out_shape=jax.ShapeDtypeStruct((group, share, rows), jnp.bfloat16),
        in_specs=[pl.BlockSpec(memory_space=pltpu.SMEM), VMEM],
        out_specs=VMEM,
        compiler_params=pltpu.CompilerParams(vmem_limit_bytes=24 * 2**20),
        name="pick_features",
    )(ids, table)


def front_kernel(
    picked_ref,
    docs_ref,
    gains_ref,
    shifts_ref,
    qkv_ref,
    out_ref,
    up_ref,
    down_ref,
    bias_ref,
    turn_ref,
    low_ref,
    stream_ref,
    docs_all,
    gains,
    shifts,
    qkv,
    out,
    up,
    down,
    bias,
    turn,
    picked,
    features,
    turned,
    heads,
    mixed_turned,
    fed,
    load_sem,
    send,
    receive,
):
    group, share, rows = picked.shape
    width = gains.shape[1]
    ff_width = up.shape[1]
    layer, row, column = lax.axis_index("dp"), lax.axis_index("seq"), lax.axis_index("opt")
    here = row * 4 + column

    def member(index):
        return (layer, index // 4, index % 4)

    others = [(here + step) % group for step in range(group)]
    first_place = pl.multiple_of(here * rows, rows)
    loads = [
        pltpu.make_async_copy(picked_ref, picked, load_sem.at[0]),
        pltpu.make_async_copy(docs_ref, docs_all, load_sem.at[1]),
        pltpu.make_async_copy(gains_ref, gains, load_sem.at[2]),
        pltpu.make_async_copy(shifts_ref, shifts, load_sem.at[3]),
        pltpu.make_async_copy(bias_ref, bias, load_sem.at[4]),
        pltpu.make_async_copy(turn_ref.at[:, pl.ds(first_place, rows)], turn, load_sem.at[5]),
        pltpu.make_async_copy(qkv_ref, qkv, load_sem.at[6]),
        pltpu.make_async_copy(up_ref, up, load_sem.at[7]),
        pltpu.make_async_copy(down_ref, down, load_sem.at[8]),
        pltpu.make_async_copy(out_ref, out, load_sem.at[9]),
    ]
    for load in loads:
        load.start()
    greet([member(index) for index in others[1:]])
    loads[0].wait()

    def copy_features(step):
        return remote(
            picked.at[others[step]],
            features.at[pl.ds(pl.multiple_of(here * share, share), share)],
            send.at[0, step],
            receive.at[0, step],
            member(others[step]),
        )

    def copy_heads(step):
        return remote(
            turned.at[others[step]], heads.at[here], send.at[1, step], receive.at[1, step], member(others[step])
        )

    def copy_mixed(index, source):
        return remote(
            picked.at[index],
            mixed_turned.at[pl.ds(pl.multiple_of(source * HEAD, HEAD), HEAD)],
            send.at[2, index],
            receive.at[2, source],
            member(index),
        )

    for step in range(1, group):
        copy_features(step).start()
    features[pl.ds(pl.multiple_of(here * share, share), share)] = picked[here]
    for load in loads[1:]:
        load.wait()
    for step in range(1, group):
        copy_features(step).wait_recv()

    residual = features[...].astype(jnp.float32).T
    center = residual - jnp.mean(residual, axis=1, keepdims=True)
    variance = jnp.mean(center * center, axis=1, keepdims=True)
    unit = center * lax.rsqrt(variance + LAYER_EPSILON)
    first_norm = (unit * gains[0:1] + shifts[0:1]).astype(jnp.bfloat16)
    second_norm = (unit * gains[1:2] + shifts[1:2]).astype(jnp.bfloat16)
    half_rot = ROT // 2
    cosine, sine = turn[:half_rot], turn[half_rot:]
    for first in range(0, 3 * width, 2 * LANES):
        chunk = (
            jnp.dot(first_norm, qkv[:, first : first + 2 * LANES], preferred_element_type=jnp.float32)
            + bias[:, first : first + 2 * LANES]
        ).T
        for inner in range(0, 2 * LANES, HEAD):
            kind, head = (first + inner) // width, (first + inner) % width // HEAD
            values = chunk[inner : inner + HEAD]
            if kind < 2:
                left, right = values[:half_rot], values[half_rot:ROT]
                values = jnp.concatenate(
                    [left * cosine - right * sine, right * cosine + left * sine, values[ROT:]], axis=0
                )
            turned[head, kind * HEAD : (kind + 1) * HEAD] = values.astype(jnp.bfloat16)
    for step in range(1, group):
        copy_heads(step).start()
    heads[here] = turned[here]

    feed = residual + bias[:, 4 * width + ff_width :] + bias[:, 3 * width : 4 * width]
    for first in range(0, ff_width, 512):
        inner = (
            jnp.dot(second_norm, up[:, first : first + 512], preferred_element_type=jnp.float32)
            + bias[:, 4 * width + first : 4 * width + first + 512]
        )
        hidden = (0.5 * inner * (1.0 + lax.erf(inner * (0.5**0.5)))).astype(jnp.bfloat16)
        feed = feed + jnp.dot(hidden, down[first : first + 512], preferred_element_type=jnp.float32)
    fed[...] = feed

    for step in range(1, group):
        copy_heads(step).wait_recv()
        copy_features(step).wait_send()
    query_place = lax.broadcasted_iota(jnp.int32, (rows, rows), 0)
    key_place = lax.broadcasted_iota(jnp.int32, (rows, rows), 1)
    causal = key_place <= query_place
    scale = HEAD ** (-0.5)
    for index in reversed(range(group)):
        query = heads[index, :HEAD].astype(jnp.float32).T.astype(jnp.bfloat16)
        own_docs = jnp.broadcast_to(docs_all[index].astype(jnp.float32), (LANES, rows)).T
        own_docs = jnp.concatenate([own_docs] * (rows // LANES), axis=1)
        scores = []
        for other in range(index + 1):
            score = jnp.dot(query, heads[other, HEAD : 2 * HEAD], preferred_element_type=jnp.float32)
            allowed = own_docs == docs_all[other].astype(jnp.float32)
            if other == index:
                allowed = allowed & causal
            scores.append(jnp.where(allowed, score * scale, -1e30))
        peak = scores[0]
        for score in scores[1:]:
            peak = jnp.maximum(peak, score)
        peak = jnp.max(peak, axis=1, keepdims=True)
        weights = [jnp.exp(score - peak) for score in scores]
        total = weights[0]
        for weight in weights[1:]:
            total = total + weight
        inverse = 1.0 / jnp.sum(total, axis=1, keepdims=True)
        mixed = None
        for other in range(index + 1):
            probs = (weights[other] * inverse).astype(jnp.bfloat16)
            term = lax.dot_general(
                heads[other, 2 * HEAD :], probs, LAST_LAST, preferred_element_type=jnp.float32
            )
            mixed = term if mixed is None else mixed + term
        picked[index] = mixed.astype(jnp.bfloat16)

        @pl.when(here != index)
        def _():
            copy_mixed(index, here).start()

        @pl.when(here == index)
        def _():
            mixed_turned[pl.ds(pl.multiple_of(here * HEAD, HEAD), HEAD)] = picked[index]

    for step in range(1, group):
        copy_mixed(step, others[step]).wait_recv()
    mixed = mixed_turned[...].astype(jnp.float32).T.astype(jnp.bfloat16)
    stream = fed[...] + jnp.dot(mixed, out[...], preferred_element_type=jnp.float32)
    stream_ref[...] = stream
    low_ref[...] = stream.astype(jnp.bfloat16)
    for step in range(1, group):
        copy_heads(step).wait_send()
    for index in range(group):

        @pl.when(here != index)
        def _():
            copy_mixed(index, here).wait_send()


def rotary_table(context_len):
    half_rot = ROT // 2
    frequency = np.power(np.float32(10000.0), np.float32(-2.0) * np.arange(half_rot, dtype=np.float32) / np.float32(ROT))
    angles = frequency.astype(np.float32)[:, None] * np.arange(context_len, dtype=np.float32)[None, :]
    return np.concatenate([np.cos(angles.astype(np.float64)), np.sin(angles.astype(np.float64))]).astype(np.float32)


def front(picked, docs, gains, shifts, qkv, out, up, down, bias):
    group, share, rows = picked.shape
    width = gains.shape[1]
    ff_width = up.shape[1]
    bf16, f32 = jnp.bfloat16, jnp.float32
    dma = pltpu.SemaphoreType.DMA
    return pl.pallas_call(
        front_kernel,
        out_shape=(jax.ShapeDtypeStruct((rows, width), bf16), jax.ShapeDtypeStruct((rows, width), f32)),
        in_specs=[ANY] * 10,
        out_specs=(VMEM, VMEM),
        scratch_shapes=[
            pltpu.VMEM((group, 1, rows), jnp.int32),
            pltpu.VMEM((2, width), f32),
            pltpu.VMEM((2, width), f32),
            pltpu.VMEM((width, 3 * width), bf16),
            pltpu.VMEM((width, width), bf16),
            pltpu.VMEM((width, ff_width), bf16),
            pltpu.VMEM((ff_width, width), bf16),
            pltpu.VMEM(bias.shape, f32),
            pltpu.VMEM((ROT, rows), f32),
            pltpu.VMEM((group, share, rows), bf16),
            pltpu.VMEM((width, rows), bf16),
            pltpu.VMEM((group, 3 * HEAD, rows), bf16),
            pltpu.VMEM((group, 3 * HEAD, rows), bf16),
            pltpu.VMEM((width, rows), bf16),
            pltpu.VMEM((rows, width), f32),
            dma((10,)),
            dma((3, group)),
            dma((3, group)),
        ],
        compiler_params=pltpu.CompilerParams(
            collective_id=2, has_side_effects=True, vmem_limit_bytes=60 * 2**20
        ),
        cost_estimate=pl.CostEstimate(flops=2 * 10**9, bytes_accessed=14 * 10**6, transcendentals=2 * 10**6),
        name="front_part",
    )(picked, docs, gains, shifts, qkv, out, up, down, bias, jnp.asarray(rotary_table(group * rows)))


def forward_kernel(
    depth,
    own_ref,
    enc_ref,
    dec_ref,
    bias_ref,
    gathered_ref,
    relu_ref,
    recon_ref,
    total_ref,
    held,
    enc,
    dec,
    bias,
    staged,
    parts,
    send_one,
    send_two,
    send_three,
    got_one,
    got_two,
    got_three,
    load_sem,
    relu_sem,
    held_sem,
    send,
    receive,
    sum_send,
    sum_receive,
):
    rows = own_ref.shape[0]
    entries = enc.shape[0]
    width = held.shape[2]
    half = width // 2
    piece = min(entries, 1024)
    where = peers(depth)
    along, across, beside, _ = where
    loads = [
        pltpu.make_async_copy(own_ref, held.at[0, pl.ds(0, rows)], load_sem.at[0]),
        pltpu.make_async_copy(enc_ref, enc, load_sem.at[1]),
        pltpu.make_async_copy(bias_ref, bias, load_sem.at[2]),
        pltpu.make_async_copy(dec_ref, dec, load_sem.at[3]),
    ]
    for load in loads:
        load.start()
    greet(along[1:] + [across, beside])
    loads[0].wait()
    gather = Gather(depth, rows, held, send, receive, where)
    gather.open()
    total_ref[...] = jnp.zeros_like(total_ref)
    for load in loads[1:]:
        load.wait()

    def copy_one(step, part):
        source = send_one.at[step % 2, pl.ds(part * half, half)]
        device = beside if part else across
        return remote(source, got_one.at[part, step], sum_send.at[part, step], sum_receive.at[part, step], device)

    def copy_two(step, part):
        device = beside if part else across
        return remote(
            send_two.at[part, step % 2],
            got_two.at[part, step],
            sum_send.at[2 + part, step],
            sum_receive.at[2 + part, step],
            device,
        )

    def copy_three(step, device):
        return remote(
            send_three.at[step], got_three.at[step], sum_send.at[4, step], sum_receive.at[4, step], device
        )

    def copy_relu(order):
        step, column = order // 4, order % 4
        return pltpu.make_async_copy(
            staged.at[order % 2],
            relu_ref.at[step, :, pl.ds(pl.multiple_of(column * rows, rows), rows)],
            relu_sem.at[order % 2],
        )

    def copy_held(step):
        return pltpu.make_async_copy(held.at[step], gathered_ref.at[step], held_sem.at[step])

    def sum_two(step):
        copy_one(step, 0).wait_recv()
        copy_one(step, 1).wait_recv()

        @pl.when(step >= 2)
        def _():
            copy_two(step - 2, 0).wait_send()
            copy_two(step - 2, 1).wait_send()

        slot = step % 3
        upper, lower = pl.ds(0, half), pl.ds(half, half)
        send_two[1, step % 2, upper] = (parts[2, slot, upper] + got_one[0, step].astype(jnp.float32)).astype(
            jnp.bfloat16
        )
        send_two[1, step % 2, lower] = parts[2, slot, lower].astype(jnp.bfloat16)
        copy_two(step, 1).start()
        send_two[0, step % 2, upper] = parts[1, slot, upper].astype(jnp.bfloat16)
        send_two[0, step % 2, lower] = (parts[1, slot, lower] + got_one[1, step].astype(jnp.float32)).astype(
            jnp.bfloat16
        )
        copy_two(step, 0).start()

    def column_sum(step):
        copy_two(step, 0).wait_recv()
        copy_two(step, 1).wait_recv()
        return parts[0, step % 3] + got_two[0, step].astype(jnp.float32) + got_two[1, step].astype(jnp.float32)

    def sum_three(step):
        value = column_sum(step)

        @pl.when(step == 0)
        def _():
            recon_ref[...] = value

        @pl.when(step > 0)
        def _():
            send_three[step] = value.astype(jnp.bfloat16)
            layer = lax.axis_index("dp")
            target = (exclusive_or(layer, step, depth), along[0][1], along[0][2])
            copy_three(step, target).start()

    def one_block(order, carry):
        step, column = order // 4, order % 4

        @pl.when(column == 1)
        def _():
            gather.hand_on(step)

        @pl.when(column == 3)
        def _():
            gather.wait_diagonal(step)
            copy_held(step).start()

        @pl.when(order >= 2)
        def _():
            copy_relu(order - 2).wait()

        block = held[step, pl.ds(pl.multiple_of(column * rows, rows), rows)]
        recon = None
        for first in range(0, entries, piece):
            span = pl.ds(first, piece)
            shift = bias[span]
            pre = lax.dot_general(enc[span], block, LAST_LAST, preferred_element_type=jnp.float32)
            positive = jnp.maximum(pre + jnp.concatenate([shift] * (rows // LANES), axis=1), 0.0)
            staged[order % 2, span] = positive
            active = positive * positive
            folded = active[:, :LANES]
            for lane in range(LANES, rows, LANES):
                folded = folded + active[:, lane : lane + LANES]
            total_ref[span] += folded
            term = jnp.dot(dec[:, first : first + piece], active.astype(jnp.bfloat16), preferred_element_type=jnp.float32)
            recon = term if recon is None else recon + term
        copy_relu(order).start()

        @pl.when(column < 3)
        def _():
            parts[column, step % 3] = recon

        @pl.when(column == 3)
        def _():
            @pl.when(step >= 2)
            def _():
                copy_one(step - 2, 0).wait_send()
                copy_one(step - 2, 1).wait_send()

            send_one[step % 2] = recon.astype(jnp.bfloat16)
            copy_one(step, 0).start()
            copy_one(step, 1).start()

            @pl.when(step >= 1)
            def _():
                sum_two(step - 1)

        @pl.when((column == 0) & (step + 1 < depth))
        def _():
            gather.spread(step + 1)

        @pl.when((column == 2) & (step >= 2))
        def _():
            sum_three(step - 2)

        return carry

    lax.fori_loop(0, 4 * depth, one_block, 0)
    sum_two(depth - 1)
    if depth >= 2:
        sum_three(depth - 2)
    sum_three(depth - 1)
    for step in range(1, depth):
        copy_three(step, along[step]).wait_recv()
        recon_ref[...] += got_three[step].astype(jnp.float32)
    gather.close()
    for step in range(max(depth - 2, 0), depth):
        for part in range(2):
            copy_one(step, part).wait_send()
            copy_two(step, part).wait_send()
    for step in range(1, depth):
        copy_three(step, along[step]).wait_send()
    copy_relu(4 * depth - 2).wait()
    copy_relu(4 * depth - 1).wait()
    for step in range(depth):
        copy_held(step).wait()


def forward(depth, own, enc, dec_turned, bias):
    rows, width = own.shape
    entries = enc.shape[0]
    bf16, f32 = jnp.bfloat16, jnp.float32
    dma = pltpu.SemaphoreType.DMA
    return pl.pallas_call(
        functools.partial(forward_kernel, depth),
        out_shape=(
            jax.ShapeDtypeStruct((depth, 4 * rows, width), bf16),
            jax.ShapeDtypeStruct((depth, entries, 4 * rows), f32),
            jax.ShapeDtypeStruct((width, rows), f32),
            jax.ShapeDtypeStruct((entries, LANES), f32),
        ),
        in_specs=[ANY] * 4,
        out_specs=(ANY, ANY, VMEM, VMEM),
        scratch_shapes=[
            pltpu.VMEM((depth, 4 * rows, width), bf16),
            pltpu.VMEM((entries, width), bf16),
            pltpu.VMEM((width, entries), bf16),
            pltpu.VMEM((entries, LANES), f32),
            pltpu.VMEM((2, entries, rows), f32),
            pltpu.VMEM((3, 3, width, rows), f32),
            pltpu.VMEM((2, width, rows), bf16),
            pltpu.VMEM((2, 2, width, rows), bf16),
            pltpu.VMEM((depth, width, rows), bf16),
            pltpu.VMEM((2, depth, width // 2, rows), bf16),
            pltpu.VMEM((2, depth, width, rows), bf16),
            pltpu.VMEM((depth, width, rows), bf16),
            dma((4,)),
            dma((2,)),
            dma((depth,)),
            dma((5, depth)),
            dma((5, depth)),
            dma((5, depth)),
            dma((5, depth)),
        ],
        compiler_params=pltpu.CompilerParams(
            collective_id=0, has_side_effects=True, vmem_limit_bytes=60 * 2**20
        ),
        cost_estimate=pl.CostEstimate(
            flops=16 * depth * rows * entries * width, bytes_accessed=16 * depth * rows * entries, transcendentals=0
        ),
        name="forward_blocks",
    )(own, enc, dec_turned, bias)


def backward_kernel(
    depth,
    everyone,
    own_ref,
    gathered_ref,
    relu_ref,
    dec_ref,
    scale_ref,
    share_ref,
    active_ref,
    small_ref,
    enc_out,
    dec_out,
    bias_out,
    small_out,
    squares_out,
    held,
    inputs,
    dec,
    scale,
    tile,
    enc_sum,
    dec_sum,
    bias_sum,
    enc_got,
    dec_got,
    bias_got,
    active,
    active_got,
    share,
    small,
    small_got,
    squares,
    squares_got,
    load_sem,
    tile_sem,
    store_sem,
    send,
    receive,
    pair_send,
    pair_receive,
    all_send,
    all_receive,
):
    rows = own_ref.shape[0]
    entries = dec.shape[0]
    mine = entries // 2
    piece = tile.shape[1]
    tiles = entries // piece
    where = peers(depth)
    along, across, beside, partner = where
    layer, row, column = along[0]
    core = column % 2
    loads = [
        pltpu.make_async_copy(own_ref, held.at[0, pl.ds(0, rows)], load_sem.at[0]),
        pltpu.make_async_copy(dec_ref, dec, load_sem.at[1]),
        pltpu.make_async_copy(scale_ref, scale, load_sem.at[2]),
        pltpu.make_async_copy(gathered_ref, inputs, load_sem.at[3]),
        pltpu.make_async_copy(active_ref, active, load_sem.at[4]),
        pltpu.make_async_copy(small_ref, small, load_sem.at[5]),
        pltpu.make_async_copy(share_ref, share, load_sem.at[6]),
    ]
    for load in loads:
        load.start()

    def place(turn):
        return (turn + (1 - core) * (tiles // 2)) % tiles

    def copy_tile(order):
        first = pl.multiple_of(place(order % tiles) * piece, piece)
        return pltpu.make_async_copy(
            relu_ref.at[order // tiles, pl.ds(first, piece)], tile.at[order % 2], tile_sem.at[order % 2]
        )

    copy_tile(0).start()

    others = [
        ((layer + dz) % depth, (row + dy) % 2, (column + dx) % 4)
        for dz in range(depth)
        for dy in range(2)
        for dx in range(4)
    ][1:]
    greet(others)
    loads[0].wait()
    gather = Gather(depth, rows, held, send, receive, where)
    gather.open()
    for load in loads[1:]:
        load.wait()

    def small_copy(index):
        return remote(
            small, small_got.at[index], all_send.at[0, index], all_receive.at[0, index], others[index - 1]
        )

    def squares_copy(index):
        return remote(
            squares, squares_got.at[index], all_send.at[1, index], all_receive.at[1, index], others[index - 1]
        )

    for index in range(1, everyone):
        small_copy(index).start()

    theirs = (1 - core) * mine
    active_copy = remote(
        active.at[pl.ds(pl.multiple_of(theirs, mine), mine)], active_got, pair_send.at[3, 0], pair_receive.at[3, 0], partner
    )
    active_copy.start()
    enc_sum[...] = jnp.zeros_like(enc_sum)
    dec_sum[...] = jnp.zeros_like(dec_sum)
    bias_sum[...] = jnp.zeros_like(bias_sum)

    def pair_copy(kind, turn):
        source, target = ((enc_sum, enc_got), (dec_sum, dec_got), (bias_sum, bias_got))[kind]
        first = pl.multiple_of(theirs + turn * piece, piece)
        return remote(
            source.at[pl.ds(first, piece)],
            target.at[pl.ds(pl.multiple_of(turn * piece, piece), piece)],
            pair_send.at[kind, turn],
            pair_receive.at[kind, turn],
            partner,
        )

    def prepare(step):
        gather.hand_on(step)

    if depth > 1:
        gather.spread(1)
    prepare(0)

    def one_tile(order, carry):
        step, turn = order // tiles, order % tiles

        @pl.when(order + 1 < depth * tiles)
        def _():
            copy_tile(order + 1).start()

        @pl.when(turn == 0)
        def _():
            gather.wait_diagonal(step)

        copy_tile(order).wait()
        span = pl.ds(pl.multiple_of(place(turn) * piece, piece), piece)
        upstream = held[step]
        back = lax.dot_general(dec[span], upstream, LAST_LAST, preferred_element_type=jnp.float32)
        positive = tile[order % 2]
        shift = jnp.concatenate([scale[span]] * (4 * rows // LANES), axis=1)
        slope = ((back + shift) * (2.0 * positive)).astype(jnp.bfloat16)
        act_low = (positive * positive).astype(jnp.bfloat16)
        wide = slope.astype(jnp.float32)
        folded = wide[:, :LANES]
        for lane in range(LANES, 4 * rows, LANES):
            folded = folded + wide[:, lane : lane + LANES]
        bias_sum[span] += folded
        enc_sum[span] += jnp.dot(slope, inputs[step], preferred_element_type=jnp.float32)
        dec_sum[span] += jnp.dot(act_low, upstream, preferred_element_type=jnp.float32)

        @pl.when((turn == 0) & (step + 2 < depth))
        def _():
            gather.spread(step + 2)

        @pl.when((turn == tiles // 2) & (step + 1 < depth))
        def _():
            prepare(step + 1)

        @pl.when((step == depth - 1) & (turn < tiles // 2))
        def _():
            for kind in range(3):
                pair_copy(kind, turn).start()

        return carry

    lax.fori_loop(0, depth * tiles, one_tile, 0)

    ours = core * mine
    active_copy.wait_recv()
    span = pl.ds(pl.multiple_of(ours, mine), mine)
    act_total = jnp.sum(active[span] + active_got[...], axis=1, keepdims=True)
    partial = jnp.zeros((8, LANES), jnp.float32)

    def fold(values):
        total = values[:8]
        for first in range(8, values.shape[0], 8):
            total = total + values[first : first + 8]
        narrow = total[:, :LANES]
        for lane in range(LANES, values.shape[1], LANES):
            narrow = narrow + total[:, lane : lane + LANES]
        return narrow

    stores = []
    for turn in range(tiles // 2):
        for kind in range(3):
            pair_copy(kind, turn).wait_recv()
        near = pl.ds(pl.multiple_of(ours + turn * piece, piece), piece)
        there = pl.ds(turn * piece, piece)
        enc_grad = enc_sum[near] + enc_got[there]
        enc_got[there] = enc_grad
        partial = partial + fold(enc_grad * enc_grad)
        dec_grad = dec_sum[near] + dec_got[there]
        dec_grad = dec_grad + (
            COEFFICIENT * act_total[turn * piece : (turn + 1) * piece] / share[there, :1]
        ) * dec[near].astype(jnp.float32)
        dec_got[there] = dec_grad
        partial = partial + fold(dec_grad * dec_grad)
        bias_grad = jnp.sum(bias_sum[near] + bias_got[there], axis=1, keepdims=True)
        bias_out[there] = jnp.broadcast_to(bias_grad, (piece, LANES))
        partial = partial + fold(jnp.broadcast_to(bias_grad * bias_grad, (piece, LANES)) * (1.0 / LANES))
    squares[...] = partial
    for index in range(1, everyone):
        squares_copy(index).start()
    stores = [
        pltpu.make_async_copy(enc_got, enc_out, store_sem.at[0]),
        pltpu.make_async_copy(dec_got, dec_out, store_sem.at[1]),
    ]
    for store in stores:
        store.start()
    total_small = small[...]
    for index in range(1, everyone):
        small_copy(index).wait_recv()
        total_small = total_small + small_got[index]
    small_out[...] = total_small
    total_squares = squares[...]
    for index in range(1, everyone):
        squares_copy(index).wait_recv()
        total_squares = total_squares + squares_got[index]
    squares_out[...] = total_squares
    gather.close()
    for index in range(1, everyone):
        small_copy(index).wait_send()
        squares_copy(index).wait_send()
    active_copy.wait_send()
    for turn in range(tiles // 2):
        for kind in range(3):
            pair_copy(kind, turn).wait_send()
    for store in stores:
        store.wait()


def backward(depth, own, gathered, relu, dec, scale, share, active, small):
    rows, width = own.shape
    entries = dec.shape[0]
    mine = entries // 2
    piece = min(512, mine)
    everyone = depth * 8
    bf16, f32 = jnp.bfloat16, jnp.float32
    dma = pltpu.SemaphoreType.DMA
    return pl.pallas_call(
        functools.partial(backward_kernel, depth, everyone),
        out_shape=(
            jax.ShapeDtypeStruct((mine, width), f32),
            jax.ShapeDtypeStruct((mine, width), f32),
            jax.ShapeDtypeStruct((mine, LANES), f32),
            jax.ShapeDtypeStruct(small.shape, f32),
            jax.ShapeDtypeStruct((8, LANES), f32),
        ),
        in_specs=[ANY] * 8,
        out_specs=(ANY, ANY, VMEM, VMEM, VMEM),
        scratch_shapes=[
            pltpu.VMEM((depth, 4 * rows, width), bf16),
            pltpu.VMEM((depth, 4 * rows, width), bf16),
            pltpu.VMEM((entries, width), bf16),
            pltpu.VMEM((entries, LANES), f32),
            pltpu.VMEM((2, piece, 4 * rows), f32),
            pltpu.VMEM((entries, width), f32),
            pltpu.VMEM((entries, width), f32),
            pltpu.VMEM((entries, LANES), f32),
            pltpu.VMEM((mine, width), f32),
            pltpu.VMEM((mine, width), f32),
            pltpu.VMEM((mine, LANES), f32),
            pltpu.VMEM((entries, LANES), f32),
            pltpu.VMEM((mine, LANES), f32),
            pltpu.VMEM((mine, LANES), f32),
            pltpu.VMEM(small.shape, f32),
            pltpu.VMEM((everyone,) + small.shape, f32),
            pltpu.VMEM((8, LANES), f32),
            pltpu.VMEM((everyone, 8, LANES), f32),
            dma((7,)),
            dma((2,)),
            dma((2,)),
            dma((5, depth)),
            dma((5, depth)),
            dma((4, entries // piece)),
            dma((4, entries // piece)),
            dma((2, everyone)),
            dma((2, everyone)),
        ],
        compiler_params=pltpu.CompilerParams(
            collective_id=1, has_side_effects=True, vmem_limit_bytes=60 * 2**20
        ),
        cost_estimate=pl.CostEstimate(
            flops=24 * depth * rows * entries * width, bytes_accessed=16 * depth * rows * entries, transcendentals=0
        ),
        name="backward_blocks",
    )(own, gathered, relu, dec, scale, share, active, small)


def body(
    depth,
    token_ids,
    doc_ids,
    embed,
    norm_gains,
    norm_shifts,
    qkv_weight,
    out_weight,
    up_weight,
    down_weight,
    proj_biases,
    enc_weight,
    dec_weight,
    enc_bias,
    dec_bias,
    enc_first,
    enc_second,
    dec_first,
    dec_second,
    enc_bias_first,
    enc_bias_second,
    dec_bias_first,
    dec_bias_second,
):
    model_width = norm_gains.shape[1]
    all_ids, all_docs = gather_ids(token_ids, doc_ids, model_width // embed.shape[1])
    inputs_low, target = front(
        pick(all_ids, embed.T),
        all_docs,
        norm_gains,
        norm_shifts,
        qkv_weight,
        out_weight,
        up_weight,
        down_weight,
        proj_biases[None],
    )

    enc_own = enc_weight.astype(jnp.bfloat16)
    dec_own = dec_weight.astype(jnp.bfloat16)
    norms_own = row_norms(dec_own)
    pairs = [[0, 1], [2, 3]]

    def both(values):
        return lax.all_gather(values, "opt", axis=0, tiled=True, axis_index_groups=pairs)

    enc_both, dec_both = both(enc_own), both(dec_own)
    bias_both = both(enc_bias)
    norms_both = row_norms(dec_both)
    gathered, relu, recon_turned, active = forward(
        depth,
        inputs_low,
        enc_both,
        dec_both.T,
        jnp.broadcast_to(bias_both[:, None], bias_both.shape + (LANES,)),
    )
    error = recon_turned.T + dec_bias - target
    grad_out = (2.0 * error).astype(jnp.bfloat16)
    entry_count = enc_own.shape[0]
    loss_part = jnp.sum(error * error) + COEFFICIENT * jnp.sum(active * norms_both[:, None])
    dec_bias_part = jnp.sum(grad_out.astype(jnp.float32), axis=0)
    small = jnp.concatenate(
        [
            dec_bias_part[None],
            jnp.full((1, model_width), loss_part, jnp.float32),
            jnp.zeros((6, model_width), jnp.float32),
        ]
    )
    enc_acc, dec_grad, enc_bias_wide, small_sum, squares = backward(
        depth,
        grad_out,
        gathered,
        relu,
        dec_both,
        jnp.broadcast_to((COEFFICIENT * norms_both)[:, None], (2 * entry_count, LANES)),
        jnp.broadcast_to(norms_own[:, None], (entry_count, LANES)),
        active,
        small,
    )
    enc_bias_grad = enc_bias_wide[:, 0]
    dec_bias_grad = small_sum[0]
    loss_sum = small_sum[1, 0]
    grad_norm = jnp.sqrt(jnp.sum(squares) + jnp.sum(dec_bias_grad * dec_bias_grad))
    clip_scale = jnp.minimum(1.0, CLIP_NORM / (grad_norm + 1e-06))
    enc_new, enc_one, enc_two = adam_step(
        enc_weight, enc_first, enc_second, enc_acc, clip_scale, RATE_MATRIX, WEIGHT_DECAY
    )
    dec_new, dec_one, dec_two = adam_step(
        dec_weight, dec_first, dec_second, dec_grad, clip_scale, RATE_MATRIX, WEIGHT_DECAY
    )
    dec_new = dec_new * lax.rsqrt(jnp.sum(dec_new * dec_new, axis=1, keepdims=True) + NORM_EPSILON)
    bias_new, bias_one, bias_two = adam_step(
        enc_bias, enc_bias_first, enc_bias_second, enc_bias_grad, clip_scale, RATE_BIAS, 0.0
    )
    shift_new, shift_one, shift_two = adam_step(
        dec_bias, dec_bias_first, dec_bias_second, dec_bias_grad, clip_scale, RATE_BIAS, 0.0
    )
    return (
        enc_new,
        enc_one,
        enc_two,
        dec_new,
        dec_one,
        dec_two,
        bias_new,
        bias_one,
        bias_two,
        shift_new,
        shift_one,
        shift_two,
        grad_norm,
        loss_sum,
    )


def solution(mesh):
    split = P(("dp", "seq", "opt"), None)
    split_vector = P(("dp", "seq", "opt"))
    in_specs = (
        P("dp", ("seq", "opt")),
        P("dp", ("seq", "opt")),
        P(None, ("seq", "opt")),
        P(),
        P(),
        P(),
        P(),
        P(),
        P(),
        P(),
        split,
        split,
        split_vector,
        P(),
        split,
        split,
        split,
        split,
        split_vector,
        split_vector,
        P(),
        P(),
    )
    out_specs = (split,) * 6 + (split_vector,) * 3 + (P(),) * 5
    return jax.shard_map(
        functools.partial(body, mesh.shape["dp"]),
        mesh=mesh,
        in_specs=in_specs,
        out_specs=out_specs,
        check_vma=False,
    )
```

```python
import functools

import jax
import jax.numpy as jnp
import numpy as np
from jax import lax
from jax.experimental import pallas as pl
from jax.experimental.pallas import tpu as pltpu
from jax.sharding import PartitionSpec as P

HEAD = 64
ROT = 16
STEP = 4
RAMP = 80


LAYER_EPSILON = 1e-05
NORM_EPSILON = 1e-08
BETA_FIRST = 0.9
BETA_SECOND = 0.999
ADAM_EPSILON = 1e-08
RATE_MATRIX = 0.02
RATE_BIAS = 0.1
WEIGHT_DECAY = 0.01
CLIP_NORM = 1.0
SPARSITY_TOP = 5.0
COEFFICIENT = SPARSITY_TOP * min(1.0, STEP / RAMP)
LAST_LAST = (((1,), (1,)), ((), ()))
MESH = pl.DeviceIdType.MESH
ANY = pl.BlockSpec(memory_space=pl.ANY)
VMEM = pl.BlockSpec(memory_space=pltpu.VMEM)
LANES = 128


def adam_step(parameter, moment_one, moment_two, gradient, clip_scale, step_rate, decay_rate):
    gradient = gradient * clip_scale
    moment_one = BETA_FIRST * moment_one + (1.0 - BETA_FIRST) * gradient
    moment_two = BETA_SECOND * moment_two + (1.0 - BETA_SECOND) * gradient * gradient
    first_share, second_share = 1.0 / (1.0 - BETA_FIRST**STEP), 1.0 / (1.0 - BETA_SECOND**STEP)
    adjust = moment_one * first_share / (jnp.sqrt(moment_two * second_share) + ADAM_EPSILON)
    return (parameter - step_rate * (adjust + decay_rate * parameter), moment_one, moment_two)


def exclusive_or(left, right, size):
    total, bit = 0, 1
    while bit < size:
        total = total + ((left // bit + right // bit) % 2) * bit
        bit *= 2
    return total


def peers(depth):
    layer, row, column = lax.axis_index("dp"), lax.axis_index("seq"), lax.axis_index("opt")
    along = [(exclusive_or(layer, step, depth), row, column) for step in range(depth)]
    across = (layer, row, (column + 2) % 4)
    beside = (layer, 1 - row, column)
    partner = (layer, row, column + 1 - 2 * (column % 2))
    return along, across, beside, partner


def remote(source, target, send, receive, device):
    return pltpu.make_async_remote_copy(
        src_ref=source,
        dst_ref=target,
        send_sem=send,
        recv_sem=receive,
        device_id=device,
        device_id_type=MESH,
    )


def greet(devices):
    barrier = pltpu.get_barrier_semaphore()
    for device in devices:
        pl.semaphore_signal(barrier, inc=1, device_id=device, device_id_type=MESH)
    pl.semaphore_wait(barrier, len(devices))


def fold(values):
    total = values[:8]
    for first in range(8, values.shape[0], 8):
        total = total + values[first : first + 8]
    narrow = total[:, :LANES]
    for lane in range(LANES, values.shape[1], LANES):
        narrow = narrow + total[:, lane : lane + LANES]
    return narrow


class Gather:
    def __init__(self, depth, rows, held, send, receive, where):
        self.depth, self.rows, self.held = depth, rows, held
        self.send, self.receive = send, receive
        self.along, self.across, self.beside, _ = where

    def block(self, step, column, part=None):
        first, rows = (step * 4 + column) * self.rows, self.rows
        if part is not None:
            rows = self.rows // 2
            first = first + part * rows
        return self.held.at[pl.ds(pl.multiple_of(first, rows), rows)]

    def copy_along(self, step):
        return remote(
            self.block(0, 0), self.block(step, 0), self.send.at[0, step], self.receive.at[0, step], self.along[step]
        )

    def copy_across(self, step):
        return remote(
            self.block(step, 0), self.block(step, 1), self.send.at[1, step], self.receive.at[1, step], self.across
        )

    def copy_beside(self, step):
        return remote(
            self.block(step, 0), self.block(step, 2), self.send.at[2, step], self.receive.at[2, step], self.beside
        )

    def pass_across(self, step):
        return remote(
            self.block(step, 2, 0), self.block(step, 3, 0), self.send.at[3, step], self.receive.at[3, step], self.across
        )

    def pass_beside(self, step):
        return remote(
            self.block(step, 1, 1), self.block(step, 3, 1), self.send.at[4, step], self.receive.at[4, step], self.beside
        )

    def wait_along(self, step):
        remote(
            self.block(0, 0), self.block(step, 0), self.send.at[0, step], self.receive.at[0, step], self.along[0]
        ).wait_recv()

    def open(self):
        self.copy_across(0).start()
        self.copy_beside(0).start()
        for step in range(1, self.depth):
            self.copy_along(step).start()

    def spread(self, step):
        self.wait_along(step)
        self.copy_across(step).start()
        self.copy_beside(step).start()

    def hand_on(self, step):
        self.copy_across(step).wait_recv()
        self.pass_beside(step).start()
        self.copy_beside(step).wait_recv()
        self.pass_across(step).start()

    def wait_diagonal(self, step):
        self.pass_across(step).wait_recv()
        self.pass_beside(step).wait_recv()

    def close(self):
        for step in range(1, self.depth):
            self.copy_along(step).wait_send()

        def done(step, carry):
            self.copy_across(step).wait_send()
            self.copy_beside(step).wait_send()
            self.pass_across(step).wait_send()
            self.pass_beside(step).wait_send()
            return carry

        lax.fori_loop(0, self.depth, done, 0)


def ids_kernel(ids_ref, docs_ref, ids_out, docs_out, ids_all, docs_all, load_sem, send, receive):
    group = ids_all.shape[0]
    layer, row, column = lax.axis_index("dp"), lax.axis_index("seq"), lax.axis_index("opt")
    here = row * 4 + column
    others = [(here + step) % group for step in range(group)]
    devices = [(layer, index // 4, index % 4) for index in others]
    loads = [
        pltpu.make_async_copy(ids_ref, ids_all.at[here], load_sem.at[0]),
        pltpu.make_async_copy(docs_ref, docs_all.at[here], load_sem.at[1]),
    ]
    for load in loads:
        load.start()
    greet(devices[1:])
    for load in loads:
        load.wait()
    copies = []
    for step in range(1, group):
        for kind, held in enumerate((ids_all, docs_all)):
            copies.append(
                remote(held.at[here], held.at[here], send.at[kind, step], receive.at[kind, step], devices[step])
            )
    for copy in copies:
        copy.start()
    for copy in copies:
        copy.wait()
    ids_out[...] = ids_all[...]
    docs_out[...] = docs_all[...]


def gather_ids(ids, docs, group):
    rows = ids.shape[1]
    dma = pltpu.SemaphoreType.DMA
    whole = jax.ShapeDtypeStruct((group, 1, rows), jnp.int32)
    return pl.pallas_call(
        ids_kernel,
        out_shape=(whole, whole),
        in_specs=[ANY] * 2,
        out_specs=(VMEM, VMEM),
        scratch_shapes=[
            pltpu.VMEM((group, 1, rows), jnp.int32),
            pltpu.VMEM((group, 1, rows), jnp.int32),
            dma((2,)),
            dma((2, group)),
            dma((2, group)),
        ],
        compiler_params=pltpu.CompilerParams(collective_id=3, has_side_effects=True, vmem_limit_bytes=60 * 2**20),
        name="gather_ids",
    )(ids, docs)


def pick_kernel(ids_ref, table_ref, picked, table, load_sem):
    group, _, rows = ids_ref.shape
    share, vocabulary = table.shape
    parts = 3 if vocabulary % (3 * LANES) == 0 else 1
    loads = [
        pltpu.make_async_copy(
            table_ref.at[:, pl.ds(part * (vocabulary // parts), vocabulary // parts)],
            table.at[:, pl.ds(part * (vocabulary // parts), vocabulary // parts)],
            load_sem.at[part],
        )
        for part in range(parts)
    ]
    for load in loads:
        load.start()
    lanes = lax.broadcasted_iota(jnp.int32, (share, LANES), 1)
    for load in loads:
        load.wait()

    def some(part, carry):
        source, first = part // (rows // LANES), part % (rows // LANES) * LANES
        found = None
        for place in range(LANES):
            token = ids_ref[source, 0, first + place]
            start = lax.bitwise_and(token, -LANES)
            tile = table[:, pl.ds(pl.multiple_of(start, LANES), LANES)].astype(jnp.float32)
            moved = pltpu.roll(tile, lax.bitwise_and(place - token, LANES - 1), 1)
            found = moved if found is None else jnp.where(lanes >= place, moved, found)
        picked[source, :, pl.ds(pl.multiple_of(first, LANES), LANES)] = found.astype(jnp.bfloat16)
        return carry

    lax.fori_loop(0, group * rows // LANES, some, 0)


def pick(ids, table):
    group, _, rows = ids.shape
    share = table.shape[0]
    return pl.pallas_call(
        pick_kernel,
        out_shape=jax.ShapeDtypeStruct((group, share, rows), jnp.bfloat16),
        in_specs=[pl.BlockSpec(memory_space=pltpu.SMEM), ANY],
        out_specs=VMEM,
        scratch_shapes=[pltpu.VMEM(table.shape, jnp.bfloat16), pltpu.SemaphoreType.DMA((3,))],
        compiler_params=pltpu.CompilerParams(vmem_limit_bytes=60 * 2**20),
        name="pick_features",
    )(ids, table)


def front_kernel(
    picked_ref,
    docs_ref,
    gains_ref,
    shifts_ref,
    qkv_ref,
    out_ref,
    up_ref,
    down_ref,
    bias_ref,
    turn_ref,
    enc_ref,
    dec_ref,
    shift_ref,
    low_ref,
    stream_ref,
    enc_out,
    dec_out,
    turned_out,
    shift_out,
    scale_out,
    docs_all,
    gains,
    shifts,
    qkv,
    out,
    up,
    down,
    bias,
    turn,
    picked,
    features,
    turned,
    heads,
    mixed_turned,
    fed,
    enc_full,
    dec_full,
    shift_all,
    enc,
    dec,
    dec_turned,
    shift_wide,
    scale_wide,
    load_sem,
    store_sem,
    send,
    receive,
    pair_send,
    pair_receive,
):
    group, share, rows = picked.shape
    mine = enc_full.shape[0]
    dense = mine // LANES
    width = gains.shape[1]
    ff_width = up.shape[1]
    layer, row, column = lax.axis_index("dp"), lax.axis_index("seq"), lax.axis_index("opt")
    here = row * 4 + column

    def member(index):
        return (layer, index // 4, index % 4)

    others = [(here + step) % group for step in range(group)]
    first_place = pl.multiple_of(here * rows, rows)
    loads = [
        pltpu.make_async_copy(picked_ref, picked, load_sem.at[0]),
        pltpu.make_async_copy(docs_ref, docs_all, load_sem.at[1]),
        pltpu.make_async_copy(gains_ref, gains, load_sem.at[2]),
        pltpu.make_async_copy(shifts_ref, shifts, load_sem.at[3]),
        pltpu.make_async_copy(bias_ref, bias, load_sem.at[4]),
        pltpu.make_async_copy(turn_ref.at[:, pl.ds(first_place, rows)], turn, load_sem.at[5]),
        pltpu.make_async_copy(qkv_ref, qkv, load_sem.at[6]),
        pltpu.make_async_copy(up_ref, up, load_sem.at[7]),
        pltpu.make_async_copy(down_ref, down, load_sem.at[8]),
        pltpu.make_async_copy(out_ref, out, load_sem.at[9]),
        pltpu.make_async_copy(enc_ref, enc_full, load_sem.at[10]),
        pltpu.make_async_copy(dec_ref, dec_full, load_sem.at[11]),
        pltpu.make_async_copy(shift_ref, shift_all.at[column % 2], load_sem.at[12]),
    ]
    for load in loads:
        load.start()
    greet([member(index) for index in others[1:]])
    loads[0].wait()

    def copy_features(step):
        return remote(
            picked.at[others[step]],
            features.at[pl.ds(pl.multiple_of(here * share, share), share)],
            send.at[0, step],
            receive.at[0, step],
            member(others[step]),
        )

    def copy_heads(step):
        return remote(
            turned.at[others[step]], heads.at[here], send.at[1, step], receive.at[1, step], member(others[step])
        )

    def copy_mixed(index, source):
        return remote(
            picked.at[index],
            mixed_turned.at[pl.ds(pl.multiple_of(source * HEAD, HEAD), HEAD)],
            send.at[2, index],
            receive.at[2, source],
            member(index),
        )

    for step in range(1, group):
        copy_features(step).start()

    partner = (layer, row, column + 1 - 2 * (column % 2))
    own = pl.ds(pl.multiple_of(column % 2 * mine, mine), mine)
    for load in loads[10:]:
        load.wait()
    shared = []
    for kind, (full, low) in enumerate(((dec_full, dec), (enc_full, enc))):

        def cast(part, carry, full=full, low=low):
            start = pl.multiple_of(part * 256, 256)
            low[pl.ds(pl.multiple_of(column % 2 * mine + start, 256), 256)] = full[pl.ds(start, 256)].astype(
                jnp.bfloat16
            )
            return carry

        lax.fori_loop(0, mine // 256, cast, 0)
        shared.append(remote(low.at[own], low.at[own], pair_send.at[kind], pair_receive.at[kind], partner))
        shared[-1].start()
    spot = shift_all.at[column % 2]
    shared.append(remote(spot, spot, pair_send.at[2], pair_receive.at[2], partner))
    shared[-1].start()
    features[pl.ds(pl.multiple_of(here * share, share), share)] = picked[here]
    for load in loads[1:10]:
        load.wait()
    for step in range(1, group):
        copy_features(step).wait_recv()

    residual = features[...].astype(jnp.float32).T
    center = residual - jnp.mean(residual, axis=1, keepdims=True)
    variance = jnp.mean(center * center, axis=1, keepdims=True)
    unit = center * lax.rsqrt(variance + LAYER_EPSILON)
    first_norm = (unit * gains[0:1] + shifts[0:1]).astype(jnp.bfloat16)
    second_norm = (unit * gains[1:2] + shifts[1:2]).astype(jnp.bfloat16)

    def bias_row(first, count):
        lines = range(first // LANES, (first + count) // LANES)
        return jnp.concatenate([bias[line : line + 1] for line in lines], axis=1)

    half_rot = ROT // 2
    cosine, sine = turn[:half_rot], turn[half_rot:]
    for first in range(0, 3 * width, 2 * LANES):
        chunk = (
            jnp.dot(first_norm, qkv[:, first : first + 2 * LANES], preferred_element_type=jnp.float32)
            + bias_row(first, 2 * LANES)
        ).T
        for inner in range(0, 2 * LANES, HEAD):
            kind, head = (first + inner) // width, (first + inner) % width // HEAD
            values = chunk[inner : inner + HEAD]
            if kind < 2:
                left, right = values[:half_rot], values[half_rot:ROT]
                values = jnp.concatenate(
                    [left * cosine - right * sine, right * cosine + left * sine, values[ROT:]], axis=0
                )
            turned[head, kind * HEAD : (kind + 1) * HEAD] = values.astype(jnp.bfloat16)
    for step in range(1, group):
        copy_heads(step).start()
    heads[here] = turned[here]

    feed = residual + bias_row(4 * width + ff_width, width) + bias_row(3 * width, width)
    for first in range(0, ff_width, 512):
        inner = (
            jnp.dot(second_norm, up[:, first : first + 512], preferred_element_type=jnp.float32)
            + bias_row(4 * width + first, 512)
        )
        hidden = (0.5 * inner * (1.0 + lax.erf(inner * (0.5**0.5)))).astype(jnp.bfloat16)
        feed = feed + jnp.dot(hidden, down[first : first + 512], preferred_element_type=jnp.float32)
    fed[...] = feed

    for copy in shared:
        copy.wait()

    def widen(part, carry):
        start = pl.multiple_of(part * LANES, LANES)
        span = pl.ds(start, LANES)
        values = dec[span].astype(jnp.float32)
        dec_turned[:, span] = values.T.astype(jnp.bfloat16)
        norms = jnp.sqrt(jnp.sum(values * values, axis=1, keepdims=True) + NORM_EPSILON)
        scale_wide[span] = jnp.broadcast_to(COEFFICIENT * norms, (LANES, LANES))
        shift_wide[span] = jnp.broadcast_to(shift_all[part // dense, pl.ds(part % dense, 1)], (LANES, LANES)).T
        return carry

    lax.fori_loop(0, 2 * dense, widen, 0)
    stores = [
        pltpu.make_async_copy(held, target, store_sem.at[index])
        for index, (held, target) in enumerate(
            (
                (enc, enc_out),
                (dec, dec_out),
                (dec_turned, turned_out),
                (shift_wide, shift_out),
                (scale_wide, scale_out),
            )
        )
    ]
    for store in stores:
        store.start()

    for step in range(1, group):
        copy_heads(step).wait_recv()
        copy_features(step).wait_send()
    query_place = lax.broadcasted_iota(jnp.int32, (rows, rows), 0)
    key_place = lax.broadcasted_iota(jnp.int32, (rows, rows), 1)
    causal = key_place <= query_place
    scale = HEAD ** (-0.5)
    for index in reversed(range(group)):
        query = heads[index, :HEAD].astype(jnp.float32).T.astype(jnp.bfloat16)
        own_docs = jnp.broadcast_to(docs_all[index].astype(jnp.float32), (LANES, rows)).T
        own_docs = jnp.concatenate([own_docs] * (rows // LANES), axis=1)
        scores = []
        for other in range(index + 1):
            score = jnp.dot(query, heads[other, HEAD : 2 * HEAD], preferred_element_type=jnp.float32)
            allowed = own_docs == docs_all[other].astype(jnp.float32)
            if other == index:
                allowed = allowed & causal
            scores.append(jnp.where(allowed, score * scale, -1e30))
        peak = scores[0]
        for score in scores[1:]:
            peak = jnp.maximum(peak, score)
        peak = jnp.max(peak, axis=1, keepdims=True)
        weights = [jnp.exp(score - peak) for score in scores]
        total = weights[0]
        for weight in weights[1:]:
            total = total + weight
        inverse = 1.0 / jnp.sum(total, axis=1, keepdims=True)
        mixed = None
        for other in range(index + 1):
            probs = (weights[other] * inverse).astype(jnp.bfloat16)
            term = lax.dot_general(
                heads[other, 2 * HEAD :], probs, LAST_LAST, preferred_element_type=jnp.float32
            )
            mixed = term if mixed is None else mixed + term
        picked[index] = mixed.astype(jnp.bfloat16)

        @pl.when(here != index)
        def _():
            copy_mixed(index, here).start()

        @pl.when(here == index)
        def _():
            mixed_turned[pl.ds(pl.multiple_of(here * HEAD, HEAD), HEAD)] = picked[index]

    for step in range(1, group):
        copy_mixed(step, others[step]).wait_recv()
    mixed = mixed_turned[...].astype(jnp.float32).T.astype(jnp.bfloat16)
    stream = fed[...] + jnp.dot(mixed, out[...], preferred_element_type=jnp.float32)
    stream_ref[...] = stream
    low_ref[...] = stream.astype(jnp.bfloat16)
    for step in range(1, group):
        copy_heads(step).wait_send()
    for index in range(group):

        @pl.when(here != index)
        def _():
            copy_mixed(index, here).wait_send()

    for store in stores:
        store.wait()


def rotary_table(context_len):
    half_rot = ROT // 2
    frequency = np.power(np.float32(10000.0), np.float32(-2.0) * np.arange(half_rot, dtype=np.float32) / np.float32(ROT))
    angles = frequency.astype(np.float32)[:, None] * np.arange(context_len, dtype=np.float32)[None, :]
    return np.concatenate([np.cos(angles.astype(np.float64)), np.sin(angles.astype(np.float64))]).astype(np.float32)


def front(picked, docs, gains, shifts, qkv, out, up, down, bias, enc, dec, shift):
    group, share, rows = picked.shape
    width = gains.shape[1]
    ff_width = up.shape[1]
    mine = enc.shape[0]
    shift = shift.reshape(mine // LANES, LANES)
    bf16, f32 = jnp.bfloat16, jnp.float32
    dma = pltpu.SemaphoreType.DMA
    return pl.pallas_call(
        front_kernel,
        out_shape=(
            jax.ShapeDtypeStruct((rows, width), bf16),
            jax.ShapeDtypeStruct((rows, width), f32),
            jax.ShapeDtypeStruct((2 * mine, width), bf16),
            jax.ShapeDtypeStruct((2 * mine, width), bf16),
            jax.ShapeDtypeStruct((width, 2 * mine), bf16),
            jax.ShapeDtypeStruct((2 * mine, LANES), f32),
            jax.ShapeDtypeStruct((2 * mine, LANES), f32),
        ),
        in_specs=[ANY] * 13,
        out_specs=(VMEM, VMEM) + (ANY,) * 5,
        scratch_shapes=[
            pltpu.VMEM((group, 1, rows), jnp.int32),
            pltpu.VMEM((2, width), f32),
            pltpu.VMEM((2, width), f32),
            pltpu.VMEM((width, 3 * width), bf16),
            pltpu.VMEM((width, width), bf16),
            pltpu.VMEM((width, ff_width), bf16),
            pltpu.VMEM((ff_width, width), bf16),
            pltpu.VMEM(bias.shape, f32),
            pltpu.VMEM((ROT, rows), f32),
            pltpu.VMEM((group, share, rows), bf16),
            pltpu.VMEM((width, rows), bf16),
            pltpu.VMEM((group, 3 * HEAD, rows), bf16),
            pltpu.VMEM((group, 3 * HEAD, rows), bf16),
            pltpu.VMEM((width, rows), bf16),
            pltpu.VMEM((rows, width), f32),
            pltpu.VMEM((mine, width), f32),
            pltpu.VMEM((mine, width), f32),
            pltpu.VMEM((2, mine // LANES, LANES), f32),
            pltpu.VMEM((2 * mine, width), bf16),
            pltpu.VMEM((2 * mine, width), bf16),
            pltpu.VMEM((width, 2 * mine), bf16),
            pltpu.VMEM((2 * mine, LANES), f32),
            pltpu.VMEM((2 * mine, LANES), f32),
            dma((13,)),
            dma((5,)),
            dma((3, group)),
            dma((3, group)),
            dma((3,)),
            dma((3,)),
        ],
        compiler_params=pltpu.CompilerParams(
            collective_id=2, has_side_effects=True, vmem_limit_bytes=60 * 2**20
        ),
        cost_estimate=pl.CostEstimate(flops=2 * 10**9, bytes_accessed=14 * 10**6, transcendentals=2 * 10**6),
        name="front_part",
    )(picked, docs, gains, shifts, qkv, out, up, down, bias, jnp.asarray(rotary_table(group * rows)), enc, dec, shift)


def forward_kernel(
    depth,
    own_ref,
    enc_ref,
    dec_ref,
    bias_ref,
    stream_ref,
    scale_ref,
    dec_bias_ref,
    gathered_ref,
    relu_ref,
    upstream_ref,
    small_ref,
    total_ref,
    recon_ref,
    stream,
    scale,
    held,
    enc,
    dec,
    bias,
    staged,
    parts,
    send_one,
    send_two,
    send_three,
    got_one,
    got_two,
    got_three,
    load_sem,
    relu_sem,
    held_sem,
    send,
    receive,
    sum_send,
    sum_receive,
):
    rows = own_ref.shape[0]
    entries = enc.shape[0]
    width = held.shape[1]
    half = width // 2
    piece = min(entries, 256)
    where = peers(depth)
    along, across, beside, _ = where
    loads = [
        pltpu.make_async_copy(own_ref, held.at[pl.ds(0, rows)], load_sem.at[0]),
        pltpu.make_async_copy(enc_ref, enc, load_sem.at[1]),
        pltpu.make_async_copy(bias_ref, bias, load_sem.at[2]),
        pltpu.make_async_copy(dec_ref, dec, load_sem.at[3]),
        pltpu.make_async_copy(stream_ref, stream, load_sem.at[4]),
        pltpu.make_async_copy(scale_ref, scale, load_sem.at[5]),
    ]
    for load in loads:
        load.start()
    greet(along[1:] + [across, beside])
    loads[0].wait()
    gather = Gather(depth, rows, held, send, receive, where)
    gather.open()
    total_ref[...] = jnp.zeros_like(total_ref)
    for load in loads[1:]:
        load.wait()

    def copy_one(step, part):
        source = send_one.at[step % 2, pl.ds(part * half, half)]
        device = beside if part else across
        return remote(source, got_one.at[part, step], sum_send.at[part, step], sum_receive.at[part, step], device)

    def copy_two(step, part):
        device = beside if part else across
        return remote(
            send_two.at[part, step % 2],
            got_two.at[part, step],
            sum_send.at[2 + part, step],
            sum_receive.at[2 + part, step],
            device,
        )

    def copy_three(step, device):
        return remote(
            send_three.at[step], got_three.at[step], sum_send.at[4, step], sum_receive.at[4, step], device
        )

    def copy_relu(order):
        return pltpu.make_async_copy(
            staged.at[order % 2],
            relu_ref.at[:, pl.ds(pl.multiple_of(order * rows, rows), rows)],
            relu_sem.at[order % 2],
        )

    def copy_held(step):
        span = pl.ds(pl.multiple_of(step * 4 * rows, 4 * rows), 4 * rows)
        return pltpu.make_async_copy(held.at[span], gathered_ref.at[span], held_sem.at[step])

    def sum_two(step):
        copy_one(step, 0).wait_recv()
        copy_one(step, 1).wait_recv()

        @pl.when(step >= 2)
        def _():
            copy_two(step - 2, 0).wait_send()
            copy_two(step - 2, 1).wait_send()

        slot = step % 3
        upper, lower = pl.ds(0, half), pl.ds(half, half)
        send_two[1, step % 2, upper] = (parts[2, slot, upper] + got_one[0, step].astype(jnp.float32)).astype(
            jnp.bfloat16
        )
        send_two[1, step % 2, lower] = parts[2, slot, lower].astype(jnp.bfloat16)
        copy_two(step, 1).start()
        send_two[0, step % 2, upper] = parts[1, slot, upper].astype(jnp.bfloat16)
        send_two[0, step % 2, lower] = (parts[1, slot, lower] + got_one[1, step].astype(jnp.float32)).astype(
            jnp.bfloat16
        )
        copy_two(step, 0).start()

    def column_sum(step):
        copy_two(step, 0).wait_recv()
        copy_two(step, 1).wait_recv()
        return parts[0, step % 3] + got_two[0, step].astype(jnp.float32) + got_two[1, step].astype(jnp.float32)

    def sum_three(step):
        value = column_sum(step)

        @pl.when(step == 0)
        def _():
            recon_ref[...] = value

        @pl.when(step > 0)
        def _():
            send_three[step] = value.astype(jnp.bfloat16)
            layer = lax.axis_index("dp")
            target = (exclusive_or(layer, step, depth), along[0][1], along[0][2])
            copy_three(step, target).start()

    def one_block(order, carry):
        step, column = order // 4, order % 4

        @pl.when(column == 1)
        def _():
            gather.hand_on(step)

        @pl.when(column == 3)
        def _():
            gather.wait_diagonal(step)
            copy_held(step).start()

        @pl.when(order >= 2)
        def _():
            copy_relu(order - 2).wait()

        block = held[pl.ds(pl.multiple_of(order * rows, rows), rows)]
        low = []
        for first in range(0, entries, piece):
            span = pl.ds(first, piece)
            shift = bias[span]
            pre = lax.dot_general(enc[span], block, LAST_LAST, preferred_element_type=jnp.float32)
            positive = jnp.maximum(pre + jnp.concatenate([shift] * (rows // LANES), axis=1), 0.0)
            staged[order % 2, span] = positive
            active = positive * positive
            folded = active[:, :LANES]
            for lane in range(LANES, rows, LANES):
                folded = folded + active[:, lane : lane + LANES]
            total_ref[span] += folded
            low.append(active.astype(jnp.bfloat16))
        recon = jnp.dot(dec[...], jnp.concatenate(low, axis=0), preferred_element_type=jnp.float32)
        copy_relu(order).start()

        @pl.when(column < 3)
        def _():
            parts[column, step % 3] = recon

        @pl.when(column == 3)
        def _():
            @pl.when(step >= 2)
            def _():
                copy_one(step - 2, 0).wait_send()
                copy_one(step - 2, 1).wait_send()

            send_one[step % 2] = recon.astype(jnp.bfloat16)
            copy_one(step, 0).start()
            copy_one(step, 1).start()

            @pl.when(step >= 1)
            def _():
                sum_two(step - 1)

        @pl.when((column == 0) & (step + 1 < depth))
        def _():
            gather.spread(step + 1)

        @pl.when((column == 2) & (step >= 2))
        def _():
            sum_three(step - 2)

        return carry

    lax.fori_loop(0, 4 * depth, one_block, 0)
    sum_two(depth - 1)
    if depth >= 2:
        sum_three(depth - 2)
    sum_three(depth - 1)
    for step in range(1, depth):
        copy_three(step, along[step]).wait_recv()
        recon_ref[...] += got_three[step].astype(jnp.float32)
    error = recon_ref[...].T + dec_bias_ref[...] - stream[...]
    upstream = (2.0 * error).astype(jnp.bfloat16)
    upstream_ref[...] = upstream
    loss = fold(error * error)
    weighted = total_ref[...] * scale[...]
    loss = loss + fold(weighted)
    small_ref[...] = jnp.zeros_like(small_ref)
    column_sums = jnp.sum(upstream.astype(jnp.float32), axis=0, keepdims=True)
    lines = width // LANES
    for line in range(lines):
        small_ref[line : line + 1] = column_sums[:, line * LANES : (line + 1) * LANES]
    small_ref[lines : lines + 1] = jnp.sum(loss, axis=0, keepdims=True)
    gather.close()
    for step in range(max(depth - 2, 0), depth):
        for part in range(2):
            copy_one(step, part).wait_send()
            copy_two(step, part).wait_send()
    for step in range(1, depth):
        copy_three(step, along[step]).wait_send()
    copy_relu(4 * depth - 2).wait()
    copy_relu(4 * depth - 1).wait()
    for step in range(depth):
        copy_held(step).wait()


def forward(depth, own, enc, dec_turned, bias, stream, scale, dec_bias):
    rows, width = own.shape
    entries = enc.shape[0]
    bf16, f32 = jnp.bfloat16, jnp.float32
    dma = pltpu.SemaphoreType.DMA
    return pl.pallas_call(
        functools.partial(forward_kernel, depth),
        out_shape=(
            jax.ShapeDtypeStruct((depth * 4 * rows, width), bf16),
            jax.ShapeDtypeStruct((entries, depth * 4 * rows), f32),
            jax.ShapeDtypeStruct((rows, width), bf16),
            jax.ShapeDtypeStruct((8, LANES), f32),
            jax.ShapeDtypeStruct((entries, LANES), f32),
        ),
        in_specs=[ANY] * 6 + [VMEM],
        out_specs=(ANY, ANY, VMEM, VMEM, VMEM),
        scratch_shapes=[
            pltpu.VMEM((width, rows), f32),
            pltpu.VMEM((rows, width), f32),
            pltpu.VMEM((entries, LANES), f32),
            pltpu.VMEM((depth * 4 * rows, width), bf16),
            pltpu.VMEM((entries, width), bf16),
            pltpu.VMEM((width, entries), bf16),
            pltpu.VMEM((entries, LANES), f32),
            pltpu.VMEM((2, entries, rows), f32),
            pltpu.VMEM((3, 3, width, rows), f32),
            pltpu.VMEM((2, width, rows), bf16),
            pltpu.VMEM((2, 2, width, rows), bf16),
            pltpu.VMEM((depth, width, rows), bf16),
            pltpu.VMEM((2, depth, width // 2, rows), bf16),
            pltpu.VMEM((2, depth, width, rows), bf16),
            pltpu.VMEM((depth, width, rows), bf16),
            dma((6,)),
            dma((2,)),
            dma((depth,)),
            dma((5, depth)),
            dma((5, depth)),
            dma((5, depth)),
            dma((5, depth)),
        ],
        compiler_params=pltpu.CompilerParams(
            collective_id=0, has_side_effects=True, vmem_limit_bytes=60 * 2**20
        ),
        cost_estimate=pl.CostEstimate(
            flops=16 * depth * rows * entries * width, bytes_accessed=16 * depth * rows * entries, transcendentals=0
        ),
        name="forward_blocks",
    )(own, enc, dec_turned, bias, stream, scale, dec_bias)


def backward_kernel(
    depth,
    everyone,
    own_ref,
    gathered_ref,
    relu_ref,
    dec_ref,
    scale_ref,
    active_ref,
    small_ref,
    enc_out,
    dec_out,
    bias_out,
    small_out,
    squares_out,
    held,
    inputs,
    dec,
    scale,
    tile,
    enc_sum,
    dec_sum,
    bias_sum,
    enc_got,
    dec_got,
    bias_got,
    active,
    active_got,
    low,
    small,
    small_got,
    squares,
    squares_got,
    load_sem,
    tile_sem,
    store_sem,
    send,
    receive,
    pair_send,
    pair_receive,
    all_send,
    all_receive,
):
    rows = own_ref.shape[0]
    entries = dec.shape[0]
    mine = entries // 2
    piece = tile.shape[1]
    tiles = entries // piece
    where = peers(depth)
    along, across, beside, partner = where
    layer, row, column = along[0]
    core = column % 2
    loads = [
        pltpu.make_async_copy(own_ref, held.at[pl.ds(0, rows)], load_sem.at[0]),
        pltpu.make_async_copy(dec_ref, dec, load_sem.at[1]),
        pltpu.make_async_copy(scale_ref, scale, load_sem.at[2]),
        pltpu.make_async_copy(gathered_ref, inputs, load_sem.at[3]),
        pltpu.make_async_copy(active_ref, active, load_sem.at[4]),
        pltpu.make_async_copy(small_ref, small, load_sem.at[5]),
    ]
    for load in loads:
        load.start()

    def place(turn):
        return (turn + (1 - core) * (tiles // 2)) % tiles

    def group_of(group):
        if group == 0:
            return 0, 3 * rows
        if group == depth:
            return (4 * depth - 1) * rows, rows
        return (4 * group - 1) * rows, 4 * rows

    def copy_tile(group, start, size, turn):
        slot = (group * tiles + turn) % 2
        first = pl.multiple_of(place(turn) * piece, piece)
        return pltpu.make_async_copy(
            relu_ref.at[pl.ds(first, piece), pl.ds(pl.multiple_of(start, rows), size)],
            tile.at[slot, :, pl.ds(0, size)],
            tile_sem.at[slot],
        )

    copy_tile(0, *group_of(0), 0).start()

    others = [
        ((layer + dz) % depth, (row + dy) % 2, (column + dx) % 4)
        for dz in range(depth)
        for dy in range(2)
        for dx in range(4)
    ][1:]
    greet(others)
    loads[0].wait()
    gather = Gather(depth, rows, held, send, receive, where)
    gather.open()
    for load in loads[1:]:
        load.wait()

    def small_copy(index):
        return remote(
            small, small_got.at[index], all_send.at[0, index], all_receive.at[0, index], others[index - 1]
        )

    def squares_copy(index):
        return remote(
            squares, squares_got.at[index], all_send.at[1, index], all_receive.at[1, index], others[index - 1]
        )

    for index in range(1, everyone):
        small_copy(index).start()

    theirs = (1 - core) * mine
    active_copy = remote(
        active.at[pl.ds(pl.multiple_of(theirs, mine), mine)], active_got, pair_send.at[3, 0], pair_receive.at[3, 0], partner
    )
    active_copy.start()
    enc_sum[...] = jnp.zeros_like(enc_sum)
    dec_sum[...] = jnp.zeros_like(dec_sum)
    bias_sum[...] = jnp.zeros_like(bias_sum)

    def pair_copy(kind, turn):
        source, target = ((low.at[0], enc_got), (low.at[1], dec_got), (bias_sum, bias_got))[kind]
        there = pl.ds(pl.multiple_of(turn * piece, piece), piece)
        return remote(
            source.at[pl.ds(pl.multiple_of(theirs + turn * piece, piece), piece) if kind == 2 else there],
            target.at[there],
            pair_send.at[kind, turn],
            pair_receive.at[kind, turn],
            partner,
        )

    if depth > 1:
        gather.spread(1)
    gather.hand_on(0)

    def one_tile(group, start, size, turn):
        slot = (group * tiles + turn) % 2
        copy_tile(group, start, size, turn).wait()
        span = pl.ds(pl.multiple_of(place(turn) * piece, piece), piece)
        tokens = pl.ds(pl.multiple_of(start, rows), size)
        upstream = held[tokens]
        back = lax.dot_general(dec[span], upstream, LAST_LAST, preferred_element_type=jnp.float32)
        positive = tile[slot, :, :size]
        shift = jnp.concatenate([scale[span]] * (size // LANES), axis=1)
        slope = ((back + shift) * (2.0 * positive)).astype(jnp.bfloat16)
        act_low = (positive * positive).astype(jnp.bfloat16)
        wide = slope.astype(jnp.float32)
        folded = wide[:, :LANES]
        for lane in range(LANES, size, LANES):
            folded = folded + wide[:, lane : lane + LANES]
        bias_sum[span] += folded
        enc_sum[span] += jnp.dot(slope, inputs[tokens], preferred_element_type=jnp.float32)
        dec_sum[span] += jnp.dot(act_low, upstream, preferred_element_type=jnp.float32)

    def first_group(turn, carry):
        start, size = group_of(0)

        @pl.when(turn + 1 < tiles)
        def _():
            copy_tile(0, start, size, turn + 1).start()

        @pl.when(turn + 1 == tiles)
        def _():
            copy_tile(1, *group_of(1), 0).start()

        one_tile(0, start, size, turn)
        return carry

    def middle_group(group, carry):
        start, size = (4 * group - 1) * rows, 4 * rows
        gather.hand_on(group)

        @pl.when(group == 1)
        def _():
            if depth > 2:
                gather.spread(2)

        gather.wait_diagonal(group - 1)

        def one(turn, carry):
            @pl.when(turn + 1 < tiles)
            def _():
                copy_tile(group, start, size, turn + 1).start()

            @pl.when((turn + 1 == tiles) & (group + 1 < depth))
            def _():
                copy_tile(group + 1, start + 4 * rows, size, 0).start()

            @pl.when((turn + 1 == tiles) & (group + 1 == depth))
            def _():
                copy_tile(depth, *group_of(depth), 0).start()

            one_tile(group, start, size, turn)

            @pl.when((turn == tiles // 2) & (group + 2 < depth))
            def _():
                gather.spread(group + 2)

            return carry

        return lax.fori_loop(0, tiles, one, carry)

    def last_group(turn, carry):
        start, size = group_of(depth)

        @pl.when(turn + 1 < tiles)
        def _():
            copy_tile(depth, start, size, turn + 1).start()

        one_tile(depth, start, size, turn)

        @pl.when(turn < tiles // 2)
        def _():
            span = pl.ds(pl.multiple_of(place(turn) * piece, piece), piece)
            there = pl.ds(pl.multiple_of(turn * piece, piece), piece)
            low[0, there] = enc_sum[span].astype(jnp.bfloat16)
            low[1, there] = dec_sum[span].astype(jnp.bfloat16)
            for kind in range(3):
                pair_copy(kind, turn).start()

        return carry

    lax.fori_loop(0, tiles, first_group, 0)
    lax.fori_loop(1, depth, middle_group, 0)
    gather.wait_diagonal(depth - 1)
    lax.fori_loop(0, tiles, last_group, 0)

    ours = core * mine
    active_copy.wait_recv()
    span = pl.ds(pl.multiple_of(ours, mine), mine)
    act_total = jnp.sum(active[span] + active_got[...], axis=1, keepdims=True)
    partial = jnp.zeros((8, LANES), jnp.float32)

    stores = []
    rows_of = lax.broadcasted_iota(jnp.int32, (LANES, LANES), 0)
    lanes_of = lax.broadcasted_iota(jnp.int32, (LANES, LANES), 1)
    for turn in range(tiles // 2):
        for kind in range(3):
            pair_copy(kind, turn).wait_recv()
        near = pl.ds(pl.multiple_of(ours + turn * piece, piece), piece)
        there = pl.ds(turn * piece, piece)
        enc_grad = enc_sum[near] + enc_got[there].astype(jnp.float32)
        enc_sum[near] = enc_grad
        partial = partial + fold(enc_grad * enc_grad)
        dec_grad = dec_sum[near] + dec_got[there].astype(jnp.float32)
        dec_grad = dec_grad + (
            COEFFICIENT * COEFFICIENT * act_total[turn * piece : (turn + 1) * piece] / scale[near, :1]
        ) * dec[near].astype(jnp.float32)
        dec_sum[near] = dec_grad
        partial = partial + fold(dec_grad * dec_grad)
        stores += [
            pltpu.make_async_copy(enc_sum.at[near], enc_out.at[there], store_sem.at[0, turn]),
            pltpu.make_async_copy(dec_sum.at[near], dec_out.at[there], store_sem.at[1, turn]),
        ]
        stores[-2].start()
        stores[-1].start()
        bias_grad = jnp.sum(bias_sum[near] + bias_got[there], axis=1, keepdims=True)
        for first in range(0, piece, LANES):
            wide = jnp.broadcast_to(bias_grad[first : first + LANES], (LANES, LANES))
            line = jnp.sum(jnp.where(rows_of == lanes_of, wide, 0.0), axis=0, keepdims=True)
            index = (turn * piece + first) // LANES
            bias_out[index : index + 1] = line
            partial = partial + jnp.where(rows_of[:8] == 0, line * line, 0.0)
    squares[...] = partial
    for index in range(1, everyone):
        squares_copy(index).start()
    total_small = small[...]
    for index in range(1, everyone):
        small_copy(index).wait_recv()
        total_small = total_small + small_got[index]
    small_out[...] = total_small
    total_squares = squares[...]
    for index in range(1, everyone):
        squares_copy(index).wait_recv()
        total_squares = total_squares + squares_got[index]
    squares_out[...] = total_squares
    gather.close()
    for index in range(1, everyone):
        small_copy(index).wait_send()
        squares_copy(index).wait_send()
    active_copy.wait_send()
    for turn in range(tiles // 2):
        for kind in range(3):
            pair_copy(kind, turn).wait_send()
    for store in stores:
        store.wait()


def backward(depth, own, gathered, relu, dec, scale, active, small):
    rows, width = own.shape
    entries = dec.shape[0]
    mine = entries // 2
    piece = min(512, mine)
    everyone = depth * 8
    bf16, f32 = jnp.bfloat16, jnp.float32
    dma = pltpu.SemaphoreType.DMA
    return pl.pallas_call(
        functools.partial(backward_kernel, depth, everyone),
        out_shape=(
            jax.ShapeDtypeStruct((mine, width), f32),
            jax.ShapeDtypeStruct((mine, width), f32),
            jax.ShapeDtypeStruct((mine // LANES, LANES), f32),
            jax.ShapeDtypeStruct(small.shape, f32),
            jax.ShapeDtypeStruct((8, LANES), f32),
        ),
        in_specs=[ANY] * 7,
        out_specs=(ANY, ANY, VMEM, VMEM, VMEM),
        scratch_shapes=[
            pltpu.VMEM((depth * 4 * rows, width), bf16),
            pltpu.VMEM((depth * 4 * rows, width), bf16),
            pltpu.VMEM((entries, width), bf16),
            pltpu.VMEM((entries, LANES), f32),
            pltpu.VMEM((2, piece, 4 * rows), f32),
            pltpu.VMEM((entries, width), f32),
            pltpu.VMEM((entries, width), f32),
            pltpu.VMEM((entries, LANES), f32),
            pltpu.VMEM((mine, width), bf16),
            pltpu.VMEM((mine, width), bf16),
            pltpu.VMEM((mine, LANES), f32),
            pltpu.VMEM((entries, LANES), f32),
            pltpu.VMEM((mine, LANES), f32),
            pltpu.VMEM((2, mine, width), bf16),
            pltpu.VMEM(small.shape, f32),
            pltpu.VMEM((everyone,) + small.shape, f32),
            pltpu.VMEM((8, LANES), f32),
            pltpu.VMEM((everyone, 8, LANES), f32),
            dma((6,)),
            dma((2,)),
            dma((2, entries // piece)),
            dma((5, depth)),
            dma((5, depth)),
            dma((4, entries // piece)),
            dma((4, entries // piece)),
            dma((2, everyone)),
            dma((2, everyone)),
        ],
        compiler_params=pltpu.CompilerParams(
            collective_id=1, has_side_effects=True, vmem_limit_bytes=60 * 2**20
        ),
        cost_estimate=pl.CostEstimate(
            flops=24 * depth * rows * entries * width, bytes_accessed=16 * depth * rows * entries, transcendentals=0
        ),
        name="backward_blocks",
    )(own, gathered, relu, dec, scale, active, small)


def update_kernel(*refs):
    names = ["enc_grad", "dec_grad", "bias_grad", "small", "squares"]
    for kind in ("enc", "dec", "bias", "shift"):
        names += [kind, kind + "_one", kind + "_two"]
    given = dict(zip(names, refs[: len(names)]))
    made = refs[len(names) : len(names) + 14]
    brought, staged, load_sem, store_sem = refs[len(names) + 14 :]
    mine = given["enc"].shape[0]
    slots, _, piece, _ = staged.shape
    parts = mine // piece
    large = ["enc", "enc_one", "enc_two", "enc_grad", "dec", "dec_one", "dec_two", "dec_grad"]

    def load(part, index):
        span = pl.ds(pl.multiple_of(part * piece, piece), piece)
        slot = part % slots
        return pltpu.make_async_copy(given[large[index]].at[span], brought.at[slot, index], load_sem.at[slot, index])

    for part in range(min(slots - 1, parts)):
        for index in range(8):
            load(part, index).start()
    lines = given["shift"].shape[1] // LANES
    shift_grad = jnp.concatenate([given["small"][line : line + 1] for line in range(lines)], axis=1)
    total = jnp.sum(given["squares"][...], keepdims=True) + jnp.sum(shift_grad * shift_grad, keepdims=True)
    norm = jnp.sqrt(total)
    clip = jnp.minimum(1.0, CLIP_NORM / (norm + 1e-06))
    made[12][...] = norm
    made[13][...] = jnp.sum(given["small"][lines : lines + 1], keepdims=True)

    def store(part, index):
        span = pl.ds(pl.multiple_of(part * piece, piece), piece)
        slot = part % slots
        return pltpu.make_async_copy(staged.at[slot, index], made[index].at[span], store_sem.at[slot, index])

    def one(part, carry):
        @pl.when(part >= slots)
        def _():
            for index in range(6):
                store(part - slots, index).wait()

        @pl.when(part + slots - 1 < parts)
        def _():
            for index in range(8):
                load(part + slots - 1, index).start()

        slot = part % slots
        for index in range(8):
            load(part, index).wait()
        for index in range(2):
            new, first, second = adam_step(
                *(brought[slot, 4 * index + offset] for offset in range(4)),
                clip,
                RATE_MATRIX,
                WEIGHT_DECAY,
            )
            if index:
                new = new * lax.rsqrt(jnp.sum(new * new, axis=1, keepdims=True) + NORM_EPSILON)
            for offset, value in enumerate((new, first, second)):
                staged[slot, 3 * index + offset] = value
        for index in range(6):
            store(part, index).start()
        return carry

    lax.fori_loop(0, parts, one, 0)
    for offset, (kind, gradient) in enumerate((("bias", given["bias_grad"][...]), ("shift", shift_grad))):
        results = adam_step(
            given[kind][...], given[kind + "_one"][...], given[kind + "_two"][...], gradient, clip, RATE_BIAS, 0.0
        )
        for index, value in enumerate(results):
            made[6 + 3 * offset + index][...] = value
    for part in range(max(parts - slots, 0), parts):
        for index in range(6):
            store(part, index).wait()


def update(*arrays):
    f32 = jnp.float32
    mine, width = arrays[0].shape
    dense, flat = (mine // LANES, LANES), (1, width)
    arrays = list(arrays)
    for index in range(11, 14):
        arrays[index] = arrays[index].reshape(dense)
    for index in range(14, 17):
        arrays[index] = arrays[index].reshape(flat)
    piece, slots = min(128, mine), 3
    made = pl.pallas_call(
        update_kernel,
        out_shape=[jax.ShapeDtypeStruct((mine, width), f32)] * 6
        + [jax.ShapeDtypeStruct(dense, f32)] * 3
        + [jax.ShapeDtypeStruct(flat, f32)] * 3
        + [jax.ShapeDtypeStruct((1, 1), f32)] * 2,
        in_specs=[ANY] * 2 + [VMEM] * 3 + [ANY] * 6 + [VMEM] * 6,
        out_specs=[ANY] * 6 + [VMEM] * 8,
        scratch_shapes=[
            pltpu.VMEM((slots, 8, piece, width), f32),
            pltpu.VMEM((slots, 6, piece, width), f32),
            pltpu.SemaphoreType.DMA((slots, 8)),
            pltpu.SemaphoreType.DMA((slots, 6)),
        ],
        compiler_params=pltpu.CompilerParams(vmem_limit_bytes=60 * 2**20),
        cost_estimate=pl.CostEstimate(flops=60 * mine * width, bytes_accessed=56 * mine * width, transcendentals=4 * mine * width),
        name="update",
    )(*arrays)
    return (
        *made[:6],
        *(value.reshape(mine) for value in made[6:9]),
        *(value.reshape(width) for value in made[9:12]),
        made[12].reshape(()),
        made[13].reshape(()),
    )


def body(
    depth,
    token_ids,
    doc_ids,
    embed,
    norm_gains,
    norm_shifts,
    qkv_weight,
    out_weight,
    up_weight,
    down_weight,
    proj_biases,
    enc_weight,
    dec_weight,
    enc_bias,
    dec_bias,
    enc_first,
    enc_second,
    dec_first,
    dec_second,
    enc_bias_first,
    enc_bias_second,
    dec_bias_first,
    dec_bias_second,
):
    model_width = norm_gains.shape[1]
    all_ids, all_docs = gather_ids(token_ids, doc_ids, model_width // embed.shape[1])
    low, stream, enc_both, dec_both, dec_turned, shift_wide, scale_wide = front(
        pick(all_ids, embed.T),
        all_docs,
        norm_gains,
        norm_shifts,
        qkv_weight,
        out_weight,
        up_weight,
        down_weight,
        proj_biases.reshape(-1, LANES),
        enc_weight,
        dec_weight,
        enc_bias,
    )
    gathered, relu, upstream, small, active = forward(
        depth, low, enc_both, dec_turned, shift_wide, stream, scale_wide, dec_bias[None]
    )
    enc_grad, dec_grad, enc_bias_grad, small_sum, squares = backward(
        depth, upstream, gathered, relu, dec_both, scale_wide, active, small
    )
    return update(
        enc_grad,
        dec_grad,
        enc_bias_grad,
        small_sum,
        squares,
        enc_weight,
        enc_first,
        enc_second,
        dec_weight,
        dec_first,
        dec_second,
        enc_bias,
        enc_bias_first,
        enc_bias_second,
        dec_bias,
        dec_bias_first,
        dec_bias_second,
    )


def solution(mesh):
    split = P(("dp", "seq", "opt"), None)
    split_vector = P(("dp", "seq", "opt"))
    in_specs = (
        P("dp", ("seq", "opt")),
        P("dp", ("seq", "opt")),
        P(None, ("seq", "opt")),
        P(),
        P(),
        P(),
        P(),
        P(),
        P(),
        P(),
        split,
        split,
        split_vector,
        P(),
        split,
        split,
        split,
        split,
        split_vector,
        split_vector,
        P(),
        P(),
    )
    out_specs = (split,) * 6 + (split_vector,) * 3 + (P(),) * 5
    return jax.shard_map(
        functools.partial(body, mesh.shape["dp"]),
        mesh=mesh,
        in_specs=in_specs,
        out_specs=out_specs,
        check_vma=False,
    )
```

```python
import functools

import jax
import jax.numpy as jnp
import numpy as np
from jax import lax
from jax.experimental import pallas as pl
from jax.experimental.pallas import tpu as pltpu
from jax.sharding import PartitionSpec as P

HEAD = 64
ROT = 16
STEP = 4
RAMP = 80


LAYER_EPSILON = 1e-05
NORM_EPSILON = 1e-08
BETA_FIRST = 0.9
BETA_SECOND = 0.999
ADAM_EPSILON = 1e-08
RATE_MATRIX = 0.02
RATE_BIAS = 0.1
WEIGHT_DECAY = 0.01
CLIP_NORM = 1.0
SPARSITY_TOP = 5.0
COEFFICIENT = SPARSITY_TOP * min(1.0, STEP / RAMP)
LAST_LAST = (((1,), (1,)), ((), ()))
MESH = pl.DeviceIdType.MESH
ANY = pl.BlockSpec(memory_space=pl.ANY)
VMEM = pl.BlockSpec(memory_space=pltpu.VMEM)
LANES = 128


def adam_step(parameter, moment_one, moment_two, gradient, clip_scale, step_rate, decay_rate):
    gradient = gradient * clip_scale
    moment_one = BETA_FIRST * moment_one + (1.0 - BETA_FIRST) * gradient
    moment_two = BETA_SECOND * moment_two + (1.0 - BETA_SECOND) * gradient * gradient
    first_share, second_share = 1.0 / (1.0 - BETA_FIRST**STEP), 1.0 / (1.0 - BETA_SECOND**STEP)
    adjust = moment_one * first_share / (jnp.sqrt(moment_two * second_share) + ADAM_EPSILON)
    return (parameter - step_rate * (adjust + decay_rate * parameter), moment_one, moment_two)


def place_of(depth, layer, other):
    distance = jnp.abs(other - layer)
    margin = jnp.minimum(layer, depth - 1 - layer)
    near = jnp.where(other < layer, 2 * distance - 1, 2 * distance)
    return jnp.where(distance <= margin, near, distance + margin)


def layer_at(depth, layer, turn):
    margin = jnp.minimum(layer, depth - 1 - layer)
    near = jnp.where(turn % 2 == 1, layer - (turn + 1) // 2, layer + turn // 2)
    far = jnp.where(2 * layer < depth - 1, layer + turn - margin, layer - turn + margin)
    return jnp.where(turn <= 2 * margin, near, far)


def crosswise(turn):
    return (turn == 0) | (turn >= 3)


def takers(depth, layer):
    return [
        (layer + 1, layer + 1 < depth),
        (layer - 1, layer >= 1),
        (layer * 0, layer == 2),
        (layer * 0 + depth - 1, layer == depth - 3),
    ]


def peers(depth):
    layer, row, column = lax.axis_index("dp"), lax.axis_index("seq"), lax.axis_index("opt")
    across = (layer, row, (column + 2) % 4)
    beside = (layer, 1 - row, column)
    partner = (layer, row, column + 1 - 2 * (column % 2))
    return (layer, row, column), across, beside, partner


def remote(source, target, send, receive, device):
    return pltpu.make_async_remote_copy(
        src_ref=source,
        dst_ref=target,
        send_sem=send,
        recv_sem=receive,
        device_id=device,
        device_id_type=MESH,
    )


def greet(devices):
    barrier = pltpu.get_barrier_semaphore()
    for device in devices:
        pl.semaphore_signal(barrier, inc=1, device_id=device, device_id_type=MESH)
    pl.semaphore_wait(barrier, len(devices))


def fold(values):
    total = values[:8]
    for first in range(8, values.shape[0], 8):
        total = total + values[first : first + 8]
    narrow = total[:, :LANES]
    for lane in range(LANES, values.shape[1], LANES):
        narrow = narrow + total[:, lane : lane + LANES]
    return narrow


class Gather:
    def __init__(self, depth, rows, held, send, receive, where):
        self.depth, self.rows, self.held = depth, rows, held
        self.send, self.receive = send, receive
        self.here, self.across, self.beside, _ = where

    def block(self, turn, column, part=None):
        first, rows = (turn * 4 + column) * self.rows, self.rows
        if part is not None:
            rows = self.rows // 2
            first = first + part * rows
        return self.held.at[pl.ds(pl.multiple_of(first, rows), rows)]

    def device(self, layer):
        return (layer, self.here[1], self.here[2])

    def copy_along(self, distance, sign):
        layer = self.here[0] + sign * distance
        turn = place_of(self.depth, layer, self.here[0])
        return remote(
            self.block(0, 0),
            self.block(turn, 0),
            self.send.at[(1 - sign) // 2, distance],
            self.receive.at[0, turn],
            self.device(layer),
        )

    def copy_across(self, turn):
        return remote(
            self.block(turn, 0), self.block(turn, 1), self.send.at[2, turn], self.receive.at[1, turn], self.across
        )

    def copy_beside(self, turn):
        return remote(
            self.block(turn, 0), self.block(turn, 2), self.send.at[3, turn], self.receive.at[2, turn], self.beside
        )

    def pass_across(self, turn):
        return remote(
            self.block(turn, 2, 0), self.block(turn, 3, 0), self.send.at[4, turn], self.receive.at[3, turn], self.across
        )

    def pass_beside(self, turn):
        return remote(
            self.block(turn, 1, 1), self.block(turn, 3, 1), self.send.at[5, turn], self.receive.at[4, turn], self.beside
        )

    def pass_along(self, index, layer):
        turn = place_of(self.depth, layer, self.here[0])
        return remote(
            self.block(0, 3), self.block(turn, 3), self.send.at[6, index], self.receive.at[5, turn], self.device(layer)
        )

    def wave(self, distance, act):
        for sign in (1, -1):
            layer = self.here[0] + sign * distance

            @pl.when((layer >= 0) & (layer < self.depth))
            def _(sign=sign):
                act(self.copy_along(distance, sign))

    def open(self):
        self.copy_across(0).start()
        self.copy_beside(0).start()
        self.wave(1, lambda copy: copy.start())

    def second_wave(self):
        if self.depth > 2:
            self.wave(2, lambda copy: copy.start())

    def spread(self, turn):
        remote(
            self.block(0, 0), self.block(turn, 0), self.send.at[0, 0], self.receive.at[0, turn], self.across
        ).wait_recv()
        self.copy_across(turn).start()
        self.copy_beside(turn).start()

    def hand_on(self, turn):
        self.copy_across(turn).wait_recv()

        @pl.when(crosswise(turn))
        def _():
            self.pass_beside(turn).start()

        self.copy_beside(turn).wait_recv()

        @pl.when(crosswise(turn))
        def _():
            self.pass_across(turn).start()

    def wait_diagonal(self, turn):
        @pl.when(crosswise(turn))
        def _():
            self.pass_across(turn).wait_recv()
            self.pass_beside(turn).wait_recv()

        @pl.when((turn == 1) | (turn == 2))
        def _():
            remote(
                self.block(0, 3), self.block(turn, 3), self.send.at[6, 0], self.receive.at[5, turn], self.across
            ).wait_recv()

        @pl.when(turn == 0)
        def _():
            for index, (layer, there) in enumerate(takers(self.depth, self.here[0])):

                @pl.when(there)
                def _(index=index, layer=layer):
                    self.pass_along(index, layer).start()

            for distance in range(3, self.depth):
                self.wave(distance, lambda copy: copy.start())

    def close(self):
        for distance in range(1, self.depth):
            self.wave(distance, lambda copy: copy.wait_send())
        for index, (layer, there) in enumerate(takers(self.depth, self.here[0])):

            @pl.when(there)
            def _(index=index, layer=layer):
                self.pass_along(index, layer).wait_send()

        def done(turn, carry):
            self.copy_across(turn).wait_send()
            self.copy_beside(turn).wait_send()

            @pl.when(crosswise(turn))
            def _():
                self.pass_across(turn).wait_send()
                self.pass_beside(turn).wait_send()

            return carry

        lax.fori_loop(0, self.depth, done, 0)


def ids_kernel(ids_ref, docs_ref, ids_out, docs_out, ids_all, docs_all, load_sem, send, receive):
    group = ids_all.shape[0]
    layer, row, column = lax.axis_index("dp"), lax.axis_index("seq"), lax.axis_index("opt")
    here = row * 4 + column
    others = [(here + step) % group for step in range(group)]
    devices = [(layer, index // 4, index % 4) for index in others]
    loads = [
        pltpu.make_async_copy(ids_ref, ids_all.at[here], load_sem.at[0]),
        pltpu.make_async_copy(docs_ref, docs_all.at[here], load_sem.at[1]),
    ]
    for load in loads:
        load.start()
    greet(devices[1:])
    for load in loads:
        load.wait()
    copies = []
    for step in range(1, group):
        for kind, held in enumerate((ids_all, docs_all)):
            copies.append(
                remote(held.at[here], held.at[here], send.at[kind, step], receive.at[kind, step], devices[step])
            )
    for copy in copies:
        copy.start()
    for copy in copies:
        copy.wait()
    ids_out[...] = ids_all[...]
    docs_out[...] = docs_all[...]


def gather_ids(ids, docs, group):
    rows = ids.shape[1]
    dma = pltpu.SemaphoreType.DMA
    whole = jax.ShapeDtypeStruct((group, 1, rows), jnp.int32)
    return pl.pallas_call(
        ids_kernel,
        out_shape=(whole, whole),
        in_specs=[ANY] * 2,
        out_specs=(VMEM, VMEM),
        scratch_shapes=[
            pltpu.VMEM((group, 1, rows), jnp.int32),
            pltpu.VMEM((group, 1, rows), jnp.int32),
            dma((2,)),
            dma((2, group)),
            dma((2, group)),
        ],
        compiler_params=pltpu.CompilerParams(collective_id=3, has_side_effects=True, vmem_limit_bytes=60 * 2**20),
        name="gather_ids",
    )(ids, docs)


def pick_kernel(ids_ref, table_ref, picked, table, load_sem):
    group, _, rows = ids_ref.shape
    share, vocabulary = table.shape
    parts = 3 if vocabulary % (3 * LANES) == 0 else 1
    loads = [
        pltpu.make_async_copy(
            table_ref.at[:, pl.ds(part * (vocabulary // parts), vocabulary // parts)],
            table.at[:, pl.ds(part * (vocabulary // parts), vocabulary // parts)],
            load_sem.at[part],
        )
        for part in range(parts)
    ]
    for load in loads:
        load.start()
    lanes = lax.broadcasted_iota(jnp.int32, (share, LANES), 1)
    for load in loads:
        load.wait()

    def some(part, carry):
        source, first = part // (rows // LANES), part % (rows // LANES) * LANES
        found = None
        for place in range(LANES):
            token = ids_ref[source, 0, first + place]
            start = lax.bitwise_and(token, -LANES)
            tile = table[:, pl.ds(pl.multiple_of(start, LANES), LANES)].astype(jnp.float32)
            moved = pltpu.roll(tile, lax.bitwise_and(place - token, LANES - 1), 1)
            found = moved if found is None else jnp.where(lanes >= place, moved, found)
        picked[source, :, pl.ds(pl.multiple_of(first, LANES), LANES)] = found.astype(jnp.bfloat16)
        return carry

    lax.fori_loop(0, group * rows // LANES, some, 0)


def pick(ids, table):
    group, _, rows = ids.shape
    share = table.shape[0]
    return pl.pallas_call(
        pick_kernel,
        out_shape=jax.ShapeDtypeStruct((group, share, rows), jnp.bfloat16),
        in_specs=[pl.BlockSpec(memory_space=pltpu.SMEM), ANY],
        out_specs=VMEM,
        scratch_shapes=[pltpu.VMEM(table.shape, jnp.bfloat16), pltpu.SemaphoreType.DMA((3,))],
        compiler_params=pltpu.CompilerParams(vmem_limit_bytes=60 * 2**20),
        name="pick_features",
    )(ids, table)


def front_kernel(
    picked_ref,
    docs_ref,
    gains_ref,
    shifts_ref,
    qkv_ref,
    out_ref,
    up_ref,
    down_ref,
    bias_ref,
    turn_ref,
    enc_ref,
    dec_ref,
    shift_ref,
    low_ref,
    stream_ref,
    enc_out,
    dec_out,
    turned_out,
    shift_out,
    scale_out,
    docs_all,
    gains,
    shifts,
    qkv,
    out,
    up,
    down,
    bias,
    turn,
    picked,
    features,
    turned,
    heads,
    mixed_turned,
    fed,
    enc_full,
    dec_full,
    shift_all,
    enc,
    dec,
    dec_turned,
    shift_wide,
    scale_wide,
    load_sem,
    store_sem,
    send,
    receive,
    pair_send,
    pair_receive,
):
    group, share, rows = picked.shape
    mine = enc_full.shape[0]
    dense = mine // LANES
    width = gains.shape[1]
    ff_width = up.shape[1]
    layer, row, column = lax.axis_index("dp"), lax.axis_index("seq"), lax.axis_index("opt")
    here = row * 4 + column

    def member(index):
        return (layer, index // 4, index % 4)

    others = [(here + step) % group for step in range(group)]
    first_place = pl.multiple_of(here * rows, rows)
    loads = [
        pltpu.make_async_copy(picked_ref, picked, load_sem.at[0]),
        pltpu.make_async_copy(docs_ref, docs_all, load_sem.at[1]),
        pltpu.make_async_copy(gains_ref, gains, load_sem.at[2]),
        pltpu.make_async_copy(shifts_ref, shifts, load_sem.at[3]),
        pltpu.make_async_copy(bias_ref, bias, load_sem.at[4]),
        pltpu.make_async_copy(turn_ref.at[:, pl.ds(first_place, rows)], turn, load_sem.at[5]),
        pltpu.make_async_copy(qkv_ref, qkv, load_sem.at[6]),
        pltpu.make_async_copy(up_ref, up, load_sem.at[7]),
        pltpu.make_async_copy(down_ref, down, load_sem.at[8]),
        pltpu.make_async_copy(out_ref, out, load_sem.at[9]),
        pltpu.make_async_copy(enc_ref, enc_full, load_sem.at[10]),
        pltpu.make_async_copy(dec_ref, dec_full, load_sem.at[11]),
        pltpu.make_async_copy(shift_ref, shift_all.at[column % 2], load_sem.at[12]),
    ]
    for load in loads:
        load.start()
    greet([member(index) for index in others[1:]])
    loads[0].wait()

    def copy_features(step):
        return remote(
            picked.at[others[step]],
            features.at[pl.ds(pl.multiple_of(here * share, share), share)],
            send.at[0, step],
            receive.at[0, step],
            member(others[step]),
        )

    def copy_heads(step):
        return remote(
            turned.at[others[step]], heads.at[here], send.at[1, step], receive.at[1, step], member(others[step])
        )

    def copy_mixed(index, source):
        return remote(
            picked.at[index],
            mixed_turned.at[pl.ds(pl.multiple_of(source * HEAD, HEAD), HEAD)],
            send.at[2, index],
            receive.at[2, source],
            member(index),
        )

    for step in range(1, group):
        copy_features(step).start()

    partner = (layer, row, column + 1 - 2 * (column % 2))
    own = pl.ds(pl.multiple_of(column % 2 * mine, mine), mine)
    for load in loads[10:]:
        load.wait()
    shared = []
    for kind, (full, low) in enumerate(((dec_full, dec), (enc_full, enc))):

        def cast(part, carry, full=full, low=low):
            start = pl.multiple_of(part * 256, 256)
            low[pl.ds(pl.multiple_of(column % 2 * mine + start, 256), 256)] = full[pl.ds(start, 256)].astype(
                jnp.bfloat16
            )
            return carry

        lax.fori_loop(0, mine // 256, cast, 0)
        shared.append(remote(low.at[own], low.at[own], pair_send.at[kind], pair_receive.at[kind], partner))
        shared[-1].start()
    spot = shift_all.at[column % 2]
    shared.append(remote(spot, spot, pair_send.at[2], pair_receive.at[2], partner))
    shared[-1].start()
    features[pl.ds(pl.multiple_of(here * share, share), share)] = picked[here]
    for load in loads[1:10]:
        load.wait()
    for step in range(1, group):
        copy_features(step).wait_recv()

    residual = features[...].astype(jnp.float32).T
    center = residual - jnp.mean(residual, axis=1, keepdims=True)
    variance = jnp.mean(center * center, axis=1, keepdims=True)
    unit = center * lax.rsqrt(variance + LAYER_EPSILON)
    first_norm = (unit * gains[0:1] + shifts[0:1]).astype(jnp.bfloat16)
    second_norm = (unit * gains[1:2] + shifts[1:2]).astype(jnp.bfloat16)

    def bias_row(first, count):
        lines = range(first // LANES, (first + count) // LANES)
        return jnp.concatenate([bias[line : line + 1] for line in lines], axis=1)

    half_rot = ROT // 2
    cosine, sine = turn[:half_rot], turn[half_rot:]
    for first in range(0, 3 * width, 2 * LANES):
        chunk = (
            jnp.dot(first_norm, qkv[:, first : first + 2 * LANES], preferred_element_type=jnp.float32)
            + bias_row(first, 2 * LANES)
        ).T
        for inner in range(0, 2 * LANES, HEAD):
            kind, head = (first + inner) // width, (first + inner) % width // HEAD
            values = chunk[inner : inner + HEAD]
            if kind < 2:
                left, right = values[:half_rot], values[half_rot:ROT]
                values = jnp.concatenate(
                    [left * cosine - right * sine, right * cosine + left * sine, values[ROT:]], axis=0
                )
            turned[head, kind * HEAD : (kind + 1) * HEAD] = values.astype(jnp.bfloat16)
    for step in range(1, group):
        copy_heads(step).start()
    heads[here] = turned[here]

    feed = residual + bias_row(4 * width + ff_width, width) + bias_row(3 * width, width)
    for first in range(0, ff_width, 512):
        inner = (
            jnp.dot(second_norm, up[:, first : first + 512], preferred_element_type=jnp.float32)
            + bias_row(4 * width + first, 512)
        )
        hidden = (0.5 * inner * (1.0 + lax.erf(inner * (0.5**0.5)))).astype(jnp.bfloat16)
        feed = feed + jnp.dot(hidden, down[first : first + 512], preferred_element_type=jnp.float32)
    fed[...] = feed

    for copy in shared:
        copy.wait()

    def widen(part, carry):
        start = pl.multiple_of(part * LANES, LANES)
        span = pl.ds(start, LANES)
        values = dec[span].astype(jnp.float32)
        dec_turned[:, span] = values.T.astype(jnp.bfloat16)
        norms = jnp.sqrt(jnp.sum(values * values, axis=1, keepdims=True) + NORM_EPSILON)
        scale_wide[span] = jnp.broadcast_to(COEFFICIENT * norms, (LANES, LANES))
        shift_wide[span] = jnp.broadcast_to(shift_all[part // dense, pl.ds(part % dense, 1)], (LANES, LANES)).T
        return carry

    lax.fori_loop(0, 2 * dense, widen, 0)
    stores = [
        pltpu.make_async_copy(held, target, store_sem.at[index])
        for index, (held, target) in enumerate(
            (
                (enc, enc_out),
                (dec, dec_out),
                (dec_turned, turned_out),
                (shift_wide, shift_out),
                (scale_wide, scale_out),
            )
        )
    ]
    for store in stores:
        store.start()

    for step in range(1, group):
        copy_heads(step).wait_recv()
        copy_features(step).wait_send()
    query_place = lax.broadcasted_iota(jnp.int32, (rows, rows), 0)
    key_place = lax.broadcasted_iota(jnp.int32, (rows, rows), 1)
    causal = key_place <= query_place
    scale = HEAD ** (-0.5)
    for index in reversed(range(group)):
        query = heads[index, :HEAD].astype(jnp.float32).T.astype(jnp.bfloat16)
        own_docs = jnp.broadcast_to(docs_all[index].astype(jnp.float32), (LANES, rows)).T
        own_docs = jnp.concatenate([own_docs] * (rows // LANES), axis=1)
        scores = []
        for other in range(index + 1):
            score = jnp.dot(query, heads[other, HEAD : 2 * HEAD], preferred_element_type=jnp.float32)
            allowed = own_docs == docs_all[other].astype(jnp.float32)
            if other == index:
                allowed = allowed & causal
            scores.append(jnp.where(allowed, score * scale, -1e30))
        peak = scores[0]
        for score in scores[1:]:
            peak = jnp.maximum(peak, score)
        peak = jnp.max(peak, axis=1, keepdims=True)
        weights = [jnp.exp(score - peak) for score in scores]
        total = weights[0]
        for weight in weights[1:]:
            total = total + weight
        inverse = 1.0 / jnp.sum(total, axis=1, keepdims=True)
        mixed = None
        for other in range(index + 1):
            probs = (weights[other] * inverse).astype(jnp.bfloat16)
            term = lax.dot_general(
                heads[other, 2 * HEAD :], probs, LAST_LAST, preferred_element_type=jnp.float32
            )
            mixed = term if mixed is None else mixed + term
        picked[index] = mixed.astype(jnp.bfloat16)

        @pl.when(here != index)
        def _():
            copy_mixed(index, here).start()

        @pl.when(here == index)
        def _():
            mixed_turned[pl.ds(pl.multiple_of(here * HEAD, HEAD), HEAD)] = picked[index]

    for step in range(1, group):
        copy_mixed(step, others[step]).wait_recv()
    mixed = mixed_turned[...].astype(jnp.float32).T.astype(jnp.bfloat16)
    stream = fed[...] + jnp.dot(mixed, out[...], preferred_element_type=jnp.float32)
    stream_ref[...] = stream
    low_ref[...] = stream.astype(jnp.bfloat16)
    for step in range(1, group):
        copy_heads(step).wait_send()
    for index in range(group):

        @pl.when(here != index)
        def _():
            copy_mixed(index, here).wait_send()

    for store in stores:
        store.wait()


def rotary_table(context_len):
    half_rot = ROT // 2
    frequency = np.power(np.float32(10000.0), np.float32(-2.0) * np.arange(half_rot, dtype=np.float32) / np.float32(ROT))
    angles = frequency.astype(np.float32)[:, None] * np.arange(context_len, dtype=np.float32)[None, :]
    return np.concatenate([np.cos(angles.astype(np.float64)), np.sin(angles.astype(np.float64))]).astype(np.float32)


def front(picked, docs, gains, shifts, qkv, out, up, down, bias, enc, dec, shift):
    group, share, rows = picked.shape
    width = gains.shape[1]
    ff_width = up.shape[1]
    mine = enc.shape[0]
    shift = shift.reshape(mine // LANES, LANES)
    bf16, f32 = jnp.bfloat16, jnp.float32
    dma = pltpu.SemaphoreType.DMA
    return pl.pallas_call(
        front_kernel,
        out_shape=(
            jax.ShapeDtypeStruct((rows, width), bf16),
            jax.ShapeDtypeStruct((rows, width), f32),
            jax.ShapeDtypeStruct((2 * mine, width), bf16),
            jax.ShapeDtypeStruct((2 * mine, width), bf16),
            jax.ShapeDtypeStruct((width, 2 * mine), bf16),
            jax.ShapeDtypeStruct((2 * mine, LANES), f32),
            jax.ShapeDtypeStruct((2 * mine, LANES), f32),
        ),
        in_specs=[ANY] * 13,
        out_specs=(VMEM, VMEM) + (ANY,) * 5,
        scratch_shapes=[
            pltpu.VMEM((group, 1, rows), jnp.int32),
            pltpu.VMEM((2, width), f32),
            pltpu.VMEM((2, width), f32),
            pltpu.VMEM((width, 3 * width), bf16),
            pltpu.VMEM((width, width), bf16),
            pltpu.VMEM((width, ff_width), bf16),
            pltpu.VMEM((ff_width, width), bf16),
            pltpu.VMEM(bias.shape, f32),
            pltpu.VMEM((ROT, rows), f32),
            pltpu.VMEM((group, share, rows), bf16),
            pltpu.VMEM((width, rows), bf16),
            pltpu.VMEM((group, 3 * HEAD, rows), bf16),
            pltpu.VMEM((group, 3 * HEAD, rows), bf16),
            pltpu.VMEM((width, rows), bf16),
            pltpu.VMEM((rows, width), f32),
            pltpu.VMEM((mine, width), f32),
            pltpu.VMEM((mine, width), f32),
            pltpu.VMEM((2, mine // LANES, LANES), f32),
            pltpu.VMEM((2 * mine, width), bf16),
            pltpu.VMEM((2 * mine, width), bf16),
            pltpu.VMEM((width, 2 * mine), bf16),
            pltpu.VMEM((2 * mine, LANES), f32),
            pltpu.VMEM((2 * mine, LANES), f32),
            dma((13,)),
            dma((5,)),
            dma((3, group)),
            dma((3, group)),
            dma((3,)),
            dma((3,)),
        ],
        compiler_params=pltpu.CompilerParams(
            collective_id=2, has_side_effects=True, vmem_limit_bytes=60 * 2**20
        ),
        cost_estimate=pl.CostEstimate(flops=2 * 10**9, bytes_accessed=14 * 10**6, transcendentals=2 * 10**6),
        name="front_part",
    )(picked, docs, gains, shifts, qkv, out, up, down, bias, jnp.asarray(rotary_table(group * rows)), enc, dec, shift)


def forward_kernel(
    depth,
    own_ref,
    enc_ref,
    dec_ref,
    bias_ref,
    stream_ref,
    scale_ref,
    dec_bias_ref,
    gathered_ref,
    relu_ref,
    upstream_ref,
    small_ref,
    total_ref,
    recon_ref,
    stream,
    scale,
    held,
    enc,
    dec,
    bias,
    staged,
    parts,
    send_zero,
    send_one,
    send_two,
    send_three,
    got_zero,
    got_one,
    got_two,
    got_three,
    load_sem,
    relu_sem,
    held_sem,
    send,
    receive,
    sum_send,
    sum_receive,
):
    rows = own_ref.shape[0]
    entries = enc.shape[0]
    width = held.shape[1]
    half = width // 2
    piece = min(entries, 256)
    where = peers(depth)
    (layer, row, place), across, beside, _ = where
    others = [((layer + step) % depth, row, place) for step in range(1, depth)]
    loads = [
        pltpu.make_async_copy(own_ref, held.at[pl.ds(0, rows)], load_sem.at[0]),
        pltpu.make_async_copy(enc_ref, enc, load_sem.at[1]),
        pltpu.make_async_copy(bias_ref, bias, load_sem.at[2]),
        pltpu.make_async_copy(dec_ref, dec, load_sem.at[3]),
        pltpu.make_async_copy(stream_ref, stream, load_sem.at[4]),
        pltpu.make_async_copy(scale_ref, scale, load_sem.at[5]),
    ]
    for load in loads:
        load.start()
    greet(others + [across, beside])
    loads[0].wait()
    gather = Gather(depth, rows, held, send, receive, where)
    gather.open()
    total_ref[...] = jnp.zeros_like(total_ref)
    for load in loads[1:]:
        load.wait()

    def part_slot(turn):
        return jnp.where(turn == 0, 4, turn % 4)

    def copy_zero(turn):
        layer_there = layer_at(depth, layer, turn)
        index = jnp.where(
            jnp.abs(layer_there - layer) == 1,
            jnp.where(layer > layer_there, 0, 1),
            jnp.where(layer == 0, 2, 3),
        )
        return remote(
            send_zero.at[turn - 1],
            got_zero.at[index],
            sum_send.at[5, turn],
            sum_receive.at[5, index],
            (layer_there, row, place),
        )

    def one_slot(turn):
        return jnp.where(turn == 0, 2, turn % 2)

    def copy_one(turn, part):
        source = send_one.at[one_slot(turn), pl.ds(part * half, half)]
        device = beside if part else across
        return remote(source, got_one.at[part, turn], sum_send.at[part, turn], sum_receive.at[part, turn], device)

    def two_slot(turn):
        return jnp.where(turn == 0, 3, turn % 3)

    def copy_two(turn, part):
        device = beside if part else across
        return remote(
            send_two.at[part, two_slot(turn)],
            got_two.at[part, turn],
            sum_send.at[2 + part, turn],
            sum_receive.at[2 + part, turn],
            device,
        )

    def copy_three(turn):
        layer_there = layer_at(depth, layer, turn)
        index = place_of(depth, layer_there, layer)
        return remote(
            send_three.at[turn],
            got_three.at[index],
            sum_send.at[4, turn],
            sum_receive.at[4, index],
            (layer_there, row, place),
        )

    def copy_relu(order):
        return pltpu.make_async_copy(
            staged.at[order % 2],
            relu_ref.at[:, pl.ds(pl.multiple_of(order * rows, rows), rows)],
            relu_sem.at[order % 2],
        )

    def copy_held(step):
        span = pl.ds(pl.multiple_of(step * 4 * rows, 4 * rows), 4 * rows)
        return pltpu.make_async_copy(held.at[span], gathered_ref.at[span], held_sem.at[step])

    def sum_one(turn, value):
        @pl.when(turn >= 5)
        def _():
            copy_one(turn - 2, 0).wait_send()
            copy_one(turn - 2, 1).wait_send()

        send_one[one_slot(turn)] = value.astype(jnp.bfloat16)
        copy_one(turn, 0).start()
        copy_one(turn, 1).start()

    def sum_two(turn):
        @pl.when(turn >= 4)
        def _():
            copy_two(turn - 3, 0).wait_send()
            copy_two(turn - 3, 1).wait_send()

        slot, target = part_slot(turn), two_slot(turn)
        upper, lower = pl.ds(0, half), pl.ds(half, half)

        @pl.when(crosswise(turn))
        def _():
            copy_one(turn, 0).wait_recv()
            copy_one(turn, 1).wait_recv()
            send_two[1, target, upper] = (parts[2, slot, upper] + got_one[0, turn].astype(jnp.float32)).astype(
                jnp.bfloat16
            )
            send_two[0, target, lower] = (parts[1, slot, lower] + got_one[1, turn].astype(jnp.float32)).astype(
                jnp.bfloat16
            )

        @pl.when((turn == 1) | (turn == 2))
        def _():
            send_two[1, target, upper] = parts[2, slot, upper].astype(jnp.bfloat16)
            send_two[0, target, lower] = parts[1, slot, lower].astype(jnp.bfloat16)

        send_two[1, target, lower] = parts[2, slot, lower].astype(jnp.bfloat16)
        send_two[0, target, upper] = parts[1, slot, upper].astype(jnp.bfloat16)
        copy_two(turn, 1).start()
        copy_two(turn, 0).start()

    def column_sum(turn):
        copy_two(turn, 0).wait_recv()
        copy_two(turn, 1).wait_recv()
        return parts[0, part_slot(turn)] + got_two[0, turn].astype(jnp.float32) + got_two[1, turn].astype(jnp.float32)

    def sum_three(turn):
        send_three[turn] = column_sum(turn).astype(jnp.bfloat16)
        copy_three(turn).start()

    def one_block(order, carry):
        turn, column = order // 4, order % 4

        @pl.when(column == 1)
        def _():
            gather.hand_on(turn)

        @pl.when(column == 3)
        def _():
            gather.wait_diagonal(turn)
            copy_held(turn).start()

        @pl.when(order >= 2)
        def _():
            copy_relu(order - 2).wait()

        block = held[pl.ds(pl.multiple_of(order * rows, rows), rows)]
        low = []
        for first in range(0, entries, piece):
            span = pl.ds(first, piece)
            shift = bias[span]
            pre = lax.dot_general(enc[span], block, LAST_LAST, preferred_element_type=jnp.float32)
            positive = jnp.maximum(pre + jnp.concatenate([shift] * (rows // LANES), axis=1), 0.0)
            staged[order % 2, span] = positive
            active = positive * positive
            folded = active[:, :LANES]
            for lane in range(LANES, rows, LANES):
                folded = folded + active[:, lane : lane + LANES]
            total_ref[span] += folded
            low.append(active.astype(jnp.bfloat16))
        recon = jnp.dot(dec[...], jnp.concatenate(low, axis=0), preferred_element_type=jnp.float32)
        copy_relu(order).start()

        @pl.when((column < 3) | (turn == 0))
        def _():
            parts[column, part_slot(turn)] = recon

        @pl.when((column == 3) & (turn >= 3))
        def _():
            sum_one(turn, recon)

        @pl.when((column == 3) & ((turn == 1) | (turn == 2)))
        def _():
            send_zero[turn - 1] = recon.astype(jnp.bfloat16)
            copy_zero(turn).start()

        @pl.when((column == 0) & (turn + 1 < depth))
        def _():
            gather.spread(turn + 1)

        @pl.when(order == 0)
        def _():
            gather.second_wave()

        @pl.when((column == 1) & (turn >= 3))
        def _():
            sum_two(turn - 2)

        @pl.when((column == 2) & (turn == depth - 1))
        def _():
            sum_two(depth - 2)

        @pl.when((column == 3) & (turn >= 4))
        def _():
            sum_three(turn - 3)

        return carry

    lax.fori_loop(0, 4 * depth, one_block, 0)
    sum_three(depth - 3)
    sum_three(depth - 2)
    sum_two(depth - 1)
    for index, (_, there) in enumerate(takers(depth, layer)):

        @pl.when(there)
        def _(index=index):
            remote(
                send_zero.at[0], got_zero.at[index], sum_send.at[5, 0], sum_receive.at[5, index], across
            ).wait_recv()
            parts[3, 4] += got_zero[index].astype(jnp.float32)

    sum_one(0, parts[3, 4])
    sum_two(0)
    sum_three(depth - 1)
    recon_ref[...] = column_sum(0)
    for turn in range(1, depth):
        remote(
            send_three.at[turn], got_three.at[turn], sum_send.at[4, turn], sum_receive.at[4, turn], across
        ).wait_recv()
        recon_ref[...] += got_three[turn].astype(jnp.float32)
    error = recon_ref[...].T + dec_bias_ref[...] - stream[...]
    upstream = (2.0 * error).astype(jnp.bfloat16)
    upstream_ref[...] = upstream
    loss = fold(error * error)
    weighted = total_ref[...] * scale[...]
    loss = loss + fold(weighted)
    small_ref[...] = jnp.zeros_like(small_ref)
    column_sums = jnp.sum(upstream.astype(jnp.float32), axis=0, keepdims=True)
    lines = width // LANES
    for line in range(lines):
        small_ref[line : line + 1] = column_sums[:, line * LANES : (line + 1) * LANES]
    small_ref[lines : lines + 1] = jnp.sum(loss, axis=0, keepdims=True)
    gather.close()
    for turn in [0] + list(range(max(depth - 2, 3), depth)):
        for part in range(2):
            copy_one(turn, part).wait_send()
    for turn in [0] + list(range(max(depth - 3, 1), depth)):
        for part in range(2):
            copy_two(turn, part).wait_send()
    for turn in range(1, depth):
        copy_three(turn).wait_send()
    for turn in (1, 2):
        copy_zero(turn).wait_send()
    copy_relu(4 * depth - 2).wait()
    copy_relu(4 * depth - 1).wait()
    for step in range(depth):
        copy_held(step).wait()


def forward(depth, own, enc, dec_turned, bias, stream, scale, dec_bias):
    rows, width = own.shape
    entries = enc.shape[0]
    bf16, f32 = jnp.bfloat16, jnp.float32
    dma = pltpu.SemaphoreType.DMA
    return pl.pallas_call(
        functools.partial(forward_kernel, depth),
        out_shape=(
            jax.ShapeDtypeStruct((depth * 4 * rows, width), bf16),
            jax.ShapeDtypeStruct((entries, depth * 4 * rows), f32),
            jax.ShapeDtypeStruct((rows, width), bf16),
            jax.ShapeDtypeStruct((8, LANES), f32),
            jax.ShapeDtypeStruct((entries, LANES), f32),
        ),
        in_specs=[ANY] * 6 + [VMEM],
        out_specs=(ANY, ANY, VMEM, VMEM, VMEM),
        scratch_shapes=[
            pltpu.VMEM((width, rows), f32),
            pltpu.VMEM((rows, width), f32),
            pltpu.VMEM((entries, LANES), f32),
            pltpu.VMEM((depth * 4 * rows, width), bf16),
            pltpu.VMEM((entries, width), bf16),
            pltpu.VMEM((width, entries), bf16),
            pltpu.VMEM((entries, LANES), f32),
            pltpu.VMEM((2, entries, rows), f32),
            pltpu.VMEM((4, 5, width, rows), f32),
            pltpu.VMEM((2, width, rows), bf16),
            pltpu.VMEM((3, width, rows), bf16),
            pltpu.VMEM((2, 4, width, rows), bf16),
            pltpu.VMEM((depth, width, rows), bf16),
            pltpu.VMEM((4, width, rows), bf16),
            pltpu.VMEM((2, depth, width // 2, rows), bf16),
            pltpu.VMEM((2, depth, width, rows), bf16),
            pltpu.VMEM((depth, width, rows), bf16),
            dma((6,)),
            dma((2,)),
            dma((depth,)),
            dma((7, max(depth, 4))),
            dma((7, max(depth, 4))),
            dma((6, max(depth, 4))),
            dma((6, max(depth, 4))),
        ],
        compiler_params=pltpu.CompilerParams(
            collective_id=0, has_side_effects=True, vmem_limit_bytes=60 * 2**20
        ),
        cost_estimate=pl.CostEstimate(
            flops=16 * depth * rows * entries * width, bytes_accessed=16 * depth * rows * entries, transcendentals=0
        ),
        name="forward_blocks",
    )(own, enc, dec_turned, bias, stream, scale, dec_bias)


def backward_kernel(
    depth,
    everyone,
    own_ref,
    gathered_ref,
    relu_ref,
    dec_ref,
    scale_ref,
    active_ref,
    small_ref,
    enc_out,
    dec_out,
    bias_out,
    small_out,
    squares_out,
    held,
    inputs,
    dec,
    scale,
    tile,
    enc_sum,
    dec_sum,
    bias_sum,
    enc_got,
    dec_got,
    bias_got,
    active,
    active_got,
    low,
    small,
    small_got,
    squares,
    squares_got,
    load_sem,
    tile_sem,
    store_sem,
    send,
    receive,
    pair_send,
    pair_receive,
    all_send,
    all_receive,
):
    rows = own_ref.shape[0]
    entries = dec.shape[0]
    mine = entries // 2
    piece = tile.shape[1]
    tiles = entries // piece
    where = peers(depth)
    (layer, row, column), _, _, partner = where
    core = column % 2
    inner = (layer >= 1) & (layer < depth - 1)
    loads = [
        pltpu.make_async_copy(own_ref, held.at[pl.ds(0, rows)], load_sem.at[0]),
        pltpu.make_async_copy(dec_ref, dec, load_sem.at[1]),
        pltpu.make_async_copy(scale_ref, scale, load_sem.at[2]),
        pltpu.make_async_copy(gathered_ref, inputs, load_sem.at[3]),
        pltpu.make_async_copy(active_ref, active, load_sem.at[4]),
        pltpu.make_async_copy(small_ref, small, load_sem.at[5]),
    ]
    for load in loads:
        load.start()

    def place(turn):
        return (turn + (1 - core) * (tiles // 2)) % tiles

    def group_of(group):
        if group == 0:
            return 0, 3 * rows
        if group == depth:
            return (4 * depth - 1) * rows, rows
        return (4 * group - 1) * rows, 4 * rows

    def copy_tile(group, start, size, turn):
        slot = (group * tiles + turn) % 2
        first = pl.multiple_of(place(turn) * piece, piece)
        return pltpu.make_async_copy(
            relu_ref.at[pl.ds(first, piece), pl.ds(pl.multiple_of(start, rows), size)],
            tile.at[slot, :, pl.ds(0, size)],
            tile_sem.at[slot],
        )

    copy_tile(0, *group_of(0), 0).start()

    others = [
        ((layer + dz) % depth, (row + dy) % 2, (column + dx) % 4)
        for dz in range(depth)
        for dy in range(2)
        for dx in range(4)
    ][1:]
    greet(others)
    loads[0].wait()
    gather = Gather(depth, rows, held, send, receive, where)
    gather.open()
    for load in loads[1:]:
        load.wait()

    def small_copy(index):
        return remote(
            small, small_got.at[index], all_send.at[0, index], all_receive.at[0, index], others[index - 1]
        )

    def squares_copy(index):
        return remote(
            squares, squares_got.at[index], all_send.at[1, index], all_receive.at[1, index], others[index - 1]
        )

    for index in range(1, everyone):
        small_copy(index).start()

    theirs = (1 - core) * mine
    active_copy = remote(
        active.at[pl.ds(pl.multiple_of(theirs, mine), mine)], active_got, pair_send.at[3, 0], pair_receive.at[3, 0], partner
    )
    active_copy.start()
    enc_sum[...] = jnp.zeros_like(enc_sum)
    dec_sum[...] = jnp.zeros_like(dec_sum)
    bias_sum[...] = jnp.zeros_like(bias_sum)

    def pair_copy(kind, turn):
        source, target = ((low.at[0], enc_got), (low.at[1], dec_got), (bias_sum, bias_got))[kind]
        there = pl.ds(pl.multiple_of(turn * piece, piece), piece)
        return remote(
            source.at[pl.ds(pl.multiple_of(theirs + turn * piece, piece), piece) if kind == 2 else there],
            target.at[there],
            pair_send.at[kind, turn],
            pair_receive.at[kind, turn],
            partner,
        )

    gather.spread(1)
    gather.second_wave()
    gather.hand_on(0)

    def one_tile(group, start, size, turn):
        slot = (group * tiles + turn) % 2
        copy_tile(group, start, size, turn).wait()
        span = pl.ds(pl.multiple_of(place(turn) * piece, piece), piece)
        tokens = pl.ds(pl.multiple_of(start, rows), size)
        upstream = held[tokens]
        back = lax.dot_general(dec[span], upstream, LAST_LAST, preferred_element_type=jnp.float32)
        positive = tile[slot, :, :size]
        shift = jnp.concatenate([scale[span]] * (size // LANES), axis=1)
        slope = ((back + shift) * (2.0 * positive)).astype(jnp.bfloat16)
        act_low = (positive * positive).astype(jnp.bfloat16)
        wide = slope.astype(jnp.float32)
        folded = wide[:, :LANES]
        for lane in range(LANES, size, LANES):
            folded = folded + wide[:, lane : lane + LANES]
        bias_sum[span] += folded
        enc_sum[span] += jnp.dot(slope, inputs[tokens], preferred_element_type=jnp.float32)
        dec_sum[span] += jnp.dot(act_low, upstream, preferred_element_type=jnp.float32)

    def first_group(turn, carry):
        start, size = group_of(0)

        @pl.when(turn + 1 < tiles)
        def _():
            copy_tile(0, start, size, turn + 1).start()

        @pl.when(turn + 1 == tiles)
        def _():
            copy_tile(1, *group_of(1), 0).start()

        one_tile(0, start, size, turn)

        @pl.when((turn == tiles // 2) & inner)
        def _():
            gather.spread(2)

        return carry

    def middle_group(group, carry):
        start, size = (4 * group - 1) * rows, 4 * rows
        gather.wait_diagonal(group - 1)

        @pl.when(jnp.logical_not(inner) & (group + 1 < depth))
        def _():
            gather.spread(group + 1)

        gather.hand_on(group)

        @pl.when(inner & (group + 2 < depth))
        def _():
            gather.spread(group + 2)

        def one(turn, carry):
            @pl.when(turn + 1 < tiles)
            def _():
                copy_tile(group, start, size, turn + 1).start()

            @pl.when((turn + 1 == tiles) & (group + 1 < depth))
            def _():
                copy_tile(group + 1, start + 4 * rows, size, 0).start()

            @pl.when((turn + 1 == tiles) & (group + 1 == depth))
            def _():
                copy_tile(depth, *group_of(depth), 0).start()

            one_tile(group, start, size, turn)
            return carry

        return lax.fori_loop(0, tiles, one, carry)

    def last_group(turn, carry):
        start, size = group_of(depth)

        @pl.when(turn + 1 < tiles)
        def _():
            copy_tile(depth, start, size, turn + 1).start()

        one_tile(depth, start, size, turn)

        @pl.when(turn < tiles // 2)
        def _():
            span = pl.ds(pl.multiple_of(place(turn) * piece, piece), piece)
            there = pl.ds(pl.multiple_of(turn * piece, piece), piece)
            low[0, there] = enc_sum[span].astype(jnp.bfloat16)
            low[1, there] = dec_sum[span].astype(jnp.bfloat16)
            for kind in range(3):
                pair_copy(kind, turn).start()

        return carry

    lax.fori_loop(0, tiles, first_group, 0)
    lax.fori_loop(1, depth, middle_group, 0)
    gather.wait_diagonal(depth - 1)
    lax.fori_loop(0, tiles, last_group, 0)

    ours = core * mine
    active_copy.wait_recv()
    span = pl.ds(pl.multiple_of(ours, mine), mine)
    act_total = jnp.sum(active[span] + active_got[...], axis=1, keepdims=True)
    partial = jnp.zeros((8, LANES), jnp.float32)

    stores = []
    rows_of = lax.broadcasted_iota(jnp.int32, (LANES, LANES), 0)
    lanes_of = lax.broadcasted_iota(jnp.int32, (LANES, LANES), 1)
    for turn in range(tiles // 2):
        for kind in range(3):
            pair_copy(kind, turn).wait_recv()
        near = pl.ds(pl.multiple_of(ours + turn * piece, piece), piece)
        there = pl.ds(turn * piece, piece)
        enc_grad = enc_sum[near] + enc_got[there].astype(jnp.float32)
        enc_sum[near] = enc_grad
        partial = partial + fold(enc_grad * enc_grad)
        dec_grad = dec_sum[near] + dec_got[there].astype(jnp.float32)
        dec_grad = dec_grad + (
            COEFFICIENT * COEFFICIENT * act_total[turn * piece : (turn + 1) * piece] / scale[near, :1]
        ) * dec[near].astype(jnp.float32)
        dec_sum[near] = dec_grad
        partial = partial + fold(dec_grad * dec_grad)
        stores += [
            pltpu.make_async_copy(enc_sum.at[near], enc_out.at[there], store_sem.at[0, turn]),
            pltpu.make_async_copy(dec_sum.at[near], dec_out.at[there], store_sem.at[1, turn]),
        ]
        stores[-2].start()
        stores[-1].start()
        bias_grad = jnp.sum(bias_sum[near] + bias_got[there], axis=1, keepdims=True)
        for first in range(0, piece, LANES):
            wide = jnp.broadcast_to(bias_grad[first : first + LANES], (LANES, LANES))
            line = jnp.sum(jnp.where(rows_of == lanes_of, wide, 0.0), axis=0, keepdims=True)
            index = (turn * piece + first) // LANES
            bias_out[index : index + 1] = line
            partial = partial + jnp.where(rows_of[:8] == 0, line * line, 0.0)
    squares[...] = partial
    for index in range(1, everyone):
        squares_copy(index).start()
    total_small = small[...]
    for index in range(1, everyone):
        small_copy(index).wait_recv()
        total_small = total_small + small_got[index]
    small_out[...] = total_small
    total_squares = squares[...]
    for index in range(1, everyone):
        squares_copy(index).wait_recv()
        total_squares = total_squares + squares_got[index]
    squares_out[...] = total_squares
    gather.close()
    for index in range(1, everyone):
        small_copy(index).wait_send()
        squares_copy(index).wait_send()
    active_copy.wait_send()
    for turn in range(tiles // 2):
        for kind in range(3):
            pair_copy(kind, turn).wait_send()
    for store in stores:
        store.wait()


def backward(depth, own, gathered, relu, dec, scale, active, small):
    rows, width = own.shape
    entries = dec.shape[0]
    mine = entries // 2
    piece = min(512, mine)
    everyone = depth * 8
    bf16, f32 = jnp.bfloat16, jnp.float32
    dma = pltpu.SemaphoreType.DMA
    return pl.pallas_call(
        functools.partial(backward_kernel, depth, everyone),
        out_shape=(
            jax.ShapeDtypeStruct((mine, width), f32),
            jax.ShapeDtypeStruct((mine, width), f32),
            jax.ShapeDtypeStruct((mine // LANES, LANES), f32),
            jax.ShapeDtypeStruct(small.shape, f32),
            jax.ShapeDtypeStruct((8, LANES), f32),
        ),
        in_specs=[ANY] * 7,
        out_specs=(ANY, ANY, VMEM, VMEM, VMEM),
        scratch_shapes=[
            pltpu.VMEM((depth * 4 * rows, width), bf16),
            pltpu.VMEM((depth * 4 * rows, width), bf16),
            pltpu.VMEM((entries, width), bf16),
            pltpu.VMEM((entries, LANES), f32),
            pltpu.VMEM((2, piece, 4 * rows), f32),
            pltpu.VMEM((entries, width), f32),
            pltpu.VMEM((entries, width), f32),
            pltpu.VMEM((entries, LANES), f32),
            pltpu.VMEM((mine, width), bf16),
            pltpu.VMEM((mine, width), bf16),
            pltpu.VMEM((mine, LANES), f32),
            pltpu.VMEM((entries, LANES), f32),
            pltpu.VMEM((mine, LANES), f32),
            pltpu.VMEM((2, mine, width), bf16),
            pltpu.VMEM(small.shape, f32),
            pltpu.VMEM((everyone,) + small.shape, f32),
            pltpu.VMEM((8, LANES), f32),
            pltpu.VMEM((everyone, 8, LANES), f32),
            dma((6,)),
            dma((2,)),
            dma((2, entries // piece)),
            dma((7, max(depth, 4))),
            dma((7, max(depth, 4))),
            dma((4, entries // piece)),
            dma((4, entries // piece)),
            dma((2, everyone)),
            dma((2, everyone)),
        ],
        compiler_params=pltpu.CompilerParams(
            collective_id=1, has_side_effects=True, vmem_limit_bytes=60 * 2**20
        ),
        cost_estimate=pl.CostEstimate(
            flops=24 * depth * rows * entries * width, bytes_accessed=16 * depth * rows * entries, transcendentals=0
        ),
        name="backward_blocks",
    )(own, gathered, relu, dec, scale, active, small)


def update_kernel(*refs):
    names = ["enc_grad", "dec_grad", "bias_grad", "small", "squares"]
    for kind in ("enc", "dec", "bias", "shift"):
        names += [kind, kind + "_one", kind + "_two"]
    given = dict(zip(names, refs[: len(names)]))
    made = refs[len(names) : len(names) + 14]
    brought, staged, load_sem, store_sem = refs[len(names) + 14 :]
    mine = given["enc"].shape[0]
    slots, _, piece, _ = staged.shape
    parts = mine // piece
    large = ["enc", "enc_one", "enc_two", "enc_grad", "dec", "dec_one", "dec_two", "dec_grad"]

    def load(part, index):
        span = pl.ds(pl.multiple_of(part * piece, piece), piece)
        slot = part % slots
        return pltpu.make_async_copy(given[large[index]].at[span], brought.at[slot, index], load_sem.at[slot, index])

    for part in range(min(slots - 1, parts)):
        for index in range(8):
            load(part, index).start()
    lines = given["shift"].shape[1] // LANES
    shift_grad = jnp.concatenate([given["small"][line : line + 1] for line in range(lines)], axis=1)
    total = jnp.sum(given["squares"][...], keepdims=True) + jnp.sum(shift_grad * shift_grad, keepdims=True)
    norm = jnp.sqrt(total)
    clip = jnp.minimum(1.0, CLIP_NORM / (norm + 1e-06))
    made[12][...] = norm
    made[13][...] = jnp.sum(given["small"][lines : lines + 1], keepdims=True)

    def store(part, index):
        span = pl.ds(pl.multiple_of(part * piece, piece), piece)
        slot = part % slots
        return pltpu.make_async_copy(staged.at[slot, index], made[index].at[span], store_sem.at[slot, index])

    def one(part, carry):
        @pl.when(part >= slots)
        def _():
            for index in range(6):
                store(part - slots, index).wait()

        @pl.when(part + slots - 1 < parts)
        def _():
            for index in range(8):
                load(part + slots - 1, index).start()

        slot = part % slots
        for index in range(8):
            load(part, index).wait()
        for index in range(2):
            new, first, second = adam_step(
                *(brought[slot, 4 * index + offset] for offset in range(4)),
                clip,
                RATE_MATRIX,
                WEIGHT_DECAY,
            )
            if index:
                new = new * lax.rsqrt(jnp.sum(new * new, axis=1, keepdims=True) + NORM_EPSILON)
            for offset, value in enumerate((new, first, second)):
                staged[slot, 3 * index + offset] = value
        for index in range(6):
            store(part, index).start()
        return carry

    lax.fori_loop(0, parts, one, 0)
    for offset, (kind, gradient) in enumerate((("bias", given["bias_grad"][...]), ("shift", shift_grad))):
        results = adam_step(
            given[kind][...], given[kind + "_one"][...], given[kind + "_two"][...], gradient, clip, RATE_BIAS, 0.0
        )
        for index, value in enumerate(results):
            made[6 + 3 * offset + index][...] = value
    for part in range(max(parts - slots, 0), parts):
        for index in range(6):
            store(part, index).wait()


def update(*arrays):
    f32 = jnp.float32
    mine, width = arrays[0].shape
    dense, flat = (mine // LANES, LANES), (1, width)
    arrays = list(arrays)
    for index in range(11, 14):
        arrays[index] = arrays[index].reshape(dense)
    for index in range(14, 17):
        arrays[index] = arrays[index].reshape(flat)
    piece, slots = min(128, mine), 3
    made = pl.pallas_call(
        update_kernel,
        out_shape=[jax.ShapeDtypeStruct((mine, width), f32)] * 6
        + [jax.ShapeDtypeStruct(dense, f32)] * 3
        + [jax.ShapeDtypeStruct(flat, f32)] * 3
        + [jax.ShapeDtypeStruct((1, 1), f32)] * 2,
        in_specs=[ANY] * 2 + [VMEM] * 3 + [ANY] * 6 + [VMEM] * 6,
        out_specs=[ANY] * 6 + [VMEM] * 8,
        scratch_shapes=[
            pltpu.VMEM((slots, 8, piece, width), f32),
            pltpu.VMEM((slots, 6, piece, width), f32),
            pltpu.SemaphoreType.DMA((slots, 8)),
            pltpu.SemaphoreType.DMA((slots, 6)),
        ],
        compiler_params=pltpu.CompilerParams(vmem_limit_bytes=60 * 2**20),
        cost_estimate=pl.CostEstimate(flops=60 * mine * width, bytes_accessed=56 * mine * width, transcendentals=4 * mine * width),
        name="update",
    )(*arrays)
    return (
        *made[:6],
        *(value.reshape(mine) for value in made[6:9]),
        *(value.reshape(width) for value in made[9:12]),
        made[12].reshape(()),
        made[13].reshape(()),
    )


def body(
    depth,
    token_ids,
    doc_ids,
    embed,
    norm_gains,
    norm_shifts,
    qkv_weight,
    out_weight,
    up_weight,
    down_weight,
    proj_biases,
    enc_weight,
    dec_weight,
    enc_bias,
    dec_bias,
    enc_first,
    enc_second,
    dec_first,
    dec_second,
    enc_bias_first,
    enc_bias_second,
    dec_bias_first,
    dec_bias_second,
):
    model_width = norm_gains.shape[1]
    all_ids, all_docs = gather_ids(token_ids, doc_ids, model_width // embed.shape[1])
    low, stream, enc_both, dec_both, dec_turned, shift_wide, scale_wide = front(
        pick(all_ids, embed.T),
        all_docs,
        norm_gains,
        norm_shifts,
        qkv_weight,
        out_weight,
        up_weight,
        down_weight,
        proj_biases.reshape(-1, LANES),
        enc_weight,
        dec_weight,
        enc_bias,
    )
    gathered, relu, upstream, small, active = forward(
        depth, low, enc_both, dec_turned, shift_wide, stream, scale_wide, dec_bias[None]
    )
    enc_grad, dec_grad, enc_bias_grad, small_sum, squares = backward(
        depth, upstream, gathered, relu, dec_both, scale_wide, active, small
    )
    return update(
        enc_grad,
        dec_grad,
        enc_bias_grad,
        small_sum,
        squares,
        enc_weight,
        enc_first,
        enc_second,
        dec_weight,
        dec_first,
        dec_second,
        enc_bias,
        enc_bias_first,
        enc_bias_second,
        dec_bias,
        dec_bias_first,
        dec_bias_second,
    )


def solution(mesh):
    split = P(("dp", "seq", "opt"), None)
    split_vector = P(("dp", "seq", "opt"))
    in_specs = (
        P("dp", ("seq", "opt")),
        P("dp", ("seq", "opt")),
        P(None, ("seq", "opt")),
        P(),
        P(),
        P(),
        P(),
        P(),
        P(),
        P(),
        split,
        split,
        split_vector,
        P(),
        split,
        split,
        split,
        split,
        split_vector,
        split_vector,
        P(),
        P(),
    )
    out_specs = (split,) * 6 + (split_vector,) * 3 + (P(),) * 5
    return jax.shard_map(
        functools.partial(body, mesh.shape["dp"]),
        mesh=mesh,
        in_specs=in_specs,
        out_specs=out_specs,
        check_vma=False,
    )
```

```python
import functools

import jax
import jax.numpy as jnp
import numpy as np
from jax import lax
from jax.experimental import pallas as pl
from jax.experimental.pallas import tpu as pltpu
from jax.sharding import PartitionSpec as P

HEAD = 64
ROT = 16
STEP = 4
RAMP = 80


LAYER_EPSILON = 1e-05
NORM_EPSILON = 1e-08
BETA_FIRST = 0.9
BETA_SECOND = 0.999
ADAM_EPSILON = 1e-08
RATE_MATRIX = 0.02
RATE_BIAS = 0.1
WEIGHT_DECAY = 0.01
CLIP_NORM = 1.0
SPARSITY_TOP = 5.0
COEFFICIENT = SPARSITY_TOP * min(1.0, STEP / RAMP)
LAST_LAST = (((1,), (1,)), ((), ()))
MESH = pl.DeviceIdType.MESH
ANY = pl.BlockSpec(memory_space=pl.ANY)
VMEM = pl.BlockSpec(memory_space=pltpu.VMEM)
LANES = 128


def adam_step(parameter, moment_one, moment_two, gradient, clip_scale, step_rate, decay_rate):
    gradient = gradient * clip_scale
    moment_one = BETA_FIRST * moment_one + (1.0 - BETA_FIRST) * gradient
    moment_two = BETA_SECOND * moment_two + (1.0 - BETA_SECOND) * gradient * gradient
    first_share, second_share = 1.0 / (1.0 - BETA_FIRST**STEP), 1.0 / (1.0 - BETA_SECOND**STEP)
    adjust = moment_one * first_share / (jnp.sqrt(moment_two * second_share) + ADAM_EPSILON)
    return (parameter - step_rate * (adjust + decay_rate * parameter), moment_one, moment_two)


def place_of(depth, layer, other):
    distance = jnp.abs(other - layer)
    margin = jnp.minimum(layer, depth - 1 - layer)
    near = jnp.where(other < layer, 2 * distance - 1, 2 * distance)
    return jnp.where(distance <= margin, near, distance + margin)


def layer_at(depth, layer, turn):
    margin = jnp.minimum(layer, depth - 1 - layer)
    near = jnp.where(turn % 2 == 1, layer - (turn + 1) // 2, layer + turn // 2)
    far = jnp.where(2 * layer < depth - 1, layer + turn - margin, layer - turn + margin)
    return jnp.where(turn <= 2 * margin, near, far)


def crosswise(turn):
    return (turn == 0) | (turn >= 3)


def slot_of(depth, turn, column):
    last = 4 * (depth - 1)
    own = jnp.maximum(4 * turn - 3, 0)
    diagonal = jnp.where(turn == depth - 1, last, jnp.where(turn == depth - 2, last + 1, 4 * turn + 4))
    return jnp.where(column == 0, own, jnp.where(column == 3, diagonal, 4 * turn + 1 + column))


def takers(depth, layer):
    return [
        (layer + 1, layer + 1 < depth),
        (layer - 1, layer >= 1),
        (layer * 0, layer == 2),
        (layer * 0 + depth - 1, layer == depth - 3),
    ]


def peers(depth):
    layer, row, column = lax.axis_index("dp"), lax.axis_index("seq"), lax.axis_index("opt")
    across = (layer, row, (column + 2) % 4)
    beside = (layer, 1 - row, column)
    partner = (layer, row, column + 1 - 2 * (column % 2))
    return (layer, row, column), across, beside, partner


def remote(source, target, send, receive, device):
    return pltpu.make_async_remote_copy(
        src_ref=source,
        dst_ref=target,
        send_sem=send,
        recv_sem=receive,
        device_id=device,
        device_id_type=MESH,
    )


def greet(devices):
    barrier = pltpu.get_barrier_semaphore()
    for device in devices:
        pl.semaphore_signal(barrier, inc=1, device_id=device, device_id_type=MESH)
    pl.semaphore_wait(barrier, len(devices))


def fold(values):
    total = values[:8]
    for first in range(8, values.shape[0], 8):
        total = total + values[first : first + 8]
    narrow = total[:, :LANES]
    for lane in range(LANES, values.shape[1], LANES):
        narrow = narrow + total[:, lane : lane + LANES]
    return narrow


class Gather:
    def __init__(self, depth, rows, held, send, receive, where):
        self.depth, self.rows, self.held = depth, rows, held
        self.send, self.receive = send, receive
        self.here, self.across, self.beside, _ = where

    def block(self, turn, column, part=None):
        first, rows = slot_of(self.depth, turn, column) * self.rows, self.rows
        if part is not None:
            rows = self.rows // 2
            first = first + part * rows
        return self.held.at[pl.ds(pl.multiple_of(first, rows), rows)]

    def device(self, layer):
        return (layer, self.here[1], self.here[2])

    def copy_along(self, turn, sign, part):
        layer = self.here[0] + sign
        source = layer_at(self.depth, self.here[0], turn)
        there = place_of(self.depth, layer, source)
        row, index = (part, turn) if sign == 1 else (part + 8, turn)
        return remote(
            self.block(turn, 0, part),
            self.block(there, 0, part),
            self.send.at[row, index],
            self.receive.at[part, there],
            self.device(layer),
        )

    def along(self, turn, act):
        source, layer = layer_at(self.depth, self.here[0], turn), self.here[0]
        for sign, onward in ((1, source <= layer), (-1, source >= layer)):

            @pl.when(onward & (layer + sign >= 0) & (layer + sign < self.depth))
            def _(sign=sign):
                for part in range(2):
                    act(self.copy_along(turn, sign, part))

    def copy_across(self, turn, part):
        return remote(
            self.block(turn, 0, part),
            self.block(turn, 1, part),
            self.send.at[2 + part, turn],
            self.receive.at[2 + part, turn],
            self.across,
        )

    def copy_beside(self, turn, part):
        return remote(
            self.block(turn, 0, part),
            self.block(turn, 2, part),
            self.send.at[4 + part, turn],
            self.receive.at[4 + part, turn],
            self.beside,
        )

    def pass_across(self, turn):
        return remote(
            self.block(turn, 2, 0), self.block(turn, 3, 0), self.send.at[6, turn], self.receive.at[6, turn], self.across
        )

    def pass_beside(self, turn):
        return remote(
            self.block(turn, 1, 1), self.block(turn, 3, 1), self.send.at[7, turn], self.receive.at[7, turn], self.beside
        )

    def pass_along(self, index, layer):
        turn = place_of(self.depth, layer, self.here[0])
        return remote(
            self.block(0, 3), self.block(turn, 3), self.send.at[10, index], self.receive.at[8, turn], self.device(layer)
        )

    def to_neighbours(self, turn):
        for part in range(2):
            self.copy_across(turn, 1 - part).start()
            self.copy_beside(turn, part).start()

    def open(self):
        self.to_neighbours(0)
        self.along(0, lambda copy: copy.start())

    def arrive(self, turn):
        for part in range(2):
            remote(
                self.block(0, 0, part),
                self.block(turn, 0, part),
                self.send.at[part, 0],
                self.receive.at[part, turn],
                self.across,
            ).wait_recv()
        self.along(turn, lambda copy: copy.start())

    def hand_on(self, turn):
        self.copy_across(turn, 1).wait_recv()

        @pl.when(crosswise(turn))
        def _():
            self.pass_beside(turn).start()

        self.copy_beside(turn, 0).wait_recv()

        @pl.when(crosswise(turn))
        def _():
            self.pass_across(turn).start()

        self.copy_across(turn, 0).wait_recv()
        self.copy_beside(turn, 1).wait_recv()

    def wait_diagonal(self, turn):
        @pl.when(crosswise(turn))
        def _():
            self.pass_across(turn).wait_recv()
            self.pass_beside(turn).wait_recv()

        @pl.when((turn == 1) | (turn == 2))
        def _():
            remote(
                self.block(0, 3), self.block(turn, 3), self.send.at[10, 0], self.receive.at[8, turn], self.across
            ).wait_recv()

        @pl.when(turn == 0)
        def _():
            for index, (layer, there) in enumerate(takers(self.depth, self.here[0])):

                @pl.when(there)
                def _(index=index, layer=layer):
                    self.pass_along(index, layer).start()

    def close(self):
        for index, (layer, there) in enumerate(takers(self.depth, self.here[0])):

            @pl.when(there)
            def _(index=index, layer=layer):
                self.pass_along(index, layer).wait_send()

        def done(turn, carry):
            self.along(turn, lambda copy: copy.wait_send())
            for part in range(2):
                self.copy_across(turn, part).wait_send()
                self.copy_beside(turn, part).wait_send()

            @pl.when(crosswise(turn))
            def _():
                self.pass_across(turn).wait_send()
                self.pass_beside(turn).wait_send()

            return carry

        lax.fori_loop(0, self.depth, done, 0)


def ids_kernel(ids_ref, docs_ref, ids_out, docs_out, ids_all, docs_all, load_sem, send, receive):
    group = ids_all.shape[0]
    layer, row, column = lax.axis_index("dp"), lax.axis_index("seq"), lax.axis_index("opt")
    here = row * 4 + column
    others = [(here + step) % group for step in range(group)]
    devices = [(layer, index // 4, index % 4) for index in others]
    loads = [
        pltpu.make_async_copy(ids_ref, ids_all.at[here], load_sem.at[0]),
        pltpu.make_async_copy(docs_ref, docs_all.at[here], load_sem.at[1]),
    ]
    for load in loads:
        load.start()
    greet(devices[1:])
    for load in loads:
        load.wait()
    copies = []
    for step in range(1, group):
        for kind, held in enumerate((ids_all, docs_all)):
            copies.append(
                remote(held.at[here], held.at[here], send.at[kind, step], receive.at[kind, step], devices[step])
            )
    for copy in copies:
        copy.start()
    for copy in copies:
        copy.wait()
    ids_out[...] = ids_all[...]
    docs_out[...] = docs_all[...]


def gather_ids(ids, docs, group):
    rows = ids.shape[1]
    dma = pltpu.SemaphoreType.DMA
    whole = jax.ShapeDtypeStruct((group, 1, rows), jnp.int32)
    return pl.pallas_call(
        ids_kernel,
        out_shape=(whole, whole),
        in_specs=[ANY] * 2,
        out_specs=(VMEM, VMEM),
        scratch_shapes=[
            pltpu.VMEM((group, 1, rows), jnp.int32),
            pltpu.VMEM((group, 1, rows), jnp.int32),
            dma((2,)),
            dma((2, group)),
            dma((2, group)),
        ],
        compiler_params=pltpu.CompilerParams(collective_id=3, has_side_effects=True, vmem_limit_bytes=60 * 2**20),
        name="gather_ids",
    )(ids, docs)


def pick_kernel(ids_ref, table_ref, picked, table, load_sem):
    group, _, rows = ids_ref.shape
    share, vocabulary = table.shape
    parts = 3 if vocabulary % (3 * LANES) == 0 else 1
    loads = [
        pltpu.make_async_copy(
            table_ref.at[:, pl.ds(part * (vocabulary // parts), vocabulary // parts)],
            table.at[:, pl.ds(part * (vocabulary // parts), vocabulary // parts)],
            load_sem.at[part],
        )
        for part in range(parts)
    ]
    for load in loads:
        load.start()
    lanes = lax.broadcasted_iota(jnp.int32, (share, LANES), 1)
    for load in loads:
        load.wait()

    def some(part, carry):
        source, first = part // (rows // LANES), part % (rows // LANES) * LANES
        found = None
        for place in range(LANES):
            token = ids_ref[source, 0, first + place]
            start = lax.bitwise_and(token, -LANES)
            tile = table[:, pl.ds(pl.multiple_of(start, LANES), LANES)].astype(jnp.float32)
            moved = pltpu.roll(tile, lax.bitwise_and(place - token, LANES - 1), 1)
            found = moved if found is None else jnp.where(lanes >= place, moved, found)
        picked[source, :, pl.ds(pl.multiple_of(first, LANES), LANES)] = found.astype(jnp.bfloat16)
        return carry

    lax.fori_loop(0, group * rows // LANES, some, 0)


def pick(ids, table):
    group, _, rows = ids.shape
    share = table.shape[0]
    return pl.pallas_call(
        pick_kernel,
        out_shape=jax.ShapeDtypeStruct((group, share, rows), jnp.bfloat16),
        in_specs=[pl.BlockSpec(memory_space=pltpu.SMEM), ANY],
        out_specs=VMEM,
        scratch_shapes=[pltpu.VMEM(table.shape, jnp.bfloat16), pltpu.SemaphoreType.DMA((3,))],
        compiler_params=pltpu.CompilerParams(vmem_limit_bytes=60 * 2**20),
        name="pick_features",
    )(ids, table)


def front_kernel(
    picked_ref,
    docs_ref,
    gains_ref,
    shifts_ref,
    qkv_ref,
    out_ref,
    up_ref,
    down_ref,
    bias_ref,
    turn_ref,
    enc_ref,
    dec_ref,
    shift_ref,
    low_ref,
    stream_ref,
    enc_out,
    dec_out,
    turned_out,
    shift_out,
    scale_out,
    docs_all,
    gains,
    shifts,
    qkv,
    out,
    up,
    down,
    bias,
    turn,
    picked,
    features,
    turned,
    heads,
    mixed_turned,
    fed,
    enc_full,
    dec_full,
    shift_all,
    enc,
    dec,
    dec_turned,
    shift_wide,
    scale_wide,
    load_sem,
    store_sem,
    send,
    receive,
    pair_send,
    pair_receive,
):
    group, share, rows = picked.shape
    mine = enc_full.shape[0]
    dense = mine // LANES
    width = gains.shape[1]
    ff_width = up.shape[1]
    layer, row, column = lax.axis_index("dp"), lax.axis_index("seq"), lax.axis_index("opt")
    here = row * 4 + column

    def member(index):
        return (layer, index // 4, index % 4)

    others = [(here + step) % group for step in range(group)]
    first_place = pl.multiple_of(here * rows, rows)
    loads = [
        pltpu.make_async_copy(picked_ref, picked, load_sem.at[0]),
        pltpu.make_async_copy(docs_ref, docs_all, load_sem.at[1]),
        pltpu.make_async_copy(gains_ref, gains, load_sem.at[2]),
        pltpu.make_async_copy(shifts_ref, shifts, load_sem.at[3]),
        pltpu.make_async_copy(bias_ref, bias, load_sem.at[4]),
        pltpu.make_async_copy(turn_ref.at[:, pl.ds(first_place, rows)], turn, load_sem.at[5]),
        pltpu.make_async_copy(qkv_ref, qkv, load_sem.at[6]),
        pltpu.make_async_copy(up_ref, up, load_sem.at[7]),
        pltpu.make_async_copy(down_ref, down, load_sem.at[8]),
        pltpu.make_async_copy(out_ref, out, load_sem.at[9]),
        pltpu.make_async_copy(enc_ref, enc_full, load_sem.at[10]),
        pltpu.make_async_copy(dec_ref, dec_full, load_sem.at[11]),
        pltpu.make_async_copy(shift_ref, shift_all.at[column % 2], load_sem.at[12]),
    ]
    for load in loads:
        load.start()
    greet([member(index) for index in others[1:]])
    loads[0].wait()

    def copy_features(step):
        return remote(
            picked.at[others[step]],
            features.at[pl.ds(pl.multiple_of(here * share, share), share)],
            send.at[0, step],
            receive.at[0, step],
            member(others[step]),
        )

    def copy_heads(step):
        return remote(
            turned.at[others[step]], heads.at[here], send.at[1, step], receive.at[1, step], member(others[step])
        )

    def copy_mixed(index, source):
        return remote(
            picked.at[index],
            mixed_turned.at[pl.ds(pl.multiple_of(source * HEAD, HEAD), HEAD)],
            send.at[2, index],
            receive.at[2, source],
            member(index),
        )

    for step in range(1, group):
        copy_features(step).start()

    partner = (layer, row, column + 1 - 2 * (column % 2))
    own = pl.ds(pl.multiple_of(column % 2 * mine, mine), mine)
    for load in loads[10:]:
        load.wait()
    shared = []
    for kind, (full, low) in enumerate(((dec_full, dec), (enc_full, enc))):

        def cast(part, carry, full=full, low=low):
            start = pl.multiple_of(part * 256, 256)
            low[pl.ds(pl.multiple_of(column % 2 * mine + start, 256), 256)] = full[pl.ds(start, 256)].astype(
                jnp.bfloat16
            )
            return carry

        lax.fori_loop(0, mine // 256, cast, 0)
        shared.append(remote(low.at[own], low.at[own], pair_send.at[kind], pair_receive.at[kind], partner))
        shared[-1].start()
    spot = shift_all.at[column % 2]
    shared.append(remote(spot, spot, pair_send.at[2], pair_receive.at[2], partner))
    shared[-1].start()
    features[pl.ds(pl.multiple_of(here * share, share), share)] = picked[here]
    for load in loads[1:10]:
        load.wait()
    for step in range(1, group):
        copy_features(step).wait_recv()

    residual = features[...].astype(jnp.float32).T
    center = residual - jnp.mean(residual, axis=1, keepdims=True)
    variance = jnp.mean(center * center, axis=1, keepdims=True)
    unit = center * lax.rsqrt(variance + LAYER_EPSILON)
    first_norm = (unit * gains[0:1] + shifts[0:1]).astype(jnp.bfloat16)
    second_norm = (unit * gains[1:2] + shifts[1:2]).astype(jnp.bfloat16)

    def bias_row(first, count):
        lines = range(first // LANES, (first + count) // LANES)
        return jnp.concatenate([bias[line : line + 1] for line in lines], axis=1)

    half_rot = ROT // 2
    cosine, sine = turn[:half_rot], turn[half_rot:]
    for first in range(0, 3 * width, 2 * LANES):
        chunk = (
            jnp.dot(first_norm, qkv[:, first : first + 2 * LANES], preferred_element_type=jnp.float32)
            + bias_row(first, 2 * LANES)
        ).T
        for inner in range(0, 2 * LANES, HEAD):
            kind, head = (first + inner) // width, (first + inner) % width // HEAD
            values = chunk[inner : inner + HEAD]
            if kind < 2:
                left, right = values[:half_rot], values[half_rot:ROT]
                values = jnp.concatenate(
                    [left * cosine - right * sine, right * cosine + left * sine, values[ROT:]], axis=0
                )
            turned[head, kind * HEAD : (kind + 1) * HEAD] = values.astype(jnp.bfloat16)
    for step in range(1, group):
        copy_heads(step).start()
    heads[here] = turned[here]

    feed = residual + bias_row(4 * width + ff_width, width) + bias_row(3 * width, width)
    for first in range(0, ff_width, 512):
        inner = (
            jnp.dot(second_norm, up[:, first : first + 512], preferred_element_type=jnp.float32)
            + bias_row(4 * width + first, 512)
        )
        hidden = (0.5 * inner * (1.0 + lax.erf(inner * (0.5**0.5)))).astype(jnp.bfloat16)
        feed = feed + jnp.dot(hidden, down[first : first + 512], preferred_element_type=jnp.float32)
    fed[...] = feed

    for copy in shared:
        copy.wait()

    def widen(part, carry):
        start = pl.multiple_of(part * LANES, LANES)
        span = pl.ds(start, LANES)
        values = dec[span].astype(jnp.float32)
        dec_turned[:, span] = values.T.astype(jnp.bfloat16)
        norms = jnp.sqrt(jnp.sum(values * values, axis=1, keepdims=True) + NORM_EPSILON)
        scale_wide[span] = jnp.broadcast_to(COEFFICIENT * norms, (LANES, LANES))
        shift_wide[span] = jnp.broadcast_to(shift_all[part // dense, pl.ds(part % dense, 1)], (LANES, LANES)).T
        return carry

    lax.fori_loop(0, 2 * dense, widen, 0)
    stores = [
        pltpu.make_async_copy(held, target, store_sem.at[index])
        for index, (held, target) in enumerate(
            (
                (enc, enc_out),
                (dec, dec_out),
                (dec_turned, turned_out),
                (shift_wide, shift_out),
                (scale_wide, scale_out),
            )
        )
    ]
    for store in stores:
        store.start()

    for step in range(1, group):
        copy_features(step).wait_send()
    query_place = lax.broadcasted_iota(jnp.int32, (rows, rows), 0)
    key_place = lax.broadcasted_iota(jnp.int32, (rows, rows), 1)
    causal = key_place <= query_place
    scale = HEAD ** (-0.5)
    for index in range(group):

        @pl.when(here != index)
        def _():
            arrived = receive.at[1, (here + group - index) % group]
            remote(turned.at[index], heads.at[index], send.at[1, 0], arrived, member(others[1])).wait_recv()

        query = heads[index, :HEAD].astype(jnp.float32).T.astype(jnp.bfloat16)
        own_docs = jnp.broadcast_to(docs_all[index].astype(jnp.float32), (LANES, rows)).T
        own_docs = jnp.concatenate([own_docs] * (rows // LANES), axis=1)
        scores = []
        for other in range(index + 1):
            score = jnp.dot(query, heads[other, HEAD : 2 * HEAD], preferred_element_type=jnp.float32)
            allowed = own_docs == docs_all[other].astype(jnp.float32)
            if other == index:
                allowed = allowed & causal
            scores.append(jnp.where(allowed, score * scale, -1e30))
        peak = scores[0]
        for score in scores[1:]:
            peak = jnp.maximum(peak, score)
        peak = jnp.max(peak, axis=1, keepdims=True)
        weights = [jnp.exp(score - peak) for score in scores]
        total = weights[0]
        for weight in weights[1:]:
            total = total + weight
        inverse = 1.0 / jnp.sum(total, axis=1, keepdims=True)
        mixed = None
        for other in range(index + 1):
            probs = (weights[other] * inverse).astype(jnp.bfloat16)
            term = lax.dot_general(
                heads[other, 2 * HEAD :], probs, LAST_LAST, preferred_element_type=jnp.float32
            )
            mixed = term if mixed is None else mixed + term
        picked[index] = mixed.astype(jnp.bfloat16)

        @pl.when(here != index)
        def _():
            copy_mixed(index, here).start()

        @pl.when(here == index)
        def _():
            mixed_turned[pl.ds(pl.multiple_of(here * HEAD, HEAD), HEAD)] = picked[index]

    for step in range(1, group):
        copy_mixed(step, others[step]).wait_recv()
    mixed = mixed_turned[...].astype(jnp.float32).T.astype(jnp.bfloat16)
    stream = fed[...] + jnp.dot(mixed, out[...], preferred_element_type=jnp.float32)
    stream_ref[...] = stream
    low_ref[...] = stream.astype(jnp.bfloat16)
    for step in range(1, group):
        copy_heads(step).wait_send()
    for index in range(group):

        @pl.when(here != index)
        def _():
            copy_mixed(index, here).wait_send()

    for store in stores:
        store.wait()


def rotary_table(context_len):
    half_rot = ROT // 2
    frequency = np.power(np.float32(10000.0), np.float32(-2.0) * np.arange(half_rot, dtype=np.float32) / np.float32(ROT))
    angles = frequency.astype(np.float32)[:, None] * np.arange(context_len, dtype=np.float32)[None, :]
    return np.concatenate([np.cos(angles.astype(np.float64)), np.sin(angles.astype(np.float64))]).astype(np.float32)


def front(picked, docs, gains, shifts, qkv, out, up, down, bias, enc, dec, shift):
    group, share, rows = picked.shape
    width = gains.shape[1]
    ff_width = up.shape[1]
    mine = enc.shape[0]
    shift = shift.reshape(mine // LANES, LANES)
    bf16, f32 = jnp.bfloat16, jnp.float32
    dma = pltpu.SemaphoreType.DMA
    return pl.pallas_call(
        front_kernel,
        out_shape=(
            jax.ShapeDtypeStruct((rows, width), bf16),
            jax.ShapeDtypeStruct((rows, width), f32),
            jax.ShapeDtypeStruct((2 * mine, width), bf16),
            jax.ShapeDtypeStruct((2 * mine, width), bf16),
            jax.ShapeDtypeStruct((width, 2 * mine), bf16),
            jax.ShapeDtypeStruct((2 * mine, LANES), f32),
            jax.ShapeDtypeStruct((2 * mine, LANES), f32),
        ),
        in_specs=[ANY] * 13,
        out_specs=(VMEM, VMEM) + (ANY,) * 5,
        scratch_shapes=[
            pltpu.VMEM((group, 1, rows), jnp.int32),
            pltpu.VMEM((2, width), f32),
            pltpu.VMEM((2, width), f32),
            pltpu.VMEM((width, 3 * width), bf16),
            pltpu.VMEM((width, width), bf16),
            pltpu.VMEM((width, ff_width), bf16),
            pltpu.VMEM((ff_width, width), bf16),
            pltpu.VMEM(bias.shape, f32),
            pltpu.VMEM((ROT, rows), f32),
            pltpu.VMEM((group, share, rows), bf16),
            pltpu.VMEM((width, rows), bf16),
            pltpu.VMEM((group, 3 * HEAD, rows), bf16),
            pltpu.VMEM((group, 3 * HEAD, rows), bf16),
            pltpu.VMEM((width, rows), bf16),
            pltpu.VMEM((rows, width), f32),
            pltpu.VMEM((mine, width), f32),
            pltpu.VMEM((mine, width), f32),
            pltpu.VMEM((2, mine // LANES, LANES), f32),
            pltpu.VMEM((2 * mine, width), bf16),
            pltpu.VMEM((2 * mine, width), bf16),
            pltpu.VMEM((width, 2 * mine), bf16),
            pltpu.VMEM((2 * mine, LANES), f32),
            pltpu.VMEM((2 * mine, LANES), f32),
            dma((13,)),
            dma((5,)),
            dma((3, group)),
            dma((3, group)),
            dma((3,)),
            dma((3,)),
        ],
        compiler_params=pltpu.CompilerParams(
            collective_id=2, has_side_effects=True, vmem_limit_bytes=60 * 2**20
        ),
        cost_estimate=pl.CostEstimate(flops=2 * 10**9, bytes_accessed=14 * 10**6, transcendentals=2 * 10**6),
        name="front_part",
    )(picked, docs, gains, shifts, qkv, out, up, down, bias, jnp.asarray(rotary_table(group * rows)), enc, dec, shift)


def forward_kernel(
    depth,
    own_ref,
    enc_ref,
    dec_ref,
    bias_ref,
    stream_ref,
    scale_ref,
    dec_bias_ref,
    gathered_ref,
    relu_ref,
    upstream_ref,
    small_ref,
    total_ref,
    recon_ref,
    stream,
    scale,
    held,
    enc,
    dec,
    bias,
    staged,
    parts,
    send_zero,
    send_one,
    send_two,
    send_three,
    got_zero,
    got_one,
    got_two,
    got_three,
    load_sem,
    relu_sem,
    held_sem,
    send,
    receive,
    sum_send,
    sum_receive,
):
    rows = own_ref.shape[0]
    entries = enc.shape[0]
    width = held.shape[1]
    half = width // 2
    piece = min(entries, 256)
    where = peers(depth)
    (layer, row, place), across, beside, _ = where
    inner = (layer >= 1) & (layer < depth - 1)
    others = [((layer + step) % depth, row, place) for step in range(1, depth)]
    loads = [
        pltpu.make_async_copy(own_ref, held.at[pl.ds(0, rows)], load_sem.at[0]),
        pltpu.make_async_copy(enc_ref, enc, load_sem.at[1]),
        pltpu.make_async_copy(bias_ref, bias, load_sem.at[2]),
        pltpu.make_async_copy(dec_ref, dec, load_sem.at[3]),
        pltpu.make_async_copy(stream_ref, stream, load_sem.at[4]),
        pltpu.make_async_copy(scale_ref, scale, load_sem.at[5]),
    ]
    for load in loads:
        load.start()
    greet(others + [across, beside])
    loads[0].wait()
    gather = Gather(depth, rows, held, send, receive, where)
    gather.open()
    total_ref[...] = jnp.zeros_like(total_ref)
    for load in loads[1:]:
        load.wait()

    def part_slot(turn):
        return jnp.where(turn == 0, 4, turn % 4)

    def copy_zero(turn):
        layer_there = layer_at(depth, layer, turn)
        index = jnp.where(
            jnp.abs(layer_there - layer) == 1,
            jnp.where(layer > layer_there, 0, 1),
            jnp.where(layer == 0, 2, 3),
        )
        return remote(
            send_zero.at[turn - 1],
            got_zero.at[index],
            sum_send.at[5, turn],
            sum_receive.at[5, index],
            (layer_there, row, place),
        )

    def one_slot(turn):
        return jnp.where(turn == 0, 2, turn % 2)

    def copy_one(turn, part):
        source = send_one.at[one_slot(turn), pl.ds(part * half, half)]
        device = beside if part else across
        return remote(source, got_one.at[part, turn], sum_send.at[part, turn], sum_receive.at[part, turn], device)

    def two_slot(turn):
        return jnp.where(turn == 0, 3, turn % 3)

    def copy_two(turn, part, side):
        device = beside if part else across
        span = pl.ds(side * half, half)
        return remote(
            send_two.at[part, two_slot(turn), span],
            got_two.at[part, turn, span],
            sum_send.at[6 + 2 * part + side, turn],
            sum_receive.at[6 + 2 * part + side, turn],
            device,
        )

    def each_two(turn, act):
        for part in range(2):
            for side in range(2):
                act(copy_two(turn, part, side))

    def copy_three(turn):
        layer_there = layer_at(depth, layer, turn)
        index = place_of(depth, layer_there, layer)
        return remote(
            send_three.at[turn],
            got_three.at[index],
            sum_send.at[4, turn],
            sum_receive.at[4, index],
            (layer_there, row, place),
        )

    def copy_relu(order):
        first = slot_of(depth, order // 4, order % 4) * rows
        return pltpu.make_async_copy(
            staged.at[order % 2],
            relu_ref.at[:, pl.ds(pl.multiple_of(first, rows), rows)],
            relu_sem.at[order % 2],
        )

    def copy_held(step):
        span = pl.ds(pl.multiple_of(step * 4 * rows, 4 * rows), 4 * rows)
        return pltpu.make_async_copy(held.at[span], gathered_ref.at[span], held_sem.at[step])

    def sum_one(turn, value):
        @pl.when(turn >= 5)
        def _():
            copy_one(turn - 2, 0).wait_send()
            copy_one(turn - 2, 1).wait_send()

        send_one[one_slot(turn)] = value.astype(jnp.bfloat16)
        copy_one(turn, 0).start()
        copy_one(turn, 1).start()

    def send_half(turn, part, side, extra=None):
        span = pl.ds(side * half, half)
        value = parts[1 + part, part_slot(turn), span]
        if extra is not None:
            value = value + extra.astype(jnp.float32)
        send_two[part, two_slot(turn), span] = value.astype(jnp.bfloat16)
        copy_two(turn, part, side).start()

    def sum_two_own(turn):
        @pl.when(turn >= 4)
        def _():
            each_two(turn - 3, lambda copy: copy.wait_send())

        send_half(turn, 1, 1)
        send_half(turn, 0, 0)

    def sum_two(turn):
        @pl.when(crosswise(turn))
        def _():
            copy_one(turn, 0).wait_recv()
            send_half(turn, 1, 0, got_one[0, turn])
            copy_one(turn, 1).wait_recv()
            send_half(turn, 0, 1, got_one[1, turn])

        @pl.when((turn == 1) | (turn == 2))
        def _():
            send_half(turn, 1, 0)
            send_half(turn, 0, 1)

    def column_sum(turn):
        each_two(turn, lambda copy: copy.wait_recv())
        return parts[0, part_slot(turn)] + got_two[0, turn].astype(jnp.float32) + got_two[1, turn].astype(jnp.float32)

    def sum_three(turn):
        send_three[turn] = column_sum(turn).astype(jnp.bfloat16)
        copy_three(turn).start()

    def one_block(order, carry):
        turn, column = order // 4, order % 4

        @pl.when(column == 1)
        def _():
            gather.hand_on(turn)

        @pl.when(column == 3)
        def _():
            gather.wait_diagonal(turn)

        @pl.when(order >= 2)
        def _():
            copy_relu(order - 2).wait()

        first_row = slot_of(depth, turn, column) * rows
        block = held[pl.ds(pl.multiple_of(first_row, rows), rows)]
        low = []
        for first in range(0, entries, piece):
            span = pl.ds(first, piece)
            shift = bias[span]
            pre = lax.dot_general(enc[span], block, LAST_LAST, preferred_element_type=jnp.float32)
            positive = jnp.maximum(pre + jnp.concatenate([shift] * (rows // LANES), axis=1), 0.0)
            staged[order % 2, span] = positive
            active = positive * positive
            folded = active[:, :LANES]
            for lane in range(LANES, rows, LANES):
                folded = folded + active[:, lane : lane + LANES]
            total_ref[span] += folded
            low.append(active.astype(jnp.bfloat16))
        recon = jnp.dot(dec[...], jnp.concatenate(low, axis=0), preferred_element_type=jnp.float32)
        copy_relu(order).start()

        @pl.when((column < 3) | (turn == 0))
        def _():
            parts[column, part_slot(turn)] = recon

        @pl.when((column == 3) & (turn >= 3))
        def _():
            sum_one(turn, recon)

        @pl.when((column == 3) & ((turn == 1) | (turn == 2)))
        def _():
            send_zero[turn - 1] = recon.astype(jnp.bfloat16)
            copy_zero(turn).start()

        @pl.when(order == 0)
        def _():
            gather.arrive(1)

        @pl.when((order == 0) & inner)
        def _():
            gather.arrive(2)

        @pl.when((order == 2) & inner)
        def _():
            gather.arrive(3)

        @pl.when((column == 0) & (turn >= 1) & (turn + 1 < depth) & (jnp.logical_not(inner) | (turn >= 3)))
        def _():
            gather.arrive(turn + 1)

        @pl.when((column == 0) & (turn + 1 < depth))
        def _():
            gather.to_neighbours(turn + 1)

        @pl.when((column == 1) & (turn >= 3))
        def _():
            sum_two_own(turn - 2)
            sum_two(turn - 2)

        @pl.when((column == 2) & (turn == depth - 1))
        def _():
            sum_two_own(depth - 2)
            sum_two(depth - 2)

        @pl.when((column == 3) & (turn >= 4))
        def _():
            sum_three(turn - 3)

        return carry

    lax.fori_loop(0, 4 * depth, one_block, 0)
    for step in range(depth):
        copy_held(step).start()
    sum_two_own(depth - 1)
    sum_three(depth - 3)
    sum_two(depth - 1)
    sum_three(depth - 2)
    for index, (_, there) in enumerate(takers(depth, layer)):

        @pl.when(there)
        def _(index=index):
            remote(
                send_zero.at[0], got_zero.at[index], sum_send.at[5, 0], sum_receive.at[5, index], across
            ).wait_recv()
            parts[3, 4] += got_zero[index].astype(jnp.float32)

    sum_one(0, parts[3, 4])
    sum_two_own(0)
    sum_three(depth - 1)
    sum_two(0)
    recon_ref[...] = column_sum(0)
    for turn in range(1, depth):
        remote(
            send_three.at[turn], got_three.at[turn], sum_send.at[4, turn], sum_receive.at[4, turn], across
        ).wait_recv()
        recon_ref[...] += got_three[turn].astype(jnp.float32)
    error = recon_ref[...].T + dec_bias_ref[...] - stream[...]
    upstream = (2.0 * error).astype(jnp.bfloat16)
    upstream_ref[...] = upstream
    loss = fold(error * error)
    weighted = total_ref[...] * scale[...]
    loss = loss + fold(weighted)
    small_ref[...] = jnp.zeros_like(small_ref)
    column_sums = jnp.sum(upstream.astype(jnp.float32), axis=0, keepdims=True)
    lines = width // LANES
    for line in range(lines):
        small_ref[line : line + 1] = column_sums[:, line * LANES : (line + 1) * LANES]
    small_ref[lines : lines + 1] = jnp.sum(loss, axis=0, keepdims=True)
    gather.close()
    for turn in [0] + list(range(max(depth - 2, 3), depth)):
        for part in range(2):
            copy_one(turn, part).wait_send()
    for turn in [0] + list(range(max(depth - 3, 1), depth)):
        each_two(turn, lambda copy: copy.wait_send())
    for turn in range(1, depth):
        copy_three(turn).wait_send()
    for turn in (1, 2):
        copy_zero(turn).wait_send()
    copy_relu(4 * depth - 2).wait()
    copy_relu(4 * depth - 1).wait()
    for step in range(depth):
        copy_held(step).wait()


def forward(depth, own, enc, dec_turned, bias, stream, scale, dec_bias):
    rows, width = own.shape
    entries = enc.shape[0]
    bf16, f32 = jnp.bfloat16, jnp.float32
    dma = pltpu.SemaphoreType.DMA
    return pl.pallas_call(
        functools.partial(forward_kernel, depth),
        out_shape=(
            jax.ShapeDtypeStruct((depth * 4 * rows, width), bf16),
            jax.ShapeDtypeStruct((entries, depth * 4 * rows), f32),
            jax.ShapeDtypeStruct((rows, width), bf16),
            jax.ShapeDtypeStruct((8, LANES), f32),
            jax.ShapeDtypeStruct((entries, LANES), f32),
        ),
        in_specs=[ANY] * 6 + [VMEM],
        out_specs=(ANY, ANY, VMEM, VMEM, VMEM),
        scratch_shapes=[
            pltpu.VMEM((width, rows), f32),
            pltpu.VMEM((rows, width), f32),
            pltpu.VMEM((entries, LANES), f32),
            pltpu.VMEM((depth * 4 * rows, width), bf16),
            pltpu.VMEM((entries, width), bf16),
            pltpu.VMEM((width, entries), bf16),
            pltpu.VMEM((entries, LANES), f32),
            pltpu.VMEM((2, entries, rows), f32),
            pltpu.VMEM((4, 5, width, rows), f32),
            pltpu.VMEM((2, width, rows), bf16),
            pltpu.VMEM((3, width, rows), bf16),
            pltpu.VMEM((2, 4, width, rows), bf16),
            pltpu.VMEM((depth, width, rows), bf16),
            pltpu.VMEM((4, width, rows), bf16),
            pltpu.VMEM((2, depth, width // 2, rows), bf16),
            pltpu.VMEM((2, depth, width, rows), bf16),
            pltpu.VMEM((depth, width, rows), bf16),
            dma((6,)),
            dma((2,)),
            dma((depth,)),
            dma((11, max(depth, 4))),
            dma((9, max(depth, 4))),
            dma((10, max(depth, 4))),
            dma((10, max(depth, 4))),
        ],
        compiler_params=pltpu.CompilerParams(
            collective_id=0, has_side_effects=True, vmem_limit_bytes=60 * 2**20
        ),
        cost_estimate=pl.CostEstimate(
            flops=16 * depth * rows * entries * width, bytes_accessed=16 * depth * rows * entries, transcendentals=0
        ),
        name="forward_blocks",
    )(own, enc, dec_turned, bias, stream, scale, dec_bias)


def backward_kernel(
    depth,
    everyone,
    own_ref,
    gathered_ref,
    relu_ref,
    dec_ref,
    scale_ref,
    active_ref,
    small_ref,
    enc_out,
    dec_out,
    bias_out,
    small_out,
    squares_out,
    held,
    inputs,
    dec,
    scale,
    tile,
    held_last,
    inputs_last,
    relu_last,
    enc_sum,
    dec_sum,
    bias_sum,
    enc_got,
    dec_got,
    bias_got,
    active,
    active_got,
    low,
    small,
    small_got,
    squares,
    squares_got,
    load_sem,
    tile_sem,
    store_sem,
    send,
    receive,
    pair_send,
    pair_receive,
    last_send,
    last_receive,
    all_send,
    all_receive,
):
    rows = own_ref.shape[0]
    entries = dec.shape[0]
    mine = entries // 2
    piece = tile.shape[1]
    tiles = entries // piece
    where = peers(depth)
    (layer, row, column), _, _, partner = where
    core = column % 2
    inner = (layer >= 1) & (layer < depth - 1)
    loads = [
        pltpu.make_async_copy(own_ref, held.at[pl.ds(0, rows)], load_sem.at[0]),
        pltpu.make_async_copy(dec_ref, dec, load_sem.at[1]),
        pltpu.make_async_copy(scale_ref, scale, load_sem.at[2]),
        pltpu.make_async_copy(gathered_ref, inputs, load_sem.at[3]),
        pltpu.make_async_copy(active_ref, active, load_sem.at[4]),
        pltpu.make_async_copy(small_ref, small, load_sem.at[5]),
    ]
    for load in loads:
        load.start()

    def place(turn):
        return (turn + (1 - core) * (tiles // 2)) % tiles

    def group_of(group):
        if group == depth - 1:
            return (4 * group + 1) * rows, 3 * rows
        if group == depth:
            return (4 * group - 4) * rows, rows
        return 4 * group * rows, 4 * rows

    def copy_tile(group, start, size, turn):
        slot = (group * tiles + turn) % 2
        first = pl.multiple_of(place(turn) * piece, piece)
        return pltpu.make_async_copy(
            relu_ref.at[pl.ds(first, piece), pl.ds(pl.multiple_of(start, rows), size)],
            tile.at[slot, :, pl.ds(0, size)],
            tile_sem.at[slot],
        )

    copy_tile(0, *group_of(0), 0).start()

    others = [
        ((layer + dz) % depth, (row + dy) % 2, (column + dx) % 4)
        for dz in range(depth)
        for dy in range(2)
        for dx in range(4)
    ][1:]
    greet(others)
    loads[0].wait()
    gather = Gather(depth, rows, held, send, receive, where)
    gather.open()
    for load in loads[1:]:
        load.wait()

    def small_copy(index):
        return remote(
            small, small_got.at[index], all_send.at[0, index], all_receive.at[0, index], others[index - 1]
        )

    def squares_copy(index):
        return remote(
            squares, squares_got.at[index], all_send.at[1, index], all_receive.at[1, index], others[index - 1]
        )

    for index in range(1, everyone):
        small_copy(index).start()

    theirs = (1 - core) * mine
    active_copy = remote(
        active.at[pl.ds(pl.multiple_of(theirs, mine), mine)], active_got, pair_send.at[3, 0], pair_receive.at[3, 0], partner
    )
    active_copy.start()
    last = pl.ds(4 * (depth - 1) * rows, rows)
    last_copies = [
        remote(
            relu_ref.at[pl.ds(pl.multiple_of(theirs, mine), mine), last],
            relu_last,
            last_send.at[0],
            last_receive.at[0],
            partner,
        ),
        remote(inputs.at[last], inputs_last, last_send.at[1], last_receive.at[1], partner),
        remote(held.at[last], held_last, last_send.at[2], last_receive.at[2], partner),
    ]
    last_copies[0].start()
    last_copies[1].start()
    enc_sum[...] = jnp.zeros_like(enc_sum)
    dec_sum[...] = jnp.zeros_like(dec_sum)
    bias_sum[...] = jnp.zeros_like(bias_sum)

    def pair_copy(kind, turn):
        source, target = ((low.at[0], enc_got), (low.at[1], dec_got), (bias_sum, bias_got))[kind]
        there = pl.ds(pl.multiple_of(turn * piece, piece), piece)
        return remote(
            source.at[pl.ds(pl.multiple_of(theirs + turn * piece, piece), piece) if kind == 2 else there],
            target.at[there],
            pair_send.at[kind, turn],
            pair_receive.at[kind, turn],
            partner,
        )

    gather.arrive(1)

    @pl.when(inner)
    def _():
        gather.arrive(2)

    gather.to_neighbours(1)
    gather.hand_on(0)

    def one_tile(group, start, size, turn):
        slot = (group * tiles + turn) % 2
        copy_tile(group, start, size, turn).wait()
        span = pl.ds(pl.multiple_of(place(turn) * piece, piece), piece)
        tokens = pl.ds(pl.multiple_of(start, rows), size)
        upstream, given, positive = held[tokens], inputs[tokens], tile[slot, :, :size]
        if group is depth:
            there = pl.ds(pl.multiple_of((turn - tiles // 2) * piece, piece), piece)
            upstream = jnp.concatenate([upstream, held_last[...]], axis=0)
            given = jnp.concatenate([given, inputs_last[...]], axis=0)
            positive = jnp.concatenate([positive, relu_last[there]], axis=1)
            size = 2 * size
        back = lax.dot_general(dec[span], upstream, LAST_LAST, preferred_element_type=jnp.float32)
        shift = jnp.concatenate([scale[span]] * (size // LANES), axis=1)
        slope = ((back + shift) * (2.0 * positive)).astype(jnp.bfloat16)
        act_low = (positive * positive).astype(jnp.bfloat16)
        wide = slope.astype(jnp.float32)
        folded = wide[:, :LANES]
        for lane in range(LANES, size, LANES):
            folded = folded + wide[:, lane : lane + LANES]
        bias_sum[span] += folded
        enc_sum[span] += jnp.dot(slope, given, preferred_element_type=jnp.float32)
        dec_sum[span] += jnp.dot(act_low, upstream, preferred_element_type=jnp.float32)

    def take_in(group, turn):
        @pl.when((group == 0) & (turn == tiles // 2))
        def _():
            if depth > 3:

                @pl.when(inner)
                def _():
                    gather.arrive(3)

            @pl.when(jnp.logical_not(inner))
            def _():
                gather.arrive(2)

            gather.to_neighbours(2)

        @pl.when((group >= 1) & (turn == 0) & (group + 2 < depth))
        def _():
            @pl.when(jnp.logical_not(inner) | (group >= 2))
            def _():
                gather.arrive(group + 2)

            gather.to_neighbours(group + 2)

        @pl.when((group == depth - 2) & (turn == 0))
        def _():
            gather.hand_on(depth - 1)

        @pl.when(turn == tiles // 2)
        def _():
            gather.wait_diagonal(group)

    def middle_group(group, carry):
        start, size = 4 * group * rows, 4 * rows

        @pl.when(group >= 1)
        def _():
            gather.hand_on(group)

        def one(turn, carry):
            @pl.when(turn + 1 < tiles)
            def _():
                copy_tile(group, start, size, turn + 1).start()

            @pl.when((turn + 1 == tiles) & (group + 2 < depth))
            def _():
                copy_tile(group + 1, start + 4 * rows, size, 0).start()

            @pl.when((turn + 1 == tiles) & (group + 2 == depth))
            def _():
                copy_tile(depth - 1, *group_of(depth - 1), 0).start()

            one_tile(group, start, size, turn)
            take_in(group, turn)
            return carry

        return lax.fori_loop(0, tiles, one, carry)

    def late_group(turn, carry):
        start, size = group_of(depth - 1)

        @pl.when(turn + 1 < tiles)
        def _():
            copy_tile(depth - 1, start, size, turn + 1).start()

        @pl.when(turn + 1 == tiles)
        def _():
            copy_tile(depth, *group_of(depth), tiles // 2).start()

        one_tile(depth - 1, start, size, turn)

        @pl.when(turn < tiles // 2)
        def _():
            span = pl.ds(pl.multiple_of(place(turn) * piece, piece), piece)
            there = pl.ds(pl.multiple_of(turn * piece, piece), piece)
            low[0, there] = enc_sum[span].astype(jnp.bfloat16)
            low[1, there] = dec_sum[span].astype(jnp.bfloat16)
            for kind in range(3):
                pair_copy(kind, turn).start()

        return carry

    def last_group(turn, carry):
        start, size = group_of(depth)

        @pl.when(turn + 1 < tiles)
        def _():
            copy_tile(depth, start, size, turn + 1).start()

        one_tile(depth, start, size, turn)
        return carry

    lax.fori_loop(0, depth - 1, middle_group, 0)
    gather.wait_diagonal(depth - 1)
    last_copies[2].start()
    lax.fori_loop(0, tiles, late_group, 0)
    for copy in last_copies:
        copy.wait_recv()
    lax.fori_loop(tiles // 2, tiles, last_group, 0)

    ours = core * mine
    active_copy.wait_recv()
    span = pl.ds(pl.multiple_of(ours, mine), mine)
    act_total = jnp.sum(active[span] + active_got[...], axis=1, keepdims=True)
    partial = jnp.zeros((8, LANES), jnp.float32)

    stores = []
    rows_of = lax.broadcasted_iota(jnp.int32, (LANES, LANES), 0)
    lanes_of = lax.broadcasted_iota(jnp.int32, (LANES, LANES), 1)
    for turn in range(tiles // 2):
        for kind in range(3):
            pair_copy(kind, turn).wait_recv()
        near = pl.ds(pl.multiple_of(ours + turn * piece, piece), piece)
        there = pl.ds(turn * piece, piece)
        enc_grad = enc_sum[near] + enc_got[there].astype(jnp.float32)
        enc_sum[near] = enc_grad
        partial = partial + fold(enc_grad * enc_grad)
        dec_grad = dec_sum[near] + dec_got[there].astype(jnp.float32)
        dec_grad = dec_grad + (
            COEFFICIENT * COEFFICIENT * act_total[turn * piece : (turn + 1) * piece] / scale[near, :1]
        ) * dec[near].astype(jnp.float32)
        dec_sum[near] = dec_grad
        partial = partial + fold(dec_grad * dec_grad)
        stores += [
            pltpu.make_async_copy(enc_sum.at[near], enc_out.at[there], store_sem.at[0, turn]),
            pltpu.make_async_copy(dec_sum.at[near], dec_out.at[there], store_sem.at[1, turn]),
        ]
        stores[-2].start()
        stores[-1].start()
        bias_grad = jnp.sum(bias_sum[near] + bias_got[there], axis=1, keepdims=True)
        for first in range(0, piece, LANES):
            wide = jnp.broadcast_to(bias_grad[first : first + LANES], (LANES, LANES))
            line = jnp.sum(jnp.where(rows_of == lanes_of, wide, 0.0), axis=0, keepdims=True)
            index = (turn * piece + first) // LANES
            bias_out[index : index + 1] = line
            partial = partial + jnp.where(rows_of[:8] == 0, line * line, 0.0)
    squares[...] = partial
    for index in range(1, everyone):
        squares_copy(index).start()
    total_small = small[...]
    for index in range(1, everyone):
        small_copy(index).wait_recv()
        total_small = total_small + small_got[index]
    small_out[...] = total_small
    total_squares = squares[...]
    for index in range(1, everyone):
        squares_copy(index).wait_recv()
        total_squares = total_squares + squares_got[index]
    squares_out[...] = total_squares
    gather.close()
    for index in range(1, everyone):
        small_copy(index).wait_send()
        squares_copy(index).wait_send()
    active_copy.wait_send()
    for copy in last_copies:
        copy.wait_send()
    for turn in range(tiles // 2):
        for kind in range(3):
            pair_copy(kind, turn).wait_send()
    for store in stores:
        store.wait()


def backward(depth, own, gathered, relu, dec, scale, active, small):
    rows, width = own.shape
    entries = dec.shape[0]
    mine = entries // 2
    piece = min(512, mine)
    everyone = depth * 8
    bf16, f32 = jnp.bfloat16, jnp.float32
    dma = pltpu.SemaphoreType.DMA
    return pl.pallas_call(
        functools.partial(backward_kernel, depth, everyone),
        out_shape=(
            jax.ShapeDtypeStruct((mine, width), f32),
            jax.ShapeDtypeStruct((mine, width), f32),
            jax.ShapeDtypeStruct((mine // LANES, LANES), f32),
            jax.ShapeDtypeStruct(small.shape, f32),
            jax.ShapeDtypeStruct((8, LANES), f32),
        ),
        in_specs=[ANY] * 7,
        out_specs=(ANY, ANY, VMEM, VMEM, VMEM),
        scratch_shapes=[
            pltpu.VMEM((depth * 4 * rows, width), bf16),
            pltpu.VMEM((depth * 4 * rows, width), bf16),
            pltpu.VMEM((entries, width), bf16),
            pltpu.VMEM((entries, LANES), f32),
            pltpu.VMEM((2, piece, 4 * rows), f32),
            pltpu.VMEM((rows, width), bf16),
            pltpu.VMEM((rows, width), bf16),
            pltpu.VMEM((mine, rows), f32),
            pltpu.VMEM((entries, width), f32),
            pltpu.VMEM((entries, width), f32),
            pltpu.VMEM((entries, LANES), f32),
            pltpu.VMEM((mine, width), bf16),
            pltpu.VMEM((mine, width), bf16),
            pltpu.VMEM((mine, LANES), f32),
            pltpu.VMEM((entries, LANES), f32),
            pltpu.VMEM((mine, LANES), f32),
            pltpu.VMEM((2, mine, width), bf16),
            pltpu.VMEM(small.shape, f32),
            pltpu.VMEM((everyone,) + small.shape, f32),
            pltpu.VMEM((8, LANES), f32),
            pltpu.VMEM((everyone, 8, LANES), f32),
            dma((6,)),
            dma((2,)),
            dma((2, entries // piece)),
            dma((11, max(depth, 4))),
            dma((9, max(depth, 4))),
            dma((4, entries // piece)),
            dma((4, entries // piece)),
            dma((3,)),
            dma((3,)),
            dma((2, everyone)),
            dma((2, everyone)),
        ],
        compiler_params=pltpu.CompilerParams(
            collective_id=1, has_side_effects=True, vmem_limit_bytes=60 * 2**20
        ),
        cost_estimate=pl.CostEstimate(
            flops=24 * depth * rows * entries * width, bytes_accessed=16 * depth * rows * entries, transcendentals=0
        ),
        name="backward_blocks",
    )(own, gathered, relu, dec, scale, active, small)


def update_kernel(*refs):
    names = ["enc_grad", "dec_grad", "bias_grad", "small", "squares"]
    for kind in ("enc", "dec", "bias", "shift"):
        names += [kind, kind + "_one", kind + "_two"]
    given = dict(zip(names, refs[: len(names)]))
    made = refs[len(names) : len(names) + 14]
    brought, staged, load_sem, store_sem = refs[len(names) + 14 :]
    mine = given["enc"].shape[0]
    slots, _, piece, _ = staged.shape
    parts = mine // piece
    large = ["enc", "enc_one", "enc_two", "enc_grad", "dec", "dec_one", "dec_two", "dec_grad"]

    def load(part, index):
        span = pl.ds(pl.multiple_of(part * piece, piece), piece)
        slot = part % slots
        return pltpu.make_async_copy(given[large[index]].at[span], brought.at[slot, index], load_sem.at[slot, index])

    for part in range(min(slots - 1, parts)):
        for index in range(8):
            load(part, index).start()
    lines = given["shift"].shape[1] // LANES
    shift_grad = jnp.concatenate([given["small"][line : line + 1] for line in range(lines)], axis=1)
    total = jnp.sum(given["squares"][...], keepdims=True) + jnp.sum(shift_grad * shift_grad, keepdims=True)
    norm = jnp.sqrt(total)
    clip = jnp.minimum(1.0, CLIP_NORM / (norm + 1e-06))
    made[12][...] = norm
    made[13][...] = jnp.sum(given["small"][lines : lines + 1], keepdims=True)

    def store(part, index):
        span = pl.ds(pl.multiple_of(part * piece, piece), piece)
        slot = part % slots
        return pltpu.make_async_copy(staged.at[slot, index], made[index].at[span], store_sem.at[slot, index])

    def one(part, carry):
        @pl.when(part >= slots)
        def _():
            for index in range(6):
                store(part - slots, index).wait()

        @pl.when(part + slots - 1 < parts)
        def _():
            for index in range(8):
                load(part + slots - 1, index).start()

        slot = part % slots
        for index in range(8):
            load(part, index).wait()
        for index in range(2):
            new, first, second = adam_step(
                *(brought[slot, 4 * index + offset] for offset in range(4)),
                clip,
                RATE_MATRIX,
                WEIGHT_DECAY,
            )
            if index:
                new = new * lax.rsqrt(jnp.sum(new * new, axis=1, keepdims=True) + NORM_EPSILON)
            for offset, value in enumerate((new, first, second)):
                staged[slot, 3 * index + offset] = value
        for index in range(6):
            store(part, index).start()
        return carry

    lax.fori_loop(0, parts, one, 0)
    for offset, (kind, gradient) in enumerate((("bias", given["bias_grad"][...]), ("shift", shift_grad))):
        results = adam_step(
            given[kind][...], given[kind + "_one"][...], given[kind + "_two"][...], gradient, clip, RATE_BIAS, 0.0
        )
        for index, value in enumerate(results):
            made[6 + 3 * offset + index][...] = value
    for part in range(max(parts - slots, 0), parts):
        for index in range(6):
            store(part, index).wait()


def update(*arrays):
    f32 = jnp.float32
    mine, width = arrays[0].shape
    dense, flat = (mine // LANES, LANES), (1, width)
    arrays = list(arrays)
    for index in range(11, 14):
        arrays[index] = arrays[index].reshape(dense)
    for index in range(14, 17):
        arrays[index] = arrays[index].reshape(flat)
    piece, slots = min(128, mine), 4
    made = pl.pallas_call(
        update_kernel,
        out_shape=[jax.ShapeDtypeStruct((mine, width), f32)] * 6
        + [jax.ShapeDtypeStruct(dense, f32)] * 3
        + [jax.ShapeDtypeStruct(flat, f32)] * 3
        + [jax.ShapeDtypeStruct((1, 1), f32)] * 2,
        in_specs=[ANY] * 2 + [VMEM] * 3 + [ANY] * 6 + [VMEM] * 6,
        out_specs=[ANY] * 6 + [VMEM] * 8,
        scratch_shapes=[
            pltpu.VMEM((slots, 8, piece, width), f32),
            pltpu.VMEM((slots, 6, piece, width), f32),
            pltpu.SemaphoreType.DMA((slots, 8)),
            pltpu.SemaphoreType.DMA((slots, 6)),
        ],
        compiler_params=pltpu.CompilerParams(vmem_limit_bytes=60 * 2**20),
        cost_estimate=pl.CostEstimate(flops=60 * mine * width, bytes_accessed=56 * mine * width, transcendentals=4 * mine * width),
        name="update",
    )(*arrays)
    return (
        *made[:6],
        *(value.reshape(mine) for value in made[6:9]),
        *(value.reshape(width) for value in made[9:12]),
        made[12].reshape(()),
        made[13].reshape(()),
    )


def body(
    depth,
    token_ids,
    doc_ids,
    embed,
    norm_gains,
    norm_shifts,
    qkv_weight,
    out_weight,
    up_weight,
    down_weight,
    proj_biases,
    enc_weight,
    dec_weight,
    enc_bias,
    dec_bias,
    enc_first,
    enc_second,
    dec_first,
    dec_second,
    enc_bias_first,
    enc_bias_second,
    dec_bias_first,
    dec_bias_second,
):
    model_width = norm_gains.shape[1]
    all_ids, all_docs = gather_ids(token_ids, doc_ids, model_width // embed.shape[1])
    low, stream, enc_both, dec_both, dec_turned, shift_wide, scale_wide = front(
        pick(all_ids, embed.T),
        all_docs,
        norm_gains,
        norm_shifts,
        qkv_weight,
        out_weight,
        up_weight,
        down_weight,
        proj_biases.reshape(-1, LANES),
        enc_weight,
        dec_weight,
        enc_bias,
    )
    gathered, relu, upstream, small, active = forward(
        depth, low, enc_both, dec_turned, shift_wide, stream, scale_wide, dec_bias[None]
    )
    enc_grad, dec_grad, enc_bias_grad, small_sum, squares = backward(
        depth, upstream, gathered, relu, dec_both, scale_wide, active, small
    )
    return update(
        enc_grad,
        dec_grad,
        enc_bias_grad,
        small_sum,
        squares,
        enc_weight,
        enc_first,
        enc_second,
        dec_weight,
        dec_first,
        dec_second,
        enc_bias,
        enc_bias_first,
        enc_bias_second,
        dec_bias,
        dec_bias_first,
        dec_bias_second,
    )


def solution(mesh):
    split = P(("dp", "seq", "opt"), None)
    split_vector = P(("dp", "seq", "opt"))
    in_specs = (
        P("dp", ("seq", "opt")),
        P("dp", ("seq", "opt")),
        P(None, ("seq", "opt")),
        P(),
        P(),
        P(),
        P(),
        P(),
        P(),
        P(),
        split,
        split,
        split_vector,
        P(),
        split,
        split,
        split,
        split,
        split_vector,
        split_vector,
        P(),
        P(),
    )
    out_specs = (split,) * 6 + (split_vector,) * 3 + (P(),) * 5
    return jax.shard_map(
        functools.partial(body, mesh.shape["dp"]),
        mesh=mesh,
        in_specs=in_specs,
        out_specs=out_specs,
        check_vma=False,
    )
```

```python
import functools

import jax
import jax.numpy as jnp
import numpy as np
from jax import lax
from jax.experimental import pallas as pl
from jax.experimental.pallas import tpu as pltpu
from jax.sharding import PartitionSpec as P

HEAD = 64
ROT = 16
STEP = 4
RAMP = 80


LAYER_EPSILON = 1e-05
NORM_EPSILON = 1e-08
BETA_FIRST = 0.9
BETA_SECOND = 0.999
ADAM_EPSILON = 1e-08
RATE_MATRIX = 0.02
RATE_BIAS = 0.1
WEIGHT_DECAY = 0.01
CLIP_NORM = 1.0
SPARSITY_TOP = 5.0
COEFFICIENT = SPARSITY_TOP * min(1.0, STEP / RAMP)
LAST_LAST = (((1,), (1,)), ((), ()))
MESH = pl.DeviceIdType.MESH
ANY = pl.BlockSpec(memory_space=pl.ANY)
VMEM = pl.BlockSpec(memory_space=pltpu.VMEM)
LANES = 128


def adam_step(parameter, moment_one, moment_two, gradient, clip_scale, step_rate, decay_rate):
    gradient = gradient * clip_scale
    moment_one = BETA_FIRST * moment_one + (1.0 - BETA_FIRST) * gradient
    moment_two = BETA_SECOND * moment_two + (1.0 - BETA_SECOND) * gradient * gradient
    first_share, second_share = 1.0 / (1.0 - BETA_FIRST**STEP), 1.0 / (1.0 - BETA_SECOND**STEP)
    adjust = moment_one * first_share / (jnp.sqrt(moment_two * second_share) + ADAM_EPSILON)
    return (parameter - step_rate * (adjust + decay_rate * parameter), moment_one, moment_two)


def place_of(depth, layer, other):
    distance = jnp.abs(other - layer)
    margin = jnp.minimum(layer, depth - 1 - layer)
    near = jnp.where(other < layer, 2 * distance - 1, 2 * distance)
    return jnp.where(distance <= margin, near, distance + margin)


def layer_at(depth, layer, turn):
    margin = jnp.minimum(layer, depth - 1 - layer)
    near = jnp.where(turn % 2 == 1, layer - (turn + 1) // 2, layer + turn // 2)
    far = jnp.where(2 * layer < depth - 1, layer + turn - margin, layer - turn + margin)
    return jnp.where(turn <= 2 * margin, near, far)


def crosswise(turn):
    return (turn == 0) | (turn >= 3)


def slot_of(depth, turn, column):
    last = 4 * (depth - 1)
    own = jnp.maximum(4 * turn - 3, 0)
    diagonal = jnp.where(turn == depth - 1, last, jnp.where(turn == depth - 2, last + 1, 4 * turn + 4))
    return jnp.where(column == 0, own, jnp.where(column == 3, diagonal, 4 * turn + 1 + column))


def takers(depth, layer):
    return [
        (layer + 1, layer + 1 < depth),
        (layer - 1, layer >= 1),
        (layer * 0, layer == 2),
        (layer * 0 + depth - 1, layer == depth - 3),
    ]


def peers(depth):
    layer, row, column = lax.axis_index("dp"), lax.axis_index("seq"), lax.axis_index("opt")
    across = (layer, row, (column + 2) % 4)
    beside = (layer, 1 - row, column)
    partner = (layer, row, column + 1 - 2 * (column % 2))
    return (layer, row, column), across, beside, partner


def remote(source, target, send, receive, device):
    return pltpu.make_async_remote_copy(
        src_ref=source,
        dst_ref=target,
        send_sem=send,
        recv_sem=receive,
        device_id=device,
        device_id_type=MESH,
    )


def greet(devices):
    barrier = pltpu.get_barrier_semaphore()
    for device in devices:
        pl.semaphore_signal(barrier, inc=1, device_id=device, device_id_type=MESH)
    pl.semaphore_wait(barrier, len(devices))


def fold(values):
    total = values[:8]
    for first in range(8, values.shape[0], 8):
        total = total + values[first : first + 8]
    narrow = total[:, :LANES]
    for lane in range(LANES, values.shape[1], LANES):
        narrow = narrow + total[:, lane : lane + LANES]
    return narrow


class Gather:
    def __init__(self, depth, rows, held, send, receive, where):
        self.depth, self.rows, self.held = depth, rows, held
        self.send, self.receive = send, receive
        self.here, self.across, self.beside, _ = where

    def block(self, turn, column, part=None):
        first, rows = slot_of(self.depth, turn, column) * self.rows, self.rows
        if part is not None:
            rows = self.rows // 2
            first = first + part * rows
        return self.held.at[pl.ds(pl.multiple_of(first, rows), rows)]

    def device(self, layer):
        return (layer, self.here[1], self.here[2])

    def copy_along(self, turn, sign, part):
        layer = self.here[0] + sign
        source = layer_at(self.depth, self.here[0], turn)
        there = place_of(self.depth, layer, source)
        row, index = (part, turn) if sign == 1 else (part + 8, turn)
        return remote(
            self.block(turn, 0, part),
            self.block(there, 0, part),
            self.send.at[row, index],
            self.receive.at[part, there],
            self.device(layer),
        )

    def along(self, turn, act):
        source, layer = layer_at(self.depth, self.here[0], turn), self.here[0]
        for sign, onward in ((1, source <= layer), (-1, source >= layer)):

            @pl.when(onward & (layer + sign >= 0) & (layer + sign < self.depth))
            def _(sign=sign):
                for part in range(2):
                    act(self.copy_along(turn, sign, part))

    def copy_across(self, turn, part):
        return remote(
            self.block(turn, 0, part),
            self.block(turn, 1, part),
            self.send.at[2 + part, turn],
            self.receive.at[2 + part, turn],
            self.across,
        )

    def copy_beside(self, turn, part):
        return remote(
            self.block(turn, 0, part),
            self.block(turn, 2, part),
            self.send.at[4 + part, turn],
            self.receive.at[4 + part, turn],
            self.beside,
        )

    def pass_across(self, turn):
        return remote(
            self.block(turn, 2, 0), self.block(turn, 3, 0), self.send.at[6, turn], self.receive.at[6, turn], self.across
        )

    def pass_beside(self, turn):
        return remote(
            self.block(turn, 1, 1), self.block(turn, 3, 1), self.send.at[7, turn], self.receive.at[7, turn], self.beside
        )

    def pass_along(self, index, layer):
        turn = place_of(self.depth, layer, self.here[0])
        return remote(
            self.block(0, 3), self.block(turn, 3), self.send.at[10, index], self.receive.at[8, turn], self.device(layer)
        )

    def to_neighbours(self, turn):
        for part in range(2):
            self.copy_across(turn, 1 - part).start()
            self.copy_beside(turn, part).start()

    def open(self):
        self.to_neighbours(0)
        self.along(0, lambda copy: copy.start())

    def arrive(self, turn):
        for part in range(2):
            remote(
                self.block(0, 0, part),
                self.block(turn, 0, part),
                self.send.at[part, 0],
                self.receive.at[part, turn],
                self.across,
            ).wait_recv()
        self.along(turn, lambda copy: copy.start())

    def hand_on(self, turn):
        self.copy_across(turn, 1).wait_recv()

        @pl.when(crosswise(turn))
        def _():
            self.pass_beside(turn).start()

        self.copy_beside(turn, 0).wait_recv()

        @pl.when(crosswise(turn))
        def _():
            self.pass_across(turn).start()

        self.copy_across(turn, 0).wait_recv()
        self.copy_beside(turn, 1).wait_recv()

    def wait_diagonal(self, turn):
        @pl.when(crosswise(turn))
        def _():
            self.pass_across(turn).wait_recv()
            self.pass_beside(turn).wait_recv()

        @pl.when((turn == 1) | (turn == 2))
        def _():
            remote(
                self.block(0, 3), self.block(turn, 3), self.send.at[10, 0], self.receive.at[8, turn], self.across
            ).wait_recv()

        @pl.when(turn == 0)
        def _():
            for index, (layer, there) in enumerate(takers(self.depth, self.here[0])):

                @pl.when(there)
                def _(index=index, layer=layer):
                    self.pass_along(index, layer).start()

    def close(self):
        for index, (layer, there) in enumerate(takers(self.depth, self.here[0])):

            @pl.when(there)
            def _(index=index, layer=layer):
                self.pass_along(index, layer).wait_send()

        def done(turn, carry):
            self.along(turn, lambda copy: copy.wait_send())
            for part in range(2):
                self.copy_across(turn, part).wait_send()
                self.copy_beside(turn, part).wait_send()

            @pl.when(crosswise(turn))
            def _():
                self.pass_across(turn).wait_send()
                self.pass_beside(turn).wait_send()

            return carry

        lax.fori_loop(0, self.depth, done, 0)


def ids_kernel(ids_ref, docs_ref, ids_out, docs_out, ids_all, docs_all, load_sem, send, receive):
    group = ids_all.shape[0]
    layer, row, column = lax.axis_index("dp"), lax.axis_index("seq"), lax.axis_index("opt")
    here = row * 4 + column
    others = [(here + step) % group for step in range(group)]
    devices = [(layer, index // 4, index % 4) for index in others]
    loads = [
        pltpu.make_async_copy(ids_ref, ids_all.at[here], load_sem.at[0]),
        pltpu.make_async_copy(docs_ref, docs_all.at[here], load_sem.at[1]),
    ]
    for load in loads:
        load.start()
    greet(devices[1:])
    for load in loads:
        load.wait()
    copies = []
    for step in range(1, group):
        for kind, held in enumerate((ids_all, docs_all)):
            copies.append(
                remote(held.at[here], held.at[here], send.at[kind, step], receive.at[kind, step], devices[step])
            )
    for copy in copies:
        copy.start()
    for copy in copies:
        copy.wait()
    ids_out[...] = ids_all[...]
    docs_out[...] = docs_all[...]


def gather_ids(ids, docs, group):
    rows = ids.shape[1]
    dma = pltpu.SemaphoreType.DMA
    whole = jax.ShapeDtypeStruct((group, 1, rows), jnp.int32)
    return pl.pallas_call(
        ids_kernel,
        out_shape=(whole, whole),
        in_specs=[ANY] * 2,
        out_specs=(VMEM, VMEM),
        scratch_shapes=[
            pltpu.VMEM((group, 1, rows), jnp.int32),
            pltpu.VMEM((group, 1, rows), jnp.int32),
            dma((2,)),
            dma((2, group)),
            dma((2, group)),
        ],
        compiler_params=pltpu.CompilerParams(collective_id=3, has_side_effects=True, vmem_limit_bytes=60 * 2**20),
        name="gather_ids",
    )(ids, docs)


def pick_kernel(ids_ref, table_ref, picked, table, load_sem):
    group, _, rows = ids_ref.shape
    share, vocabulary = table.shape
    parts = 3 if vocabulary % (3 * LANES) == 0 else 1
    loads = [
        pltpu.make_async_copy(
            table_ref.at[:, pl.ds(part * (vocabulary // parts), vocabulary // parts)],
            table.at[:, pl.ds(part * (vocabulary // parts), vocabulary // parts)],
            load_sem.at[part],
        )
        for part in range(parts)
    ]
    for load in loads:
        load.start()
    lanes = lax.broadcasted_iota(jnp.int32, (share, LANES), 1)
    for load in loads:
        load.wait()

    def some(part, carry):
        source, first = part // (rows // LANES), part % (rows // LANES) * LANES
        found = None
        for place in range(LANES):
            token = ids_ref[source, 0, first + place]
            start = lax.bitwise_and(token, -LANES)
            tile = table[:, pl.ds(pl.multiple_of(start, LANES), LANES)].astype(jnp.float32)
            moved = pltpu.roll(tile, lax.bitwise_and(place - token, LANES - 1), 1)
            found = moved if found is None else jnp.where(lanes >= place, moved, found)
        picked[source, :, pl.ds(pl.multiple_of(first, LANES), LANES)] = found.astype(jnp.bfloat16)
        return carry

    lax.fori_loop(0, group * rows // LANES, some, 0)


def pick(ids, table):
    group, _, rows = ids.shape
    share = table.shape[0]
    return pl.pallas_call(
        pick_kernel,
        out_shape=jax.ShapeDtypeStruct((group, share, rows), jnp.bfloat16),
        in_specs=[pl.BlockSpec(memory_space=pltpu.SMEM), ANY],
        out_specs=VMEM,
        scratch_shapes=[pltpu.VMEM(table.shape, jnp.bfloat16), pltpu.SemaphoreType.DMA((3,))],
        compiler_params=pltpu.CompilerParams(vmem_limit_bytes=60 * 2**20),
        name="pick_features",
    )(ids, table)


def front_kernel(
    picked_ref,
    docs_ref,
    gains_ref,
    shifts_ref,
    qkv_ref,
    out_ref,
    up_ref,
    down_ref,
    bias_ref,
    turn_ref,
    enc_ref,
    dec_ref,
    shift_ref,
    low_ref,
    stream_ref,
    enc_out,
    dec_out,
    turned_out,
    shift_out,
    scale_out,
    docs_all,
    gains,
    shifts,
    qkv,
    out,
    up,
    down,
    bias,
    turn,
    picked,
    features,
    turned,
    heads,
    mixed_turned,
    fed,
    enc_full,
    dec_full,
    shift_all,
    enc,
    dec,
    dec_turned,
    shift_wide,
    scale_wide,
    load_sem,
    store_sem,
    send,
    receive,
    pair_send,
    pair_receive,
):
    group, share, rows = picked.shape
    mine = enc_full.shape[0]
    dense = mine // LANES
    width = gains.shape[1]
    ff_width = up.shape[1]
    layer, row, column = lax.axis_index("dp"), lax.axis_index("seq"), lax.axis_index("opt")
    here = row * 4 + column

    def member(index):
        return (layer, index // 4, index % 4)

    others = [(here + step) % group for step in range(group)]
    first_place = pl.multiple_of(here * rows, rows)
    loads = [
        pltpu.make_async_copy(picked_ref, picked, load_sem.at[0]),
        pltpu.make_async_copy(docs_ref, docs_all, load_sem.at[1]),
        pltpu.make_async_copy(gains_ref, gains, load_sem.at[2]),
        pltpu.make_async_copy(shifts_ref, shifts, load_sem.at[3]),
        pltpu.make_async_copy(bias_ref, bias, load_sem.at[4]),
        pltpu.make_async_copy(turn_ref.at[:, pl.ds(first_place, rows)], turn, load_sem.at[5]),
        pltpu.make_async_copy(qkv_ref, qkv, load_sem.at[6]),
        pltpu.make_async_copy(up_ref, up, load_sem.at[7]),
        pltpu.make_async_copy(down_ref, down, load_sem.at[8]),
        pltpu.make_async_copy(out_ref, out, load_sem.at[9]),
        pltpu.make_async_copy(enc_ref, enc_full, load_sem.at[10]),
        pltpu.make_async_copy(dec_ref, dec_full, load_sem.at[11]),
        pltpu.make_async_copy(shift_ref, shift_all.at[column % 2], load_sem.at[12]),
    ]
    for load in loads:
        load.start()
    greet([member(index) for index in others[1:]])
    loads[0].wait()

    def copy_features(step):
        return remote(
            picked.at[others[step]],
            features.at[pl.ds(pl.multiple_of(here * share, share), share)],
            send.at[0, step],
            receive.at[0, step],
            member(others[step]),
        )

    def copy_heads(step):
        return remote(
            turned.at[others[step]], heads.at[here], send.at[1, step], receive.at[1, step], member(others[step])
        )

    def copy_mixed(index, source):
        return remote(
            picked.at[index],
            mixed_turned.at[pl.ds(pl.multiple_of(source * HEAD, HEAD), HEAD)],
            send.at[2, index],
            receive.at[2, source],
            member(index),
        )

    for step in range(1, group):
        copy_features(step).start()

    partner = (layer, row, column + 1 - 2 * (column % 2))
    own = pl.ds(pl.multiple_of(column % 2 * mine, mine), mine)
    for load in loads[10:]:
        load.wait()
    shared = []
    for kind, (full, low) in enumerate(((dec_full, dec), (enc_full, enc))):

        def cast(part, carry, full=full, low=low):
            start = pl.multiple_of(part * 256, 256)
            low[pl.ds(pl.multiple_of(column % 2 * mine + start, 256), 256)] = full[pl.ds(start, 256)].astype(
                jnp.bfloat16
            )
            return carry

        lax.fori_loop(0, mine // 256, cast, 0)
        shared.append(remote(low.at[own], low.at[own], pair_send.at[kind], pair_receive.at[kind], partner))
        shared[-1].start()
    spot = shift_all.at[column % 2]
    shared.append(remote(spot, spot, pair_send.at[2], pair_receive.at[2], partner))
    shared[-1].start()
    features[pl.ds(pl.multiple_of(here * share, share), share)] = picked[here]
    for load in loads[1:10]:
        load.wait()
    for step in range(1, group):
        copy_features(step).wait_recv()

    residual = features[...].astype(jnp.float32).T
    center = residual - jnp.mean(residual, axis=1, keepdims=True)
    variance = jnp.mean(center * center, axis=1, keepdims=True)
    unit = center * lax.rsqrt(variance + LAYER_EPSILON)
    first_norm = (unit * gains[0:1] + shifts[0:1]).astype(jnp.bfloat16)
    second_norm = (unit * gains[1:2] + shifts[1:2]).astype(jnp.bfloat16)

    def bias_row(first, count):
        lines = range(first // LANES, (first + count) // LANES)
        return jnp.concatenate([bias[line : line + 1] for line in lines], axis=1)

    half_rot = ROT // 2
    cosine, sine = turn[:half_rot], turn[half_rot:]
    for first in range(0, 3 * width, 2 * LANES):
        chunk = (
            jnp.dot(first_norm, qkv[:, first : first + 2 * LANES], preferred_element_type=jnp.float32)
            + bias_row(first, 2 * LANES)
        ).T
        for inner in range(0, 2 * LANES, HEAD):
            kind, head = (first + inner) // width, (first + inner) % width // HEAD
            values = chunk[inner : inner + HEAD]
            if kind < 2:
                left, right = values[:half_rot], values[half_rot:ROT]
                values = jnp.concatenate(
                    [left * cosine - right * sine, right * cosine + left * sine, values[ROT:]], axis=0
                )
            turned[head, kind * HEAD : (kind + 1) * HEAD] = values.astype(jnp.bfloat16)
    for step in range(1, group):
        copy_heads(step).start()
    heads[here] = turned[here]

    feed = residual + bias_row(4 * width + ff_width, width) + bias_row(3 * width, width)
    for first in range(0, ff_width, 512):
        inner = (
            jnp.dot(second_norm, up[:, first : first + 512], preferred_element_type=jnp.float32)
            + bias_row(4 * width + first, 512)
        )
        hidden = (0.5 * inner * (1.0 + lax.erf(inner * (0.5**0.5)))).astype(jnp.bfloat16)
        feed = feed + jnp.dot(hidden, down[first : first + 512], preferred_element_type=jnp.float32)
    fed[...] = feed

    for copy in shared:
        copy.wait()

    def widen(part, carry):
        start = pl.multiple_of(part * LANES, LANES)
        span = pl.ds(start, LANES)
        values = dec[span].astype(jnp.float32)
        dec_turned[:, span] = values.T.astype(jnp.bfloat16)
        norms = jnp.sqrt(jnp.sum(values * values, axis=1, keepdims=True) + NORM_EPSILON)
        scale_wide[span] = jnp.broadcast_to(COEFFICIENT * norms, (LANES, LANES))
        shift_wide[span] = jnp.broadcast_to(shift_all[part // dense, pl.ds(part % dense, 1)], (LANES, LANES)).T
        return carry

    lax.fori_loop(0, 2 * dense, widen, 0)
    stores = [
        pltpu.make_async_copy(held, target, store_sem.at[index])
        for index, (held, target) in enumerate(
            (
                (enc, enc_out),
                (dec, dec_out),
                (dec_turned, turned_out),
                (shift_wide, shift_out),
                (scale_wide, scale_out),
            )
        )
    ]
    for store in stores:
        store.start()

    for step in range(1, group):
        copy_features(step).wait_send()
    query_place = lax.broadcasted_iota(jnp.int32, (rows, rows), 0)
    key_place = lax.broadcasted_iota(jnp.int32, (rows, rows), 1)
    causal = key_place <= query_place
    scale = HEAD ** (-0.5)
    values_of = []
    for index in range(group):

        @pl.when(here != index)
        def _():
            arrived = receive.at[1, (here + group - index) % group]
            remote(turned.at[index], heads.at[index], send.at[1, 0], arrived, member(others[1])).wait_recv()

        values_of.append(heads[index, 2 * HEAD :].astype(jnp.float32).T.astype(jnp.bfloat16))
        query = heads[index, :HEAD].astype(jnp.float32).T.astype(jnp.bfloat16)
        own_docs = jnp.broadcast_to(docs_all[index].astype(jnp.float32), (LANES, rows)).T
        own_docs = jnp.concatenate([own_docs] * (rows // LANES), axis=1)
        scores = []
        for other in range(index + 1):
            score = jnp.dot(query, heads[other, HEAD : 2 * HEAD], preferred_element_type=jnp.float32)
            allowed = own_docs == docs_all[other].astype(jnp.float32)
            if other == index:
                allowed = allowed & causal
            scores.append(jnp.where(allowed, score * scale, -1e30))
        peak = scores[0]
        for score in scores[1:]:
            peak = jnp.maximum(peak, score)
        peak = jnp.max(peak, axis=1, keepdims=True)
        weights = [jnp.exp(score - peak) for score in scores]
        total = weights[0]
        for weight in weights[1:]:
            total = total + weight
        inverse = 1.0 / jnp.sum(total, axis=1, keepdims=True)
        mixed = None
        for other in range(index + 1):
            probs = (weights[other] * inverse).astype(jnp.bfloat16)
            term = jnp.dot(probs, values_of[other], preferred_element_type=jnp.float32)
            mixed = term if mixed is None else mixed + term
        mixed = mixed.T
        picked[index] = mixed.astype(jnp.bfloat16)

        @pl.when(here != index)
        def _():
            copy_mixed(index, here).start()

        @pl.when(here == index)
        def _():
            mixed_turned[pl.ds(pl.multiple_of(here * HEAD, HEAD), HEAD)] = picked[index]

    for step in range(1, group):
        copy_mixed(step, others[step]).wait_recv()
    mixed = mixed_turned[...].astype(jnp.float32).T.astype(jnp.bfloat16)
    stream = fed[...] + jnp.dot(mixed, out[...], preferred_element_type=jnp.float32)
    stream_ref[...] = stream
    low_ref[...] = stream.astype(jnp.bfloat16)
    for step in range(1, group):
        copy_heads(step).wait_send()
    for index in range(group):

        @pl.when(here != index)
        def _():
            copy_mixed(index, here).wait_send()

    for store in stores:
        store.wait()


def rotary_table(context_len):
    half_rot = ROT // 2
    frequency = np.power(np.float32(10000.0), np.float32(-2.0) * np.arange(half_rot, dtype=np.float32) / np.float32(ROT))
    angles = frequency.astype(np.float32)[:, None] * np.arange(context_len, dtype=np.float32)[None, :]
    return np.concatenate([np.cos(angles.astype(np.float64)), np.sin(angles.astype(np.float64))]).astype(np.float32)


def front(picked, docs, gains, shifts, qkv, out, up, down, bias, enc, dec, shift):
    group, share, rows = picked.shape
    width = gains.shape[1]
    ff_width = up.shape[1]
    mine = enc.shape[0]
    shift = shift.reshape(mine // LANES, LANES)
    bf16, f32 = jnp.bfloat16, jnp.float32
    dma = pltpu.SemaphoreType.DMA
    return pl.pallas_call(
        front_kernel,
        out_shape=(
            jax.ShapeDtypeStruct((rows, width), bf16),
            jax.ShapeDtypeStruct((rows, width), f32),
            jax.ShapeDtypeStruct((2 * mine, width), bf16),
            jax.ShapeDtypeStruct((2 * mine, width), bf16),
            jax.ShapeDtypeStruct((width, 2 * mine), bf16),
            jax.ShapeDtypeStruct((2 * mine, LANES), f32),
            jax.ShapeDtypeStruct((2 * mine, LANES), f32),
        ),
        in_specs=[ANY] * 13,
        out_specs=(VMEM, VMEM) + (ANY,) * 5,
        scratch_shapes=[
            pltpu.VMEM((group, 1, rows), jnp.int32),
            pltpu.VMEM((2, width), f32),
            pltpu.VMEM((2, width), f32),
            pltpu.VMEM((width, 3 * width), bf16),
            pltpu.VMEM((width, width), bf16),
            pltpu.VMEM((width, ff_width), bf16),
            pltpu.VMEM((ff_width, width), bf16),
            pltpu.VMEM(bias.shape, f32),
            pltpu.VMEM((ROT, rows), f32),
            pltpu.VMEM((group, share, rows), bf16),
            pltpu.VMEM((width, rows), bf16),
            pltpu.VMEM((group, 3 * HEAD, rows), bf16),
            pltpu.VMEM((group, 3 * HEAD, rows), bf16),
            pltpu.VMEM((width, rows), bf16),
            pltpu.VMEM((rows, width), f32),
            pltpu.VMEM((mine, width), f32),
            pltpu.VMEM((mine, width), f32),
            pltpu.VMEM((2, mine // LANES, LANES), f32),
            pltpu.VMEM((2 * mine, width), bf16),
            pltpu.VMEM((2 * mine, width), bf16),
            pltpu.VMEM((width, 2 * mine), bf16),
            pltpu.VMEM((2 * mine, LANES), f32),
            pltpu.VMEM((2 * mine, LANES), f32),
            dma((13,)),
            dma((5,)),
            dma((3, group)),
            dma((3, group)),
            dma((3,)),
            dma((3,)),
        ],
        compiler_params=pltpu.CompilerParams(
            collective_id=2, has_side_effects=True, vmem_limit_bytes=60 * 2**20
        ),
        cost_estimate=pl.CostEstimate(flops=2 * 10**9, bytes_accessed=14 * 10**6, transcendentals=2 * 10**6),
        name="front_part",
    )(picked, docs, gains, shifts, qkv, out, up, down, bias, jnp.asarray(rotary_table(group * rows)), enc, dec, shift)


def forward_kernel(
    depth,
    own_ref,
    enc_ref,
    dec_ref,
    bias_ref,
    stream_ref,
    scale_ref,
    dec_bias_ref,
    gathered_ref,
    relu_ref,
    upstream_ref,
    small_ref,
    total_ref,
    recon_ref,
    stream,
    scale,
    held,
    enc,
    dec,
    bias,
    staged,
    parts,
    send_zero,
    send_one,
    send_two,
    send_three,
    got_zero,
    got_one,
    got_two,
    got_three,
    load_sem,
    relu_sem,
    held_sem,
    send,
    receive,
    sum_send,
    sum_receive,
):
    rows = own_ref.shape[0]
    entries = enc.shape[0]
    width = held.shape[1]
    half = width // 2
    piece = min(entries, 256)
    where = peers(depth)
    (layer, row, place), across, beside, _ = where
    inner = (layer >= 1) & (layer < depth - 1)
    others = [((layer + step) % depth, row, place) for step in range(1, depth)]
    loads = [
        pltpu.make_async_copy(own_ref, held.at[pl.ds(0, rows)], load_sem.at[0]),
        pltpu.make_async_copy(enc_ref, enc, load_sem.at[1]),
        pltpu.make_async_copy(bias_ref, bias, load_sem.at[2]),
        pltpu.make_async_copy(dec_ref, dec, load_sem.at[3]),
        pltpu.make_async_copy(stream_ref, stream, load_sem.at[4]),
        pltpu.make_async_copy(scale_ref, scale, load_sem.at[5]),
    ]
    for load in loads:
        load.start()
    greet(others + [across, beside])
    loads[0].wait()
    gather = Gather(depth, rows, held, send, receive, where)
    gather.open()
    total_ref[...] = jnp.zeros_like(total_ref)
    for load in loads[1:]:
        load.wait()

    def part_slot(turn):
        return jnp.where(turn == 0, 4, turn % 4)

    def copy_zero(turn):
        layer_there = layer_at(depth, layer, turn)
        index = jnp.where(
            jnp.abs(layer_there - layer) == 1,
            jnp.where(layer > layer_there, 0, 1),
            jnp.where(layer == 0, 2, 3),
        )
        return remote(
            send_zero.at[turn - 1],
            got_zero.at[index],
            sum_send.at[5, turn],
            sum_receive.at[5, index],
            (layer_there, row, place),
        )

    def one_slot(turn):
        return jnp.where(turn == 0, 2, turn % 2)

    def copy_one(turn, part):
        source = send_one.at[one_slot(turn), pl.ds(part * half, half)]
        device = beside if part else across
        return remote(source, got_one.at[part, turn], sum_send.at[part, turn], sum_receive.at[part, turn], device)

    def two_slot(turn):
        return jnp.where(turn == 0, 3, turn % 3)

    def copy_two(turn, part, side):
        device = beside if part else across
        span = pl.ds(side * half, half)
        return remote(
            send_two.at[part, two_slot(turn), span],
            got_two.at[part, turn, span],
            sum_send.at[6 + 2 * part + side, turn],
            sum_receive.at[6 + 2 * part + side, turn],
            device,
        )

    def each_two(turn, act):
        for part in range(2):
            for side in range(2):
                act(copy_two(turn, part, side))

    def copy_three(turn):
        layer_there = layer_at(depth, layer, turn)
        index = place_of(depth, layer_there, layer)
        return remote(
            send_three.at[turn],
            got_three.at[index],
            sum_send.at[4, turn],
            sum_receive.at[4, index],
            (layer_there, row, place),
        )

    def copy_relu(order):
        first = slot_of(depth, order // 4, order % 4) * rows
        return pltpu.make_async_copy(
            staged.at[order % 2],
            relu_ref.at[:, pl.ds(pl.multiple_of(first, rows), rows)],
            relu_sem.at[order % 2],
        )

    def copy_held(step):
        span = pl.ds(pl.multiple_of(step * 4 * rows, 4 * rows), 4 * rows)
        return pltpu.make_async_copy(held.at[span], gathered_ref.at[span], held_sem.at[step])

    def sum_one(turn, value):
        @pl.when(turn >= 5)
        def _():
            copy_one(turn - 2, 0).wait_send()
            copy_one(turn - 2, 1).wait_send()

        send_one[one_slot(turn)] = value.astype(jnp.bfloat16)
        copy_one(turn, 0).start()
        copy_one(turn, 1).start()

    def send_half(turn, part, side, extra=None):
        span = pl.ds(side * half, half)
        value = parts[1 + part, part_slot(turn), span]
        if extra is not None:
            value = value + extra.astype(jnp.float32)
        send_two[part, two_slot(turn), span] = value.astype(jnp.bfloat16)
        copy_two(turn, part, side).start()

    def sum_two_own(turn):
        @pl.when(turn >= 4)
        def _():
            each_two(turn - 3, lambda copy: copy.wait_send())

        send_half(turn, 1, 1)
        send_half(turn, 0, 0)

    def sum_two(turn):
        @pl.when(crosswise(turn))
        def _():
            copy_one(turn, 0).wait_recv()
            send_half(turn, 1, 0, got_one[0, turn])
            copy_one(turn, 1).wait_recv()
            send_half(turn, 0, 1, got_one[1, turn])

        @pl.when((turn == 1) | (turn == 2))
        def _():
            send_half(turn, 1, 0)
            send_half(turn, 0, 1)

    def column_sum(turn):
        each_two(turn, lambda copy: copy.wait_recv())
        return parts[0, part_slot(turn)] + got_two[0, turn].astype(jnp.float32) + got_two[1, turn].astype(jnp.float32)

    def sum_three(turn):
        send_three[turn] = column_sum(turn).astype(jnp.bfloat16)
        copy_three(turn).start()

    def one_block(order, carry):
        turn, column = order // 4, order % 4

        @pl.when(column == 1)
        def _():
            gather.hand_on(turn)

        @pl.when(column == 3)
        def _():
            gather.wait_diagonal(turn)

        @pl.when(order >= 2)
        def _():
            copy_relu(order - 2).wait()

        first_row = slot_of(depth, turn, column) * rows
        block = held[pl.ds(pl.multiple_of(first_row, rows), rows)]
        low = []
        for first in range(0, entries, piece):
            span = pl.ds(first, piece)
            shift = bias[span]
            pre = lax.dot_general(enc[span], block, LAST_LAST, preferred_element_type=jnp.float32)
            positive = jnp.maximum(pre + jnp.concatenate([shift] * (rows // LANES), axis=1), 0.0)
            staged[order % 2, span] = positive
            active = positive * positive
            folded = active[:, :LANES]
            for lane in range(LANES, rows, LANES):
                folded = folded + active[:, lane : lane + LANES]
            total_ref[span] += folded
            low.append(active.astype(jnp.bfloat16))
        recon = jnp.dot(dec[...], jnp.concatenate(low, axis=0), preferred_element_type=jnp.float32)
        copy_relu(order).start()

        @pl.when((column < 3) | (turn == 0))
        def _():
            parts[column, part_slot(turn)] = recon

        @pl.when((column == 3) & (turn >= 3))
        def _():
            sum_one(turn, recon)

        @pl.when((column == 3) & ((turn == 1) | (turn == 2)))
        def _():
            send_zero[turn - 1] = recon.astype(jnp.bfloat16)
            copy_zero(turn).start()

        @pl.when(order == 0)
        def _():
            gather.arrive(1)

        @pl.when((order == 0) & inner)
        def _():
            gather.arrive(2)

        @pl.when((order == 2) & inner)
        def _():
            gather.arrive(3)

        @pl.when((column == 0) & (turn >= 1) & (turn + 1 < depth) & (jnp.logical_not(inner) | (turn >= 3)))
        def _():
            gather.arrive(turn + 1)

        @pl.when((column == 0) & (turn + 1 < depth))
        def _():
            gather.to_neighbours(turn + 1)

        @pl.when((column == 1) & (turn >= 3))
        def _():
            sum_two_own(turn - 2)
            sum_two(turn - 2)

        @pl.when((column == 2) & (turn == depth - 1))
        def _():
            sum_two_own(depth - 2)
            sum_two(depth - 2)

        @pl.when((column == 3) & (turn >= 4))
        def _():
            sum_three(turn - 3)

        return carry

    lax.fori_loop(0, 4 * depth, one_block, 0)
    for step in range(depth):
        copy_held(step).start()
    sum_two_own(depth - 1)
    sum_three(depth - 3)
    sum_two(depth - 1)
    sum_three(depth - 2)
    for index, (_, there) in enumerate(takers(depth, layer)):

        @pl.when(there)
        def _(index=index):
            remote(
                send_zero.at[0], got_zero.at[index], sum_send.at[5, 0], sum_receive.at[5, index], across
            ).wait_recv()
            parts[3, 4] += got_zero[index].astype(jnp.float32)

    sum_one(0, parts[3, 4])
    sum_two_own(0)
    sum_three(depth - 1)
    sum_two(0)
    recon_ref[...] = column_sum(0)
    for turn in range(1, depth):
        remote(
            send_three.at[turn], got_three.at[turn], sum_send.at[4, turn], sum_receive.at[4, turn], across
        ).wait_recv()
        recon_ref[...] += got_three[turn].astype(jnp.float32)
    error = recon_ref[...].T + dec_bias_ref[...] - stream[...]
    upstream = (2.0 * error).astype(jnp.bfloat16)
    upstream_ref[...] = upstream
    loss = fold(error * error)
    weighted = total_ref[...] * scale[...]
    loss = loss + fold(weighted)
    small_ref[...] = jnp.zeros_like(small_ref)
    column_sums = jnp.sum(upstream.astype(jnp.float32), axis=0, keepdims=True)
    lines = width // LANES
    for line in range(lines):
        small_ref[line : line + 1] = column_sums[:, line * LANES : (line + 1) * LANES]
    small_ref[lines : lines + 1] = jnp.sum(loss, axis=0, keepdims=True)
    gather.close()
    for turn in [0] + list(range(max(depth - 2, 3), depth)):
        for part in range(2):
            copy_one(turn, part).wait_send()
    for turn in [0] + list(range(max(depth - 3, 1), depth)):
        each_two(turn, lambda copy: copy.wait_send())
    for turn in range(1, depth):
        copy_three(turn).wait_send()
    for turn in (1, 2):
        copy_zero(turn).wait_send()
    copy_relu(4 * depth - 2).wait()
    copy_relu(4 * depth - 1).wait()
    for step in range(depth):
        copy_held(step).wait()


def forward(depth, own, enc, dec_turned, bias, stream, scale, dec_bias):
    rows, width = own.shape
    entries = enc.shape[0]
    bf16, f32 = jnp.bfloat16, jnp.float32
    dma = pltpu.SemaphoreType.DMA
    return pl.pallas_call(
        functools.partial(forward_kernel, depth),
        out_shape=(
            jax.ShapeDtypeStruct((depth * 4 * rows, width), bf16),
            jax.ShapeDtypeStruct((entries, depth * 4 * rows), f32),
            jax.ShapeDtypeStruct((rows, width), bf16),
            jax.ShapeDtypeStruct((8, LANES), f32),
            jax.ShapeDtypeStruct((entries, LANES), f32),
        ),
        in_specs=[ANY] * 6 + [VMEM],
        out_specs=(ANY, ANY, VMEM, VMEM, VMEM),
        scratch_shapes=[
            pltpu.VMEM((width, rows), f32),
            pltpu.VMEM((rows, width), f32),
            pltpu.VMEM((entries, LANES), f32),
            pltpu.VMEM((depth * 4 * rows, width), bf16),
            pltpu.VMEM((entries, width), bf16),
            pltpu.VMEM((width, entries), bf16),
            pltpu.VMEM((entries, LANES), f32),
            pltpu.VMEM((2, entries, rows), f32),
            pltpu.VMEM((4, 5, width, rows), f32),
            pltpu.VMEM((2, width, rows), bf16),
            pltpu.VMEM((3, width, rows), bf16),
            pltpu.VMEM((2, 4, width, rows), bf16),
            pltpu.VMEM((depth, width, rows), bf16),
            pltpu.VMEM((4, width, rows), bf16),
            pltpu.VMEM((2, depth, width // 2, rows), bf16),
            pltpu.VMEM((2, depth, width, rows), bf16),
            pltpu.VMEM((depth, width, rows), bf16),
            dma((6,)),
            dma((2,)),
            dma((depth,)),
            dma((11, max(depth, 4))),
            dma((9, max(depth, 4))),
            dma((10, max(depth, 4))),
            dma((10, max(depth, 4))),
        ],
        compiler_params=pltpu.CompilerParams(
            collective_id=0, has_side_effects=True, vmem_limit_bytes=60 * 2**20
        ),
        cost_estimate=pl.CostEstimate(
            flops=16 * depth * rows * entries * width, bytes_accessed=16 * depth * rows * entries, transcendentals=0
        ),
        name="forward_blocks",
    )(own, enc, dec_turned, bias, stream, scale, dec_bias)


def backward_kernel(
    depth,
    everyone,
    own_ref,
    gathered_ref,
    relu_ref,
    dec_ref,
    scale_ref,
    active_ref,
    small_ref,
    enc_out,
    dec_out,
    bias_out,
    small_out,
    squares_out,
    held,
    inputs,
    dec,
    scale,
    tile,
    held_last,
    inputs_last,
    relu_last,
    enc_sum,
    dec_sum,
    bias_sum,
    enc_got,
    dec_got,
    bias_got,
    active,
    active_got,
    low,
    small,
    two,
    two_got,
    sums,
    sums_got,
    load_sem,
    tile_sem,
    store_sem,
    send,
    receive,
    pair_send,
    pair_receive,
    last_send,
    last_receive,
    all_send,
    all_receive,
):
    rows = own_ref.shape[0]
    entries = dec.shape[0]
    mine = entries // 2
    piece = tile.shape[1]
    tiles = entries // piece
    where = peers(depth)
    (layer, row, column), _, _, partner = where
    core = column % 2
    inner = (layer >= 1) & (layer < depth - 1)
    loads = [
        pltpu.make_async_copy(own_ref, held.at[pl.ds(0, rows)], load_sem.at[0]),
        pltpu.make_async_copy(dec_ref, dec, load_sem.at[1]),
        pltpu.make_async_copy(scale_ref, scale, load_sem.at[2]),
        pltpu.make_async_copy(gathered_ref, inputs, load_sem.at[3]),
        pltpu.make_async_copy(active_ref, active, load_sem.at[4]),
        pltpu.make_async_copy(small_ref, small, load_sem.at[5]),
    ]
    for load in loads:
        load.start()

    def place(turn):
        return (turn + (1 - core) * (tiles // 2)) % tiles

    def group_of(group):
        if group == depth - 1:
            return (4 * group + 1) * rows, 3 * rows
        if group == depth:
            return (4 * group - 4) * rows, rows
        return 4 * group * rows, 4 * rows

    def copy_tile(group, start, size, turn):
        slot = (group * tiles + turn) % 2
        first = pl.multiple_of(place(turn) * piece, piece)
        return pltpu.make_async_copy(
            relu_ref.at[pl.ds(first, piece), pl.ds(pl.multiple_of(start, rows), size)],
            tile.at[slot, :, pl.ds(0, size)],
            tile_sem.at[slot],
        )

    copy_tile(0, *group_of(0), 0).start()

    others = [
        ((layer + dz) % depth, (row + dy) % 2, (column + 2 * dx) % 4)
        for dz in range(depth)
        for dy in range(2)
        for dx in range(2)
    ]
    greet(others[1:] + [partner])
    loads[0].wait()
    gather = Gather(depth, rows, held, send, receive, where)
    gather.open()
    for load in loads[1:]:
        load.wait()

    def sums_copy(index):
        return remote(
            sums, sums_got.at[index], all_send.at[index], all_receive.at[index], others[index]
        )

    def two_copy(kind):
        return remote(
            two.at[kind], two_got.at[kind], last_send.at[3 + kind], last_receive.at[3 + kind], partner
        )

    two[0] = small[...]
    two_copy(0).start()

    theirs = (1 - core) * mine
    active_copy = remote(
        active.at[pl.ds(pl.multiple_of(theirs, mine), mine)], active_got, pair_send.at[3, 0], pair_receive.at[3, 0], partner
    )
    active_copy.start()
    last = pl.ds(4 * (depth - 1) * rows, rows)
    last_copies = [
        remote(
            relu_ref.at[pl.ds(pl.multiple_of(theirs, mine), mine), last],
            relu_last,
            last_send.at[0],
            last_receive.at[0],
            partner,
        ),
        remote(inputs.at[last], inputs_last, last_send.at[1], last_receive.at[1], partner),
        remote(held.at[last], held_last, last_send.at[2], last_receive.at[2], partner),
    ]
    last_copies[0].start()
    last_copies[1].start()
    enc_sum[...] = jnp.zeros_like(enc_sum)
    dec_sum[...] = jnp.zeros_like(dec_sum)
    bias_sum[...] = jnp.zeros_like(bias_sum)

    def pair_copy(kind, turn):
        source, target = ((low.at[0], enc_got), (low.at[1], dec_got), (bias_sum, bias_got))[kind]
        there = pl.ds(pl.multiple_of(turn * piece, piece), piece)
        return remote(
            source.at[pl.ds(pl.multiple_of(theirs + turn * piece, piece), piece) if kind == 2 else there],
            target.at[there],
            pair_send.at[kind, turn],
            pair_receive.at[kind, turn],
            partner,
        )

    gather.arrive(1)

    @pl.when(inner)
    def _():
        gather.arrive(2)

    gather.to_neighbours(1)
    gather.hand_on(0)

    def one_tile(group, start, size, turn):
        slot = (group * tiles + turn) % 2
        copy_tile(group, start, size, turn).wait()
        span = pl.ds(pl.multiple_of(place(turn) * piece, piece), piece)
        tokens = pl.ds(pl.multiple_of(start, rows), size)
        upstream, given, positive = held[tokens], inputs[tokens], tile[slot, :, :size]
        if group is depth:
            there = pl.ds(pl.multiple_of((turn - tiles // 2) * piece, piece), piece)
            upstream = jnp.concatenate([upstream, held_last[...]], axis=0)
            given = jnp.concatenate([given, inputs_last[...]], axis=0)
            positive = jnp.concatenate([positive, relu_last[there]], axis=1)
            size = 2 * size
        back = lax.dot_general(dec[span], upstream, LAST_LAST, preferred_element_type=jnp.float32)
        shift = jnp.concatenate([scale[span]] * (size // LANES), axis=1)
        slope = ((back + shift) * (2.0 * positive)).astype(jnp.bfloat16)
        act_low = (positive * positive).astype(jnp.bfloat16)
        wide = slope.astype(jnp.float32)
        folded = wide[:, :LANES]
        for lane in range(LANES, size, LANES):
            folded = folded + wide[:, lane : lane + LANES]
        bias_sum[span] += folded
        enc_sum[span] += jnp.dot(slope, given, preferred_element_type=jnp.float32)
        dec_sum[span] += jnp.dot(act_low, upstream, preferred_element_type=jnp.float32)

    def take_in(group, turn):
        @pl.when((group == 0) & (turn == tiles // 2))
        def _():
            if depth > 3:

                @pl.when(inner)
                def _():
                    gather.arrive(3)

            @pl.when(jnp.logical_not(inner))
            def _():
                gather.arrive(2)

            gather.to_neighbours(2)

        @pl.when((group >= 1) & (turn == 0) & (group + 2 < depth))
        def _():
            @pl.when(jnp.logical_not(inner) | (group >= 2))
            def _():
                gather.arrive(group + 2)

            gather.to_neighbours(group + 2)

        @pl.when((group == depth - 2) & (turn == 0))
        def _():
            gather.hand_on(depth - 1)

        @pl.when(turn == tiles // 2)
        def _():
            gather.wait_diagonal(group)

    def middle_group(group, carry):
        start, size = 4 * group * rows, 4 * rows

        @pl.when(group >= 1)
        def _():
            gather.hand_on(group)

        def one(turn, carry):
            @pl.when(turn + 1 < tiles)
            def _():
                copy_tile(group, start, size, turn + 1).start()

            @pl.when((turn + 1 == tiles) & (group + 2 < depth))
            def _():
                copy_tile(group + 1, start + 4 * rows, size, 0).start()

            @pl.when((turn + 1 == tiles) & (group + 2 == depth))
            def _():
                copy_tile(depth - 1, *group_of(depth - 1), 0).start()

            one_tile(group, start, size, turn)
            take_in(group, turn)
            return carry

        return lax.fori_loop(0, tiles, one, carry)

    def late_group(turn, carry):
        start, size = group_of(depth - 1)

        @pl.when(turn + 1 < tiles)
        def _():
            copy_tile(depth - 1, start, size, turn + 1).start()

        @pl.when(turn + 1 == tiles)
        def _():
            copy_tile(depth, *group_of(depth), tiles // 2).start()

        one_tile(depth - 1, start, size, turn)

        @pl.when(turn < tiles // 2)
        def _():
            span = pl.ds(pl.multiple_of(place(turn) * piece, piece), piece)
            there = pl.ds(pl.multiple_of(turn * piece, piece), piece)
            low[0, there] = enc_sum[span].astype(jnp.bfloat16)
            low[1, there] = dec_sum[span].astype(jnp.bfloat16)
            for kind in range(3):
                pair_copy(kind, turn).start()

        return carry

    def last_group(turn, carry):
        start, size = group_of(depth)

        @pl.when(turn + 1 < tiles)
        def _():
            copy_tile(depth, start, size, turn + 1).start()

        one_tile(depth, start, size, turn)
        return carry

    lax.fori_loop(0, depth - 1, middle_group, 0)
    gather.wait_diagonal(depth - 1)
    last_copies[2].start()
    lax.fori_loop(0, tiles, late_group, 0)
    for copy in last_copies:
        copy.wait_recv()
    lax.fori_loop(tiles // 2, tiles, last_group, 0)

    ours = core * mine
    active_copy.wait_recv()
    span = pl.ds(pl.multiple_of(ours, mine), mine)
    act_total = jnp.sum(active[span] + active_got[...], axis=1, keepdims=True)
    partial = jnp.zeros((8, LANES), jnp.float32)

    stores = []
    rows_of = lax.broadcasted_iota(jnp.int32, (LANES, LANES), 0)
    lanes_of = lax.broadcasted_iota(jnp.int32, (LANES, LANES), 1)
    for turn in range(tiles // 2):
        for kind in range(3):
            pair_copy(kind, turn).wait_recv()
        near = pl.ds(pl.multiple_of(ours + turn * piece, piece), piece)
        there = pl.ds(turn * piece, piece)
        enc_grad = enc_sum[near] + enc_got[there].astype(jnp.float32)
        enc_sum[near] = enc_grad
        partial = partial + fold(enc_grad * enc_grad)
        dec_grad = dec_sum[near] + dec_got[there].astype(jnp.float32)
        dec_grad = dec_grad + (
            COEFFICIENT * COEFFICIENT * act_total[turn * piece : (turn + 1) * piece] / scale[near, :1]
        ) * dec[near].astype(jnp.float32)
        dec_sum[near] = dec_grad
        partial = partial + fold(dec_grad * dec_grad)
        stores += [
            pltpu.make_async_copy(enc_sum.at[near], enc_out.at[there], store_sem.at[0, turn]),
            pltpu.make_async_copy(dec_sum.at[near], dec_out.at[there], store_sem.at[1, turn]),
        ]
        stores[-2].start()
        stores[-1].start()
        bias_grad = jnp.sum(bias_sum[near] + bias_got[there], axis=1, keepdims=True)
        for first in range(0, piece, LANES):
            wide = jnp.broadcast_to(bias_grad[first : first + LANES], (LANES, LANES))
            line = jnp.sum(jnp.where(rows_of == lanes_of, wide, 0.0), axis=0, keepdims=True)
            index = (turn * piece + first) // LANES
            bias_out[index : index + 1] = line
            partial = partial + jnp.where(rows_of[:8] == 0, line * line, 0.0)
    two[1] = partial
    two_copy(1).start()
    for kind in range(2):
        two_copy(kind).wait_recv()
        sums[kind] = two[kind] + two_got[kind]
    for index in range(1, everyone):
        sums_copy(index).start()
    total = sums[...]
    for index in range(1, everyone):
        sums_copy(index).wait_recv()
        total = total + sums_got[index]
    small_out[...] = total[0]
    squares_out[...] = total[1]
    gather.close()
    for index in range(1, everyone):
        sums_copy(index).wait_send()
    for kind in range(2):
        two_copy(kind).wait_send()
    active_copy.wait_send()
    for copy in last_copies:
        copy.wait_send()
    for turn in range(tiles // 2):
        for kind in range(3):
            pair_copy(kind, turn).wait_send()
    for store in stores:
        store.wait()


def backward(depth, own, gathered, relu, dec, scale, active, small):
    rows, width = own.shape
    entries = dec.shape[0]
    mine = entries // 2
    piece = min(512, mine)
    everyone = depth * 4
    bf16, f32 = jnp.bfloat16, jnp.float32
    dma = pltpu.SemaphoreType.DMA
    return pl.pallas_call(
        functools.partial(backward_kernel, depth, everyone),
        out_shape=(
            jax.ShapeDtypeStruct((mine, width), f32),
            jax.ShapeDtypeStruct((mine, width), f32),
            jax.ShapeDtypeStruct((mine // LANES, LANES), f32),
            jax.ShapeDtypeStruct(small.shape, f32),
            jax.ShapeDtypeStruct((8, LANES), f32),
        ),
        in_specs=[ANY] * 7,
        out_specs=(ANY, ANY, VMEM, VMEM, VMEM),
        scratch_shapes=[
            pltpu.VMEM((depth * 4 * rows, width), bf16),
            pltpu.VMEM((depth * 4 * rows, width), bf16),
            pltpu.VMEM((entries, width), bf16),
            pltpu.VMEM((entries, LANES), f32),
            pltpu.VMEM((2, piece, 4 * rows), f32),
            pltpu.VMEM((rows, width), bf16),
            pltpu.VMEM((rows, width), bf16),
            pltpu.VMEM((mine, rows), f32),
            pltpu.VMEM((entries, width), f32),
            pltpu.VMEM((entries, width), f32),
            pltpu.VMEM((entries, LANES), f32),
            pltpu.VMEM((mine, width), bf16),
            pltpu.VMEM((mine, width), bf16),
            pltpu.VMEM((mine, LANES), f32),
            pltpu.VMEM((entries, LANES), f32),
            pltpu.VMEM((mine, LANES), f32),
            pltpu.VMEM((2, mine, width), bf16),
            pltpu.VMEM(small.shape, f32),
            pltpu.VMEM((2, 8, LANES), f32),
            pltpu.VMEM((2, 8, LANES), f32),
            pltpu.VMEM((2, 8, LANES), f32),
            pltpu.VMEM((everyone, 2, 8, LANES), f32),
            dma((6,)),
            dma((2,)),
            dma((2, entries // piece)),
            dma((11, max(depth, 4))),
            dma((9, max(depth, 4))),
            dma((4, entries // piece)),
            dma((4, entries // piece)),
            dma((5,)),
            dma((5,)),
            dma((everyone,)),
            dma((everyone,)),
        ],
        compiler_params=pltpu.CompilerParams(
            collective_id=1, has_side_effects=True, vmem_limit_bytes=60 * 2**20
        ),
        cost_estimate=pl.CostEstimate(
            flops=24 * depth * rows * entries * width, bytes_accessed=16 * depth * rows * entries, transcendentals=0
        ),
        name="backward_blocks",
    )(own, gathered, relu, dec, scale, active, small)


def update_kernel(*refs):
    names = ["enc_grad", "dec_grad", "bias_grad", "small", "squares"]
    for kind in ("enc", "dec", "bias", "shift"):
        names += [kind, kind + "_one", kind + "_two"]
    given = dict(zip(names, refs[: len(names)]))
    made = refs[len(names) : len(names) + 14]
    brought, staged, load_sem, store_sem = refs[len(names) + 14 :]
    mine = given["enc"].shape[0]
    slots, _, piece, _ = staged.shape
    parts = mine // piece
    large = ["enc", "enc_one", "enc_two", "enc_grad", "dec", "dec_one", "dec_two", "dec_grad"]

    def load(part, index):
        span = pl.ds(pl.multiple_of(part * piece, piece), piece)
        slot = part % slots
        return pltpu.make_async_copy(given[large[index]].at[span], brought.at[slot, index], load_sem.at[slot, index])

    for part in range(min(slots - 1, parts)):
        for index in range(8):
            load(part, index).start()
    lines = given["shift"].shape[1] // LANES
    shift_grad = jnp.concatenate([given["small"][line : line + 1] for line in range(lines)], axis=1)
    total = jnp.sum(given["squares"][...], keepdims=True) + jnp.sum(shift_grad * shift_grad, keepdims=True)
    norm = jnp.sqrt(total)
    clip = jnp.minimum(1.0, CLIP_NORM / (norm + 1e-06))
    made[12][...] = norm
    made[13][...] = jnp.sum(given["small"][lines : lines + 1], keepdims=True)

    def store(part, index):
        span = pl.ds(pl.multiple_of(part * piece, piece), piece)
        slot = part % slots
        return pltpu.make_async_copy(staged.at[slot, index], made[index].at[span], store_sem.at[slot, index])

    def one(part, carry):
        @pl.when(part >= slots)
        def _():
            for index in range(6):
                store(part - slots, index).wait()

        @pl.when(part + slots - 1 < parts)
        def _():
            for index in range(8):
                load(part + slots - 1, index).start()

        slot = part % slots
        for index in range(8):
            load(part, index).wait()
        for index in range(2):
            new, first, second = adam_step(
                *(brought[slot, 4 * index + offset] for offset in range(4)),
                clip,
                RATE_MATRIX,
                WEIGHT_DECAY,
            )
            if index:
                new = new * lax.rsqrt(jnp.sum(new * new, axis=1, keepdims=True) + NORM_EPSILON)
            for offset, value in enumerate((new, first, second)):
                staged[slot, 3 * index + offset] = value
        for index in range(6):
            store(part, index).start()
        return carry

    lax.fori_loop(0, parts, one, 0)
    for offset, (kind, gradient) in enumerate((("bias", given["bias_grad"][...]), ("shift", shift_grad))):
        results = adam_step(
            given[kind][...], given[kind + "_one"][...], given[kind + "_two"][...], gradient, clip, RATE_BIAS, 0.0
        )
        for index, value in enumerate(results):
            made[6 + 3 * offset + index][...] = value
    for part in range(max(parts - slots, 0), parts):
        for index in range(6):
            store(part, index).wait()


def update(*arrays):
    f32 = jnp.float32
    mine, width = arrays[0].shape
    dense, flat = (mine // LANES, LANES), (1, width)
    arrays = list(arrays)
    for index in range(11, 14):
        arrays[index] = arrays[index].reshape(dense)
    for index in range(14, 17):
        arrays[index] = arrays[index].reshape(flat)
    piece, slots = min(128, mine), 4
    made = pl.pallas_call(
        update_kernel,
        out_shape=[jax.ShapeDtypeStruct((mine, width), f32)] * 6
        + [jax.ShapeDtypeStruct(dense, f32)] * 3
        + [jax.ShapeDtypeStruct(flat, f32)] * 3
        + [jax.ShapeDtypeStruct((1, 1), f32)] * 2,
        in_specs=[ANY] * 2 + [VMEM] * 3 + [ANY] * 6 + [VMEM] * 6,
        out_specs=[ANY] * 6 + [VMEM] * 8,
        scratch_shapes=[
            pltpu.VMEM((slots, 8, piece, width), f32),
            pltpu.VMEM((slots, 6, piece, width), f32),
            pltpu.SemaphoreType.DMA((slots, 8)),
            pltpu.SemaphoreType.DMA((slots, 6)),
        ],
        compiler_params=pltpu.CompilerParams(vmem_limit_bytes=60 * 2**20),
        cost_estimate=pl.CostEstimate(flops=60 * mine * width, bytes_accessed=56 * mine * width, transcendentals=4 * mine * width),
        name="update",
    )(*arrays)
    return (
        *made[:6],
        *(value.reshape(mine) for value in made[6:9]),
        *(value.reshape(width) for value in made[9:12]),
        made[12].reshape(()),
        made[13].reshape(()),
    )


def body(
    depth,
    token_ids,
    doc_ids,
    embed,
    norm_gains,
    norm_shifts,
    qkv_weight,
    out_weight,
    up_weight,
    down_weight,
    proj_biases,
    enc_weight,
    dec_weight,
    enc_bias,
    dec_bias,
    enc_first,
    enc_second,
    dec_first,
    dec_second,
    enc_bias_first,
    enc_bias_second,
    dec_bias_first,
    dec_bias_second,
):
    model_width = norm_gains.shape[1]
    all_ids, all_docs = gather_ids(token_ids, doc_ids, model_width // embed.shape[1])
    low, stream, enc_both, dec_both, dec_turned, shift_wide, scale_wide = front(
        pick(all_ids, embed.T),
        all_docs,
        norm_gains,
        norm_shifts,
        qkv_weight,
        out_weight,
        up_weight,
        down_weight,
        proj_biases.reshape(-1, LANES),
        enc_weight,
        dec_weight,
        enc_bias,
    )
    gathered, relu, upstream, small, active = forward(
        depth, low, enc_both, dec_turned, shift_wide, stream, scale_wide, dec_bias[None]
    )
    enc_grad, dec_grad, enc_bias_grad, small_sum, squares = backward(
        depth, upstream, gathered, relu, dec_both, scale_wide, active, small
    )
    return update(
        enc_grad,
        dec_grad,
        enc_bias_grad,
        small_sum,
        squares,
        enc_weight,
        enc_first,
        enc_second,
        dec_weight,
        dec_first,
        dec_second,
        enc_bias,
        enc_bias_first,
        enc_bias_second,
        dec_bias,
        dec_bias_first,
        dec_bias_second,
    )


def solution(mesh):
    split = P(("dp", "seq", "opt"), None)
    split_vector = P(("dp", "seq", "opt"))
    in_specs = (
        P("dp", ("seq", "opt")),
        P("dp", ("seq", "opt")),
        P(None, ("seq", "opt")),
        P(),
        P(),
        P(),
        P(),
        P(),
        P(),
        P(),
        split,
        split,
        split_vector,
        P(),
        split,
        split,
        split,
        split,
        split_vector,
        split_vector,
        P(),
        P(),
    )
    out_specs = (split,) * 6 + (split_vector,) * 3 + (P(),) * 5
    return jax.shard_map(
        functools.partial(body, mesh.shape["dp"]),
        mesh=mesh,
        in_specs=in_specs,
        out_specs=out_specs,
        check_vma=False,
    )
```

```python
import functools

import jax
import jax.numpy as jnp
import numpy as np
from jax import lax
from jax.experimental import pallas as pl
from jax.experimental.pallas import tpu as pltpu
from jax.sharding import PartitionSpec as P

HEAD = 64
ROT = 16
STEP = 4
RAMP = 80


LAYER_EPSILON = 1e-05
NORM_EPSILON = 1e-08
BETA_FIRST = 0.9
BETA_SECOND = 0.999
ADAM_EPSILON = 1e-08
RATE_MATRIX = 0.02
RATE_BIAS = 0.1
WEIGHT_DECAY = 0.01
CLIP_NORM = 1.0
SPARSITY_TOP = 5.0
COEFFICIENT = SPARSITY_TOP * min(1.0, STEP / RAMP)
LAST_LAST = (((1,), (1,)), ((), ()))
MESH = pl.DeviceIdType.MESH
ANY = pl.BlockSpec(memory_space=pl.ANY)
VMEM = pl.BlockSpec(memory_space=pltpu.VMEM)
LANES = 128


def adam_step(parameter, moment_one, moment_two, gradient, clip_scale, step_rate, decay_rate):
    gradient = gradient * clip_scale
    moment_one = BETA_FIRST * moment_one + (1.0 - BETA_FIRST) * gradient
    moment_two = BETA_SECOND * moment_two + (1.0 - BETA_SECOND) * gradient * gradient
    first_share, second_share = 1.0 / (1.0 - BETA_FIRST**STEP), 1.0 / (1.0 - BETA_SECOND**STEP)
    adjust = moment_one * first_share / (jnp.sqrt(moment_two * second_share) + ADAM_EPSILON)
    return (parameter - step_rate * (adjust + decay_rate * parameter), moment_one, moment_two)


def place_of(depth, layer, other):
    distance = jnp.abs(other - layer)
    margin = jnp.minimum(layer, depth - 1 - layer)
    near = jnp.where(other < layer, 2 * distance - 1, 2 * distance)
    return jnp.where(distance <= margin, near, distance + margin)


def layer_at(depth, layer, turn):
    margin = jnp.minimum(layer, depth - 1 - layer)
    near = jnp.where(turn % 2 == 1, layer - (turn + 1) // 2, layer + turn // 2)
    far = jnp.where(2 * layer < depth - 1, layer + turn - margin, layer - turn + margin)
    return jnp.where(turn <= 2 * margin, near, far)


def crosswise(turn):
    return (turn == 0) | (turn >= 3)


def slot_of(depth, turn, column):
    last = 4 * (depth - 1)
    own = jnp.maximum(4 * turn - 3, 0)
    diagonal = jnp.where(turn == depth - 1, last, jnp.where(turn == depth - 2, last + 1, 4 * turn + 4))
    return jnp.where(column == 0, own, jnp.where(column == 3, diagonal, 4 * turn + 1 + column))


def takers(depth, layer):
    return [
        (layer + 1, layer + 1 < depth),
        (layer - 1, layer >= 1),
        (layer * 0, layer == 2),
        (layer * 0 + depth - 1, layer == depth - 3),
    ]


def peers(depth):
    layer, row, column = lax.axis_index("dp"), lax.axis_index("seq"), lax.axis_index("opt")
    across = (layer, row, (column + 2) % 4)
    beside = (layer, 1 - row, column)
    partner = (layer, row, column + 1 - 2 * (column % 2))
    return (layer, row, column), across, beside, partner


def remote(source, target, send, receive, device):
    return pltpu.make_async_remote_copy(
        src_ref=source,
        dst_ref=target,
        send_sem=send,
        recv_sem=receive,
        device_id=device,
        device_id_type=MESH,
    )


def greet(devices):
    barrier = pltpu.get_barrier_semaphore()
    for device in devices:
        pl.semaphore_signal(barrier, inc=1, device_id=device, device_id_type=MESH)
    pl.semaphore_wait(barrier, len(devices))


def fold(values):
    total = values[:8]
    for first in range(8, values.shape[0], 8):
        total = total + values[first : first + 8]
    narrow = total[:, :LANES]
    for lane in range(LANES, values.shape[1], LANES):
        narrow = narrow + total[:, lane : lane + LANES]
    return narrow


class Gather:
    def __init__(self, depth, rows, held, send, receive, where):
        self.depth, self.rows, self.held = depth, rows, held
        self.send, self.receive = send, receive
        self.here, self.across, self.beside, _ = where

    def block(self, turn, column, part=None):
        first, rows = slot_of(self.depth, turn, column) * self.rows, self.rows
        if part is not None:
            rows = self.rows // 2
            first = first + part * rows
        return self.held.at[pl.ds(pl.multiple_of(first, rows), rows)]

    def device(self, layer):
        return (layer, self.here[1], self.here[2])

    def copy_along(self, turn, sign, part):
        layer = self.here[0] + sign
        source = layer_at(self.depth, self.here[0], turn)
        there = place_of(self.depth, layer, source)
        row, index = (part, turn) if sign == 1 else (part + 8, turn)
        return remote(
            self.block(turn, 0, part),
            self.block(there, 0, part),
            self.send.at[row, index],
            self.receive.at[part, there],
            self.device(layer),
        )

    def along(self, turn, act):
        source, layer = layer_at(self.depth, self.here[0], turn), self.here[0]
        for sign, onward in ((1, source <= layer), (-1, source >= layer)):

            @pl.when(onward & (layer + sign >= 0) & (layer + sign < self.depth))
            def _(sign=sign):
                for part in range(2):
                    act(self.copy_along(turn, sign, part))

    def copy_across(self, turn, part):
        return remote(
            self.block(turn, 0, part),
            self.block(turn, 1, part),
            self.send.at[2 + part, turn],
            self.receive.at[2 + part, turn],
            self.across,
        )

    def copy_beside(self, turn, part):
        return remote(
            self.block(turn, 0, part),
            self.block(turn, 2, part),
            self.send.at[4 + part, turn],
            self.receive.at[4 + part, turn],
            self.beside,
        )

    def pass_across(self, turn):
        return remote(
            self.block(turn, 2, 0), self.block(turn, 3, 0), self.send.at[6, turn], self.receive.at[6, turn], self.across
        )

    def pass_beside(self, turn):
        return remote(
            self.block(turn, 1, 1), self.block(turn, 3, 1), self.send.at[7, turn], self.receive.at[7, turn], self.beside
        )

    def pass_along(self, index, layer):
        turn = place_of(self.depth, layer, self.here[0])
        return remote(
            self.block(0, 3), self.block(turn, 3), self.send.at[10, index], self.receive.at[8, turn], self.device(layer)
        )

    def to_neighbours(self, turn):
        for part in range(2):
            self.copy_across(turn, 1 - part).start()
            self.copy_beside(turn, part).start()

    def open(self):
        self.to_neighbours(0)
        self.along(0, lambda copy: copy.start())

    def arrive(self, turn):
        for part in range(2):
            remote(
                self.block(0, 0, part),
                self.block(turn, 0, part),
                self.send.at[part, 0],
                self.receive.at[part, turn],
                self.across,
            ).wait_recv()
        self.along(turn, lambda copy: copy.start())

    def hand_on(self, turn):
        self.copy_across(turn, 1).wait_recv()

        @pl.when(crosswise(turn))
        def _():
            self.pass_beside(turn).start()

        self.copy_beside(turn, 0).wait_recv()

        @pl.when(crosswise(turn))
        def _():
            self.pass_across(turn).start()

        self.copy_across(turn, 0).wait_recv()
        self.copy_beside(turn, 1).wait_recv()

    def wait_diagonal(self, turn):
        @pl.when(crosswise(turn))
        def _():
            self.pass_across(turn).wait_recv()
            self.pass_beside(turn).wait_recv()

        @pl.when((turn == 1) | (turn == 2))
        def _():
            remote(
                self.block(0, 3), self.block(turn, 3), self.send.at[10, 0], self.receive.at[8, turn], self.across
            ).wait_recv()

        @pl.when(turn == 0)
        def _():
            for index, (layer, there) in enumerate(takers(self.depth, self.here[0])):

                @pl.when(there)
                def _(index=index, layer=layer):
                    self.pass_along(index, layer).start()

    def close(self):
        for index, (layer, there) in enumerate(takers(self.depth, self.here[0])):

            @pl.when(there)
            def _(index=index, layer=layer):
                self.pass_along(index, layer).wait_send()

        def done(turn, carry):
            self.along(turn, lambda copy: copy.wait_send())
            for part in range(2):
                self.copy_across(turn, part).wait_send()
                self.copy_beside(turn, part).wait_send()

            @pl.when(crosswise(turn))
            def _():
                self.pass_across(turn).wait_send()
                self.pass_beside(turn).wait_send()

            return carry

        lax.fori_loop(0, self.depth, done, 0)


def ids_kernel(ids_ref, docs_ref, ids_out, docs_out, ids_all, docs_all, load_sem, send, receive):
    group = ids_all.shape[0]
    layer, row, column = lax.axis_index("dp"), lax.axis_index("seq"), lax.axis_index("opt")
    here = row * 4 + column
    others = [(here + step) % group for step in range(group)]
    devices = [(layer, index // 4, index % 4) for index in others]
    loads = [
        pltpu.make_async_copy(ids_ref, ids_all.at[here], load_sem.at[0]),
        pltpu.make_async_copy(docs_ref, docs_all.at[here], load_sem.at[1]),
    ]
    for load in loads:
        load.start()
    greet(devices[1:])
    for load in loads:
        load.wait()
    copies = []
    for step in range(1, group):
        for kind, held in enumerate((ids_all, docs_all)):
            copies.append(
                remote(held.at[here], held.at[here], send.at[kind, step], receive.at[kind, step], devices[step])
            )
    for copy in copies:
        copy.start()
    for copy in copies:
        copy.wait()
    ids_out[...] = ids_all[...]
    docs_out[...] = docs_all[...]


def gather_ids(ids, docs, group):
    rows = ids.shape[1]
    dma = pltpu.SemaphoreType.DMA
    whole = jax.ShapeDtypeStruct((group, 1, rows), jnp.int32)
    return pl.pallas_call(
        ids_kernel,
        out_shape=(whole, whole),
        in_specs=[ANY] * 2,
        out_specs=(VMEM, VMEM),
        scratch_shapes=[
            pltpu.VMEM((group, 1, rows), jnp.int32),
            pltpu.VMEM((group, 1, rows), jnp.int32),
            dma((2,)),
            dma((2, group)),
            dma((2, group)),
        ],
        compiler_params=pltpu.CompilerParams(collective_id=3, has_side_effects=True, vmem_limit_bytes=60 * 2**20),
        name="gather_ids",
    )(ids, docs)


def pick_kernel(ids_ref, table_ref, picked, table, load_sem):
    group, _, rows = ids_ref.shape
    share, vocabulary = table.shape
    parts = 3 if vocabulary % (3 * LANES) == 0 else 1
    loads = [
        pltpu.make_async_copy(
            table_ref.at[:, pl.ds(part * (vocabulary // parts), vocabulary // parts)],
            table.at[:, pl.ds(part * (vocabulary // parts), vocabulary // parts)],
            load_sem.at[part],
        )
        for part in range(parts)
    ]
    for load in loads:
        load.start()
    lanes = lax.broadcasted_iota(jnp.int32, (share, LANES), 1)
    for load in loads:
        load.wait()

    def some(part, carry):
        source, first = part // (rows // LANES), part % (rows // LANES) * LANES
        found = None
        for place in range(LANES):
            token = ids_ref[source, 0, first + place]
            start = lax.bitwise_and(token, -LANES)
            tile = table[:, pl.ds(pl.multiple_of(start, LANES), LANES)].astype(jnp.float32)
            moved = pltpu.roll(tile, lax.bitwise_and(place - token, LANES - 1), 1)
            found = moved if found is None else jnp.where(lanes >= place, moved, found)
        picked[source, :, pl.ds(pl.multiple_of(first, LANES), LANES)] = found.astype(jnp.bfloat16)
        return carry

    lax.fori_loop(0, group * rows // LANES, some, 0)


def pick(ids, table):
    group, _, rows = ids.shape
    share = table.shape[0]
    return pl.pallas_call(
        pick_kernel,
        out_shape=jax.ShapeDtypeStruct((group, share, rows), jnp.bfloat16),
        in_specs=[pl.BlockSpec(memory_space=pltpu.SMEM), ANY],
        out_specs=VMEM,
        scratch_shapes=[pltpu.VMEM(table.shape, jnp.bfloat16), pltpu.SemaphoreType.DMA((3,))],
        compiler_params=pltpu.CompilerParams(vmem_limit_bytes=60 * 2**20),
        name="pick_features",
    )(ids, table)


def front_kernel(
    picked_ref,
    docs_ref,
    gains_ref,
    shifts_ref,
    qkv_ref,
    out_ref,
    up_ref,
    down_ref,
    bias_ref,
    turn_ref,
    enc_ref,
    dec_ref,
    shift_ref,
    low_ref,
    stream_ref,
    enc_out,
    dec_out,
    turned_out,
    shift_out,
    scale_out,
    docs_all,
    gains,
    shifts,
    qkv,
    out,
    up,
    down,
    bias,
    turn,
    picked,
    features,
    turned,
    heads,
    mixed_turned,
    fed,
    enc_full,
    dec_full,
    shift_all,
    enc,
    dec,
    dec_turned,
    shift_wide,
    scale_wide,
    load_sem,
    store_sem,
    send,
    receive,
    pair_send,
    pair_receive,
    depth=1,
):
    group, share, rows = picked.shape
    mine = enc_full.shape[0]
    dense = mine // LANES
    width = gains.shape[1]
    ff_width = up.shape[1]
    layer, row, column = lax.axis_index("dp"), lax.axis_index("seq"), lax.axis_index("opt")
    here = row * 4 + column

    def member(index):
        return (layer, index // 4, index % 4)

    others = [(here + step) % group for step in range(group)]
    first_place = pl.multiple_of(here * rows, rows)
    loads = [
        pltpu.make_async_copy(picked_ref, picked, load_sem.at[0]),
        pltpu.make_async_copy(docs_ref, docs_all, load_sem.at[1]),
        pltpu.make_async_copy(gains_ref, gains, load_sem.at[2]),
        pltpu.make_async_copy(shifts_ref, shifts, load_sem.at[3]),
        pltpu.make_async_copy(bias_ref, bias, load_sem.at[4]),
        pltpu.make_async_copy(turn_ref.at[:, pl.ds(first_place, rows)], turn, load_sem.at[5]),
        pltpu.make_async_copy(qkv_ref, qkv, load_sem.at[6]),
        pltpu.make_async_copy(up_ref, up, load_sem.at[7]),
        pltpu.make_async_copy(down_ref, down, load_sem.at[8]),
        pltpu.make_async_copy(out_ref, out, load_sem.at[9]),
        pltpu.make_async_copy(enc_ref, enc_full, load_sem.at[10]),
        pltpu.make_async_copy(dec_ref, dec_full, load_sem.at[11]),
        pltpu.make_async_copy(shift_ref, shift_all.at[column % 2], load_sem.at[12]),
    ]
    for load in loads:
        load.start()
    greet([member(index) for index in others[1:]] + [((layer + step) % depth, row, column) for step in range(1, depth)])
    loads[0].wait()

    def copy_features(step):
        return remote(
            picked.at[others[step]],
            features.at[pl.ds(pl.multiple_of(here * share, share), share)],
            send.at[0, step],
            receive.at[0, step],
            member(others[step]),
        )

    def copy_heads(step):
        return remote(
            turned.at[others[step]], heads.at[here], send.at[1, step], receive.at[1, step], member(others[step])
        )

    def copy_mixed(index, source):
        return remote(
            picked.at[index],
            mixed_turned.at[pl.ds(pl.multiple_of(source * HEAD, HEAD), HEAD)],
            send.at[2, index],
            receive.at[2, source],
            member(index),
        )

    for step in range(1, group):
        copy_features(step).start()

    partner = (layer, row, column + 1 - 2 * (column % 2))
    own = pl.ds(pl.multiple_of(column % 2 * mine, mine), mine)
    for load in loads[10:]:
        load.wait()
    shared = []
    for kind, (full, low) in enumerate(((dec_full, dec), (enc_full, enc))):

        def cast(part, carry, full=full, low=low):
            start = pl.multiple_of(part * 256, 256)
            low[pl.ds(pl.multiple_of(column % 2 * mine + start, 256), 256)] = full[pl.ds(start, 256)].astype(
                jnp.bfloat16
            )
            return carry

        lax.fori_loop(0, mine // 256, cast, 0)
        shared.append(remote(low.at[own], low.at[own], pair_send.at[kind], pair_receive.at[kind], partner))
        shared[-1].start()
    spot = shift_all.at[column % 2]
    shared.append(remote(spot, spot, pair_send.at[2], pair_receive.at[2], partner))
    shared[-1].start()
    features[pl.ds(pl.multiple_of(here * share, share), share)] = picked[here]
    for load in loads[1:10]:
        load.wait()
    for step in range(1, group):
        copy_features(step).wait_recv()

    residual = features[...].astype(jnp.float32).T
    center = residual - jnp.mean(residual, axis=1, keepdims=True)
    variance = jnp.mean(center * center, axis=1, keepdims=True)
    unit = center * lax.rsqrt(variance + LAYER_EPSILON)
    first_norm = (unit * gains[0:1] + shifts[0:1]).astype(jnp.bfloat16)
    second_norm = (unit * gains[1:2] + shifts[1:2]).astype(jnp.bfloat16)

    def bias_row(first, count):
        lines = range(first // LANES, (first + count) // LANES)
        return jnp.concatenate([bias[line : line + 1] for line in lines], axis=1)

    half_rot = ROT // 2
    cosine, sine = turn[:half_rot], turn[half_rot:]
    for first in range(0, 3 * width, 2 * LANES):
        chunk = (
            jnp.dot(first_norm, qkv[:, first : first + 2 * LANES], preferred_element_type=jnp.float32)
            + bias_row(first, 2 * LANES)
        ).T
        for inner in range(0, 2 * LANES, HEAD):
            kind, head = (first + inner) // width, (first + inner) % width // HEAD
            values = chunk[inner : inner + HEAD]
            if kind < 2:
                left, right = values[:half_rot], values[half_rot:ROT]
                values = jnp.concatenate(
                    [left * cosine - right * sine, right * cosine + left * sine, values[ROT:]], axis=0
                )
            turned[head, kind * HEAD : (kind + 1) * HEAD] = values.astype(jnp.bfloat16)
    for step in range(1, group):
        copy_heads(step).start()
    heads[here] = turned[here]

    feed = residual + bias_row(4 * width + ff_width, width) + bias_row(3 * width, width)
    for first in range(0, ff_width, 512):
        inner = (
            jnp.dot(second_norm, up[:, first : first + 512], preferred_element_type=jnp.float32)
            + bias_row(4 * width + first, 512)
        )
        hidden = (0.5 * inner * (1.0 + lax.erf(inner * (0.5**0.5)))).astype(jnp.bfloat16)
        feed = feed + jnp.dot(hidden, down[first : first + 512], preferred_element_type=jnp.float32)
    fed[...] = feed

    for copy in shared:
        copy.wait()

    def widen(part, carry):
        start = pl.multiple_of(part * LANES, LANES)
        span = pl.ds(start, LANES)
        values = dec[span].astype(jnp.float32)
        dec_turned[:, span] = values.T.astype(jnp.bfloat16)
        norms = jnp.sqrt(jnp.sum(values * values, axis=1, keepdims=True) + NORM_EPSILON)
        scale_wide[span] = jnp.broadcast_to(COEFFICIENT * norms, (LANES, LANES))
        shift_wide[span] = jnp.broadcast_to(shift_all[part // dense, pl.ds(part % dense, 1)], (LANES, LANES)).T
        return carry

    lax.fori_loop(0, 2 * dense, widen, 0)
    stores = [
        pltpu.make_async_copy(held, target, store_sem.at[index])
        for index, (held, target) in enumerate(
            (
                (enc, enc_out),
                (dec, dec_out),
                (dec_turned, turned_out),
                (shift_wide, shift_out),
                (scale_wide, scale_out),
            )
        )
        if target is not None
    ]
    for store in stores:
        store.start()

    for step in range(1, group):
        copy_features(step).wait_send()
    query_place = lax.broadcasted_iota(jnp.int32, (rows, rows), 0)
    key_place = lax.broadcasted_iota(jnp.int32, (rows, rows), 1)
    causal = key_place <= query_place
    scale = HEAD ** (-0.5)
    values_of = []
    for index in range(group):

        @pl.when(here != index)
        def _():
            arrived = receive.at[1, (here + group - index) % group]
            remote(turned.at[index], heads.at[index], send.at[1, 0], arrived, member(others[1])).wait_recv()

        values_of.append(heads[index, 2 * HEAD :].astype(jnp.float32).T.astype(jnp.bfloat16))
        query = heads[index, :HEAD].astype(jnp.float32).T.astype(jnp.bfloat16)
        own_docs = jnp.broadcast_to(docs_all[index].astype(jnp.float32), (LANES, rows)).T
        own_docs = jnp.concatenate([own_docs] * (rows // LANES), axis=1)
        scores = []
        for other in range(index + 1):
            score = jnp.dot(query, heads[other, HEAD : 2 * HEAD], preferred_element_type=jnp.float32)
            allowed = own_docs == docs_all[other].astype(jnp.float32)
            if other == index:
                allowed = allowed & causal
            scores.append(jnp.where(allowed, score * scale, -1e30))
        peak = scores[0]
        for score in scores[1:]:
            peak = jnp.maximum(peak, score)
        peak = jnp.max(peak, axis=1, keepdims=True)
        weights = [jnp.exp(score - peak) for score in scores]
        total = weights[0]
        for weight in weights[1:]:
            total = total + weight
        inverse = 1.0 / jnp.sum(total, axis=1, keepdims=True)
        mixed = None
        for other in range(index + 1):
            probs = (weights[other] * inverse).astype(jnp.bfloat16)
            term = jnp.dot(probs, values_of[other], preferred_element_type=jnp.float32)
            mixed = term if mixed is None else mixed + term
        mixed = mixed.T
        picked[index] = mixed.astype(jnp.bfloat16)

        @pl.when(here != index)
        def _():
            copy_mixed(index, here).start()

        @pl.when(here == index)
        def _():
            mixed_turned[pl.ds(pl.multiple_of(here * HEAD, HEAD), HEAD)] = picked[index]

    for step in range(1, group):
        copy_mixed(step, others[step]).wait_recv()
    mixed = mixed_turned[...].astype(jnp.float32).T.astype(jnp.bfloat16)
    stream = fed[...] + jnp.dot(mixed, out[...], preferred_element_type=jnp.float32)
    stream_ref[...] = stream
    low_ref[...] = stream.astype(jnp.bfloat16)
    for step in range(1, group):
        copy_heads(step).wait_send()
    for index in range(group):

        @pl.when(here != index)
        def _():
            copy_mixed(index, here).wait_send()

    for store in stores:
        store.wait()


def rotary_table(context_len):
    half_rot = ROT // 2
    frequency = np.power(np.float32(10000.0), np.float32(-2.0) * np.arange(half_rot, dtype=np.float32) / np.float32(ROT))
    angles = frequency.astype(np.float32)[:, None] * np.arange(context_len, dtype=np.float32)[None, :]
    return np.concatenate([np.cos(angles.astype(np.float64)), np.sin(angles.astype(np.float64))]).astype(np.float32)


def front_scratch(picked, gains, qkv, out, up, down, bias, enc):
    group, share, rows = picked.shape
    width, mine, ff_width = gains.shape[1], enc.shape[0], up.shape[1]
    bf16, f32 = jnp.bfloat16, jnp.float32
    dma = pltpu.SemaphoreType.DMA
    return [
        pltpu.VMEM((group, 1, rows), jnp.int32),
        pltpu.VMEM((2, width), f32),
        pltpu.VMEM((2, width), f32),
        pltpu.VMEM((width, 3 * width), bf16),
        pltpu.VMEM((width, width), bf16),
        pltpu.VMEM((width, ff_width), bf16),
        pltpu.VMEM((ff_width, width), bf16),
        pltpu.VMEM(bias.shape, f32),
        pltpu.VMEM((ROT, rows), f32),
        pltpu.VMEM((group, share, rows), bf16),
        pltpu.VMEM((width, rows), bf16),
        pltpu.VMEM((group, 3 * HEAD, rows), bf16),
        pltpu.VMEM((group, 3 * HEAD, rows), bf16),
        pltpu.VMEM((width, rows), bf16),
        pltpu.VMEM((rows, width), f32),
        pltpu.VMEM((mine, width), f32),
        pltpu.VMEM((mine, width), f32),
        pltpu.VMEM((2, mine // LANES, LANES), f32),
        pltpu.VMEM((2 * mine, width), bf16),
        pltpu.VMEM((2 * mine, width), bf16),
        pltpu.VMEM((width, 2 * mine), bf16),
        pltpu.VMEM((2 * mine, LANES), f32),
        pltpu.VMEM((2 * mine, LANES), f32),
        dma((13,)),
        dma((5,)),
        dma((3, group)),
        dma((3, group)),
        dma((3,)),
        dma((3,)),
    ]


def front(picked, docs, gains, shifts, qkv, out, up, down, bias, enc, dec, shift):
    group, share, rows = picked.shape
    width = gains.shape[1]
    ff_width = up.shape[1]
    mine = enc.shape[0]
    shift = shift.reshape(mine // LANES, LANES)
    bf16, f32 = jnp.bfloat16, jnp.float32
    dma = pltpu.SemaphoreType.DMA
    return pl.pallas_call(
        front_kernel,
        out_shape=(
            jax.ShapeDtypeStruct((rows, width), bf16),
            jax.ShapeDtypeStruct((rows, width), f32),
            jax.ShapeDtypeStruct((2 * mine, width), bf16),
            jax.ShapeDtypeStruct((2 * mine, width), bf16),
            jax.ShapeDtypeStruct((width, 2 * mine), bf16),
            jax.ShapeDtypeStruct((2 * mine, LANES), f32),
            jax.ShapeDtypeStruct((2 * mine, LANES), f32),
        ),
        in_specs=[ANY] * 13,
        out_specs=(VMEM, VMEM) + (ANY,) * 5,
        scratch_shapes=front_scratch(picked, gains, qkv, out, up, down, bias, enc),
        compiler_params=pltpu.CompilerParams(
            collective_id=2, has_side_effects=True, vmem_limit_bytes=60 * 2**20
        ),
        cost_estimate=pl.CostEstimate(flops=2 * 10**9, bytes_accessed=14 * 10**6, transcendentals=2 * 10**6),
        name="front_part",
    )(picked, docs, gains, shifts, qkv, out, up, down, bias, jnp.asarray(rotary_table(group * rows)), enc, dec, shift)


def forward_kernel(
    depth,
    own_ref,
    enc_ref,
    dec_ref,
    bias_ref,
    stream_ref,
    scale_ref,
    dec_bias_ref,
    gathered_ref,
    relu_ref,
    upstream_ref,
    small_ref,
    total_ref,
    recon_ref,
    stream,
    scale,
    held,
    enc,
    dec,
    bias,
    staged,
    parts,
    own_diagonal,
    send_zero,
    send_one,
    send_two,
    send_three,
    got_zero,
    got_one,
    got_two,
    got_three,
    load_sem,
    relu_sem,
    held_sem,
    send,
    receive,
    sum_send,
    sum_receive,
    ready=False,
):
    rows = upstream_ref.shape[0]
    entries = enc.shape[0]
    width = held.shape[1]
    half = width // 2
    piece = min(entries, 256)
    where = peers(depth)
    (layer, row, place), across, beside, _ = where
    inner = (layer >= 1) & (layer < depth - 1)
    others = [((layer + step) % depth, row, place) for step in range(1, depth)]
    loads = []
    if not ready:
        loads = [
            pltpu.make_async_copy(own_ref, held.at[pl.ds(0, rows)], load_sem.at[0]),
            pltpu.make_async_copy(enc_ref, enc, load_sem.at[1]),
            pltpu.make_async_copy(bias_ref, bias, load_sem.at[2]),
            pltpu.make_async_copy(dec_ref, dec, load_sem.at[3]),
            pltpu.make_async_copy(stream_ref, stream, load_sem.at[4]),
            pltpu.make_async_copy(scale_ref, scale, load_sem.at[5]),
        ]
        for load in loads:
            load.start()
        greet(others + [across, beside])
        loads[0].wait()
    gather = Gather(depth, rows, held, send, receive, where)
    gather.open()
    total_ref[...] = jnp.zeros_like(total_ref)
    for load in loads[1:]:
        load.wait()

    def part_slot(turn):
        return jnp.where(turn <= 1, 4 + turn, turn % 4)

    def copy_zero(turn):
        layer_there = layer_at(depth, layer, turn)
        index = jnp.where(
            jnp.abs(layer_there - layer) == 1,
            jnp.where(layer > layer_there, 0, 1),
            jnp.where(layer == 0, 2, 3),
        )
        return remote(
            send_zero.at[turn - 1],
            got_zero.at[index],
            sum_send.at[5, turn],
            sum_receive.at[5, index],
            (layer_there, row, place),
        )

    def one_slot(turn):
        return jnp.where(turn == 0, 2, turn % 2)

    def copy_one(turn, part):
        source = send_one.at[one_slot(turn), pl.ds(part * half, half)]
        device = beside if part else across
        return remote(source, got_one.at[part, turn], sum_send.at[part, turn], sum_receive.at[part, turn], device)

    def two_slot(turn):
        return jnp.where(turn <= 1, 3 + turn, turn % 3)

    def copy_two(turn, part, side):
        device = beside if part else across
        span = pl.ds(side * half, half)
        return remote(
            send_two.at[part, two_slot(turn), span],
            got_two.at[part, turn, span],
            sum_send.at[6 + 2 * part + side, turn],
            sum_receive.at[6 + 2 * part + side, turn],
            device,
        )

    def each_two(turn, act):
        for part in range(2):
            for side in range(2):
                act(copy_two(turn, part, side))

    def copy_three(turn):
        layer_there = layer_at(depth, layer, turn)
        index = place_of(depth, layer_there, layer)
        return remote(
            send_three.at[turn],
            got_three.at[index],
            sum_send.at[4, turn],
            sum_receive.at[4, index],
            (layer_there, row, place),
        )

    def copy_relu(order):
        first = slot_of(depth, order // 4, order % 4) * rows
        return pltpu.make_async_copy(
            staged.at[order % 2],
            relu_ref.at[:, pl.ds(pl.multiple_of(first, rows), rows)],
            relu_sem.at[order % 2],
        )

    def copy_held(step):
        span = pl.ds(pl.multiple_of(step * 4 * rows, 4 * rows), 4 * rows)
        return pltpu.make_async_copy(held.at[span], gathered_ref.at[span], held_sem.at[step])

    def sum_one(turn, value):
        @pl.when(turn >= 5)
        def _():
            copy_one(turn - 2, 0).wait_send()
            copy_one(turn - 2, 1).wait_send()

        send_one[one_slot(turn)] = value.astype(jnp.bfloat16)
        copy_one(turn, 0).start()
        copy_one(turn, 1).start()

    def send_half(turn, part, side, extra=None):
        span = pl.ds(side * half, half)
        value = parts[1 + part, part_slot(turn), span]
        if extra is not None:
            value = value + extra.astype(jnp.float32)
        send_two[part, two_slot(turn), span] = value.astype(jnp.bfloat16)
        copy_two(turn, part, side).start()

    def sum_two_own(turn):
        @pl.when(turn >= 5)
        def _():
            each_two(turn - 3, lambda copy: copy.wait_send())

        send_half(turn, 1, 1)
        send_half(turn, 0, 0)

    def sum_two(turn):
        @pl.when(crosswise(turn))
        def _():
            copy_one(turn, 0).wait_recv()
            send_half(turn, 1, 0, got_one[0, turn])
            copy_one(turn, 1).wait_recv()
            send_half(turn, 0, 1, got_one[1, turn])

        @pl.when((turn == 1) | (turn == 2))
        def _():
            send_half(turn, 1, 0)
            send_half(turn, 0, 1)

    def column_sum(turn):
        each_two(turn, lambda copy: copy.wait_recv())
        return parts[0, part_slot(turn)] + got_two[0, turn].astype(jnp.float32) + got_two[1, turn].astype(jnp.float32)

    def sum_three(turn):
        send_three[turn] = column_sum(turn).astype(jnp.bfloat16)
        copy_three(turn).start()

    def one_block(order, carry):
        turn, column = order // 4, order % 4

        @pl.when(column == 1)
        def _():
            gather.hand_on(turn)

        @pl.when(column == 3)
        def _():
            gather.wait_diagonal(turn)

        @pl.when((order == 3) & jnp.logical_not(inner))
        def _():
            gather.arrive(2)

        @pl.when(order == 3)
        def _():
            gather.to_neighbours(2)

        @pl.when((column == 2) & (turn >= 1) & (turn + 2 < depth))
        def _():
            @pl.when(jnp.logical_not(inner) | (turn >= 2))
            def _():
                gather.arrive(turn + 2)

            gather.to_neighbours(turn + 2)

        @pl.when(order >= 2)
        def _():
            copy_relu(order - 2).wait()

        first_row = slot_of(depth, turn, column) * rows
        block = held[pl.ds(pl.multiple_of(first_row, rows), rows)]
        low = []
        for first in range(0, entries, piece):
            span = pl.ds(first, piece)
            shift = bias[span]
            pre = lax.dot_general(enc[span], block, LAST_LAST, preferred_element_type=jnp.float32)
            positive = jnp.maximum(pre + jnp.concatenate([shift] * (rows // LANES), axis=1), 0.0)
            staged[order % 2, span] = positive
            active = positive * positive
            folded = active[:, :LANES]
            for lane in range(LANES, rows, LANES):
                folded = folded + active[:, lane : lane + LANES]
            total_ref[span] += folded
            low.append(active.astype(jnp.bfloat16))
        recon = jnp.dot(dec[...], jnp.concatenate(low, axis=0), preferred_element_type=jnp.float32)
        copy_relu(order).start()

        @pl.when(column < 3)
        def _():
            parts[column, part_slot(turn)] = recon

        @pl.when((column == 3) & (turn == 0))
        def _():
            own_diagonal[...] = recon

        @pl.when((column == 3) & (turn >= 3))
        def _():
            sum_one(turn, recon)

        @pl.when((column == 3) & ((turn == 1) | (turn == 2)))
        def _():
            send_zero[turn - 1] = recon.astype(jnp.bfloat16)
            copy_zero(turn).start()

        @pl.when(order == 0)
        def _():
            gather.arrive(1)

        @pl.when((order == 0) & inner)
        def _():
            gather.arrive(2)

        @pl.when(order == 0)
        def _():
            gather.to_neighbours(1)

        @pl.when((order == 2) & inner)
        def _():
            gather.arrive(3)

        @pl.when((column == 1) & (turn >= 4))
        def _():
            sum_two_own(turn - 2)
            sum_two(turn - 2)

        @pl.when((column == (1 if depth == 4 else 2)) & (turn == depth - 1))
        def _():
            sum_two_own(depth - 2)
            sum_two(depth - 2)

        @pl.when((column == 3) & (turn >= 5))
        def _():
            sum_three(turn - 3)

        return carry

    lax.fori_loop(0, 4 * depth, one_block, 0)
    for step in range(depth):
        copy_held(step).start()
    sum_two_own(depth - 1)
    if depth > 4:
        sum_three(depth - 3)
    sum_two(depth - 1)
    sum_two_own(1)
    sum_two(1)
    sum_three(depth - 2)
    for index, (_, there) in enumerate(takers(depth, layer)):

        @pl.when(there)
        def _(index=index):
            remote(
                send_zero.at[0], got_zero.at[index], sum_send.at[5, 0], sum_receive.at[5, index], across
            ).wait_recv()
            own_diagonal[...] += got_zero[index].astype(jnp.float32)

    sum_one(0, own_diagonal[...])
    sum_two_own(0)
    sum_three(depth - 1)
    sum_three(1)
    sum_two(0)
    recon_ref[...] = column_sum(0)
    for turn in range(1, depth):
        remote(
            send_three.at[turn], got_three.at[turn], sum_send.at[4, turn], sum_receive.at[4, turn], across
        ).wait_recv()
        recon_ref[...] += got_three[turn].astype(jnp.float32)
    error = recon_ref[...].T + dec_bias_ref[...] - stream[...]
    upstream = (2.0 * error).astype(jnp.bfloat16)
    upstream_ref[...] = upstream
    loss = fold(error * error)
    weighted = total_ref[...] * scale[...]
    loss = loss + fold(weighted)
    small_ref[...] = jnp.zeros_like(small_ref)
    column_sums = jnp.sum(upstream.astype(jnp.float32), axis=0, keepdims=True)
    lines = width // LANES
    for line in range(lines):
        small_ref[line : line + 1] = column_sums[:, line * LANES : (line + 1) * LANES]
    small_ref[lines : lines + 1] = jnp.sum(loss, axis=0, keepdims=True)
    gather.close()
    for turn in [0] + list(range(max(depth - 2, 3), depth)):
        for part in range(2):
            copy_one(turn, part).wait_send()
    for turn in [0, 1] + list(range(max(depth - 3, 2), depth)):
        each_two(turn, lambda copy: copy.wait_send())
    for turn in range(1, depth):
        copy_three(turn).wait_send()
    for turn in (1, 2):
        copy_zero(turn).wait_send()
    copy_relu(4 * depth - 2).wait()
    copy_relu(4 * depth - 1).wait()
    for step in range(depth):
        copy_held(step).wait()


def forward_scratch(depth, rows, width, entries):
    bf16, f32 = jnp.bfloat16, jnp.float32
    dma = pltpu.SemaphoreType.DMA
    return [
        pltpu.VMEM((width, rows), f32),
        pltpu.VMEM((rows, width), f32),
        pltpu.VMEM((entries, LANES), f32),
        pltpu.VMEM((depth * 4 * rows, width), bf16),
        pltpu.VMEM((entries, width), bf16),
        pltpu.VMEM((width, entries), bf16),
        pltpu.VMEM((entries, LANES), f32),
        pltpu.VMEM((2, entries, rows), f32),
        pltpu.VMEM((3, 6, width, rows), f32),
        pltpu.VMEM((width, rows), f32),
        pltpu.VMEM((2, width, rows), bf16),
        pltpu.VMEM((3, width, rows), bf16),
        pltpu.VMEM((2, 5, width, rows), bf16),
        pltpu.VMEM((depth, width, rows), bf16),
        pltpu.VMEM((4, width, rows), bf16),
        pltpu.VMEM((2, depth, width // 2, rows), bf16),
        pltpu.VMEM((2, depth, width, rows), bf16),
        pltpu.VMEM((depth, width, rows), bf16),
        dma((6,)),
        dma((2,)),
        dma((depth,)),
        dma((11, max(depth, 4))),
        dma((9, max(depth, 4))),
        dma((10, max(depth, 4))),
        dma((10, max(depth, 4))),
    ]


def forward(depth, own, enc, dec_turned, bias, stream, scale, dec_bias):
    rows, width = own.shape
    entries = enc.shape[0]
    bf16, f32 = jnp.bfloat16, jnp.float32
    dma = pltpu.SemaphoreType.DMA
    return pl.pallas_call(
        functools.partial(forward_kernel, depth),
        out_shape=(
            jax.ShapeDtypeStruct((depth * 4 * rows, width), bf16),
            jax.ShapeDtypeStruct((entries, depth * 4 * rows), f32),
            jax.ShapeDtypeStruct((rows, width), bf16),
            jax.ShapeDtypeStruct((8, LANES), f32),
            jax.ShapeDtypeStruct((entries, LANES), f32),
        ),
        in_specs=[ANY] * 6 + [VMEM],
        out_specs=(ANY, ANY, VMEM, VMEM, VMEM),
        scratch_shapes=forward_scratch(depth, rows, width, entries),
        compiler_params=pltpu.CompilerParams(
            collective_id=0, has_side_effects=True, vmem_limit_bytes=60 * 2**20
        ),
        cost_estimate=pl.CostEstimate(
            flops=16 * depth * rows * entries * width, bytes_accessed=16 * depth * rows * entries, transcendentals=0
        ),
        name="forward_blocks",
    )(own, enc, dec_turned, bias, stream, scale, dec_bias)


def joint_kernel(depth, *refs):
    given, dec_bias_ref = refs[:13], refs[13]
    dec_out, scale_out, gathered_ref, relu_ref, upstream_ref, small_ref, total_ref = refs[14:21]
    first, second = refs[21:50], refs[50:]
    recon_ref, stream, held, *rest = second
    rows = upstream_ref.shape[0]
    enc, dec_turned, shift_wide, scale_wide = first[18], first[20], first[21], first[22]
    front_kernel(
        *given, held.at[pl.ds(0, rows)], stream, None, dec_out, None, None, scale_out, *first, depth=depth
    )
    forward_kernel(
        depth,
        *([None] * 6),
        dec_bias_ref,
        gathered_ref,
        relu_ref,
        upstream_ref,
        small_ref,
        total_ref,
        recon_ref,
        stream,
        scale_wide,
        held,
        enc,
        dec_turned,
        shift_wide,
        *rest,
        ready=True,
    )


def joint(depth, picked, docs, gains, shifts, qkv, out, up, down, bias, enc, dec, shift, dec_bias):
    group, share, rows = picked.shape
    width, mine = gains.shape[1], enc.shape[0]
    entries = 2 * mine
    bf16, f32 = jnp.bfloat16, jnp.float32
    first = front_scratch(picked, gains, qkv, out, up, down, bias, enc)
    second = forward_scratch(depth, rows, width, entries)
    second = second[:2] + second[3:4] + second[7:]
    return pl.pallas_call(
        functools.partial(joint_kernel, depth),
        out_shape=(
            jax.ShapeDtypeStruct((entries, width), bf16),
            jax.ShapeDtypeStruct((entries, LANES), f32),
            jax.ShapeDtypeStruct((depth * 4 * rows, width), bf16),
            jax.ShapeDtypeStruct((entries, depth * 4 * rows), f32),
            jax.ShapeDtypeStruct((rows, width), bf16),
            jax.ShapeDtypeStruct((8, LANES), f32),
            jax.ShapeDtypeStruct((entries, LANES), f32),
        ),
        in_specs=[ANY] * 13 + [VMEM],
        out_specs=(ANY, ANY, ANY, ANY, VMEM, VMEM, VMEM),
        scratch_shapes=first + second,
        compiler_params=pltpu.CompilerParams(
            collective_id=2, has_side_effects=True, vmem_limit_bytes=62 * 2**20
        ),
        cost_estimate=pl.CostEstimate(
            flops=16 * depth * rows * entries * width, bytes_accessed=48 * 10**6, transcendentals=2 * 10**6
        ),
        name="joint_part",
    )(
        picked,
        docs,
        gains,
        shifts,
        qkv,
        out,
        up,
        down,
        bias,
        jnp.asarray(rotary_table(group * rows)),
        enc,
        dec,
        shift.reshape(mine // LANES, LANES),
        dec_bias,
    )


def backward_kernel(
    depth,
    everyone,
    own_ref,
    gathered_ref,
    relu_ref,
    dec_ref,
    scale_ref,
    active_ref,
    small_ref,
    enc_out,
    dec_out,
    bias_out,
    small_out,
    squares_out,
    held,
    inputs,
    dec,
    scale,
    tile,
    held_last,
    inputs_last,
    relu_last,
    enc_sum,
    dec_sum,
    bias_sum,
    enc_got,
    dec_got,
    bias_got,
    active,
    active_got,
    low,
    small,
    two,
    two_got,
    sums,
    sums_got,
    load_sem,
    tile_sem,
    store_sem,
    send,
    receive,
    pair_send,
    pair_receive,
    last_send,
    last_receive,
    all_send,
    all_receive,
):
    rows = own_ref.shape[0]
    entries = dec.shape[0]
    mine = entries // 2
    piece = tile.shape[1]
    tiles = entries // piece
    where = peers(depth)
    (layer, row, column), _, _, partner = where
    core = column % 2
    inner = (layer >= 1) & (layer < depth - 1)
    loads = [
        pltpu.make_async_copy(own_ref, held.at[pl.ds(0, rows)], load_sem.at[0]),
        pltpu.make_async_copy(dec_ref, dec, load_sem.at[1]),
        pltpu.make_async_copy(scale_ref, scale, load_sem.at[2]),
        pltpu.make_async_copy(gathered_ref, inputs, load_sem.at[3]),
        pltpu.make_async_copy(active_ref, active, load_sem.at[4]),
        pltpu.make_async_copy(small_ref, small, load_sem.at[5]),
    ]
    for load in loads:
        load.start()

    def place(turn):
        return (turn + (1 - core) * (tiles // 2)) % tiles

    def group_of(group):
        if group == depth - 1:
            return (4 * group + 1) * rows, 3 * rows
        if group == depth:
            return (4 * group - 4) * rows, rows
        return 4 * group * rows, 4 * rows

    def copy_tile(group, start, size, turn):
        slot = (group * tiles + turn) % 2
        first = pl.multiple_of(place(turn) * piece, piece)
        return pltpu.make_async_copy(
            relu_ref.at[pl.ds(first, piece), pl.ds(pl.multiple_of(start, rows), size)],
            tile.at[slot, :, pl.ds(0, size)],
            tile_sem.at[slot],
        )

    copy_tile(0, *group_of(0), 0).start()

    others = [
        ((layer + dz) % depth, (row + dy) % 2, (column + 2 * dx) % 4)
        for dz in range(depth)
        for dy in range(2)
        for dx in range(2)
    ]
    greet(others[1:] + [partner])
    loads[0].wait()
    gather = Gather(depth, rows, held, send, receive, where)
    gather.open()
    for load in loads[1:]:
        load.wait()

    def sums_copy(index):
        return remote(
            sums, sums_got.at[index], all_send.at[index], all_receive.at[index], others[index]
        )

    def two_copy(kind):
        return remote(
            two.at[kind], two_got.at[kind], last_send.at[3 + kind], last_receive.at[3 + kind], partner
        )

    two[0] = small[...]
    two_copy(0).start()

    theirs = (1 - core) * mine
    active_copy = remote(
        active.at[pl.ds(pl.multiple_of(theirs, mine), mine)], active_got, pair_send.at[3, 0], pair_receive.at[3, 0], partner
    )
    active_copy.start()
    last = pl.ds(4 * (depth - 1) * rows, rows)
    last_copies = [
        remote(
            relu_ref.at[pl.ds(pl.multiple_of(theirs, mine), mine), last],
            relu_last,
            last_send.at[0],
            last_receive.at[0],
            partner,
        ),
        remote(inputs.at[last], inputs_last, last_send.at[1], last_receive.at[1], partner),
        remote(held.at[last], held_last, last_send.at[2], last_receive.at[2], partner),
    ]
    last_copies[0].start()
    last_copies[1].start()
    enc_sum[...] = jnp.zeros_like(enc_sum)
    dec_sum[...] = jnp.zeros_like(dec_sum)
    bias_sum[...] = jnp.zeros_like(bias_sum)

    def pair_copy(kind, turn):
        source, target = ((low.at[0], enc_got), (low.at[1], dec_got), (bias_sum, bias_got))[kind]
        there = pl.ds(pl.multiple_of(turn * piece, piece), piece)
        return remote(
            source.at[pl.ds(pl.multiple_of(theirs + turn * piece, piece), piece) if kind == 2 else there],
            target.at[there],
            pair_send.at[kind, turn],
            pair_receive.at[kind, turn],
            partner,
        )

    gather.arrive(1)

    @pl.when(inner)
    def _():
        gather.arrive(2)

    gather.to_neighbours(1)
    gather.hand_on(0)

    def one_tile(group, start, size, turn):
        slot = (group * tiles + turn) % 2
        copy_tile(group, start, size, turn).wait()
        span = pl.ds(pl.multiple_of(place(turn) * piece, piece), piece)
        tokens = pl.ds(pl.multiple_of(start, rows), size)
        upstream, given, positive = held[tokens], inputs[tokens], tile[slot, :, :size]
        if group is depth:
            there = pl.ds(pl.multiple_of((turn - tiles // 2) * piece, piece), piece)
            upstream = jnp.concatenate([upstream, held_last[...]], axis=0)
            given = jnp.concatenate([given, inputs_last[...]], axis=0)
            positive = jnp.concatenate([positive, relu_last[there]], axis=1)
            size = 2 * size
        back = lax.dot_general(dec[span], upstream, LAST_LAST, preferred_element_type=jnp.float32)
        shift = jnp.concatenate([scale[span]] * (size // LANES), axis=1)
        slope = ((back + shift) * (2.0 * positive)).astype(jnp.bfloat16)
        act_low = (positive * positive).astype(jnp.bfloat16)
        wide = slope.astype(jnp.float32)
        folded = wide[:, :LANES]
        for lane in range(LANES, size, LANES):
            folded = folded + wide[:, lane : lane + LANES]
        bias_sum[span] += folded
        enc_sum[span] += jnp.dot(slope, given, preferred_element_type=jnp.float32)
        dec_sum[span] += jnp.dot(act_low, upstream, preferred_element_type=jnp.float32)

    def take_in(group, turn):
        @pl.when((group == 0) & (turn == tiles // 2))
        def _():
            if depth > 3:

                @pl.when(inner)
                def _():
                    gather.arrive(3)

            @pl.when(jnp.logical_not(inner))
            def _():
                gather.arrive(2)

            gather.to_neighbours(2)

        @pl.when((group >= 1) & (turn == 0) & (group + 2 < depth))
        def _():
            @pl.when(jnp.logical_not(inner) | (group >= 2))
            def _():
                gather.arrive(group + 2)

            gather.to_neighbours(group + 2)

        @pl.when((group == depth - 2) & (turn == 0))
        def _():
            gather.hand_on(depth - 1)

        @pl.when(turn == tiles // 2)
        def _():
            gather.wait_diagonal(group)

    def middle_group(group, carry):
        start, size = 4 * group * rows, 4 * rows

        @pl.when(group >= 1)
        def _():
            gather.hand_on(group)

        def one(turn, carry):
            @pl.when(turn + 1 < tiles)
            def _():
                copy_tile(group, start, size, turn + 1).start()

            @pl.when((turn + 1 == tiles) & (group + 2 < depth))
            def _():
                copy_tile(group + 1, start + 4 * rows, size, 0).start()

            @pl.when((turn + 1 == tiles) & (group + 2 == depth))
            def _():
                copy_tile(depth - 1, *group_of(depth - 1), 0).start()

            one_tile(group, start, size, turn)
            take_in(group, turn)
            return carry

        return lax.fori_loop(0, tiles, one, carry)

    def late_group(turn, carry):
        start, size = group_of(depth - 1)

        @pl.when(turn + 1 < tiles)
        def _():
            copy_tile(depth - 1, start, size, turn + 1).start()

        @pl.when(turn + 1 == tiles)
        def _():
            copy_tile(depth, *group_of(depth), tiles // 2).start()

        one_tile(depth - 1, start, size, turn)

        @pl.when(turn < tiles // 2)
        def _():
            span = pl.ds(pl.multiple_of(place(turn) * piece, piece), piece)
            there = pl.ds(pl.multiple_of(turn * piece, piece), piece)
            low[0, there] = enc_sum[span].astype(jnp.bfloat16)
            low[1, there] = dec_sum[span].astype(jnp.bfloat16)
            for kind in range(3):
                pair_copy(kind, turn).start()

        return carry

    def last_group(turn, carry):
        start, size = group_of(depth)

        @pl.when(turn + 1 < tiles)
        def _():
            copy_tile(depth, start, size, turn + 1).start()

        one_tile(depth, start, size, turn)
        return carry

    lax.fori_loop(0, depth - 1, middle_group, 0)
    gather.wait_diagonal(depth - 1)
    last_copies[2].start()
    lax.fori_loop(0, tiles, late_group, 0)
    for copy in last_copies:
        copy.wait_recv()
    lax.fori_loop(tiles // 2, tiles, last_group, 0)

    ours = core * mine
    active_copy.wait_recv()
    span = pl.ds(pl.multiple_of(ours, mine), mine)
    act_total = jnp.sum(active[span] + active_got[...], axis=1, keepdims=True)
    partial = jnp.zeros((8, LANES), jnp.float32)

    stores = []
    rows_of = lax.broadcasted_iota(jnp.int32, (LANES, LANES), 0)
    lanes_of = lax.broadcasted_iota(jnp.int32, (LANES, LANES), 1)
    for turn in range(tiles // 2):
        for kind in range(3):
            pair_copy(kind, turn).wait_recv()
        near = pl.ds(pl.multiple_of(ours + turn * piece, piece), piece)
        there = pl.ds(turn * piece, piece)
        enc_grad = enc_sum[near] + enc_got[there].astype(jnp.float32)
        enc_sum[near] = enc_grad
        partial = partial + fold(enc_grad * enc_grad)
        dec_grad = dec_sum[near] + dec_got[there].astype(jnp.float32)
        dec_grad = dec_grad + (
            COEFFICIENT * COEFFICIENT * act_total[turn * piece : (turn + 1) * piece] / scale[near, :1]
        ) * dec[near].astype(jnp.float32)
        dec_sum[near] = dec_grad
        partial = partial + fold(dec_grad * dec_grad)
        stores += [
            pltpu.make_async_copy(enc_sum.at[near], enc_out.at[there], store_sem.at[0, turn]),
            pltpu.make_async_copy(dec_sum.at[near], dec_out.at[there], store_sem.at[1, turn]),
        ]
        stores[-2].start()
        stores[-1].start()
        bias_grad = jnp.sum(bias_sum[near] + bias_got[there], axis=1, keepdims=True)
        for first in range(0, piece, LANES):
            wide = jnp.broadcast_to(bias_grad[first : first + LANES], (LANES, LANES))
            line = jnp.sum(jnp.where(rows_of == lanes_of, wide, 0.0), axis=0, keepdims=True)
            index = (turn * piece + first) // LANES
            bias_out[index : index + 1] = line
            partial = partial + jnp.where(rows_of[:8] == 0, line * line, 0.0)
    two[1] = partial
    two_copy(1).start()
    for kind in range(2):
        two_copy(kind).wait_recv()
        sums[kind] = two[kind] + two_got[kind]
    for index in range(1, everyone):
        sums_copy(index).start()
    total = sums[...]
    for index in range(1, everyone):
        sums_copy(index).wait_recv()
        total = total + sums_got[index]
    small_out[...] = total[0]
    squares_out[...] = total[1]
    gather.close()
    for index in range(1, everyone):
        sums_copy(index).wait_send()
    for kind in range(2):
        two_copy(kind).wait_send()
    active_copy.wait_send()
    for copy in last_copies:
        copy.wait_send()
    for turn in range(tiles // 2):
        for kind in range(3):
            pair_copy(kind, turn).wait_send()
    for store in stores:
        store.wait()


def backward(depth, own, gathered, relu, dec, scale, active, small):
    rows, width = own.shape
    entries = dec.shape[0]
    mine = entries // 2
    piece = min(512, mine)
    everyone = depth * 4
    bf16, f32 = jnp.bfloat16, jnp.float32
    dma = pltpu.SemaphoreType.DMA
    return pl.pallas_call(
        functools.partial(backward_kernel, depth, everyone),
        out_shape=(
            jax.ShapeDtypeStruct((mine, width), f32),
            jax.ShapeDtypeStruct((mine, width), f32),
            jax.ShapeDtypeStruct((mine // LANES, LANES), f32),
            jax.ShapeDtypeStruct(small.shape, f32),
            jax.ShapeDtypeStruct((8, LANES), f32),
        ),
        in_specs=[ANY] * 7,
        out_specs=(ANY, ANY, VMEM, VMEM, VMEM),
        scratch_shapes=[
            pltpu.VMEM((depth * 4 * rows, width), bf16),
            pltpu.VMEM((depth * 4 * rows, width), bf16),
            pltpu.VMEM((entries, width), bf16),
            pltpu.VMEM((entries, LANES), f32),
            pltpu.VMEM((2, piece, 4 * rows), f32),
            pltpu.VMEM((rows, width), bf16),
            pltpu.VMEM((rows, width), bf16),
            pltpu.VMEM((mine, rows), f32),
            pltpu.VMEM((entries, width), f32),
            pltpu.VMEM((entries, width), f32),
            pltpu.VMEM((entries, LANES), f32),
            pltpu.VMEM((mine, width), bf16),
            pltpu.VMEM((mine, width), bf16),
            pltpu.VMEM((mine, LANES), f32),
            pltpu.VMEM((entries, LANES), f32),
            pltpu.VMEM((mine, LANES), f32),
            pltpu.VMEM((2, mine, width), bf16),
            pltpu.VMEM(small.shape, f32),
            pltpu.VMEM((2, 8, LANES), f32),
            pltpu.VMEM((2, 8, LANES), f32),
            pltpu.VMEM((2, 8, LANES), f32),
            pltpu.VMEM((everyone, 2, 8, LANES), f32),
            dma((6,)),
            dma((2,)),
            dma((2, entries // piece)),
            dma((11, max(depth, 4))),
            dma((9, max(depth, 4))),
            dma((4, entries // piece)),
            dma((4, entries // piece)),
            dma((5,)),
            dma((5,)),
            dma((everyone,)),
            dma((everyone,)),
        ],
        compiler_params=pltpu.CompilerParams(
            collective_id=1, has_side_effects=True, vmem_limit_bytes=60 * 2**20
        ),
        cost_estimate=pl.CostEstimate(
            flops=24 * depth * rows * entries * width, bytes_accessed=16 * depth * rows * entries, transcendentals=0
        ),
        name="backward_blocks",
    )(own, gathered, relu, dec, scale, active, small)


def update_kernel(*refs):
    names = ["enc_grad", "dec_grad", "bias_grad", "small", "squares"]
    for kind in ("enc", "dec", "bias", "shift"):
        names += [kind, kind + "_one", kind + "_two"]
    given = dict(zip(names, refs[: len(names)]))
    made = refs[len(names) : len(names) + 14]
    brought, staged, load_sem, store_sem = refs[len(names) + 14 :]
    mine = given["enc"].shape[0]
    slots, _, piece, _ = staged.shape
    parts = mine // piece
    large = ["enc", "enc_one", "enc_two", "enc_grad", "dec", "dec_one", "dec_two", "dec_grad"]

    def load(part, index):
        span = pl.ds(pl.multiple_of(part * piece, piece), piece)
        slot = part % slots
        return pltpu.make_async_copy(given[large[index]].at[span], brought.at[slot, index], load_sem.at[slot, index])

    for part in range(min(slots - 1, parts)):
        for index in range(8):
            load(part, index).start()
    lines = given["shift"].shape[1] // LANES
    shift_grad = jnp.concatenate([given["small"][line : line + 1] for line in range(lines)], axis=1)
    total = jnp.sum(given["squares"][...], keepdims=True) + jnp.sum(shift_grad * shift_grad, keepdims=True)
    norm = jnp.sqrt(total)
    clip = jnp.minimum(1.0, CLIP_NORM / (norm + 1e-06))
    made[12][...] = norm
    made[13][...] = jnp.sum(given["small"][lines : lines + 1], keepdims=True)

    def store(part, index):
        span = pl.ds(pl.multiple_of(part * piece, piece), piece)
        slot = part % slots
        return pltpu.make_async_copy(staged.at[slot, index], made[index].at[span], store_sem.at[slot, index])

    def one(part, carry):
        @pl.when(part >= slots)
        def _():
            for index in range(6):
                store(part - slots, index).wait()

        @pl.when(part + slots - 1 < parts)
        def _():
            for index in range(8):
                load(part + slots - 1, index).start()

        slot = part % slots
        for index in range(8):
            load(part, index).wait()
        for index in range(2):
            new, first, second = adam_step(
                *(brought[slot, 4 * index + offset] for offset in range(4)),
                clip,
                RATE_MATRIX,
                WEIGHT_DECAY,
            )
            if index:
                new = new * lax.rsqrt(jnp.sum(new * new, axis=1, keepdims=True) + NORM_EPSILON)
            for offset, value in enumerate((new, first, second)):
                staged[slot, 3 * index + offset] = value
        for index in range(6):
            store(part, index).start()
        return carry

    lax.fori_loop(0, parts, one, 0)
    for offset, (kind, gradient) in enumerate((("bias", given["bias_grad"][...]), ("shift", shift_grad))):
        results = adam_step(
            given[kind][...], given[kind + "_one"][...], given[kind + "_two"][...], gradient, clip, RATE_BIAS, 0.0
        )
        for index, value in enumerate(results):
            made[6 + 3 * offset + index][...] = value
    for part in range(max(parts - slots, 0), parts):
        for index in range(6):
            store(part, index).wait()


def update(*arrays):
    f32 = jnp.float32
    mine, width = arrays[0].shape
    dense, flat = (mine // LANES, LANES), (1, width)
    arrays = list(arrays)
    for index in range(11, 14):
        arrays[index] = arrays[index].reshape(dense)
    for index in range(14, 17):
        arrays[index] = arrays[index].reshape(flat)
    piece, slots = min(128, mine), 4
    made = pl.pallas_call(
        update_kernel,
        out_shape=[jax.ShapeDtypeStruct((mine, width), f32)] * 6
        + [jax.ShapeDtypeStruct(dense, f32)] * 3
        + [jax.ShapeDtypeStruct(flat, f32)] * 3
        + [jax.ShapeDtypeStruct((1, 1), f32)] * 2,
        in_specs=[ANY] * 2 + [VMEM] * 3 + [ANY] * 6 + [VMEM] * 6,
        out_specs=[ANY] * 6 + [VMEM] * 8,
        scratch_shapes=[
            pltpu.VMEM((slots, 8, piece, width), f32),
            pltpu.VMEM((slots, 6, piece, width), f32),
            pltpu.SemaphoreType.DMA((slots, 8)),
            pltpu.SemaphoreType.DMA((slots, 6)),
        ],
        compiler_params=pltpu.CompilerParams(vmem_limit_bytes=60 * 2**20),
        cost_estimate=pl.CostEstimate(flops=60 * mine * width, bytes_accessed=56 * mine * width, transcendentals=4 * mine * width),
        name="update",
    )(*arrays)
    return (
        *made[:6],
        *(value.reshape(mine) for value in made[6:9]),
        *(value.reshape(width) for value in made[9:12]),
        made[12].reshape(()),
        made[13].reshape(()),
    )


def body(
    depth,
    token_ids,
    doc_ids,
    embed,
    norm_gains,
    norm_shifts,
    qkv_weight,
    out_weight,
    up_weight,
    down_weight,
    proj_biases,
    enc_weight,
    dec_weight,
    enc_bias,
    dec_bias,
    enc_first,
    enc_second,
    dec_first,
    dec_second,
    enc_bias_first,
    enc_bias_second,
    dec_bias_first,
    dec_bias_second,
):
    model_width = norm_gains.shape[1]
    all_ids, all_docs = gather_ids(token_ids, doc_ids, model_width // embed.shape[1])
    arguments = (
        pick(all_ids, embed.T),
        all_docs,
        norm_gains,
        norm_shifts,
        qkv_weight,
        out_weight,
        up_weight,
        down_weight,
        proj_biases.reshape(-1, LANES),
        enc_weight,
        dec_weight,
        enc_bias,
    )
    if depth <= 4:
        dec_both, scale_wide, gathered, relu, upstream, small, active = joint(depth, *arguments, dec_bias[None])
    else:
        low, stream, enc_both, dec_both, dec_turned, shift_wide, scale_wide = front(*arguments)
        gathered, relu, upstream, small, active = forward(
            depth, low, enc_both, dec_turned, shift_wide, stream, scale_wide, dec_bias[None]
        )
    enc_grad, dec_grad, enc_bias_grad, small_sum, squares = backward(
        depth, upstream, gathered, relu, dec_both, scale_wide, active, small
    )
    return update(
        enc_grad,
        dec_grad,
        enc_bias_grad,
        small_sum,
        squares,
        enc_weight,
        enc_first,
        enc_second,
        dec_weight,
        dec_first,
        dec_second,
        enc_bias,
        enc_bias_first,
        enc_bias_second,
        dec_bias,
        dec_bias_first,
        dec_bias_second,
    )


def solution(mesh):
    split = P(("dp", "seq", "opt"), None)
    split_vector = P(("dp", "seq", "opt"))
    in_specs = (
        P("dp", ("seq", "opt")),
        P("dp", ("seq", "opt")),
        P(None, ("seq", "opt")),
        P(),
        P(),
        P(),
        P(),
        P(),
        P(),
        P(),
        split,
        split,
        split_vector,
        P(),
        split,
        split,
        split,
        split,
        split_vector,
        split_vector,
        P(),
        P(),
    )
    out_specs = (split,) * 6 + (split_vector,) * 3 + (P(),) * 5
    return jax.shard_map(
        functools.partial(body, mesh.shape["dp"]),
        mesh=mesh,
        in_specs=in_specs,
        out_specs=out_specs,
        check_vma=False,
    )
```

```python
import functools

import jax
import jax.numpy as jnp
import numpy as np
from jax import lax
from jax.experimental import pallas as pl
from jax.experimental.pallas import tpu as pltpu
from jax.sharding import PartitionSpec as P

HEAD = 64
ROT = 16
STEP = 4
RAMP = 80


LAYER_EPSILON = 1e-05
NORM_EPSILON = 1e-08
BETA_FIRST = 0.9
BETA_SECOND = 0.999
ADAM_EPSILON = 1e-08
RATE_MATRIX = 0.02
RATE_BIAS = 0.1
WEIGHT_DECAY = 0.01
CLIP_NORM = 1.0
SPARSITY_TOP = 5.0
COEFFICIENT = SPARSITY_TOP * min(1.0, STEP / RAMP)
LAST_LAST = (((1,), (1,)), ((), ()))
MESH = pl.DeviceIdType.MESH
ANY = pl.BlockSpec(memory_space=pl.ANY)
VMEM = pl.BlockSpec(memory_space=pltpu.VMEM)
LANES = 128


def adam_step(parameter, moment_one, moment_two, gradient, clip_scale, step_rate, decay_rate):
    gradient = gradient * clip_scale
    moment_one = BETA_FIRST * moment_one + (1.0 - BETA_FIRST) * gradient
    moment_two = BETA_SECOND * moment_two + (1.0 - BETA_SECOND) * gradient * gradient
    first_share, second_share = 1.0 / (1.0 - BETA_FIRST**STEP), 1.0 / (1.0 - BETA_SECOND**STEP)
    adjust = moment_one * first_share / (jnp.sqrt(moment_two * second_share) + ADAM_EPSILON)
    return (parameter - step_rate * (adjust + decay_rate * parameter), moment_one, moment_two)


def place_of(depth, layer, other):
    distance = jnp.abs(other - layer)
    margin = jnp.minimum(layer, depth - 1 - layer)
    near = jnp.where(other < layer, 2 * distance - 1, 2 * distance)
    return jnp.where(distance <= margin, near, distance + margin)


def layer_at(depth, layer, turn):
    margin = jnp.minimum(layer, depth - 1 - layer)
    near = jnp.where(turn % 2 == 1, layer - (turn + 1) // 2, layer + turn // 2)
    far = jnp.where(2 * layer < depth - 1, layer + turn - margin, layer - turn + margin)
    return jnp.where(turn <= 2 * margin, near, far)


def crosswise(turn):
    return (turn == 0) | (turn >= 3)


def slot_of(depth, turn, column):
    last = 4 * (depth - 1)
    own = jnp.maximum(4 * turn - 3, 0)
    diagonal = jnp.where(turn == depth - 1, last, jnp.where(turn == depth - 2, last + 1, 4 * turn + 4))
    return jnp.where(column == 0, own, jnp.where(column == 3, diagonal, 4 * turn + 1 + column))


def takers(depth, layer):
    return [
        (layer + 1, layer + 1 < depth),
        (layer - 1, layer >= 1),
        (layer * 0, layer == 2),
        (layer * 0 + depth - 1, layer == depth - 3),
    ]


def peers(depth):
    layer, row, column = lax.axis_index("dp"), lax.axis_index("seq"), lax.axis_index("opt")
    across = (layer, row, (column + 2) % 4)
    beside = (layer, 1 - row, column)
    partner = (layer, row, column + 1 - 2 * (column % 2))
    return (layer, row, column), across, beside, partner


def remote(source, target, send, receive, device):
    return pltpu.make_async_remote_copy(
        src_ref=source,
        dst_ref=target,
        send_sem=send,
        recv_sem=receive,
        device_id=device,
        device_id_type=MESH,
    )


def greet(devices):
    barrier = pltpu.get_barrier_semaphore()
    for device in devices:
        pl.semaphore_signal(barrier, inc=1, device_id=device, device_id_type=MESH)
    pl.semaphore_wait(barrier, len(devices))


def fold(values):
    total = values[:8]
    for first in range(8, values.shape[0], 8):
        total = total + values[first : first + 8]
    narrow = total[:, :LANES]
    for lane in range(LANES, values.shape[1], LANES):
        narrow = narrow + total[:, lane : lane + LANES]
    return narrow


class Gather:
    def __init__(self, depth, rows, held, send, receive, where):
        self.depth, self.rows, self.held = depth, rows, held
        self.send, self.receive = send, receive
        self.here, self.across, self.beside, _ = where

    def block(self, turn, column, part=None):
        first, rows = slot_of(self.depth, turn, column) * self.rows, self.rows
        if part is not None:
            rows = self.rows // 2
            first = first + part * rows
        return self.held.at[pl.ds(pl.multiple_of(first, rows), rows)]

    def device(self, layer):
        return (layer, self.here[1], self.here[2])

    def copy_along(self, turn, sign, part):
        layer = self.here[0] + sign
        source = layer_at(self.depth, self.here[0], turn)
        there = place_of(self.depth, layer, source)
        row, index = (part, turn) if sign == 1 else (part + 8, turn)
        return remote(
            self.block(turn, 0, part),
            self.block(there, 0, part),
            self.send.at[row, index],
            self.receive.at[part, there],
            self.device(layer),
        )

    def along(self, turn, act):
        source, layer = layer_at(self.depth, self.here[0], turn), self.here[0]
        for sign, onward in ((1, source <= layer), (-1, source >= layer)):

            @pl.when(onward & (layer + sign >= 0) & (layer + sign < self.depth))
            def _(sign=sign):
                for part in range(2):
                    act(self.copy_along(turn, sign, part))

    def copy_across(self, turn, part):
        return remote(
            self.block(turn, 0, part),
            self.block(turn, 1, part),
            self.send.at[2 + part, turn],
            self.receive.at[2 + part, turn],
            self.across,
        )

    def copy_beside(self, turn, part):
        return remote(
            self.block(turn, 0, part),
            self.block(turn, 2, part),
            self.send.at[4 + part, turn],
            self.receive.at[4 + part, turn],
            self.beside,
        )

    def pass_across(self, turn):
        return remote(
            self.block(turn, 2, 0), self.block(turn, 3, 0), self.send.at[6, turn], self.receive.at[6, turn], self.across
        )

    def pass_beside(self, turn):
        return remote(
            self.block(turn, 1, 1), self.block(turn, 3, 1), self.send.at[7, turn], self.receive.at[7, turn], self.beside
        )

    def pass_along(self, index, layer):
        turn = place_of(self.depth, layer, self.here[0])
        return remote(
            self.block(0, 3), self.block(turn, 3), self.send.at[10, index], self.receive.at[8, turn], self.device(layer)
        )

    def to_neighbours(self, turn):
        for part in range(2):
            self.copy_across(turn, 1 - part).start()
            self.copy_beside(turn, part).start()

    def open(self):
        self.to_neighbours(0)
        self.along(0, lambda copy: copy.start())

    def arrive(self, turn):
        for part in range(2):
            remote(
                self.block(0, 0, part),
                self.block(turn, 0, part),
                self.send.at[part, 0],
                self.receive.at[part, turn],
                self.across,
            ).wait_recv()
        self.along(turn, lambda copy: copy.start())

    def hand_on(self, turn):
        self.copy_across(turn, 1).wait_recv()

        @pl.when(crosswise(turn))
        def _():
            self.pass_beside(turn).start()

        self.copy_beside(turn, 0).wait_recv()

        @pl.when(crosswise(turn))
        def _():
            self.pass_across(turn).start()

        self.copy_across(turn, 0).wait_recv()
        self.copy_beside(turn, 1).wait_recv()

    def wait_diagonal(self, turn):
        @pl.when(crosswise(turn))
        def _():
            self.pass_across(turn).wait_recv()
            self.pass_beside(turn).wait_recv()

        @pl.when((turn == 1) | (turn == 2))
        def _():
            remote(
                self.block(0, 3), self.block(turn, 3), self.send.at[10, 0], self.receive.at[8, turn], self.across
            ).wait_recv()

        @pl.when(turn == 0)
        def _():
            for index, (layer, there) in enumerate(takers(self.depth, self.here[0])):

                @pl.when(there)
                def _(index=index, layer=layer):
                    self.pass_along(index, layer).start()

    def close(self):
        for index, (layer, there) in enumerate(takers(self.depth, self.here[0])):

            @pl.when(there)
            def _(index=index, layer=layer):
                self.pass_along(index, layer).wait_send()

        def done(turn, carry):
            self.along(turn, lambda copy: copy.wait_send())
            for part in range(2):
                self.copy_across(turn, part).wait_send()
                self.copy_beside(turn, part).wait_send()

            @pl.when(crosswise(turn))
            def _():
                self.pass_across(turn).wait_send()
                self.pass_beside(turn).wait_send()

            return carry

        lax.fori_loop(0, self.depth, done, 0)


def ids_kernel(ids_ref, docs_ref, ids_out, docs_out, ids_all, docs_all, load_sem, send, receive):
    group = ids_all.shape[0]
    layer, row, column = lax.axis_index("dp"), lax.axis_index("seq"), lax.axis_index("opt")
    here = row * 4 + column
    others = [(here + step) % group for step in range(group)]
    devices = [(layer, index // 4, index % 4) for index in others]
    loads = [
        pltpu.make_async_copy(ids_ref, ids_all.at[here], load_sem.at[0]),
        pltpu.make_async_copy(docs_ref, docs_all.at[here], load_sem.at[1]),
    ]
    for load in loads:
        load.start()
    greet(devices[1:])
    for load in loads:
        load.wait()
    copies = []
    for step in range(1, group):
        for kind, held in enumerate((ids_all, docs_all)):
            copies.append(
                remote(held.at[here], held.at[here], send.at[kind, step], receive.at[kind, step], devices[step])
            )
    for copy in copies:
        copy.start()
    for copy in copies:
        copy.wait()
    ids_out[...] = ids_all[...]
    docs_out[...] = docs_all[...]


def gather_ids(ids, docs, group):
    rows = ids.shape[1]
    dma = pltpu.SemaphoreType.DMA
    whole = jax.ShapeDtypeStruct((group, 1, rows), jnp.int32)
    return pl.pallas_call(
        ids_kernel,
        out_shape=(whole, whole),
        in_specs=[ANY] * 2,
        out_specs=(VMEM, VMEM),
        scratch_shapes=[
            pltpu.VMEM((group, 1, rows), jnp.int32),
            pltpu.VMEM((group, 1, rows), jnp.int32),
            dma((2,)),
            dma((2, group)),
            dma((2, group)),
        ],
        compiler_params=pltpu.CompilerParams(collective_id=3, has_side_effects=True, vmem_limit_bytes=60 * 2**20),
        name="gather_ids",
    )(ids, docs)


def pick_kernel(ids_ref, table_ref, picked, table, load_sem):
    group, _, rows = ids_ref.shape
    share, vocabulary = table.shape
    parts = 3 if vocabulary % (3 * LANES) == 0 else 1
    loads = [
        pltpu.make_async_copy(
            table_ref.at[:, pl.ds(part * (vocabulary // parts), vocabulary // parts)],
            table.at[:, pl.ds(part * (vocabulary // parts), vocabulary // parts)],
            load_sem.at[part],
        )
        for part in range(parts)
    ]
    for load in loads:
        load.start()
    lanes = lax.broadcasted_iota(jnp.int32, (share, LANES), 1)
    for load in loads:
        load.wait()

    def some(part, carry):
        source, first = part // (rows // LANES), part % (rows // LANES) * LANES
        found = None
        for place in range(LANES):
            token = ids_ref[source, 0, first + place]
            start = lax.bitwise_and(token, -LANES)
            tile = table[:, pl.ds(pl.multiple_of(start, LANES), LANES)].astype(jnp.float32)
            moved = pltpu.roll(tile, lax.bitwise_and(place - token, LANES - 1), 1)
            found = moved if found is None else jnp.where(lanes >= place, moved, found)
        picked[source, :, pl.ds(pl.multiple_of(first, LANES), LANES)] = found.astype(jnp.bfloat16)
        return carry

    lax.fori_loop(0, group * rows // LANES, some, 0)


def pick(ids, table):
    group, _, rows = ids.shape
    share = table.shape[0]
    return pl.pallas_call(
        pick_kernel,
        out_shape=jax.ShapeDtypeStruct((group, share, rows), jnp.bfloat16),
        in_specs=[pl.BlockSpec(memory_space=pltpu.SMEM), ANY],
        out_specs=VMEM,
        scratch_shapes=[pltpu.VMEM(table.shape, jnp.bfloat16), pltpu.SemaphoreType.DMA((3,))],
        compiler_params=pltpu.CompilerParams(vmem_limit_bytes=60 * 2**20),
        name="pick_features",
    )(ids, table)


def front_kernel(
    picked_ref,
    docs_ref,
    gains_ref,
    shifts_ref,
    qkv_ref,
    out_ref,
    up_ref,
    down_ref,
    bias_ref,
    turn_ref,
    enc_ref,
    dec_ref,
    shift_ref,
    low_ref,
    stream_ref,
    enc_out,
    dec_out,
    turned_out,
    shift_out,
    scale_out,
    docs_all,
    gains,
    shifts,
    qkv,
    out,
    up,
    down,
    bias,
    turn,
    picked,
    features,
    turned,
    heads,
    mixed_turned,
    fed,
    enc_full,
    dec_full,
    shift_all,
    enc,
    dec,
    dec_turned,
    shift_wide,
    scale_wide,
    load_sem,
    store_sem,
    send,
    receive,
    pair_send,
    pair_receive,
    depth=1,
):
    group, share, rows = picked.shape
    mine = enc_full.shape[0]
    dense = mine // LANES
    width = gains.shape[1]
    ff_width = up.shape[1]
    layer, row, column = lax.axis_index("dp"), lax.axis_index("seq"), lax.axis_index("opt")
    here = row * 4 + column

    def member(index):
        return (layer, index // 4, index % 4)

    others = [(here + step) % group for step in range(group)]
    first_place = pl.multiple_of(here * rows, rows)
    loads = [
        pltpu.make_async_copy(picked_ref, picked, load_sem.at[0]),
        pltpu.make_async_copy(docs_ref, docs_all, load_sem.at[1]),
        pltpu.make_async_copy(gains_ref, gains, load_sem.at[2]),
        pltpu.make_async_copy(shifts_ref, shifts, load_sem.at[3]),
        pltpu.make_async_copy(bias_ref, bias, load_sem.at[4]),
        pltpu.make_async_copy(turn_ref.at[:, pl.ds(first_place, rows)], turn, load_sem.at[5]),
        pltpu.make_async_copy(qkv_ref, qkv, load_sem.at[6]),
        pltpu.make_async_copy(up_ref, up, load_sem.at[7]),
        pltpu.make_async_copy(down_ref, down, load_sem.at[8]),
        pltpu.make_async_copy(out_ref, out, load_sem.at[9]),
        pltpu.make_async_copy(enc_ref, enc_full, load_sem.at[10]),
        pltpu.make_async_copy(dec_ref, dec_full, load_sem.at[11]),
        pltpu.make_async_copy(shift_ref, shift_all.at[column % 2], load_sem.at[12]),
    ]
    for load in loads:
        load.start()
    greet([member(index) for index in others[1:]] + [((layer + step) % depth, row, column) for step in range(1, depth)])
    loads[0].wait()

    def copy_features(step):
        return remote(
            picked.at[others[step]],
            features.at[pl.ds(pl.multiple_of(here * share, share), share)],
            send.at[0, step],
            receive.at[0, step],
            member(others[step]),
        )

    def copy_heads(step):
        return remote(
            turned.at[others[step]], heads.at[here], send.at[1, step], receive.at[1, step], member(others[step])
        )

    def copy_mixed(index, source):
        return remote(
            picked.at[index],
            mixed_turned.at[pl.ds(pl.multiple_of(source * HEAD, HEAD), HEAD)],
            send.at[2, index],
            receive.at[2, source],
            member(index),
        )

    for step in range(1, group):
        copy_features(step).start()

    partner = (layer, row, column + 1 - 2 * (column % 2))
    own = pl.ds(pl.multiple_of(column % 2 * mine, mine), mine)
    for load in loads[10:]:
        load.wait()
    shared = []
    for kind, (full, low) in enumerate(((dec_full, dec), (enc_full, enc))):

        def cast(part, carry, full=full, low=low):
            start = pl.multiple_of(part * 256, 256)
            low[pl.ds(pl.multiple_of(column % 2 * mine + start, 256), 256)] = full[pl.ds(start, 256)].astype(
                jnp.bfloat16
            )
            return carry

        lax.fori_loop(0, mine // 256, cast, 0)
        shared.append(remote(low.at[own], low.at[own], pair_send.at[kind], pair_receive.at[kind], partner))
        shared[-1].start()
    spot = shift_all.at[column % 2]
    shared.append(remote(spot, spot, pair_send.at[2], pair_receive.at[2], partner))
    shared[-1].start()
    features[pl.ds(pl.multiple_of(here * share, share), share)] = picked[here]
    for load in loads[1:10]:
        load.wait()
    for step in range(1, group):
        copy_features(step).wait_recv()

    residual = features[...].astype(jnp.float32).T
    center = residual - jnp.mean(residual, axis=1, keepdims=True)
    variance = jnp.mean(center * center, axis=1, keepdims=True)
    unit = center * lax.rsqrt(variance + LAYER_EPSILON)
    first_norm = (unit * gains[0:1] + shifts[0:1]).astype(jnp.bfloat16)
    second_norm = (unit * gains[1:2] + shifts[1:2]).astype(jnp.bfloat16)

    def bias_row(first, count):
        lines = range(first // LANES, (first + count) // LANES)
        return jnp.concatenate([bias[line : line + 1] for line in lines], axis=1)

    half_rot = ROT // 2
    cosine, sine = turn[:half_rot], turn[half_rot:]
    for first in range(0, 3 * width, 2 * LANES):
        chunk = (
            jnp.dot(first_norm, qkv[:, first : first + 2 * LANES], preferred_element_type=jnp.float32)
            + bias_row(first, 2 * LANES)
        ).T
        for inner in range(0, 2 * LANES, HEAD):
            kind, head = (first + inner) // width, (first + inner) % width // HEAD
            values = chunk[inner : inner + HEAD]
            if kind < 2:
                left, right = values[:half_rot], values[half_rot:ROT]
                values = jnp.concatenate(
                    [left * cosine - right * sine, right * cosine + left * sine, values[ROT:]], axis=0
                )
            turned[head, kind * HEAD : (kind + 1) * HEAD] = values.astype(jnp.bfloat16)
    for step in range(1, group):
        copy_heads(step).start()
    heads[here] = turned[here]

    feed = residual + bias_row(4 * width + ff_width, width) + bias_row(3 * width, width)
    for first in range(0, ff_width, 512):
        inner = (
            jnp.dot(second_norm, up[:, first : first + 512], preferred_element_type=jnp.float32)
            + bias_row(4 * width + first, 512)
        )
        hidden = (0.5 * inner * (1.0 + lax.erf(inner * (0.5**0.5)))).astype(jnp.bfloat16)
        feed = feed + jnp.dot(hidden, down[first : first + 512], preferred_element_type=jnp.float32)
    fed[...] = feed

    for copy in shared:
        copy.wait()

    def widen(part, carry):
        start = pl.multiple_of(part * LANES, LANES)
        span = pl.ds(start, LANES)
        values = dec[span].astype(jnp.float32)
        dec_turned[:, span] = values.T.astype(jnp.bfloat16)
        norms = jnp.sqrt(jnp.sum(values * values, axis=1, keepdims=True) + NORM_EPSILON)
        scale_wide[span] = jnp.broadcast_to(COEFFICIENT * norms, (LANES, LANES))
        shift_wide[span] = jnp.broadcast_to(shift_all[part // dense, pl.ds(part % dense, 1)], (LANES, LANES)).T
        return carry

    lax.fori_loop(0, 2 * dense, widen, 0)
    stores = [
        pltpu.make_async_copy(held, target, store_sem.at[index])
        for index, (held, target) in enumerate(
            (
                (enc, enc_out),
                (dec, dec_out),
                (dec_turned, turned_out),
                (shift_wide, shift_out),
                (scale_wide, scale_out),
            )
        )
        if target is not None
    ]
    for store in stores:
        store.start()

    for step in range(1, group):
        copy_features(step).wait_send()
    query_place = lax.broadcasted_iota(jnp.int32, (rows, rows), 0)
    key_place = lax.broadcasted_iota(jnp.int32, (rows, rows), 1)
    causal = key_place <= query_place
    scale = HEAD ** (-0.5)
    values_of = []
    for index in range(group):

        @pl.when(here != index)
        def _():
            arrived = receive.at[1, (here + group - index) % group]
            remote(turned.at[index], heads.at[index], send.at[1, 0], arrived, member(others[1])).wait_recv()

        values_of.append(heads[index, 2 * HEAD :].astype(jnp.float32).T.astype(jnp.bfloat16))
        query = heads[index, :HEAD].astype(jnp.float32).T.astype(jnp.bfloat16)
        own_docs = jnp.broadcast_to(docs_all[index].astype(jnp.float32), (LANES, rows)).T
        own_docs = jnp.concatenate([own_docs] * (rows // LANES), axis=1)
        scores = []
        for other in range(index + 1):
            score = jnp.dot(query, heads[other, HEAD : 2 * HEAD], preferred_element_type=jnp.float32)
            allowed = own_docs == docs_all[other].astype(jnp.float32)
            if other == index:
                allowed = allowed & causal
            scores.append(jnp.where(allowed, score * scale, -1e30))
        peak = scores[0]
        for score in scores[1:]:
            peak = jnp.maximum(peak, score)
        peak = jnp.max(peak, axis=1, keepdims=True)
        weights = [jnp.exp(score - peak) for score in scores]
        total = weights[0]
        for weight in weights[1:]:
            total = total + weight
        inverse = 1.0 / jnp.sum(total, axis=1, keepdims=True)
        mixed = None
        for other in range(index + 1):
            probs = (weights[other] * inverse).astype(jnp.bfloat16)
            term = jnp.dot(probs, values_of[other], preferred_element_type=jnp.float32)
            mixed = term if mixed is None else mixed + term
        mixed = mixed.T
        picked[index] = mixed.astype(jnp.bfloat16)

        @pl.when(here != index)
        def _():
            copy_mixed(index, here).start()

        @pl.when(here == index)
        def _():
            mixed_turned[pl.ds(pl.multiple_of(here * HEAD, HEAD), HEAD)] = picked[index]

    for step in range(1, group):
        copy_mixed(step, others[step]).wait_recv()
    mixed = mixed_turned[...].astype(jnp.float32).T.astype(jnp.bfloat16)
    stream = fed[...] + jnp.dot(mixed, out[...], preferred_element_type=jnp.float32)
    stream_ref[...] = stream
    low_ref[...] = stream.astype(jnp.bfloat16)
    for step in range(1, group):
        copy_heads(step).wait_send()
    for index in range(group):

        @pl.when(here != index)
        def _():
            copy_mixed(index, here).wait_send()

    for store in stores:
        store.wait()


def rotary_table(context_len):
    half_rot = ROT // 2
    frequency = np.power(np.float32(10000.0), np.float32(-2.0) * np.arange(half_rot, dtype=np.float32) / np.float32(ROT))
    angles = frequency.astype(np.float32)[:, None] * np.arange(context_len, dtype=np.float32)[None, :]
    return np.concatenate([np.cos(angles.astype(np.float64)), np.sin(angles.astype(np.float64))]).astype(np.float32)


def front_scratch(picked, gains, qkv, out, up, down, bias, enc):
    group, share, rows = picked.shape
    width, mine, ff_width = gains.shape[1], enc.shape[0], up.shape[1]
    bf16, f32 = jnp.bfloat16, jnp.float32
    dma = pltpu.SemaphoreType.DMA
    return [
        pltpu.VMEM((group, 1, rows), jnp.int32),
        pltpu.VMEM((2, width), f32),
        pltpu.VMEM((2, width), f32),
        pltpu.VMEM((width, 3 * width), bf16),
        pltpu.VMEM((width, width), bf16),
        pltpu.VMEM((width, ff_width), bf16),
        pltpu.VMEM((ff_width, width), bf16),
        pltpu.VMEM(bias.shape, f32),
        pltpu.VMEM((ROT, rows), f32),
        pltpu.VMEM((group, share, rows), bf16),
        pltpu.VMEM((width, rows), bf16),
        pltpu.VMEM((group, 3 * HEAD, rows), bf16),
        pltpu.VMEM((group, 3 * HEAD, rows), bf16),
        pltpu.VMEM((width, rows), bf16),
        pltpu.VMEM((rows, width), f32),
        pltpu.VMEM((mine, width), f32),
        pltpu.VMEM((mine, width), f32),
        pltpu.VMEM((2, mine // LANES, LANES), f32),
        pltpu.VMEM((2 * mine, width), bf16),
        pltpu.VMEM((2 * mine, width), bf16),
        pltpu.VMEM((width, 2 * mine), bf16),
        pltpu.VMEM((2 * mine, LANES), f32),
        pltpu.VMEM((2 * mine, LANES), f32),
        dma((13,)),
        dma((5,)),
        dma((3, group)),
        dma((3, group)),
        dma((3,)),
        dma((3,)),
    ]


def front(picked, docs, gains, shifts, qkv, out, up, down, bias, enc, dec, shift):
    group, share, rows = picked.shape
    width = gains.shape[1]
    ff_width = up.shape[1]
    mine = enc.shape[0]
    shift = shift.reshape(mine // LANES, LANES)
    bf16, f32 = jnp.bfloat16, jnp.float32
    dma = pltpu.SemaphoreType.DMA
    return pl.pallas_call(
        front_kernel,
        out_shape=(
            jax.ShapeDtypeStruct((rows, width), bf16),
            jax.ShapeDtypeStruct((rows, width), f32),
            jax.ShapeDtypeStruct((2 * mine, width), bf16),
            jax.ShapeDtypeStruct((2 * mine, width), bf16),
            jax.ShapeDtypeStruct((width, 2 * mine), bf16),
            jax.ShapeDtypeStruct((2 * mine, LANES), f32),
            jax.ShapeDtypeStruct((2 * mine, LANES), f32),
        ),
        in_specs=[ANY] * 13,
        out_specs=(VMEM, VMEM) + (ANY,) * 5,
        scratch_shapes=front_scratch(picked, gains, qkv, out, up, down, bias, enc),
        compiler_params=pltpu.CompilerParams(
            collective_id=2, has_side_effects=True, vmem_limit_bytes=60 * 2**20
        ),
        cost_estimate=pl.CostEstimate(flops=2 * 10**9, bytes_accessed=14 * 10**6, transcendentals=2 * 10**6),
        name="front_part",
    )(picked, docs, gains, shifts, qkv, out, up, down, bias, jnp.asarray(rotary_table(group * rows)), enc, dec, shift)


def forward_kernel(
    depth,
    own_ref,
    enc_ref,
    dec_ref,
    bias_ref,
    stream_ref,
    scale_ref,
    dec_bias_ref,
    gathered_ref,
    relu_ref,
    upstream_ref,
    small_ref,
    total_ref,
    recon_ref,
    stream,
    scale,
    held,
    enc,
    dec,
    bias,
    staged,
    parts,
    own_diagonal,
    send_zero,
    send_one,
    send_two,
    send_three,
    got_zero,
    got_one,
    got_two,
    got_three,
    load_sem,
    relu_sem,
    held_sem,
    send,
    receive,
    sum_send,
    sum_receive,
    ready=False,
):
    rows = upstream_ref.shape[0]
    entries = enc.shape[0]
    width = held.shape[1]
    half = width // 2
    piece = min(entries, 256)
    where = peers(depth)
    (layer, row, place), across, beside, _ = where
    inner = (layer >= 1) & (layer < depth - 1)
    others = [((layer + step) % depth, row, place) for step in range(1, depth)]
    loads = []
    if not ready:
        loads = [
            pltpu.make_async_copy(own_ref, held.at[pl.ds(0, rows)], load_sem.at[0]),
            pltpu.make_async_copy(enc_ref, enc, load_sem.at[1]),
            pltpu.make_async_copy(bias_ref, bias, load_sem.at[2]),
            pltpu.make_async_copy(dec_ref, dec, load_sem.at[3]),
            pltpu.make_async_copy(stream_ref, stream, load_sem.at[4]),
            pltpu.make_async_copy(scale_ref, scale, load_sem.at[5]),
        ]
        for load in loads:
            load.start()
        greet(others + [across, beside])
        loads[0].wait()
    gather = Gather(depth, rows, held, send, receive, where)
    gather.open()
    total_ref[...] = jnp.zeros_like(total_ref)
    for load in loads[1:]:
        load.wait()

    def part_slot(turn):
        return jnp.where(turn <= 1, 4 + turn, turn % 4)

    def copy_zero(turn):
        layer_there = layer_at(depth, layer, turn)
        index = jnp.where(
            jnp.abs(layer_there - layer) == 1,
            jnp.where(layer > layer_there, 0, 1),
            jnp.where(layer == 0, 2, 3),
        )
        return remote(
            send_zero.at[turn - 1],
            got_zero.at[index],
            sum_send.at[5, turn],
            sum_receive.at[5, index],
            (layer_there, row, place),
        )

    def one_slot(turn):
        return jnp.where(turn == 0, 2, turn % 2)

    def copy_one(turn, part):
        source = send_one.at[one_slot(turn), pl.ds(part * half, half)]
        device = beside if part else across
        return remote(source, got_one.at[part, turn], sum_send.at[part, turn], sum_receive.at[part, turn], device)

    def two_slot(turn):
        return jnp.where(turn <= 1, 3 + turn, turn % 3)

    def copy_two(turn, part, side):
        device = beside if part else across
        span = pl.ds(side * half, half)
        return remote(
            send_two.at[part, two_slot(turn), span],
            got_two.at[part, turn, span],
            sum_send.at[6 + 2 * part + side, turn],
            sum_receive.at[6 + 2 * part + side, turn],
            device,
        )

    def each_two(turn, act):
        for part in range(2):
            for side in range(2):
                act(copy_two(turn, part, side))

    def copy_three(turn):
        layer_there = layer_at(depth, layer, turn)
        index = place_of(depth, layer_there, layer)
        return remote(
            send_three.at[turn],
            got_three.at[index],
            sum_send.at[4, turn],
            sum_receive.at[4, index],
            (layer_there, row, place),
        )

    def copy_relu(order):
        first = slot_of(depth, order // 4, order % 4) * rows
        return pltpu.make_async_copy(
            staged.at[order % 2],
            relu_ref.at[:, pl.ds(pl.multiple_of(first, rows), rows)],
            relu_sem.at[order % 2],
        )

    def copy_held(step):
        span = pl.ds(pl.multiple_of(step * 4 * rows, 4 * rows), 4 * rows)
        return pltpu.make_async_copy(held.at[span], gathered_ref.at[span], held_sem.at[step])

    def sum_one(turn, value):
        @pl.when(turn >= 5)
        def _():
            copy_one(turn - 2, 0).wait_send()
            copy_one(turn - 2, 1).wait_send()

        send_one[one_slot(turn)] = value.astype(jnp.bfloat16)
        copy_one(turn, 0).start()
        copy_one(turn, 1).start()

    def send_half(turn, part, side, extra=None):
        span = pl.ds(side * half, half)
        value = parts[1 + part, part_slot(turn), span]
        if extra is not None:
            value = value + extra.astype(jnp.float32)
        send_two[part, two_slot(turn), span] = value.astype(jnp.bfloat16)
        copy_two(turn, part, side).start()

    def sum_two_own(turn):
        @pl.when(turn >= 5)
        def _():
            each_two(turn - 3, lambda copy: copy.wait_send())

        send_half(turn, 1, 1)
        send_half(turn, 0, 0)

    def sum_two(turn):
        @pl.when(crosswise(turn))
        def _():
            copy_one(turn, 0).wait_recv()
            send_half(turn, 1, 0, got_one[0, turn])
            copy_one(turn, 1).wait_recv()
            send_half(turn, 0, 1, got_one[1, turn])

        @pl.when((turn == 1) | (turn == 2))
        def _():
            send_half(turn, 1, 0)
            send_half(turn, 0, 1)

    def column_sum(turn):
        each_two(turn, lambda copy: copy.wait_recv())
        return parts[0, part_slot(turn)] + got_two[0, turn].astype(jnp.float32) + got_two[1, turn].astype(jnp.float32)

    def sum_three(turn):
        send_three[turn] = column_sum(turn).astype(jnp.bfloat16)
        copy_three(turn).start()

    def one_block(order, carry):
        turn, column = order // 4, order % 4

        @pl.when(column == 1)
        def _():
            gather.hand_on(turn)

        @pl.when(column == 3)
        def _():
            gather.wait_diagonal(turn)

        @pl.when((order == 3) & jnp.logical_not(inner))
        def _():
            gather.arrive(2)

        @pl.when(order == 3)
        def _():
            gather.to_neighbours(2)

        @pl.when((column == 2) & (turn >= 1) & (turn + 2 < depth))
        def _():
            @pl.when(jnp.logical_not(inner) | (turn >= 2))
            def _():
                gather.arrive(turn + 2)

            gather.to_neighbours(turn + 2)

        @pl.when(order >= 2)
        def _():
            copy_relu(order - 2).wait()

        first_row = slot_of(depth, turn, column) * rows
        block = held[pl.ds(pl.multiple_of(first_row, rows), rows)]
        low = []
        for first in range(0, entries, piece):
            span = pl.ds(first, piece)
            shift = bias[span]
            pre = lax.dot_general(enc[span], block, LAST_LAST, preferred_element_type=jnp.float32)
            positive = jnp.maximum(pre + jnp.concatenate([shift] * (rows // LANES), axis=1), 0.0)
            staged[order % 2, span] = positive
            active = positive * positive
            folded = active[:, :LANES]
            for lane in range(LANES, rows, LANES):
                folded = folded + active[:, lane : lane + LANES]
            total_ref[span] += folded
            low.append(active.astype(jnp.bfloat16))
        recon = jnp.dot(dec[...], jnp.concatenate(low, axis=0), preferred_element_type=jnp.float32)
        copy_relu(order).start()

        @pl.when(column < 3)
        def _():
            parts[column, part_slot(turn)] = recon

        @pl.when((column == 3) & (turn == 0))
        def _():
            own_diagonal[...] = recon

        @pl.when((column == 3) & (turn >= 3))
        def _():
            sum_one(turn, recon)

        @pl.when((column == 3) & ((turn == 1) | (turn == 2)))
        def _():
            send_zero[turn - 1] = recon.astype(jnp.bfloat16)
            copy_zero(turn).start()

        @pl.when(order == 0)
        def _():
            gather.arrive(1)

        @pl.when((order == 0) & inner)
        def _():
            gather.arrive(2)

        @pl.when(order == 0)
        def _():
            gather.to_neighbours(1)

        @pl.when((order == 2) & inner)
        def _():
            gather.arrive(3)

        @pl.when((column == 1) & (turn >= 4))
        def _():
            sum_two_own(turn - 2)
            sum_two(turn - 2)

        @pl.when((column == (1 if depth == 4 else 2)) & (turn == depth - 1))
        def _():
            sum_two_own(depth - 2)
            sum_two(depth - 2)

        @pl.when((column == 3) & (turn >= 5))
        def _():
            sum_three(turn - 3)

        return carry

    lax.fori_loop(0, 4 * depth, one_block, 0)
    for step in range(depth):
        copy_held(step).start()
    sum_two_own(depth - 1)
    if depth > 4:
        sum_three(depth - 3)
    sum_two(depth - 1)
    sum_two_own(1)
    sum_two(1)
    sum_three(depth - 2)
    for index, (_, there) in enumerate(takers(depth, layer)):

        @pl.when(there)
        def _(index=index):
            remote(
                send_zero.at[0], got_zero.at[index], sum_send.at[5, 0], sum_receive.at[5, index], across
            ).wait_recv()
            own_diagonal[...] += got_zero[index].astype(jnp.float32)

    sum_one(0, own_diagonal[...])
    sum_two_own(0)
    sum_three(depth - 1)
    sum_three(1)
    sum_two(0)
    recon_ref[...] = column_sum(0)
    for turn in range(1, depth):
        remote(
            send_three.at[turn], got_three.at[turn], sum_send.at[4, turn], sum_receive.at[4, turn], across
        ).wait_recv()
        recon_ref[...] += got_three[turn].astype(jnp.float32)
    error = recon_ref[...].T + dec_bias_ref[...] - stream[...]
    upstream = (2.0 * error).astype(jnp.bfloat16)
    upstream_ref[...] = upstream
    loss = fold(error * error)
    weighted = total_ref[...] * scale[...]
    loss = loss + fold(weighted)
    small_ref[...] = jnp.zeros_like(small_ref)
    column_sums = jnp.sum(upstream.astype(jnp.float32), axis=0, keepdims=True)
    lines = width // LANES
    for line in range(lines):
        small_ref[line : line + 1] = column_sums[:, line * LANES : (line + 1) * LANES]
    small_ref[lines : lines + 1] = jnp.sum(loss, axis=0, keepdims=True)
    gather.close()
    for turn in [0] + list(range(max(depth - 2, 3), depth)):
        for part in range(2):
            copy_one(turn, part).wait_send()
    for turn in [0, 1] + list(range(max(depth - 3, 2), depth)):
        each_two(turn, lambda copy: copy.wait_send())
    for turn in range(1, depth):
        copy_three(turn).wait_send()
    for turn in (1, 2):
        copy_zero(turn).wait_send()
    copy_relu(4 * depth - 2).wait()
    copy_relu(4 * depth - 1).wait()
    for step in range(depth):
        copy_held(step).wait()


def forward_scratch(depth, rows, width, entries):
    bf16, f32 = jnp.bfloat16, jnp.float32
    dma = pltpu.SemaphoreType.DMA
    return [
        pltpu.VMEM((width, rows), f32),
        pltpu.VMEM((rows, width), f32),
        pltpu.VMEM((entries, LANES), f32),
        pltpu.VMEM((depth * 4 * rows, width), bf16),
        pltpu.VMEM((entries, width), bf16),
        pltpu.VMEM((width, entries), bf16),
        pltpu.VMEM((entries, LANES), f32),
        pltpu.VMEM((2, entries, rows), f32),
        pltpu.VMEM((3, 6, width, rows), f32),
        pltpu.VMEM((width, rows), f32),
        pltpu.VMEM((2, width, rows), bf16),
        pltpu.VMEM((3, width, rows), bf16),
        pltpu.VMEM((2, 5, width, rows), bf16),
        pltpu.VMEM((depth, width, rows), bf16),
        pltpu.VMEM((4, width, rows), bf16),
        pltpu.VMEM((2, depth, width // 2, rows), bf16),
        pltpu.VMEM((2, depth, width, rows), bf16),
        pltpu.VMEM((depth, width, rows), bf16),
        dma((6,)),
        dma((2,)),
        dma((depth,)),
        dma((11, max(depth, 4))),
        dma((9, max(depth, 4))),
        dma((10, max(depth, 4))),
        dma((10, max(depth, 4))),
    ]


def forward(depth, own, enc, dec_turned, bias, stream, scale, dec_bias):
    rows, width = own.shape
    entries = enc.shape[0]
    bf16, f32 = jnp.bfloat16, jnp.float32
    dma = pltpu.SemaphoreType.DMA
    return pl.pallas_call(
        functools.partial(forward_kernel, depth),
        out_shape=(
            jax.ShapeDtypeStruct((depth * 4 * rows, width), bf16),
            jax.ShapeDtypeStruct((entries, depth * 4 * rows), f32),
            jax.ShapeDtypeStruct((rows, width), bf16),
            jax.ShapeDtypeStruct((8, LANES), f32),
            jax.ShapeDtypeStruct((entries, LANES), f32),
        ),
        in_specs=[ANY] * 6 + [VMEM],
        out_specs=(ANY, ANY, VMEM, VMEM, VMEM),
        scratch_shapes=forward_scratch(depth, rows, width, entries),
        compiler_params=pltpu.CompilerParams(
            collective_id=0, has_side_effects=True, vmem_limit_bytes=60 * 2**20
        ),
        cost_estimate=pl.CostEstimate(
            flops=16 * depth * rows * entries * width, bytes_accessed=16 * depth * rows * entries, transcendentals=0
        ),
        name="forward_blocks",
    )(own, enc, dec_turned, bias, stream, scale, dec_bias)


def joint_kernel(depth, *refs):
    given, dec_bias_ref = refs[:13], refs[13]
    dec_out, scale_out, gathered_ref, relu_ref, upstream_ref, small_ref, total_ref = refs[14:21]
    first, second = refs[21:50], refs[50:]
    recon_ref, stream, held, *rest = second
    rows = upstream_ref.shape[0]
    enc, dec_turned, shift_wide, scale_wide = first[18], first[20], first[21], first[22]
    front_kernel(
        *given, held.at[pl.ds(0, rows)], stream, None, dec_out, None, None, scale_out, *first, depth=depth
    )
    forward_kernel(
        depth,
        *([None] * 6),
        dec_bias_ref,
        gathered_ref,
        relu_ref,
        upstream_ref,
        small_ref,
        total_ref,
        recon_ref,
        stream,
        scale_wide,
        held,
        enc,
        dec_turned,
        shift_wide,
        *rest,
        ready=True,
    )


def joint(depth, picked, docs, gains, shifts, qkv, out, up, down, bias, enc, dec, shift, dec_bias):
    group, share, rows = picked.shape
    width, mine = gains.shape[1], enc.shape[0]
    entries = 2 * mine
    bf16, f32 = jnp.bfloat16, jnp.float32
    first = front_scratch(picked, gains, qkv, out, up, down, bias, enc)
    second = forward_scratch(depth, rows, width, entries)
    second = second[:2] + second[3:4] + second[7:]
    return pl.pallas_call(
        functools.partial(joint_kernel, depth),
        out_shape=(
            jax.ShapeDtypeStruct((entries, width), bf16),
            jax.ShapeDtypeStruct((entries, LANES), f32),
            jax.ShapeDtypeStruct((depth * 4 * rows, width), bf16),
            jax.ShapeDtypeStruct((entries, depth * 4 * rows), f32),
            jax.ShapeDtypeStruct((rows, width), bf16),
            jax.ShapeDtypeStruct((8, LANES), f32),
            jax.ShapeDtypeStruct((entries, LANES), f32),
        ),
        in_specs=[ANY] * 13 + [VMEM],
        out_specs=(ANY, ANY, ANY, ANY, VMEM, VMEM, VMEM),
        scratch_shapes=first + second,
        compiler_params=pltpu.CompilerParams(
            collective_id=2, has_side_effects=True, vmem_limit_bytes=62 * 2**20
        ),
        cost_estimate=pl.CostEstimate(
            flops=16 * depth * rows * entries * width, bytes_accessed=48 * 10**6, transcendentals=2 * 10**6
        ),
        name="joint_part",
    )(
        picked,
        docs,
        gains,
        shifts,
        qkv,
        out,
        up,
        down,
        bias,
        jnp.asarray(rotary_table(group * rows)),
        enc,
        dec,
        shift.reshape(mine // LANES, LANES),
        dec_bias,
    )


def backward_kernel(
    depth,
    everyone,
    own_ref,
    gathered_ref,
    relu_ref,
    dec_ref,
    scale_ref,
    active_ref,
    small_ref,
    enc_out,
    dec_out,
    bias_out,
    small_out,
    squares_out,
    held,
    inputs,
    dec,
    scale,
    tile,
    held_last,
    inputs_last,
    relu_last,
    enc_sum,
    dec_sum,
    bias_sum,
    enc_got,
    dec_got,
    bias_got,
    active,
    active_got,
    low,
    small,
    two,
    two_got,
    sums,
    sums_got,
    load_sem,
    tile_sem,
    store_sem,
    send,
    receive,
    pair_send,
    pair_receive,
    last_send,
    last_receive,
    all_send,
    all_receive,
):
    rows = own_ref.shape[0]
    entries = dec.shape[0]
    mine = entries // 2
    piece = tile.shape[1]
    tiles = entries // piece
    where = peers(depth)
    (layer, row, column), _, _, partner = where
    core = column % 2
    inner = (layer >= 1) & (layer < depth - 1)
    loads = [
        pltpu.make_async_copy(own_ref, held.at[pl.ds(0, rows)], load_sem.at[0]),
        pltpu.make_async_copy(dec_ref, dec, load_sem.at[1]),
        pltpu.make_async_copy(scale_ref, scale, load_sem.at[2]),
        pltpu.make_async_copy(gathered_ref, inputs, load_sem.at[3]),
        pltpu.make_async_copy(active_ref, active, load_sem.at[4]),
        pltpu.make_async_copy(small_ref, small, load_sem.at[5]),
    ]
    for load in loads:
        load.start()

    def place(turn):
        return (turn + (1 - core) * (tiles // 2)) % tiles

    def group_of(group):
        if group == depth - 1:
            return (4 * group + 1) * rows, 3 * rows
        if group == depth:
            return (4 * group - 4) * rows, rows
        return 4 * group * rows, 4 * rows

    def tile_slot(group, turn):
        return (group * tiles + turn - (tiles // 2 if group is depth else 0)) % 2

    def copy_tile(group, start, size, turn):
        slot = tile_slot(group, turn)
        first = pl.multiple_of(place(turn) * piece, piece)
        return pltpu.make_async_copy(
            relu_ref.at[pl.ds(first, piece), pl.ds(pl.multiple_of(start, rows), size)],
            tile.at[slot, :, pl.ds(0, size)],
            tile_sem.at[slot],
        )

    copy_tile(0, *group_of(0), 0).start()

    others = [
        ((layer + dz) % depth, (row + dy) % 2, (column + 2 * dx) % 4)
        for dz in range(depth)
        for dy in range(2)
        for dx in range(2)
    ]
    greet(others[1:] + [partner])
    loads[0].wait()
    gather = Gather(depth, rows, held, send, receive, where)
    gather.open()
    for load in loads[1:]:
        load.wait()

    def sums_copy(index):
        return remote(
            sums, sums_got.at[index], all_send.at[index], all_receive.at[index], others[index]
        )

    def two_copy(kind):
        return remote(
            two.at[kind], two_got.at[kind], last_send.at[3 + kind], last_receive.at[3 + kind], partner
        )

    two[0] = small[...]
    two_copy(0).start()

    theirs = (1 - core) * mine
    active_copy = remote(
        active.at[pl.ds(pl.multiple_of(theirs, mine), mine)], active_got, pair_send.at[3, 0], pair_receive.at[3, 0], partner
    )
    active_copy.start()
    last = pl.ds(4 * (depth - 1) * rows, rows)
    last_copies = [
        remote(
            relu_ref.at[pl.ds(pl.multiple_of(theirs, mine), mine), last],
            relu_last,
            last_send.at[0],
            last_receive.at[0],
            partner,
        ),
        remote(inputs.at[last], inputs_last, last_send.at[1], last_receive.at[1], partner),
        remote(held.at[last], held_last, last_send.at[2], last_receive.at[2], partner),
    ]
    last_copies[0].start()
    last_copies[1].start()
    enc_sum[...] = jnp.zeros_like(enc_sum)
    dec_sum[...] = jnp.zeros_like(dec_sum)
    bias_sum[...] = jnp.zeros_like(bias_sum)

    def pair_copy(kind, turn):
        source, target = ((low.at[0], enc_got), (low.at[1], dec_got), (bias_sum, bias_got))[kind]
        there = pl.ds(pl.multiple_of(turn * piece, piece), piece)
        return remote(
            source.at[pl.ds(pl.multiple_of(theirs + turn * piece, piece), piece) if kind == 2 else there],
            target.at[there],
            pair_send.at[kind, turn],
            pair_receive.at[kind, turn],
            partner,
        )

    gather.arrive(1)

    @pl.when(inner)
    def _():
        gather.arrive(2)

    gather.to_neighbours(1)
    gather.hand_on(0)

    def one_tile(group, start, size, turn):
        slot = tile_slot(group, turn)
        copy_tile(group, start, size, turn).wait()
        span = pl.ds(pl.multiple_of(place(turn) * piece, piece), piece)
        tokens = pl.ds(pl.multiple_of(start, rows), size)
        upstream, given, positive = held[tokens], inputs[tokens], tile[slot, :, :size]
        if group is depth:
            there = pl.ds(pl.multiple_of((turn - tiles // 2) * piece, piece), piece)
            upstream = jnp.concatenate([upstream, held_last[...]], axis=0)
            given = jnp.concatenate([given, inputs_last[...]], axis=0)
            positive = jnp.concatenate([positive, relu_last[there]], axis=1)
            size = 2 * size
        back = lax.dot_general(dec[span], upstream, LAST_LAST, preferred_element_type=jnp.float32)
        shift = jnp.concatenate([scale[span]] * (size // LANES), axis=1)
        slope = ((back + shift) * (2.0 * positive)).astype(jnp.bfloat16)
        act_low = (positive * positive).astype(jnp.bfloat16)
        wide = slope.astype(jnp.float32)
        folded = wide[:, :LANES]
        for lane in range(LANES, size, LANES):
            folded = folded + wide[:, lane : lane + LANES]
        bias_sum[span] += folded
        enc_sum[span] += jnp.dot(slope, given, preferred_element_type=jnp.float32)
        dec_sum[span] += jnp.dot(act_low, upstream, preferred_element_type=jnp.float32)

    def take_in(group, turn):
        @pl.when((group == 0) & (turn == tiles // 2))
        def _():
            if depth > 3:

                @pl.when(inner)
                def _():
                    gather.arrive(3)

            @pl.when(jnp.logical_not(inner))
            def _():
                gather.arrive(2)

            gather.to_neighbours(2)

        @pl.when((group >= 1) & (turn == 0) & (group + 2 < depth))
        def _():
            @pl.when(jnp.logical_not(inner) | (group >= 2))
            def _():
                gather.arrive(group + 2)

            gather.to_neighbours(group + 2)

        @pl.when((group == depth - 2) & (turn == 0))
        def _():
            gather.hand_on(depth - 1)

        @pl.when(turn == tiles // 2)
        def _():
            gather.wait_diagonal(group)

    def middle_group(group, carry):
        start, size = 4 * group * rows, 4 * rows

        @pl.when(group >= 1)
        def _():
            gather.hand_on(group)

        def one(turn, carry):
            @pl.when(turn + 1 < tiles)
            def _():
                copy_tile(group, start, size, turn + 1).start()

            @pl.when((turn + 1 == tiles) & (group + 2 < depth))
            def _():
                copy_tile(group + 1, start + 4 * rows, size, 0).start()

            @pl.when((turn + 1 == tiles) & (group + 2 == depth))
            def _():
                copy_tile(depth - 1, *group_of(depth - 1), 0).start()

            one_tile(group, start, size, turn)
            take_in(group, turn)
            return carry

        return lax.fori_loop(0, tiles, one, carry)

    def late_group(turn, carry):
        start, size = group_of(depth - 1)

        @pl.when(turn + 1 < tiles)
        def _():
            copy_tile(depth - 1, start, size, turn + 1).start()

        @pl.when(turn + 1 == tiles)
        def _():
            copy_tile(depth, *group_of(depth), tiles // 2).start()

        one_tile(depth - 1, start, size, turn)

        @pl.when(turn < tiles // 2)
        def _():
            span = pl.ds(pl.multiple_of(place(turn) * piece, piece), piece)
            there = pl.ds(pl.multiple_of(turn * piece, piece), piece)
            low[0, there] = enc_sum[span].astype(jnp.bfloat16)
            low[1, there] = dec_sum[span].astype(jnp.bfloat16)
            for kind in range(3):
                pair_copy(kind, turn).start()

        return carry

    def last_group(turn, carry):
        start, size = group_of(depth)

        @pl.when(turn + 1 < tiles)
        def _():
            copy_tile(depth, start, size, turn + 1).start()

        one_tile(depth, start, size, turn)
        return carry

    lax.fori_loop(0, depth - 1, middle_group, 0)
    gather.wait_diagonal(depth - 1)
    last_copies[2].start()
    lax.fori_loop(0, tiles, late_group, 0)
    for copy in last_copies:
        copy.wait_recv()
    lax.fori_loop(tiles // 2, tiles, last_group, 0)

    ours = core * mine
    active_copy.wait_recv()
    span = pl.ds(pl.multiple_of(ours, mine), mine)
    act_total = jnp.sum(active[span] + active_got[...], axis=1, keepdims=True)
    partial = jnp.zeros((8, LANES), jnp.float32)

    stores = []
    rows_of = lax.broadcasted_iota(jnp.int32, (LANES, LANES), 0)
    lanes_of = lax.broadcasted_iota(jnp.int32, (LANES, LANES), 1)
    for turn in range(tiles // 2):
        for kind in range(3):
            pair_copy(kind, turn).wait_recv()
        near = pl.ds(pl.multiple_of(ours + turn * piece, piece), piece)
        there = pl.ds(turn * piece, piece)
        enc_grad = enc_sum[near] + enc_got[there].astype(jnp.float32)
        enc_sum[near] = enc_grad
        partial = partial + fold(enc_grad * enc_grad)
        dec_grad = dec_sum[near] + dec_got[there].astype(jnp.float32)
        dec_grad = dec_grad + (
            COEFFICIENT * COEFFICIENT * act_total[turn * piece : (turn + 1) * piece] / scale[near, :1]
        ) * dec[near].astype(jnp.float32)
        dec_sum[near] = dec_grad
        partial = partial + fold(dec_grad * dec_grad)
        stores += [
            pltpu.make_async_copy(enc_sum.at[near], enc_out.at[there], store_sem.at[0, turn]),
            pltpu.make_async_copy(dec_sum.at[near], dec_out.at[there], store_sem.at[1, turn]),
        ]
        stores[-2].start()
        stores[-1].start()
        bias_grad = jnp.sum(bias_sum[near] + bias_got[there], axis=1, keepdims=True)
        for first in range(0, piece, LANES):
            wide = jnp.broadcast_to(bias_grad[first : first + LANES], (LANES, LANES))
            line = jnp.sum(jnp.where(rows_of == lanes_of, wide, 0.0), axis=0, keepdims=True)
            index = (turn * piece + first) // LANES
            bias_out[index : index + 1] = line
            partial = partial + jnp.where(rows_of[:8] == 0, line * line, 0.0)
    two[1] = partial
    two_copy(1).start()
    for kind in range(2):
        two_copy(kind).wait_recv()
        sums[kind] = two[kind] + two_got[kind]
    for index in range(1, everyone):
        sums_copy(index).start()
    total = sums[...]
    for index in range(1, everyone):
        sums_copy(index).wait_recv()
        total = total + sums_got[index]
    small_out[...] = total[0]
    squares_out[...] = total[1]
    gather.close()
    for index in range(1, everyone):
        sums_copy(index).wait_send()
    for kind in range(2):
        two_copy(kind).wait_send()
    active_copy.wait_send()
    for copy in last_copies:
        copy.wait_send()
    for turn in range(tiles // 2):
        for kind in range(3):
            pair_copy(kind, turn).wait_send()
    for store in stores:
        store.wait()


def backward(depth, own, gathered, relu, dec, scale, active, small):
    rows, width = own.shape
    entries = dec.shape[0]
    mine = entries // 2
    piece = min(512, mine)
    everyone = depth * 4
    bf16, f32 = jnp.bfloat16, jnp.float32
    dma = pltpu.SemaphoreType.DMA
    return pl.pallas_call(
        functools.partial(backward_kernel, depth, everyone),
        out_shape=(
            jax.ShapeDtypeStruct((mine, width), f32),
            jax.ShapeDtypeStruct((mine, width), f32),
            jax.ShapeDtypeStruct((mine // LANES, LANES), f32),
            jax.ShapeDtypeStruct(small.shape, f32),
            jax.ShapeDtypeStruct((8, LANES), f32),
        ),
        in_specs=[ANY] * 7,
        out_specs=(ANY, ANY, VMEM, VMEM, VMEM),
        scratch_shapes=[
            pltpu.VMEM((depth * 4 * rows, width), bf16),
            pltpu.VMEM((depth * 4 * rows, width), bf16),
            pltpu.VMEM((entries, width), bf16),
            pltpu.VMEM((entries, LANES), f32),
            pltpu.VMEM((2, piece, 4 * rows), f32),
            pltpu.VMEM((rows, width), bf16),
            pltpu.VMEM((rows, width), bf16),
            pltpu.VMEM((mine, rows), f32),
            pltpu.VMEM((entries, width), f32),
            pltpu.VMEM((entries, width), f32),
            pltpu.VMEM((entries, LANES), f32),
            pltpu.VMEM((mine, width), bf16),
            pltpu.VMEM((mine, width), bf16),
            pltpu.VMEM((mine, LANES), f32),
            pltpu.VMEM((entries, LANES), f32),
            pltpu.VMEM((mine, LANES), f32),
            pltpu.VMEM((2, mine, width), bf16),
            pltpu.VMEM(small.shape, f32),
            pltpu.VMEM((2, 8, LANES), f32),
            pltpu.VMEM((2, 8, LANES), f32),
            pltpu.VMEM((2, 8, LANES), f32),
            pltpu.VMEM((everyone, 2, 8, LANES), f32),
            dma((6,)),
            dma((2,)),
            dma((2, entries // piece)),
            dma((11, max(depth, 4))),
            dma((9, max(depth, 4))),
            dma((4, entries // piece)),
            dma((4, entries // piece)),
            dma((5,)),
            dma((5,)),
            dma((everyone,)),
            dma((everyone,)),
        ],
        compiler_params=pltpu.CompilerParams(
            collective_id=1, has_side_effects=True, vmem_limit_bytes=60 * 2**20
        ),
        cost_estimate=pl.CostEstimate(
            flops=24 * depth * rows * entries * width, bytes_accessed=16 * depth * rows * entries, transcendentals=0
        ),
        name="backward_blocks",
    )(own, gathered, relu, dec, scale, active, small)


def update_kernel(*refs):
    names = ["enc_grad", "dec_grad", "bias_grad", "small", "squares"]
    for kind in ("enc", "dec", "bias", "shift"):
        names += [kind, kind + "_one", kind + "_two"]
    given = dict(zip(names, refs[: len(names)]))
    made = refs[len(names) : len(names) + 14]
    brought, staged, load_sem, store_sem = refs[len(names) + 14 :]
    mine = given["enc"].shape[0]
    slots, _, piece, _ = staged.shape
    parts = mine // piece
    large = ["enc", "enc_one", "enc_two", "enc_grad", "dec", "dec_one", "dec_two", "dec_grad"]

    def load(part, index):
        span = pl.ds(pl.multiple_of(part * piece, piece), piece)
        slot = part % slots
        return pltpu.make_async_copy(given[large[index]].at[span], brought.at[slot, index], load_sem.at[slot, index])

    for part in range(min(slots - 1, parts)):
        for index in range(8):
            load(part, index).start()
    lines = given["shift"].shape[1] // LANES
    shift_grad = jnp.concatenate([given["small"][line : line + 1] for line in range(lines)], axis=1)
    total = jnp.sum(given["squares"][...], keepdims=True) + jnp.sum(shift_grad * shift_grad, keepdims=True)
    norm = jnp.sqrt(total)
    clip = jnp.minimum(1.0, CLIP_NORM / (norm + 1e-06))
    made[12][...] = norm
    made[13][...] = jnp.sum(given["small"][lines : lines + 1], keepdims=True)

    def store(part, index):
        span = pl.ds(pl.multiple_of(part * piece, piece), piece)
        slot = part % slots
        return pltpu.make_async_copy(staged.at[slot, index], made[index].at[span], store_sem.at[slot, index])

    def one(part, carry):
        @pl.when(part >= slots)
        def _():
            for index in range(6):
                store(part - slots, index).wait()

        @pl.when(part + slots - 1 < parts)
        def _():
            for index in range(8):
                load(part + slots - 1, index).start()

        slot = part % slots
        for index in range(8):
            load(part, index).wait()
        for index in range(2):
            new, first, second = adam_step(
                *(brought[slot, 4 * index + offset] for offset in range(4)),
                clip,
                RATE_MATRIX,
                WEIGHT_DECAY,
            )
            if index:
                new = new * lax.rsqrt(jnp.sum(new * new, axis=1, keepdims=True) + NORM_EPSILON)
            for offset, value in enumerate((new, first, second)):
                staged[slot, 3 * index + offset] = value
        for index in range(6):
            store(part, index).start()
        return carry

    lax.fori_loop(0, parts, one, 0)
    for offset, (kind, gradient) in enumerate((("bias", given["bias_grad"][...]), ("shift", shift_grad))):
        results = adam_step(
            given[kind][...], given[kind + "_one"][...], given[kind + "_two"][...], gradient, clip, RATE_BIAS, 0.0
        )
        for index, value in enumerate(results):
            made[6 + 3 * offset + index][...] = value
    for part in range(max(parts - slots, 0), parts):
        for index in range(6):
            store(part, index).wait()


def update(*arrays):
    f32 = jnp.float32
    mine, width = arrays[0].shape
    dense, flat = (mine // LANES, LANES), (1, width)
    arrays = list(arrays)
    for index in range(11, 14):
        arrays[index] = arrays[index].reshape(dense)
    for index in range(14, 17):
        arrays[index] = arrays[index].reshape(flat)
    piece, slots = min(128, mine), 4
    made = pl.pallas_call(
        update_kernel,
        out_shape=[jax.ShapeDtypeStruct((mine, width), f32)] * 6
        + [jax.ShapeDtypeStruct(dense, f32)] * 3
        + [jax.ShapeDtypeStruct(flat, f32)] * 3
        + [jax.ShapeDtypeStruct((1, 1), f32)] * 2,
        in_specs=[ANY] * 2 + [VMEM] * 3 + [ANY] * 6 + [VMEM] * 6,
        out_specs=[ANY] * 6 + [VMEM] * 8,
        scratch_shapes=[
            pltpu.VMEM((slots, 8, piece, width), f32),
            pltpu.VMEM((slots, 6, piece, width), f32),
            pltpu.SemaphoreType.DMA((slots, 8)),
            pltpu.SemaphoreType.DMA((slots, 6)),
        ],
        compiler_params=pltpu.CompilerParams(vmem_limit_bytes=60 * 2**20),
        cost_estimate=pl.CostEstimate(flops=60 * mine * width, bytes_accessed=56 * mine * width, transcendentals=4 * mine * width),
        name="update",
    )(*arrays)
    return (
        *made[:6],
        *(value.reshape(mine) for value in made[6:9]),
        *(value.reshape(width) for value in made[9:12]),
        made[12].reshape(()),
        made[13].reshape(()),
    )


def body(
    depth,
    token_ids,
    doc_ids,
    embed,
    norm_gains,
    norm_shifts,
    qkv_weight,
    out_weight,
    up_weight,
    down_weight,
    proj_biases,
    enc_weight,
    dec_weight,
    enc_bias,
    dec_bias,
    enc_first,
    enc_second,
    dec_first,
    dec_second,
    enc_bias_first,
    enc_bias_second,
    dec_bias_first,
    dec_bias_second,
):
    model_width = norm_gains.shape[1]
    all_ids, all_docs = gather_ids(token_ids, doc_ids, model_width // embed.shape[1])
    arguments = (
        pick(all_ids, embed.T),
        all_docs,
        norm_gains,
        norm_shifts,
        qkv_weight,
        out_weight,
        up_weight,
        down_weight,
        proj_biases.reshape(-1, LANES),
        enc_weight,
        dec_weight,
        enc_bias,
    )
    if depth <= 4:
        dec_both, scale_wide, gathered, relu, upstream, small, active = joint(depth, *arguments, dec_bias[None])
    else:
        low, stream, enc_both, dec_both, dec_turned, shift_wide, scale_wide = front(*arguments)
        gathered, relu, upstream, small, active = forward(
            depth, low, enc_both, dec_turned, shift_wide, stream, scale_wide, dec_bias[None]
        )
    enc_grad, dec_grad, enc_bias_grad, small_sum, squares = backward(
        depth, upstream, gathered, relu, dec_both, scale_wide, active, small
    )
    return update(
        enc_grad,
        dec_grad,
        enc_bias_grad,
        small_sum,
        squares,
        enc_weight,
        enc_first,
        enc_second,
        dec_weight,
        dec_first,
        dec_second,
        enc_bias,
        enc_bias_first,
        enc_bias_second,
        dec_bias,
        dec_bias_first,
        dec_bias_second,
    )


def solution(mesh):
    split = P(("dp", "seq", "opt"), None)
    split_vector = P(("dp", "seq", "opt"))
    in_specs = (
        P("dp", ("seq", "opt")),
        P("dp", ("seq", "opt")),
        P(None, ("seq", "opt")),
        P(),
        P(),
        P(),
        P(),
        P(),
        P(),
        P(),
        split,
        split,
        split_vector,
        P(),
        split,
        split,
        split,
        split,
        split_vector,
        split_vector,
        P(),
        P(),
    )
    out_specs = (split,) * 6 + (split_vector,) * 3 + (P(),) * 5
    return jax.shard_map(
        functools.partial(body, mesh.shape["dp"]),
        mesh=mesh,
        in_specs=in_specs,
        out_specs=out_specs,
        check_vma=False,
    )
```
